32 devices in a mesh: grp: 2 (over y), garm: 4 (over z), body: 2 (over x), frame: 2 (over core).
Axes of the slice: x: 2, y: 2, z: 4, core: 2. Of those that a mesh axis runs over, the one named last changes fastest.
Arguments:
- garment: float32 [4, 3, 32768], P(('grp', 'frame'), None, ('garm', 'body')), parts along dimension 0, may hold values from -6 to 6
- cotangent: float32 [4, 32768], P(('grp', 'frame'), ('garm', 'body')), parts along dimension 0, may hold values from -6 to 6
- body_points: float32 [4, 3, 16384], P(('grp', 'frame'), None, ('garm', 'body')), parts along dimension 0, may hold values from -6 to 6
- stiffness: float32 [32768], P(('grp', 'garm', 'body')), parts along dimension 0, may hold values from 0.2 to 2
- pair_garment: int32 [4, 8, 8, 4], P(('grp', 'frame'), ('garm', 'body')), parts along dimension 0, may hold values from 0 to 31
- pair_body: int32 [4, 8, 8, 4], P(('grp', 'frame'), ('garm', 'body')), parts along dimension 0, may hold values from 0 to 15
- pair_count: int32 [4, 8, 8], P(('grp', 'frame'), ('garm', 'body')), parts along dimension 0, may hold values from 0 to 4, as said below
Outputs:
- garment_grad: float32 [4, 3, 32768], P(('grp', 'frame'), None, ('garm', 'body')), parts along dimension 0
- body_grad: float32 [4, 3, 16384], P(('grp', 'frame'), None, ('garm', 'body')), parts along dimension 0
- stiffness_grad: float32 [32768], P(('grp', 'garm', 'body')), parts along dimension 0
The draws below stay inside these ranges and needn't reach their ends.
There are 2 independent parts, one for each index of `grp`. The reference program is written for one: setup_inputs(seed, part) draws one part's arguments, and reference() takes and returns one part's arrays. A program takes and returns all parts, laid end to end along the dimension named above; each array names one. Nothing has to cross between parts.
Inputs may be any that keep to these rules, and one draw needn't show every extreme that they name: pair_count gives the live slots; in every frame one receiving owner gets 4 live slots from every sending owner. `pair_garment`: slots at or past the count are unused and hold arbitrary block numbers. `pair_body`: slots at or past the count are unused and hold arbitrary block numbers.
All inputs are finite; a program needn't handle non-finite values.
Results may differ from the reference program's by a relative error of at most 0.00016.
Values sent between devices are 32-bit elements; how exact they have to be, the bound alone decides.
No kernel may reach another device: no remote copies, remote signals or barrier semaphores. Data moves between devices by JAX's collectives and lax.ppermute only.
A program may use at most 64 MiB of HBM per device.

```python
import math
import jax
import jax.numpy as jnp
from jax import lax

BLOCK = 128
CAP = 4
GB_DEV = 32
BB_DEV = 16
OWNERS = 8
FRAMES = 2
VERTS = 32768
POINTS = 16384


def draw_pair_count(key, part):
    key_level = jax.random.fold_in(key, 11)
    key_raw = jax.random.fold_in(key, 12)
    key_hot = jax.random.fold_in(key, 13)
    level = jax.random.randint(key_level, (FRAMES, 1, OWNERS), 1, CAP + 1)
    raw_draw = jax.random.randint(key_raw, (FRAMES, OWNERS, OWNERS), 0, 2 * CAP + 1)
    counts = jnp.minimum(raw_draw * level // CAP, CAP)
    hottest = jax.random.randint(key_hot, (FRAMES, 1, 1), 0, OWNERS)
    owner_ids = jnp.arange(OWNERS, dtype=jnp.int32)[None, None, :]
    counts = jnp.where(owner_ids == hottest, CAP, counts)
    return counts.astype(jnp.int32)


def set_ends(values, rng, smallest, top_value):
    dims = values.shape
    spot = [jax.random.randint(jax.random.fold_in(rng, axis), (), 0, dims[axis]) for axis in range(len(dims))]
    values = values.at[tuple(spot)].set(smallest)
    longest = dims.index(max(dims))
    spot[longest] = (spot[longest] + 1) % dims[longest]
    return values.at[tuple(spot)].set(top_value)


def block_levels(own_key, extent, split, smallest, top_value):
    def one(position, blocks):
        draws = jax.random.uniform(jax.random.fold_in(jax.random.fold_in(own_key, 6), position), (blocks,), jnp.float32, smallest / len(split), top_value / len(split))
        return jnp.repeat(jnp.exp(draws), extent[position] // blocks).reshape((-1,) + (1,) * (len(extent) - position - 1))

    level = one(*split[0])
    for cut in split[1:]:
        level = level * one(*cut)
    return level


def centred(stream_key, shape, spread, reach, split=(), kind=jnp.bfloat16):
    result = jax.random.normal(stream_key, shape, jnp.float32) * spread
    if len(split) > 0:
        result = block_levels(stream_key, shape, split, -0.22, 0.18) * result
    return jnp.clip(result, min=-reach, max=reach).astype(kind)


def setup_inputs(seed: int = 0, part: int = 0) -> dict:
    streams_of = jax.random.split(jax.random.key(seed), 8)
    part_splits = jax.random.split(jax.random.fold_in(streams_of[7], part), 8)
    return {
        "garment": centred(part_splits[0], (FRAMES, 3, VERTS), 1.0, 6.0, ((0, 2), (2, 8)), jnp.float32),
        "cotangent": centred(part_splits[1], (FRAMES, VERTS), 1.0, 6.0, ((0, 2), (1, 8)), jnp.float32),
        "body_points": centred(part_splits[2], (FRAMES, 3, POINTS), 1.0, 6.0, ((0, 2), (2, 8)), jnp.float32),
        "stiffness": jnp.clip(jnp.exp(math.log(2.0) - 2.3025851 * jax.random.uniform(part_splits[3], (POINTS,), jnp.float32) ** block_levels(part_splits[3], (POINTS,), ((0, 8),), -0.2, 0.2)), 0.2, 2.0),
        "pair_garment": set_ends(jax.random.randint(part_splits[4], (FRAMES, OWNERS, OWNERS, CAP), 0, GB_DEV), jax.random.fold_in(part_splits[4], 1), 0, GB_DEV - 1).astype(jnp.int32),
        "pair_body": set_ends(jax.random.randint(part_splits[5], (FRAMES, OWNERS, OWNERS, CAP), 0, BB_DEV), jax.random.fold_in(part_splits[5], 1), 0, BB_DEV - 1).astype(jnp.int32),
        "pair_count": draw_pair_count(jax.random.fold_in(jax.random.fold_in(streams_of[7], part), 71), part),
    }


amplitude = 0.05
width_sq = 4.0


def pair_terms(garm_pos, cot_vals, body_pos, stiff_vals):
    distance = jnp.zeros((garm_pos.shape[0], garm_pos.shape[2], body_pos.shape[2]), jnp.float32)
    for coord in range(3):
        delta = garm_pos[:, coord, :, None] - body_pos[:, coord, None, :]
        distance = distance + delta * delta
    kernel = jnp.exp(-distance / width_sq)
    coupled = amplitude * cot_vals[:, :, None] * stiff_vals[:, None, :] * kernel
    row_sums = jnp.sum(coupled, axis=2)
    col_sums = jnp.sum(coupled, axis=1)
    pulled_body = jnp.einsum('nij,naj->nai', coupled, body_pos, precision=lax.Precision.HIGHEST)
    pulled_garm = jnp.einsum('nij,nai->naj', coupled, garm_pos, precision=lax.Precision.HIGHEST)
    factor = -2.0 / width_sq
    garm_grad = factor * (garm_pos * row_sums[:, None, :] - pulled_body)
    body_part = factor * (body_pos * col_sums[:, None, :] - pulled_garm)
    stiff_part = amplitude * jnp.einsum('ni,nij->nj', cot_vals, kernel, precision=lax.Precision.HIGHEST)
    return garm_grad, body_part, stiff_part


def reference(garment, cotangent, body_points, stiffness, pair_garment, pair_body, pair_count):
    owners = OWNERS
    garm_blocks = owners * GB_DEV
    body_blocks = owners * BB_DEV
    slot_ids = jnp.arange(CAP, dtype=jnp.int32)
    is_live = (slot_ids[None, None, None, :] < pair_count[:, :, :, None]).astype(jnp.float32)
    source = jnp.arange(owners, dtype=jnp.int32)[None, :, None, None]
    target = jnp.arange(owners, dtype=jnp.int32)[None, None, :, None]
    garm_index = (source * GB_DEV + pair_garment).astype(jnp.int32).reshape(FRAMES, owners, owners * CAP)
    body_index = (target * BB_DEV + pair_body).astype(jnp.int32).reshape(FRAMES, owners, owners * CAP)
    weight = is_live.reshape(FRAMES, owners, owners * CAP)
    garm_table = garment.reshape(FRAMES, 3, garm_blocks, BLOCK).transpose(0, 2, 1, 3)
    cot_table = cotangent.reshape(FRAMES, garm_blocks, BLOCK)
    body_table = body_points.reshape(FRAMES, 3, body_blocks, BLOCK).transpose(0, 2, 1, 3)
    stiff_table = stiffness.reshape(body_blocks, BLOCK)
    garm_out = []
    body_out = []
    stiff_total = jnp.zeros((body_blocks, BLOCK), jnp.float32)
    for frame_idx in range(FRAMES):
        garm_here = garm_table[frame_idx]
        cot_here = cot_table[frame_idx]
        body_here = body_table[frame_idx]

        def advance(running, inputs):
            garm_acc, body_acc, stiff_acc = running
            garm_ids, body_ids, live_wt = inputs
            garm_grad, body_part, stiff_part = pair_terms(garm_here[garm_ids], cot_here[garm_ids] * live_wt[:, None], body_here[body_ids], stiff_table[body_ids])
            return (garm_acc.at[garm_ids].add(garm_grad), body_acc.at[body_ids].add(body_part), stiff_acc.at[body_ids].add(stiff_part)), None

        start = (jnp.zeros((garm_blocks, 3, BLOCK), jnp.float32), jnp.zeros((body_blocks, 3, BLOCK), jnp.float32), jnp.zeros((body_blocks, BLOCK), jnp.float32))
        (garm_acc, body_acc, stiff_acc), _ = lax.scan(advance, start, (garm_index[frame_idx], body_index[frame_idx], weight[frame_idx]))
        garm_out.append(garm_acc.transpose(1, 0, 2).reshape(3, garm_blocks * BLOCK))
        body_out.append(body_acc.transpose(1, 0, 2).reshape(3, body_blocks * BLOCK))
        stiff_total = stiff_total + stiff_acc
    return jnp.stack(garm_out), jnp.stack(body_out), stiff_total.reshape(body_blocks * BLOCK)
```

```python
import math

import jax
import jax.numpy as jnp
from jax import lax
from jax.experimental import pallas as pl
from jax.experimental.pallas import tpu as pltpu
from jax.sharding import PartitionSpec as P

BLOCK = 128
SUB = 8

amplitude = 0.05
width_sq = 4.0

SCALE = math.sqrt(math.log2(math.e) / width_sq)
FACTOR = -2.0 / width_sq * amplitude

f32 = jnp.float32
bf16 = jnp.bfloat16


def pieces(value, count):
    out = []
    for _ in range(count - 1):
        top = value.astype(bf16).astype(f32)
        out.append(top)
        value = value - top
    out.append(value)
    return out


def features(left, right):
    lpos = [left[c] * SCALE for c in range(3)]
    rpos = [right[c] * SCALE for c in range(3)]
    lnorm = -(lpos[0] * lpos[0] + lpos[1] * lpos[1] + lpos[2] * lpos[2])
    rnorm = -(rpos[0] * rpos[0] + rpos[1] * rpos[1] + rpos[2] * rpos[2])
    one = jnp.ones_like(lnorm)
    lrows, rrows = [], []
    for c in range(3):
        l1, l2, l3 = pieces(lpos[c] * 2.0, 3)
        r1, r2, r3 = pieces(rpos[c], 3)
        lrows += [l1, l1, l2, l2, l1, l3]
        rrows += [r1, r2, r1, r2, r3, r1]
    lrows += pieces(lnorm, 3) + [one] * 3
    rrows += [one] * 3 + pieces(rnorm, 3)
    return (
        jnp.concatenate(lrows, axis=0).astype(bf16),
        jnp.concatenate(rrows, axis=0).astype(bf16),
    )


def pull(left, right):
    lfeat, rfeat = features(left, right)
    depth = lfeat.shape[0]
    weight = left[3]
    coeff = jnp.concatenate([weight * left[c] for c in range(3)] + [weight], axis=0)
    chi, clo = pieces(coeff, 2)
    chi, clo = chi.astype(bf16), clo.astype(bf16)
    lhs = jnp.concatenate(
        [
            jnp.concatenate([chi, chi], axis=1),
            jnp.concatenate([clo, jnp.zeros_like(clo)], axis=1),
        ],
        axis=0,
    )
    lfeat_t = lfeat.T
    row = lax.broadcasted_iota(jnp.int32, (depth, BLOCK), 0) % SUB
    sub = lax.broadcasted_iota(jnp.int32, (4 * SUB, BLOCK), 0) % SUB
    total = jnp.zeros((4 * SUB, BLOCK), f32)
    for pair in range(0, SUB, 2):
        rhs = jnp.concatenate(
            [rfeat * (row == pair + k).astype(f32).astype(bf16) for k in range(2)], axis=1
        )
        exponent = jnp.dot(lfeat_t, rhs, preferred_element_type=f32)
        kernel = jnp.exp2(exponent)
        khi = kernel.astype(bf16)
        klo = (kernel - khi.astype(f32)).astype(bf16)
        sums = jnp.dot(lhs, jnp.concatenate([khi, klo], axis=0), preferred_element_type=f32)
        sums = sums[: 4 * SUB] + sums[4 * SUB :]
        for k in range(2):
            total = jnp.where(sub == pair + k, sums[:, k * BLOCK : (k + 1) * BLOCK], total)
    return [total[c * SUB : (c + 1) * SUB] for c in range(4)]


def run_batches(left_ref, right_ref, grad_ref):
    batches = left_ref.shape[1] // SUB

    def step(k, carry):
        rows = pl.ds(pl.multiple_of(k * SUB, SUB), SUB)
        left = [left_ref[c, rows, :] for c in range(4)]
        right = [right_ref[c, rows, :] for c in range(4)]
        total = pull(left, right)
        for c in range(3):
            grad_ref[rows, c * BLOCK : (c + 1) * BLOCK] = (
                FACTOR * right[3] * (right[c] * total[3] - total[c])
            )
        grad_ref[rows, 3 * BLOCK :] = amplitude * total[3]
        return carry

    if batches <= 4:
        for k in range(batches):
            step(k, 0)
    else:
        lax.fori_loop(0, batches, step, 0)


def scatter(index, grad_ref, blocks):
    lane = lax.broadcasted_iota(jnp.int32, index.shape, 1).astype(f32)
    onehot_t = (index == lane).astype(f32).T[:blocks].astype(bf16)
    parts = [
        jnp.dot(onehot_t, part.astype(bf16), preferred_element_type=f32)
        for part in pieces(grad_ref[...], 3)
    ]
    return parts[0] + parts[1] + parts[2]


def pack_kernel(pg_ref, pb_ref, pc_ref, garm_ref, cot_ref, body_ref, stiff_ref, out_ref):
    cap, owners = pg_ref.shape
    tiles = stiff_ref.shape[0] // cap

    def one(d, carry):
        for s in range(cap):
            row = pl.ds(pg_ref[s, d], 1)
            for c in range(3):
                out_ref[d, c, s : s + 1, :] = garm_ref[c, row, :]
            out_ref[d, 3, s : s + 1, :] = jnp.where(s < pc_ref[0, d], cot_ref[row, :], 0.0)
            out_ref[d, 4 + 4 * tiles, s : s + 1, :] = jnp.full(
                (1, BLOCK), pb_ref[s, d].astype(f32), f32
            )
        for q in range(tiles):
            rows = slice(q * cap, (q + 1) * cap)
            for c in range(3):
                out_ref[d, 4 + c * tiles + q] = body_ref[c, rows, :]
            out_ref[d, 4 + 3 * tiles + q] = stiff_ref[rows, :]
        return carry

    if owners <= 8:
        for d in range(owners):
            one(d, 0)
    else:
        lax.fori_loop(0, owners, one, 0)


def over(count, fn):
    if count <= 8:
        for d in range(count):
            fn(d)
    else:
        lax.fori_loop(0, count, lambda d, carry: (fn(d), carry)[1], 0)


def body_kernel(own_ref, in_ref, out_ref, stiff_ref, left, right, table, index, grad):
    owners, tiles, cap, _ = in_ref.shape
    blocks = tiles - 5

    def take(d):
        rows = pl.ds(d * cap, cap)
        for c in range(4):
            left[c, rows, :] = in_ref[d, c]
        index[rows, :] = in_ref[d, tiles - 1]

    over(owners, take)
    for c in range(4):
        for q in range(blocks // 4):
            table[4 * q : 4 * q + 4, c * BLOCK : (c + 1) * BLOCK] = own_ref[
                0, 4 + c * (blocks // 4) + q
            ]
    lane = lax.broadcasted_iota(jnp.int32, index.shape, 1).astype(f32)
    onehot = (index[...] == lane).astype(f32)[:, :blocks].astype(bf16)
    chosen = [
        jnp.dot(onehot, part.astype(bf16), preferred_element_type=f32)
        for part in pieces(table[...], 3)
    ]
    chosen = chosen[0] + chosen[1] + chosen[2]
    for c in range(4):
        right[c] = chosen[:, c * BLOCK : (c + 1) * BLOCK]
    run_batches(left, right, grad)
    total = scatter(index[...], grad, blocks)
    for c in range(3):
        out_ref[c] = total[:, c * BLOCK : (c + 1) * BLOCK]
    stiff_ref[...] = total[:, 3 * BLOCK :]


def garm_kernel(pg_ref, pb_ref, own_ref, in_ref, out_ref, left, right, index, grad):
    owners, tiles, cap, _ = in_ref.shape
    blocks = tiles - 5
    garm_blocks = out_ref.shape[1]

    def take(d):
        rows = pl.ds(d * cap, cap)
        for c in range(4):
            right[c, rows, :] = own_ref[d, c]
        for s in range(cap):
            b = pb_ref[s, d]
            for c in range(4):
                left[c, pl.ds(d * cap + s, 1), :] = in_ref[
                    d, 4 + c * (blocks // 4) + b // 4, pl.ds(b % 4, 1), :
                ]
            index[pl.ds(d * cap + s, 1), :] = jnp.full((1, BLOCK), pg_ref[s, d].astype(f32), f32)

    over(owners, take)
    run_batches(left, right, grad)
    total = scatter(index[...], grad, garm_blocks)
    for c in range(3):
        out_ref[c] = total[:, c * BLOCK : (c + 1) * BLOCK]


def call(kernel, out_shape, scratch, scalars, arrays):
    specs = [pl.BlockSpec(memory_space=pltpu.SMEM)] * len(scalars)
    specs += [pl.BlockSpec(memory_space=pltpu.VMEM)] * len(arrays)
    return pl.pallas_call(
        kernel,
        out_shape=out_shape,
        in_specs=specs,
        out_specs=jax.tree.map(lambda _: pl.BlockSpec(memory_space=pltpu.VMEM), out_shape),
        scratch_shapes=scratch,
        compiler_params=pltpu.CompilerParams(vmem_limit_bytes=32 * 1024 * 1024),
    )(*scalars, *arrays)


def per_device(garment, cotangent, body_points, stiffness, pair_garment, pair_body, pair_count):
    owners = lax.axis_size(("garm", "body"))
    verts = garment.shape[2]
    points = body_points.shape[2]
    blocks = points // BLOCK
    cap = pair_garment.shape[3]
    slots = owners * cap
    pg = pair_garment.reshape(owners, cap).T
    pb = pair_body.reshape(owners, cap).T
    pc = pair_count.reshape(1, owners)
    message = call(
        pack_kernel,
        jax.ShapeDtypeStruct((owners, 5 + blocks, cap, BLOCK), f32),
        [],
        (pg, pb, pc),
        (
            garment.reshape(3, verts // BLOCK, BLOCK),
            cotangent.reshape(verts // BLOCK, BLOCK),
            body_points.reshape(3, blocks, BLOCK),
            stiffness.reshape(blocks, BLOCK),
        ),
    )
    arrived = lax.all_to_all(message, ("garm", "body"), split_axis=0, concat_axis=0, tiled=True)
    rows = pltpu.VMEM((4, slots, BLOCK), f32)
    grad = pltpu.VMEM((slots, 4 * BLOCK), f32)
    index = pltpu.VMEM((slots, BLOCK), f32)
    body_grad, stiff = call(
        body_kernel,
        (
            jax.ShapeDtypeStruct((3, blocks, BLOCK), f32),
            jax.ShapeDtypeStruct((blocks, BLOCK), f32),
        ),
        [rows, rows, pltpu.VMEM((blocks, 4 * BLOCK), f32), index, grad],
        (),
        (message, arrived),
    )
    other = lax.ppermute(stiff, "frame", [(0, 1), (1, 0)])
    garm_grad = call(
        garm_kernel,
        jax.ShapeDtypeStruct((3, verts // BLOCK, BLOCK), f32),
        [rows, rows, index, grad],
        (pg, pb),
        (message, arrived),
    )
    return (
        garm_grad.reshape(1, 3, verts),
        body_grad.reshape(1, 3, points),
        (stiff + other).reshape(points),
    )


def solution(mesh):
    in_specs = (
        P(("grp", "frame"), None, ("garm", "body")),
        P(("grp", "frame"), ("garm", "body")),
        P(("grp", "frame"), None, ("garm", "body")),
        P(("grp", "garm", "body")),
        P(("grp", "frame"), ("garm", "body"), None, None),
        P(("grp", "frame"), ("garm", "body"), None, None),
        P(("grp", "frame"), ("garm", "body"), None),
    )
    out_specs = (
        P(("grp", "frame"), None, ("garm", "body")),
        P(("grp", "frame"), None, ("garm", "body")),
        P(("grp", "garm", "body")),
    )
    return jax.shard_map(
        per_device, mesh=mesh, in_specs=in_specs, out_specs=out_specs, check_vma=False
    )
```

```python
import functools
import math

import jax
import jax.numpy as jnp
from jax import lax
from jax.experimental import pallas as pl
from jax.experimental.pallas import tpu as pltpu
from jax.sharding import PartitionSpec as P

BLOCK = 128
SUB = 8

amplitude = 0.05
width_sq = 4.0

SCALE = math.sqrt(math.log2(math.e) / width_sq)
FACTOR = -2.0 / width_sq * amplitude

f32 = jnp.float32
bf16 = jnp.bfloat16


def pieces(value, count):
    out = []
    for _ in range(count - 1):
        top = value.astype(bf16).astype(f32)
        out.append(top)
        value = value - top
    out.append(value)
    return out


def features(left, right):
    lpos = [left[c] * SCALE for c in range(3)]
    rpos = [right[c] * SCALE for c in range(3)]
    lnorm = -(lpos[0] * lpos[0] + lpos[1] * lpos[1] + lpos[2] * lpos[2])
    rnorm = -(rpos[0] * rpos[0] + rpos[1] * rpos[1] + rpos[2] * rpos[2])
    one = jnp.ones_like(lnorm)
    lrows, rrows = [], []
    for c in range(3):
        l1, l2, l3 = pieces(lpos[c] * 2.0, 3)
        r1, r2, r3 = pieces(rpos[c], 3)
        lrows += [l1, l1, l2, l2, l1, l3]
        rrows += [r1, r2, r1, r2, r3, r1]
    lrows += pieces(lnorm, 3) + [one] * 3
    rrows += [one] * 3 + pieces(rnorm, 3)
    return (
        jnp.concatenate(lrows, axis=0).astype(bf16),
        jnp.concatenate(rrows, axis=0).astype(bf16),
    )


def pull(left, right):
    lfeat, rfeat = features(left, right)
    depth = lfeat.shape[0]
    weight = left[3]
    coeff = jnp.concatenate([weight * left[c] for c in range(3)] + [weight], axis=0)
    chi, clo = pieces(coeff, 2)
    chi, clo = chi.astype(bf16), clo.astype(bf16)
    lhs = jnp.concatenate(
        [
            jnp.concatenate([chi, chi], axis=1),
            jnp.concatenate([clo, jnp.zeros_like(clo)], axis=1),
        ],
        axis=0,
    )
    lfeat_t = lfeat.T
    row = lax.broadcasted_iota(jnp.int32, (depth, BLOCK), 0) % SUB
    sub = lax.broadcasted_iota(jnp.int32, (4 * SUB, BLOCK), 0) % SUB
    total = jnp.zeros((4 * SUB, BLOCK), f32)
    for pair in range(0, SUB, 2):
        rhs = jnp.concatenate(
            [rfeat * (row == pair + k).astype(f32).astype(bf16) for k in range(2)], axis=1
        )
        exponent = jnp.dot(lfeat_t, rhs, preferred_element_type=f32)
        kernel = jnp.exp2(exponent)
        khi = kernel.astype(bf16)
        klo = (kernel - khi.astype(f32)).astype(bf16)
        sums = jnp.dot(lhs, jnp.concatenate([khi, klo], axis=0), preferred_element_type=f32)
        sums = sums[: 4 * SUB] + sums[4 * SUB :]
        for k in range(2):
            total = jnp.where(sub == pair + k, sums[:, k * BLOCK : (k + 1) * BLOCK], total)
    return [total[c * SUB : (c + 1) * SUB] for c in range(4)]


def gradients(left, right):
    total = pull(left, right)
    out = [FACTOR * right[3] * (right[c] * total[3] - total[c]) for c in range(3)]
    return out + [amplitude * total[3]]


def run_batches(left_ref, right_ref, grad_ref):
    batches = left_ref.shape[1] // SUB

    def step(k, carry):
        rows = pl.ds(pl.multiple_of(k * SUB, SUB), SUB)
        left = [left_ref[c, rows, :] for c in range(4)]
        right = [right_ref[c, rows, :] for c in range(4)]
        for c, value in enumerate(gradients(left, right)):
            grad_ref[rows, c * BLOCK : (c + 1) * BLOCK] = value
        return carry

    if batches <= 4:
        for k in range(batches):
            step(k, 0)
    else:
        lax.fori_loop(0, batches, step, 0)


def scatter(index, grads, blocks):
    lane = lax.broadcasted_iota(jnp.int32, index.shape, 1).astype(f32)
    onehot_t = (index == lane).astype(f32).T[:blocks].astype(bf16)
    parts = [
        jnp.dot(onehot_t, part.astype(bf16), preferred_element_type=f32)
        for part in pieces(grads, 3)
    ]
    return parts[0] + parts[1] + parts[2]


def pack_kernel(pg_ref, pb_ref, pc_ref, garm_ref, cot_ref, body_ref, stiff_ref, out_ref):
    cap, owners = pg_ref.shape
    tiles = stiff_ref.shape[0] // cap

    def one(d, carry):
        for s in range(cap):
            row = pl.ds(pg_ref[s, d], 1)
            for c in range(3):
                out_ref[d, c, s : s + 1, :] = garm_ref[c, row, :]
            out_ref[d, 3, s : s + 1, :] = jnp.where(s < pc_ref[0, d], cot_ref[row, :], 0.0)
            out_ref[d, 4 + 4 * tiles, s : s + 1, :] = jnp.full(
                (1, BLOCK), pb_ref[s, d].astype(f32), f32
            )
        for q in range(tiles):
            rows = slice(q * cap, (q + 1) * cap)
            for c in range(3):
                out_ref[d, 4 + c * tiles + q] = body_ref[c, rows, :]
            out_ref[d, 4 + 3 * tiles + q] = stiff_ref[rows, :]
        return carry

    if owners <= 8:
        for d in range(owners):
            one(d, 0)
    else:
        lax.fori_loop(0, owners, one, 0)


def over(count, fn):
    if count <= 8:
        for d in range(count):
            fn(d)
    else:
        lax.fori_loop(0, count, lambda d, carry: (fn(d), carry)[1], 0)


def body_kernel(own_ref, in_ref, out_ref, stiff_ref, left, right, table, index, grad):
    owners, tiles, cap, _ = in_ref.shape
    blocks = tiles - 5

    def take(d):
        rows = pl.ds(d * cap, cap)
        for c in range(4):
            left[c, rows, :] = in_ref[d, c]
        index[rows, :] = in_ref[d, tiles - 1]

    over(owners, take)
    for c in range(4):
        for q in range(blocks // 4):
            table[4 * q : 4 * q + 4, c * BLOCK : (c + 1) * BLOCK] = own_ref[
                0, 4 + c * (blocks // 4) + q
            ]
    lane = lax.broadcasted_iota(jnp.int32, index.shape, 1).astype(f32)
    onehot = (index[...] == lane).astype(f32)[:, :blocks].astype(bf16)
    chosen = [
        jnp.dot(onehot, part.astype(bf16), preferred_element_type=f32)
        for part in pieces(table[...], 3)
    ]
    chosen = chosen[0] + chosen[1] + chosen[2]
    for c in range(4):
        right[c] = chosen[:, c * BLOCK : (c + 1) * BLOCK]
    run_batches(left, right, grad)
    total = scatter(index[...], grad[...], blocks)
    for c in range(3):
        out_ref[c] = total[:, c * BLOCK : (c + 1) * BLOCK]
    stiff_ref[...] = total[:, 3 * BLOCK :]


def garm_kernel(pg_ref, pb_ref, own_ref, in_ref, out_ref, left, right, index, grad):
    owners, tiles, cap, _ = in_ref.shape
    blocks = tiles - 5
    garm_blocks = out_ref.shape[1]

    def take(d):
        rows = pl.ds(d * cap, cap)
        for c in range(4):
            right[c, rows, :] = own_ref[d, c]
        for s in range(cap):
            b = pb_ref[s, d]
            for c in range(4):
                left[c, pl.ds(d * cap + s, 1), :] = in_ref[
                    d, 4 + c * (blocks // 4) + b // 4, pl.ds(b % 4, 1), :
                ]
            index[pl.ds(d * cap + s, 1), :] = jnp.full((1, BLOCK), pg_ref[s, d].astype(f32), f32)

    over(owners, take)
    run_batches(left, right, grad)
    total = scatter(index[...], grad[...], garm_blocks)
    for c in range(3):
        out_ref[c] = total[:, c * BLOCK : (c + 1) * BLOCK]


def read_table(message_ref):
    tiles = (message_ref.shape[0] - 5) // 4
    columns = []
    for c in range(4):
        start = 4 + c * tiles
        columns.append(jnp.concatenate([message_ref[start + q] for q in range(tiles)], axis=0))
    return jnp.concatenate(columns, axis=1)


def choose(index, table):
    lane = lax.broadcasted_iota(jnp.int32, index.shape, 1).astype(f32)
    onehot = (index == lane).astype(f32)[:, : table.shape[0]].astype(bf16)
    parts = [
        jnp.dot(onehot, part.astype(bf16), preferred_element_type=f32)
        for part in pieces(table, 3)
    ]
    rows = parts[0] + parts[1] + parts[2]
    return [rows[:, c * BLOCK : (c + 1) * BLOCK] for c in range(4)]


def mix(same_ref, other_ref, tile):
    row = lax.broadcasted_iota(jnp.int32, (SUB, BLOCK), 0)
    return jnp.where(row < SUB // 2, same_ref[tile], other_ref[tile])


def body_batch(same_ref, other_ref, own_ref):
    left = [mix(same_ref, other_ref, c) for c in range(4)]
    index = mix(same_ref, other_ref, same_ref.shape[0] - 1)
    right = choose(index, read_table(own_ref))
    return jnp.concatenate(gradients(left, right), axis=1), index


def garm_batch(same_ref, other_ref, sent_ref):
    right = [sent_ref[c] for c in range(4)]
    same, other = read_table(same_ref), read_table(other_ref)
    row = lax.broadcasted_iota(jnp.int32, (SUB, BLOCK), 0)
    index = sent_ref[sent_ref.shape[0] - 1]
    index = index + jnp.where(row < SUB // 2, 0, same.shape[0]).astype(f32)
    left = choose(index, jnp.concatenate([same, other], axis=0))
    return jnp.concatenate(gradients(left, right)[:3], axis=1)


def both_kernel(same_ref, other_ref, own_ref, sent_ref, bgrad_ref, bindex_ref, ggrad_ref):
    bgrad_ref[...], bindex_ref[...] = body_batch(same_ref, other_ref, own_ref)
    ggrad_ref[...] = garm_batch(same_ref, other_ref, sent_ref)


def last_body_kernel(same_ref, other_ref, own_ref, *refs):
    *earlier, out_ref, stiff_ref = refs
    grad, index = body_batch(same_ref, other_ref, own_ref)
    count = len(earlier) // 2
    grads = jnp.concatenate([ref[...] for ref in earlier[:count]] + [grad], axis=0)
    index = jnp.concatenate([ref[...] for ref in earlier[count:]] + [index], axis=0)
    total = scatter(index, grads, out_ref.shape[1])
    for c in range(3):
        out_ref[c] = total[:, c * BLOCK : (c + 1) * BLOCK]
    stiff_ref[...] = total[:, 3 * BLOCK :]


def last_garm_kernel(same_ref, other_ref, sent_ref, index_ref, *refs):
    *earlier, out_ref = refs
    grad = garm_batch(same_ref, other_ref, sent_ref)
    grads = jnp.concatenate([ref[...] for ref in earlier] + [grad], axis=0)
    index = jnp.concatenate([index_ref[k] for k in range(index_ref.shape[0])], axis=0)
    total = scatter(index, grads, out_ref.shape[1])
    for c in range(3):
        out_ref[c] = total[:, c * BLOCK : (c + 1) * BLOCK]


def final_kernel(garm_ref, body_ref, mine_ref, other_ref, garm_out, body_out, stiff_out):
    stiff_out[...] = mine_ref[...] + other_ref[...]
    body_out[...] = body_ref[...]
    garm_out[...] = garm_ref[...]


def stage_kernel(order, *refs):
    hbm, (index_ref, *out_refs), vmem, sems = refs[:7], refs[7:12], refs[12:19], refs[19]
    copies = [
        pltpu.make_async_copy(src, dst, sems.at[k]) for k, (src, dst) in enumerate(zip(hbm, vmem))
    ]
    for copy in copies:
        copy.start()
    for copy in copies:
        copy.wait()
    pg_ref, pb_ref, pc_ref, garm_ref, cot_ref, body_ref, stiff_ref = vmem
    cap = pg_ref.shape[0]
    tiles = stiff_ref.shape[0]
    width = lax.axis_size("body")
    here, column = lax.axis_index("garm"), lax.axis_index("body")
    for k, out_ref in enumerate(out_refs):
        for q in range(3 * tiles):
            out_ref[4 + q] = body_ref[q]
        for q in range(tiles):
            out_ref[4 + 3 * tiles + q] = stiff_ref[q]
        for x in range(2):
            owner = (here ^ k) * width + (column ^ x)
            live = pc_ref[0, owner]
            for s in range(cap):
                g = pg_ref[s, owner]
                row, place = pl.ds(g, 1), pl.ds(x * cap + s, 1)
                for c in range(3):
                    out_ref[c, place, :] = garm_ref[c, row, :]
                out_ref[3, place, :] = jnp.where(s < live, cot_ref[row, :], 0.0)
                out_ref[4 + 4 * tiles, place, :] = jnp.full(
                    (1, BLOCK), pb_ref[s, owner].astype(f32), f32
                )
                index_ref[order.index(k), place, :] = jnp.full((1, BLOCK), g.astype(f32), f32)


def staged(garment, cotangent, body_points, stiffness, pg, pb, pc):
    verts = garment.shape[2]
    points = body_points.shape[2]
    blocks = points // BLOCK
    tiles = blocks // SUB
    garm_n = lax.axis_size("garm")
    order = (0, 3, 1, 2)
    message = jax.ShapeDtypeStruct((5 + 4 * tiles, SUB, BLOCK), f32)
    arrays = (
        pg,
        pb,
        pc,
        garment.reshape(3, verts // BLOCK, BLOCK),
        cotangent.reshape(verts // BLOCK, BLOCK),
        body_points.reshape(3 * tiles, SUB, BLOCK),
        stiffness.reshape(tiles, SUB, BLOCK),
    )
    index, *sent = pl.pallas_call(
        functools.partial(stage_kernel, order),
        out_shape=[jax.ShapeDtypeStruct((garm_n, SUB, BLOCK), f32)] + [message] * garm_n,
        in_specs=[pl.BlockSpec(memory_space=pltpu.HBM)] * len(arrays),
        out_specs=[pl.BlockSpec(memory_space=pltpu.VMEM)] * (garm_n + 1),
        scratch_shapes=[
            (pltpu.SMEM if k < 3 else pltpu.VMEM)(a.shape, a.dtype) for k, a in enumerate(arrays)
        ]
        + [pltpu.SemaphoreType.DMA((len(arrays),))],
    )(*[pltpu.with_memory_space_constraint(a, pltpu.HBM) for a in arrays])

    def along_garm(k):
        return lax.ppermute(sent[k], "garm", [(z, z ^ k) for z in range(garm_n)])

    def along_body(value):
        return lax.ppermute(value, "body", [(0, 1), (1, 0)])

    same = {k: along_garm(k) for k in (3, 2, 1)}
    same[0] = sent[0]
    other = {k: along_body(same[k]) for k in (0, 1, 2, 3)}
    body_grads, body_index, garm_grads = [], [], []
    for k in order[:-1]:
        out = call(
            both_kernel,
            (
                jax.ShapeDtypeStruct((SUB, 4 * BLOCK), f32),
                jax.ShapeDtypeStruct((SUB, BLOCK), f32),
                jax.ShapeDtypeStruct((SUB, 3 * BLOCK), f32),
            ),
            [],
            (),
            (same[k], other[k], sent[0], sent[k]),
        )
        body_grads.append(out[0])
        body_index.append(out[1])
        garm_grads.append(out[2])
    k = order[-1]
    body_shape = jax.ShapeDtypeStruct((3, blocks, BLOCK), f32)
    stiff_shape = jax.ShapeDtypeStruct((blocks, BLOCK), f32)
    garm_shape = jax.ShapeDtypeStruct((3, verts // BLOCK, BLOCK), f32)
    body_total, stiff = call(
        last_body_kernel,
        (body_shape, stiff_shape),
        [],
        (),
        (same[k], other[k], sent[0], *body_grads, *body_index),
    )
    stiff_other = lax.ppermute(stiff, "frame", [(0, 1), (1, 0)])
    garm_total = call(
        last_garm_kernel, garm_shape, [], (), (same[k], other[k], sent[k], index, *garm_grads)
    )
    return call(
        final_kernel,
        (garm_shape, body_shape, stiff_shape),
        [],
        (),
        (garm_total, body_total, stiff, stiff_other),
    )


def call(kernel, out_shape, scratch, scalars, arrays):
    specs = [pl.BlockSpec(memory_space=pltpu.SMEM)] * len(scalars)
    specs += [pl.BlockSpec(memory_space=pltpu.VMEM)] * len(arrays)
    return pl.pallas_call(
        kernel,
        out_shape=out_shape,
        in_specs=specs,
        out_specs=jax.tree.map(lambda _: pl.BlockSpec(memory_space=pltpu.VMEM), out_shape),
        scratch_shapes=scratch,
        compiler_params=pltpu.CompilerParams(vmem_limit_bytes=32 * 1024 * 1024),
    )(*scalars, *arrays)


def per_device(garment, cotangent, body_points, stiffness, pair_garment, pair_body, pair_count):
    owners = lax.axis_size(("garm", "body"))
    verts = garment.shape[2]
    points = body_points.shape[2]
    blocks = points // BLOCK
    cap = pair_garment.shape[3]
    slots = owners * cap
    pg = pair_garment.reshape(owners, cap).T
    pb = pair_body.reshape(owners, cap).T
    pc = pair_count.reshape(1, owners)
    if (lax.axis_size("garm"), lax.axis_size("body")) == (4, 2) and cap == SUB // 2:
        garm_grad, body_grad, stiff = staged(
            garment, cotangent, body_points, stiffness, pg, pb, pc
        )
        return (
            garm_grad.reshape(1, 3, verts),
            body_grad.reshape(1, 3, points),
            stiff.reshape(points),
        )
    message = call(
        pack_kernel,
        jax.ShapeDtypeStruct((owners, 5 + blocks, cap, BLOCK), f32),
        [],
        (pg, pb, pc),
        (
            garment.reshape(3, verts // BLOCK, BLOCK),
            cotangent.reshape(verts // BLOCK, BLOCK),
            body_points.reshape(3, blocks, BLOCK),
            stiffness.reshape(blocks, BLOCK),
        ),
    )
    arrived = lax.all_to_all(message, ("garm", "body"), split_axis=0, concat_axis=0, tiled=True)
    rows = pltpu.VMEM((4, slots, BLOCK), f32)
    grad = pltpu.VMEM((slots, 4 * BLOCK), f32)
    index = pltpu.VMEM((slots, BLOCK), f32)
    body_grad, stiff = call(
        body_kernel,
        (
            jax.ShapeDtypeStruct((3, blocks, BLOCK), f32),
            jax.ShapeDtypeStruct((blocks, BLOCK), f32),
        ),
        [rows, rows, pltpu.VMEM((blocks, 4 * BLOCK), f32), index, grad],
        (),
        (message, arrived),
    )
    other = lax.ppermute(stiff, "frame", [(0, 1), (1, 0)])
    garm_grad = call(
        garm_kernel,
        jax.ShapeDtypeStruct((3, verts // BLOCK, BLOCK), f32),
        [rows, rows, index, grad],
        (pg, pb),
        (message, arrived),
    )
    return (
        garm_grad.reshape(1, 3, verts),
        body_grad.reshape(1, 3, points),
        (stiff + other).reshape(points),
    )


def solution(mesh):
    in_specs = (
        P(("grp", "frame"), None, ("garm", "body")),
        P(("grp", "frame"), ("garm", "body")),
        P(("grp", "frame"), None, ("garm", "body")),
        P(("grp", "garm", "body")),
        P(("grp", "frame"), ("garm", "body"), None, None),
        P(("grp", "frame"), ("garm", "body"), None, None),
        P(("grp", "frame"), ("garm", "body"), None),
    )
    out_specs = (
        P(("grp", "frame"), None, ("garm", "body")),
        P(("grp", "frame"), None, ("garm", "body")),
        P(("grp", "garm", "body")),
    )
    return jax.shard_map(
        per_device, mesh=mesh, in_specs=in_specs, out_specs=out_specs, check_vma=False
    )
```

```python
import functools
import math

import jax
import jax.numpy as jnp
from jax import lax
from jax.experimental import pallas as pl
from jax.experimental.pallas import tpu as pltpu
from jax.sharding import PartitionSpec as P

BLOCK = 128
SUB = 8
VMEM_LIMIT = 32 * 1024 * 1024

amplitude = 0.05
width_sq = 4.0

SCALE = math.sqrt(math.log2(math.e) / width_sq)
FACTOR = -2.0 / width_sq * amplitude

f32 = jnp.float32
bf16 = jnp.bfloat16


def pieces(value, count):
    out = []
    for _ in range(count - 1):
        top = value.astype(bf16).astype(f32)
        out.append(top)
        value = value - top
    out.append(value)
    return out


def features(left, right):
    lpos = [left[c] * SCALE for c in range(3)]
    rpos = [right[c] * SCALE for c in range(3)]
    lnorm = -(lpos[0] * lpos[0] + lpos[1] * lpos[1] + lpos[2] * lpos[2])
    rnorm = -(rpos[0] * rpos[0] + rpos[1] * rpos[1] + rpos[2] * rpos[2])
    one = jnp.ones_like(lnorm)
    lrows, rrows = [], []
    for c in range(3):
        l1, l2, l3 = pieces(lpos[c] * 2.0, 3)
        r1, r2, r3 = pieces(rpos[c], 3)
        lrows += [l1, l1, l2, l2, l1, l3]
        rrows += [r1, r2, r1, r2, r3, r1]
    lrows += pieces(lnorm, 3) + [one] * 3
    rrows += [one] * 3 + pieces(rnorm, 3)
    return (
        jnp.concatenate(lrows, axis=0).astype(bf16),
        jnp.concatenate(rrows, axis=0).astype(bf16),
    )


def pull(left, right):
    lfeat, rfeat = features(left, right)
    depth = lfeat.shape[0]
    weight = left[3]
    coeff = jnp.concatenate([weight * left[c] for c in range(3)] + [weight], axis=0)
    chi, clo = pieces(coeff, 2)
    chi, clo = chi.astype(bf16), clo.astype(bf16)
    lhs = jnp.concatenate(
        [
            jnp.concatenate([chi, chi], axis=1),
            jnp.concatenate([clo, jnp.zeros_like(clo)], axis=1),
        ],
        axis=0,
    )
    lfeat_t = lfeat.T
    row = lax.broadcasted_iota(jnp.int32, (depth, BLOCK), 0) % SUB
    sub = lax.broadcasted_iota(jnp.int32, (4 * SUB, BLOCK), 0) % SUB
    total = jnp.zeros((4 * SUB, BLOCK), f32)
    for pair in range(0, SUB, 2):
        rhs = jnp.concatenate(
            [rfeat * (row == pair + k).astype(f32).astype(bf16) for k in range(2)], axis=1
        )
        exponent = jnp.dot(lfeat_t, rhs, preferred_element_type=f32)
        kernel = jnp.exp2(exponent)
        khi = kernel.astype(bf16)
        klo = (kernel - khi.astype(f32)).astype(bf16)
        sums = jnp.dot(lhs, jnp.concatenate([khi, klo], axis=0), preferred_element_type=f32)
        sums = sums[: 4 * SUB] + sums[4 * SUB :]
        for k in range(2):
            total = jnp.where(sub == pair + k, sums[:, k * BLOCK : (k + 1) * BLOCK], total)
    return [total[c * SUB : (c + 1) * SUB] for c in range(4)]


def gradients(left, right):
    total = pull(left, right)
    out = [FACTOR * right[3] * (right[c] * total[3] - total[c]) for c in range(3)]
    return out + [amplitude * total[3]]


def run_batches(left_ref, right_ref, grad_ref):
    batches = left_ref.shape[1] // SUB

    def step(k, carry):
        rows = pl.ds(pl.multiple_of(k * SUB, SUB), SUB)
        left = [left_ref[c, rows, :] for c in range(4)]
        right = [right_ref[c, rows, :] for c in range(4)]
        for c, value in enumerate(gradients(left, right)):
            grad_ref[rows, c * BLOCK : (c + 1) * BLOCK] = value
        return carry

    if batches <= 4:
        for k in range(batches):
            step(k, 0)
    else:
        lax.fori_loop(0, batches, step, 0)


def scatter(index, grads, blocks):
    lane = lax.broadcasted_iota(jnp.int32, index.shape, 1).astype(f32)
    onehot_t = (index == lane).astype(f32).T[:blocks].astype(bf16)
    parts = [
        jnp.dot(onehot_t, part.astype(bf16), preferred_element_type=f32)
        for part in pieces(grads, 3)
    ]
    return parts[0] + parts[1] + parts[2]


def pack_kernel(pg_ref, pb_ref, pc_ref, garm_ref, cot_ref, body_ref, stiff_ref, out_ref):
    cap, owners = pg_ref.shape
    tiles = stiff_ref.shape[0] // cap

    def one(d, carry):
        for s in range(cap):
            row = pl.ds(pg_ref[s, d], 1)
            for c in range(3):
                out_ref[d, c, s : s + 1, :] = garm_ref[c, row, :]
            out_ref[d, 3, s : s + 1, :] = jnp.where(s < pc_ref[0, d], cot_ref[row, :], 0.0)
            out_ref[d, 4 + 4 * tiles, s : s + 1, :] = jnp.full(
                (1, BLOCK), pb_ref[s, d].astype(f32), f32
            )
        for q in range(tiles):
            rows = slice(q * cap, (q + 1) * cap)
            for c in range(3):
                out_ref[d, 4 + c * tiles + q] = body_ref[c, rows, :]
            out_ref[d, 4 + 3 * tiles + q] = stiff_ref[rows, :]
        return carry

    if owners <= 8:
        for d in range(owners):
            one(d, 0)
    else:
        lax.fori_loop(0, owners, one, 0)


def over(count, fn):
    if count <= 8:
        for d in range(count):
            fn(d)
    else:
        lax.fori_loop(0, count, lambda d, carry: (fn(d), carry)[1], 0)


def body_kernel(own_ref, in_ref, out_ref, stiff_ref, left, right, table, index, grad):
    owners, tiles, cap, _ = in_ref.shape
    blocks = tiles - 5

    def take(d):
        rows = pl.ds(d * cap, cap)
        for c in range(4):
            left[c, rows, :] = in_ref[d, c]
        index[rows, :] = in_ref[d, tiles - 1]

    over(owners, take)
    for c in range(4):
        for q in range(blocks // 4):
            table[4 * q : 4 * q + 4, c * BLOCK : (c + 1) * BLOCK] = own_ref[
                0, 4 + c * (blocks // 4) + q
            ]
    lane = lax.broadcasted_iota(jnp.int32, index.shape, 1).astype(f32)
    onehot = (index[...] == lane).astype(f32)[:, :blocks].astype(bf16)
    chosen = [
        jnp.dot(onehot, part.astype(bf16), preferred_element_type=f32)
        for part in pieces(table[...], 3)
    ]
    chosen = chosen[0] + chosen[1] + chosen[2]
    for c in range(4):
        right[c] = chosen[:, c * BLOCK : (c + 1) * BLOCK]
    run_batches(left, right, grad)
    total = scatter(index[...], grad[...], blocks)
    for c in range(3):
        out_ref[c] = total[:, c * BLOCK : (c + 1) * BLOCK]
    stiff_ref[...] = total[:, 3 * BLOCK :]


def garm_kernel(pg_ref, pb_ref, own_ref, in_ref, out_ref, left, right, index, grad):
    owners, tiles, cap, _ = in_ref.shape
    blocks = tiles - 5
    garm_blocks = out_ref.shape[1]

    def take(d):
        rows = pl.ds(d * cap, cap)
        for c in range(4):
            right[c, rows, :] = own_ref[d, c]
        for s in range(cap):
            b = pb_ref[s, d]
            for c in range(4):
                left[c, pl.ds(d * cap + s, 1), :] = in_ref[
                    d, 4 + c * (blocks // 4) + b // 4, pl.ds(b % 4, 1), :
                ]
            index[pl.ds(d * cap + s, 1), :] = jnp.full((1, BLOCK), pg_ref[s, d].astype(f32), f32)

    over(owners, take)
    run_batches(left, right, grad)
    total = scatter(index[...], grad[...], garm_blocks)
    for c in range(3):
        out_ref[c] = total[:, c * BLOCK : (c + 1) * BLOCK]


def read_table(message_ref):
    tiles = (message_ref.shape[0] - 5) // 4
    columns = []
    for c in range(4):
        start = 4 + c * tiles
        columns.append(jnp.concatenate([message_ref[start + q] for q in range(tiles)], axis=0))
    return jnp.concatenate(columns, axis=1)


def choose(index, table):
    lane = lax.broadcasted_iota(jnp.int32, index.shape, 1).astype(f32)
    onehot = (index == lane).astype(f32)[:, : table.shape[0]].astype(bf16)
    parts = [
        jnp.dot(onehot, part.astype(bf16), preferred_element_type=f32)
        for part in pieces(table, 3)
    ]
    rows = parts[0] + parts[1] + parts[2]
    return [rows[:, c * BLOCK : (c + 1) * BLOCK] for c in range(4)]


def mix(same_ref, other_ref, tile):
    row = lax.broadcasted_iota(jnp.int32, (SUB, BLOCK), 0)
    return jnp.where(row < SUB // 2, same_ref[tile], other_ref[tile])


def body_batch(same_ref, other_ref, own_ref):
    left = [mix(same_ref, other_ref, c) for c in range(4)]
    index = mix(same_ref, other_ref, same_ref.shape[0] - 1)
    right = choose(index, read_table(own_ref))
    return jnp.concatenate(gradients(left, right), axis=1), index


def garm_batch(same_ref, other_ref, sent_ref):
    right = [sent_ref[c] for c in range(4)]
    same, other = read_table(same_ref), read_table(other_ref)
    row = lax.broadcasted_iota(jnp.int32, (SUB, BLOCK), 0)
    index = sent_ref[sent_ref.shape[0] - 1]
    index = index + jnp.where(row < SUB // 2, 0, same.shape[0]).astype(f32)
    left = choose(index, jnp.concatenate([same, other], axis=0))
    return jnp.concatenate(gradients(left, right)[:3], axis=1)


def both_kernel(same_ref, other_ref, own_ref, sent_ref, bgrad_ref, bindex_ref, ggrad_ref):
    bgrad_ref[...], bindex_ref[...] = body_batch(same_ref, other_ref, own_ref)
    ggrad_ref[...] = garm_batch(same_ref, other_ref, sent_ref)


def last_body_kernel(same_ref, other_ref, own_ref, *refs):
    *earlier, out_ref, stiff_ref = refs
    grad, index = body_batch(same_ref, other_ref, own_ref)
    count = len(earlier) // 2
    grads = jnp.concatenate([ref[...] for ref in earlier[:count]] + [grad], axis=0)
    index = jnp.concatenate([ref[...] for ref in earlier[count:]] + [index], axis=0)
    total = scatter(index, grads, out_ref.shape[1])
    for c in range(3):
        out_ref[c] = total[:, c * BLOCK : (c + 1) * BLOCK]
    stiff_ref[...] = total[:, 3 * BLOCK :]


def last_garm_kernel(same_ref, other_ref, sent_ref, index_ref, *refs):
    *earlier, out_ref = refs
    grad = garm_batch(same_ref, other_ref, sent_ref)
    grads = jnp.concatenate([ref[...] for ref in earlier] + [grad], axis=0)
    index = jnp.concatenate([index_ref[k] for k in range(index_ref.shape[0])], axis=0)
    total = scatter(index, grads, out_ref.shape[1])
    for c in range(3):
        out_ref[c] = total[:, c * BLOCK : (c + 1) * BLOCK]


def final_kernel(garm_ref, body_ref, mine_ref, other_ref, garm_out, body_out, stiff_out):
    stiff_out[...] = mine_ref[...] + other_ref[...]
    body_out[...] = body_ref[...]
    garm_out[...] = garm_ref[...]


def stage_kernel(order, *refs):
    hbm, (index_ref, *out_refs), vmem, sems = refs[:7], refs[7:12], refs[12:19], refs[19]
    copies = [
        pltpu.make_async_copy(src, dst, sems.at[k]) for k, (src, dst) in enumerate(zip(hbm, vmem))
    ]
    for copy in copies:
        copy.start()
    for copy in copies:
        copy.wait()
    pg_ref, pb_ref, pc_ref, garm_ref, cot_ref, body_ref, stiff_ref = vmem
    cap = pg_ref.shape[0]
    tiles = stiff_ref.shape[0]
    width = lax.axis_size("body")
    here, column = lax.axis_index("garm"), lax.axis_index("body")
    for k, out_ref in enumerate(out_refs):
        for q in range(3 * tiles):
            out_ref[4 + q] = body_ref[q]
        for q in range(tiles):
            out_ref[4 + 3 * tiles + q] = stiff_ref[q]
        for x in range(2):
            owner = (here ^ k) * width + (column ^ x)
            live = pc_ref[0, owner]
            for s in range(cap):
                g = pg_ref[s, owner]
                row, place = pl.ds(g, 1), pl.ds(x * cap + s, 1)
                for c in range(3):
                    out_ref[c, place, :] = garm_ref[c, row, :]
                out_ref[3, place, :] = jnp.where(s < live, cot_ref[row, :], 0.0)
                out_ref[4 + 4 * tiles, place, :] = jnp.full(
                    (1, BLOCK), pb_ref[s, owner].astype(f32), f32
                )
                index_ref[order.index(k), place, :] = jnp.full((1, BLOCK), g.astype(f32), f32)


def staged(garment, cotangent, body_points, stiffness, pg, pb, pc):
    verts = garment.shape[2]
    points = body_points.shape[2]
    blocks = points // BLOCK
    tiles = blocks // SUB
    garm_n = lax.axis_size("garm")
    order = (0, 3, 1, 2)
    message = jax.ShapeDtypeStruct((5 + 4 * tiles, SUB, BLOCK), f32)
    arrays = (
        pg,
        pb,
        pc,
        garment.reshape(3, verts // BLOCK, BLOCK),
        cotangent.reshape(verts // BLOCK, BLOCK),
        body_points.reshape(3 * tiles, SUB, BLOCK),
        stiffness.reshape(tiles, SUB, BLOCK),
    )
    index, *sent = pl.pallas_call(
        functools.partial(stage_kernel, order),
        out_shape=[jax.ShapeDtypeStruct((garm_n, SUB, BLOCK), f32)] + [message] * garm_n,
        in_specs=[pl.BlockSpec(memory_space=pltpu.HBM)] * len(arrays),
        out_specs=[pl.BlockSpec(memory_space=pltpu.VMEM)] * (garm_n + 1),
        scratch_shapes=[
            (pltpu.SMEM if k < 3 else pltpu.VMEM)(a.shape, a.dtype) for k, a in enumerate(arrays)
        ]
        + [pltpu.SemaphoreType.DMA((len(arrays),))],
        compiler_params=pltpu.CompilerParams(vmem_limit_bytes=VMEM_LIMIT),
    )(*[pltpu.with_memory_space_constraint(a, pltpu.HBM) for a in arrays])

    def along_garm(k):
        return lax.ppermute(sent[k], "garm", [(z, z ^ k) for z in range(garm_n)])

    def along_body(value):
        return lax.ppermute(value, "body", [(0, 1), (1, 0)])

    same = {k: along_garm(k) for k in (3, 2, 1)}
    same[0] = sent[0]
    other = {k: along_body(same[k]) for k in (0, 1, 2, 3)}
    body_grads, body_index, garm_grads = [], [], []
    for k in order[:-1]:
        out = call(
            both_kernel,
            (
                jax.ShapeDtypeStruct((SUB, 4 * BLOCK), f32),
                jax.ShapeDtypeStruct((SUB, BLOCK), f32),
                jax.ShapeDtypeStruct((SUB, 3 * BLOCK), f32),
            ),
            [],
            (),
            (same[k], other[k], sent[0], sent[k]),
        )
        body_grads.append(out[0])
        body_index.append(out[1])
        garm_grads.append(out[2])
    k = order[-1]
    body_shape = jax.ShapeDtypeStruct((3, blocks, BLOCK), f32)
    stiff_shape = jax.ShapeDtypeStruct((blocks, BLOCK), f32)
    garm_shape = jax.ShapeDtypeStruct((3, verts // BLOCK, BLOCK), f32)
    body_total, stiff = call(
        last_body_kernel,
        (body_shape, stiff_shape),
        [],
        (),
        (same[k], other[k], sent[0], *body_grads, *body_index),
    )
    stiff_other = lax.ppermute(stiff, "frame", [(0, 1), (1, 0)])
    garm_total = call(
        last_garm_kernel, garm_shape, [], (), (same[k], other[k], sent[k], index, *garm_grads)
    )
    return call(
        final_kernel,
        (garm_shape, body_shape, stiff_shape),
        [],
        (),
        (garm_total, body_total, stiff, stiff_other),
    )


def call(kernel, out_shape, scratch, scalars, arrays):
    specs = [pl.BlockSpec(memory_space=pltpu.SMEM)] * len(scalars)
    specs += [pl.BlockSpec(memory_space=pltpu.VMEM)] * len(arrays)
    return pl.pallas_call(
        kernel,
        out_shape=out_shape,
        in_specs=specs,
        out_specs=jax.tree.map(lambda _: pl.BlockSpec(memory_space=pltpu.VMEM), out_shape),
        scratch_shapes=scratch,
        compiler_params=pltpu.CompilerParams(vmem_limit_bytes=VMEM_LIMIT),
    )(*scalars, *arrays)


def per_device(garment, cotangent, body_points, stiffness, pair_garment, pair_body, pair_count):
    owners = lax.axis_size(("garm", "body"))
    verts = garment.shape[2]
    points = body_points.shape[2]
    blocks = points // BLOCK
    cap = pair_garment.shape[3]
    slots = owners * cap
    pg = pair_garment.reshape(owners, cap).T
    pb = pair_body.reshape(owners, cap).T
    pc = pair_count.reshape(1, owners)
    if (lax.axis_size("garm"), lax.axis_size("body")) == (4, 2) and cap == SUB // 2:
        garm_grad, body_grad, stiff = staged(
            garment, cotangent, body_points, stiffness, pg, pb, pc
        )
        return (
            garm_grad.reshape(1, 3, verts),
            body_grad.reshape(1, 3, points),
            stiff.reshape(points),
        )
    message = call(
        pack_kernel,
        jax.ShapeDtypeStruct((owners, 5 + blocks, cap, BLOCK), f32),
        [],
        (pg, pb, pc),
        (
            garment.reshape(3, verts // BLOCK, BLOCK),
            cotangent.reshape(verts // BLOCK, BLOCK),
            body_points.reshape(3, blocks, BLOCK),
            stiffness.reshape(blocks, BLOCK),
        ),
    )
    arrived = lax.all_to_all(message, ("garm", "body"), split_axis=0, concat_axis=0, tiled=True)
    rows = pltpu.VMEM((4, slots, BLOCK), f32)
    grad = pltpu.VMEM((slots, 4 * BLOCK), f32)
    index = pltpu.VMEM((slots, BLOCK), f32)
    body_grad, stiff = call(
        body_kernel,
        (
            jax.ShapeDtypeStruct((3, blocks, BLOCK), f32),
            jax.ShapeDtypeStruct((blocks, BLOCK), f32),
        ),
        [rows, rows, pltpu.VMEM((blocks, 4 * BLOCK), f32), index, grad],
        (),
        (message, arrived),
    )
    other = lax.ppermute(stiff, "frame", [(0, 1), (1, 0)])
    garm_grad = call(
        garm_kernel,
        jax.ShapeDtypeStruct((3, verts // BLOCK, BLOCK), f32),
        [rows, rows, index, grad],
        (pg, pb),
        (message, arrived),
    )
    return (
        garm_grad.reshape(1, 3, verts),
        body_grad.reshape(1, 3, points),
        (stiff + other).reshape(points),
    )


def solution(mesh):
    in_specs = (
        P(("grp", "frame"), None, ("garm", "body")),
        P(("grp", "frame"), ("garm", "body")),
        P(("grp", "frame"), None, ("garm", "body")),
        P(("grp", "garm", "body")),
        P(("grp", "frame"), ("garm", "body"), None, None),
        P(("grp", "frame"), ("garm", "body"), None, None),
        P(("grp", "frame"), ("garm", "body"), None),
    )
    out_specs = (
        P(("grp", "frame"), None, ("garm", "body")),
        P(("grp", "frame"), None, ("garm", "body")),
        P(("grp", "garm", "body")),
    )
    return jax.shard_map(
        per_device, mesh=mesh, in_specs=in_specs, out_specs=out_specs, check_vma=False
    )
```

```python
import math

import jax
import jax.numpy as jnp
from jax import lax
from jax.experimental import pallas as pl
from jax.experimental.pallas import tpu as pltpu
from jax.sharding import PartitionSpec as P

BLOCK = 128
SUB = 8
VMEM_LIMIT = 32 * 1024 * 1024

amplitude = 0.05
width_sq = 4.0

SCALE = math.sqrt(math.log2(math.e) / width_sq)
FACTOR = -2.0 / width_sq * amplitude

f32 = jnp.float32
bf16 = jnp.bfloat16


def pieces(value, count):
    out = []
    for _ in range(count - 1):
        top = value.astype(bf16).astype(f32)
        out.append(top)
        value = value - top
    out.append(value)
    return out


def features(left, right):
    lpos = [left[c] * SCALE for c in range(3)]
    rpos = [right[c] * SCALE for c in range(3)]
    lnorm = -(lpos[0] * lpos[0] + lpos[1] * lpos[1] + lpos[2] * lpos[2])
    rnorm = -(rpos[0] * rpos[0] + rpos[1] * rpos[1] + rpos[2] * rpos[2])
    one = jnp.ones_like(lnorm)
    lrows, rrows = [], []
    for c in range(3):
        l1, l2, l3 = pieces(lpos[c] * 2.0, 3)
        r1, r2, r3 = pieces(rpos[c], 3)
        lrows += [l1, l1, l2, l2, l1, l3]
        rrows += [r1, r2, r1, r2, r3, r1]
    lrows += pieces(lnorm, 3) + [one] * 3
    rrows += [one] * 3 + pieces(rnorm, 3)
    return (
        jnp.concatenate(lrows, axis=0).astype(bf16),
        jnp.concatenate(rrows, axis=0).astype(bf16),
    )


def pull(batches):
    made = []
    for left, right in batches:
        lfeat, rfeat = features(left, right)
        weight = left[3]
        coeff = jnp.concatenate([weight * left[c] for c in range(3)] + [weight], axis=0)
        chi, clo = [part.astype(bf16) for part in pieces(coeff, 2)]
        lhs = jnp.concatenate(
            [
                jnp.concatenate([chi, chi], axis=1),
                jnp.concatenate([clo, jnp.zeros_like(clo)], axis=1),
            ],
            axis=0,
        )
        made.append((lfeat.T, rfeat, lhs))
    row = lax.broadcasted_iota(jnp.int32, made[0][1].shape, 0) % SUB
    sub = lax.broadcasted_iota(jnp.int32, (4 * SUB, BLOCK), 0) % SUB
    totals = [jnp.zeros((4 * SUB, BLOCK), f32) for _ in batches]
    for pair in range(0, SUB, 2):
        masks = [(row == pair + k).astype(f32).astype(bf16) for k in range(2)]
        for n, (lfeat_t, rfeat, lhs) in enumerate(made):
            rhs = jnp.concatenate([rfeat * mask for mask in masks], axis=1)
            exponent = jnp.dot(lfeat_t, rhs, preferred_element_type=f32)
            kernel = jnp.exp2(exponent)
            khi = kernel.astype(bf16)
            klo = (kernel - khi.astype(f32)).astype(bf16)
            sums = jnp.dot(lhs, jnp.concatenate([khi, klo], axis=0), preferred_element_type=f32)
            sums = sums[: 4 * SUB] + sums[4 * SUB :]
            for k in range(2):
                part = sums[:, k * BLOCK : (k + 1) * BLOCK]
                totals[n] = jnp.where(sub == pair + k, part, totals[n])
    return [[total[c * SUB : (c + 1) * SUB] for c in range(4)] for total in totals]


def gradients(batches):
    out = []
    for (_, right), total in zip(batches, pull(batches)):
        rows = [FACTOR * right[3] * (right[c] * total[3] - total[c]) for c in range(3)]
        out.append(rows + [amplitude * total[3]])
    return out


def run_batches(left_ref, right_ref, grad_ref):
    batches = left_ref.shape[1] // SUB
    group = math.gcd(batches, 4)

    def step(k, carry):
        places = [pl.ds(pl.multiple_of((k * group + n) * SUB, SUB), SUB) for n in range(group)]
        work = [
            tuple([ref[c, rows, :] for c in range(4)] for ref in (left_ref, right_ref))
            for rows in places
        ]
        for rows, values in zip(places, gradients(work)):
            for c, value in enumerate(values):
                grad_ref[rows, c * BLOCK : (c + 1) * BLOCK] = value
        return carry

    lax.fori_loop(0, batches // group, step, 0)


def scatter(index, grads, blocks):
    lane = lax.broadcasted_iota(jnp.int32, index.shape, 1).astype(f32)
    onehot_t = (index == lane).astype(f32).T[:blocks].astype(bf16)
    parts = [
        jnp.dot(onehot_t, part.astype(bf16), preferred_element_type=f32)
        for part in pieces(grads, 3)
    ]
    return parts[0] + parts[1] + parts[2]


def pack_kernel(pg_ref, pb_ref, pc_ref, garm_ref, cot_ref, body_ref, stiff_ref, out_ref):
    cap, owners = pg_ref.shape
    tiles = stiff_ref.shape[0] // cap

    def one(d, carry):
        for s in range(cap):
            row = pl.ds(pg_ref[s, d], 1)
            for c in range(3):
                out_ref[d, c, s : s + 1, :] = garm_ref[c, row, :]
            out_ref[d, 3, s : s + 1, :] = jnp.where(s < pc_ref[0, d], cot_ref[row, :], 0.0)
            out_ref[d, 4 + 4 * tiles, s : s + 1, :] = jnp.full(
                (1, BLOCK), pb_ref[s, d].astype(f32), f32
            )
        for q in range(tiles):
            rows = slice(q * cap, (q + 1) * cap)
            for c in range(3):
                out_ref[d, 4 + c * tiles + q] = body_ref[c, rows, :]
            out_ref[d, 4 + 3 * tiles + q] = stiff_ref[rows, :]
        return carry

    if owners <= 8:
        for d in range(owners):
            one(d, 0)
    else:
        lax.fori_loop(0, owners, one, 0)


def over(count, fn):
    if count <= 8:
        for d in range(count):
            fn(d)
    else:
        lax.fori_loop(0, count, lambda d, carry: (fn(d), carry)[1], 0)


def body_kernel(own_ref, in_ref, out_ref, stiff_ref, left, right, table, index, grad):
    owners, tiles, cap, _ = in_ref.shape
    blocks = tiles - 5

    def take(d):
        rows = pl.ds(d * cap, cap)
        for c in range(4):
            left[c, rows, :] = in_ref[d, c]
        index[rows, :] = in_ref[d, tiles - 1]

    over(owners, take)
    for c in range(4):
        for q in range(blocks // 4):
            table[4 * q : 4 * q + 4, c * BLOCK : (c + 1) * BLOCK] = own_ref[
                0, 4 + c * (blocks // 4) + q
            ]
    lane = lax.broadcasted_iota(jnp.int32, index.shape, 1).astype(f32)
    onehot = (index[...] == lane).astype(f32)[:, :blocks].astype(bf16)
    chosen = [
        jnp.dot(onehot, part.astype(bf16), preferred_element_type=f32)
        for part in pieces(table[...], 3)
    ]
    chosen = chosen[0] + chosen[1] + chosen[2]
    for c in range(4):
        right[c] = chosen[:, c * BLOCK : (c + 1) * BLOCK]
    run_batches(left, right, grad)
    total = scatter(index[...], grad[...], blocks)
    for c in range(3):
        out_ref[c] = total[:, c * BLOCK : (c + 1) * BLOCK]
    stiff_ref[...] = total[:, 3 * BLOCK :]


def garm_kernel(pg_ref, pb_ref, own_ref, in_ref, out_ref, left, right, index, grad):
    owners, tiles, cap, _ = in_ref.shape
    blocks = tiles - 5
    garm_blocks = out_ref.shape[1]

    def take(d):
        rows = pl.ds(d * cap, cap)
        for c in range(4):
            right[c, rows, :] = own_ref[d, c]
        for s in range(cap):
            b = pb_ref[s, d]
            for c in range(4):
                left[c, pl.ds(d * cap + s, 1), :] = in_ref[
                    d, 4 + c * (blocks // 4) + b // 4, pl.ds(b % 4, 1), :
                ]
            index[pl.ds(d * cap + s, 1), :] = jnp.full((1, BLOCK), pg_ref[s, d].astype(f32), f32)

    over(owners, take)
    run_batches(left, right, grad)
    total = scatter(index[...], grad[...], garm_blocks)
    for c in range(3):
        out_ref[c] = total[:, c * BLOCK : (c + 1) * BLOCK]


def call(kernel, out_shape, scratch, scalars, arrays):
    specs = [pl.BlockSpec(memory_space=pltpu.SMEM)] * len(scalars)
    specs += [pl.BlockSpec(memory_space=pltpu.VMEM)] * len(arrays)
    return pl.pallas_call(
        kernel,
        out_shape=out_shape,
        in_specs=specs,
        out_specs=jax.tree.map(lambda _: pl.BlockSpec(memory_space=pltpu.VMEM), out_shape),
        scratch_shapes=scratch,
        compiler_params=pltpu.CompilerParams(vmem_limit_bytes=VMEM_LIMIT),
    )(*scalars, *arrays)


def read_table(ref, start, step):
    columns = [
        jnp.concatenate([ref[start + c * step + q] for q in range(step)], axis=0) for c in range(4)
    ]
    return jnp.concatenate(columns, axis=1)


def choose(index, table):
    lane = lax.broadcasted_iota(jnp.int32, index.shape, 1).astype(f32)
    onehot = (index == lane).astype(f32)[:, : table.shape[0]].astype(bf16)
    parts = [
        jnp.dot(onehot, part.astype(bf16), preferred_element_type=f32)
        for part in pieces(table, 3)
    ]
    rows = parts[0] + parts[1] + parts[2]
    return [rows[:, c * BLOCK : (c + 1) * BLOCK] for c in range(4)]


def halves(top, bottom):
    row = lax.broadcasted_iota(jnp.int32, (SUB, BLOCK), 0)
    return jnp.where(row < SUB // 2, top, bottom)


def flip(value):
    return pltpu.roll(value, SUB // 2, 0)


def body_work(tiles, table):
    return list(tiles[:4]), choose(tiles[4], table)


def garm_work(tiles, top, bottom):
    row = lax.broadcasted_iota(jnp.int32, (SUB, BLOCK), 0)
    index = tiles[4] + jnp.where(row < SUB // 2, 0, top.shape[0]).astype(f32)
    return choose(index, jnp.concatenate([top, bottom], axis=0)), list(tiles[:4])


def slot_tiles(ref):
    return [ref[c] for c in range(4)] + [ref[ref.shape[0] - 1]]


def message_table(ref):
    return read_table(ref, 4, (ref.shape[0] - 5) // 4)


def near_bundle_kernel(one_ref, two_ref, out_ref):
    body = one_ref.shape[0] - 5
    for q in range(body):
        out_ref[q] = one_ref[4 + q]
        out_ref[body + q] = two_ref[4 + q]
    for k, (a, b) in enumerate(zip(slot_tiles(one_ref), slot_tiles(two_ref))):
        out_ref[2 * body + k] = halves(flip(a), b)


def far_bundle_kernel(three_ref, near_ref, out_ref):
    del near_ref
    body = three_ref.shape[0] - 5
    for q in range(body):
        out_ref[q] = three_ref[4 + q]
    tiles = slot_tiles(three_ref)
    out_ref[body] = halves(flip(tiles[0]), tiles[1])
    out_ref[body + 1] = halves(flip(tiles[2]), tiles[3])
    out_ref[body + 2] = tiles[4]


def far_tiles(three_ref, far_ref):
    same = slot_tiles(three_ref)
    body = three_ref.shape[0] - 5
    a, b, c = [far_ref[body + k] for k in range(3)]
    other = [flip(a), a, flip(b), b, c]
    return [halves(x, y) for x, y in zip(same, other)]


def near_tiles(one_ref, two_ref):
    return [halves(a, flip(b)) for a, b in zip(slot_tiles(one_ref), slot_tiles(two_ref))]


def cross_tiles(one_ref, two_ref):
    return [halves(flip(a), b) for a, b in zip(slot_tiles(one_ref), slot_tiles(two_ref))]


def early_kernel(
    m0_ref, m1_ref, m2_ref, x0_ref, z1_ref, z2_ref, far_ref, bgrad_ref, bindex_ref, ggrad_ref
):
    del far_ref
    own = message_table(m0_ref)
    here = [halves(a, b) for a, b in zip(slot_tiles(m0_ref), slot_tiles(x0_ref))]
    near = near_tiles(z1_ref, z2_ref)
    work = [
        body_work(here, own),
        body_work(near, own),
        garm_work(slot_tiles(m0_ref), own, message_table(x0_ref)),
        garm_work(near_tiles(m1_ref, m2_ref), message_table(z1_ref), message_table(z2_ref)),
    ]
    out = gradients(work)
    for n in range(2):
        rows = slice(n * SUB, (n + 1) * SUB)
        bgrad_ref[rows, :] = jnp.concatenate(out[n], axis=1)
        ggrad_ref[rows, :] = jnp.concatenate(out[2 + n][:3], axis=1)
    bindex_ref[:SUB, :] = here[4]
    bindex_ref[SUB:, :] = near[4]


def late_body_kernel(
    m0_ref, z3_ref, near_ref, far_ref, bgrad_ref, bindex_ref, out_ref, stiff_ref
):
    own = message_table(m0_ref)
    body = z3_ref.shape[0] - 5
    near = [near_ref[2 * body + k] for k in range(5)]
    far = far_tiles(z3_ref, far_ref)
    grads = [
        jnp.concatenate(rows, axis=1)
        for rows in gradients([body_work(far, own), body_work(near, own)])
    ]
    index = jnp.concatenate([bindex_ref[...], far[4], near[4]], axis=0)
    total = scatter(index, jnp.concatenate([bgrad_ref[...]] + grads, axis=0), out_ref.shape[1])
    for c in range(3):
        out_ref[c] = total[:, c * BLOCK : (c + 1) * BLOCK]
    stiff_ref[...] = total[:, 3 * BLOCK :]


def late_garm_kernel(
    m1_ref, m2_ref, m3_ref, z3_ref, near_ref, far_ref, ggrad_ref, index_ref, out_ref
):
    body = z3_ref.shape[0] - 5
    step = body // 4
    tables = [read_table(near_ref, n * body, step) for n in range(2)]
    work = [
        garm_work(slot_tiles(m3_ref), message_table(z3_ref), read_table(far_ref, 0, step)),
        garm_work(cross_tiles(m1_ref, m2_ref), *tables),
    ]
    grads = [jnp.concatenate(rows[:3], axis=1) for rows in gradients(work)]
    index = jnp.concatenate([index_ref[k] for k in range(index_ref.shape[0])], axis=0)
    total = scatter(index, jnp.concatenate([ggrad_ref[...]] + grads, axis=0), out_ref.shape[1])
    for c in range(3):
        out_ref[c] = total[:, c * BLOCK : (c + 1) * BLOCK]


def final_kernel(garm_ref, body_ref, mine_ref, other_ref, garm_out, body_out, stiff_out):
    stiff_out[...] = mine_ref[...] + other_ref[...]
    body_out[...] = body_ref[...]
    garm_out[...] = garm_ref[...]


def stage_kernel(*refs):
    hbm, (index_ref, *out_refs), vmem, sems = refs[:7], refs[7:12], refs[12:19], refs[19]
    copies = [
        pltpu.make_async_copy(src, dst, sems.at[k]) for k, (src, dst) in enumerate(zip(hbm, vmem))
    ]
    for copy in copies:
        copy.start()
    for copy in copies:
        copy.wait()
    pg_ref, pb_ref, pc_ref, garm_ref, cot_ref, body_ref, stiff_ref = vmem
    cap = pg_ref.shape[0]
    tiles = stiff_ref.shape[0]
    width = lax.axis_size("body")
    here, column = lax.axis_index("garm"), lax.axis_index("body")
    for k, out_ref in enumerate(out_refs):
        for q in range(3 * tiles):
            out_ref[4 + q] = body_ref[q]
        for q in range(tiles):
            out_ref[4 + 3 * tiles + q] = stiff_ref[q]
        for x in range(2):
            owner = (here ^ k) * width + (column ^ x)
            live = pc_ref[0, owner]
            for s in range(cap):
                g = pg_ref[s, owner]
                row, place = pl.ds(g, 1), pl.ds(x * cap + s, 1)
                for c in range(3):
                    out_ref[c, place, :] = garm_ref[c, row, :]
                out_ref[3, place, :] = jnp.where(s < live, cot_ref[row, :], 0.0)
                out_ref[4 + 4 * tiles, place, :] = jnp.full(
                    (1, BLOCK), pb_ref[s, owner].astype(f32), f32
                )
                if k in (1, 2):
                    spot, line = 1 + 2 * x, (k - 1) * cap + s
                else:
                    spot, line = (0 if k == 0 else 2), x * cap + s
                index_ref[spot, line : line + 1, :] = jnp.full((1, BLOCK), g.astype(f32), f32)


def staged(garment, cotangent, body_points, stiffness, pg, pb, pc):
    verts = garment.shape[2]
    points = body_points.shape[2]
    blocks = points // BLOCK
    tiles = blocks // SUB
    garm_n = lax.axis_size("garm")
    message = jax.ShapeDtypeStruct((5 + 4 * tiles, SUB, BLOCK), f32)
    arrays = (
        pg,
        pb,
        pc,
        garment.reshape(3, verts // BLOCK, BLOCK),
        cotangent.reshape(verts // BLOCK, BLOCK),
        body_points.reshape(3 * tiles, SUB, BLOCK),
        stiffness.reshape(tiles, SUB, BLOCK),
    )
    index, *sent = pl.pallas_call(
        stage_kernel,
        out_shape=[jax.ShapeDtypeStruct((garm_n, SUB, BLOCK), f32)] + [message] * garm_n,
        in_specs=[pl.BlockSpec(memory_space=pltpu.HBM)] * len(arrays),
        out_specs=[pl.BlockSpec(memory_space=pltpu.VMEM)] * (garm_n + 1),
        scratch_shapes=[
            (pltpu.SMEM if k < 3 else pltpu.VMEM)(a.shape, a.dtype) for k, a in enumerate(arrays)
        ]
        + [pltpu.SemaphoreType.DMA((len(arrays),))],
        compiler_params=pltpu.CompilerParams(vmem_limit_bytes=VMEM_LIMIT),
    )(*[pltpu.with_memory_space_constraint(a, pltpu.HBM) for a in arrays])

    def along_garm(k):
        return lax.ppermute(sent[k], "garm", [(z, z ^ k) for z in range(garm_n)])

    def along_body(value):
        return lax.ppermute(value, "body", [(0, 1), (1, 0)])

    z3, z2, z1 = [along_garm(k) for k in (3, 2, 1)]
    x0 = along_body(sent[0])
    body = 4 * tiles
    near = call(
        near_bundle_kernel,
        jax.ShapeDtypeStruct((2 * body + 5, SUB, BLOCK), f32),
        [],
        (),
        (z1, z2),
    )
    far = call(
        far_bundle_kernel,
        jax.ShapeDtypeStruct((body + 3, SUB, BLOCK), f32),
        [],
        (),
        (z3, near),
    )
    near_other, far_other = along_body(near), along_body(far)
    bgrad, bindex, ggrad = call(
        early_kernel,
        (
            jax.ShapeDtypeStruct((2 * SUB, 4 * BLOCK), f32),
            jax.ShapeDtypeStruct((2 * SUB, BLOCK), f32),
            jax.ShapeDtypeStruct((2 * SUB, 3 * BLOCK), f32),
        ),
        [],
        (),
        (sent[0], sent[1], sent[2], x0, z1, z2, far),
    )
    body_shape = jax.ShapeDtypeStruct((3, blocks, BLOCK), f32)
    stiff_shape = jax.ShapeDtypeStruct((blocks, BLOCK), f32)
    garm_shape = jax.ShapeDtypeStruct((3, verts // BLOCK, BLOCK), f32)
    body_total, stiff = call(
        late_body_kernel,
        (body_shape, stiff_shape),
        [],
        (),
        (sent[0], z3, near_other, far_other, bgrad, bindex),
    )
    stiff_other = lax.ppermute(stiff, "frame", [(0, 1), (1, 0)])
    garm_total = call(
        late_garm_kernel,
        garm_shape,
        [],
        (),
        (sent[1], sent[2], sent[3], z3, near_other, far_other, ggrad, index),
    )
    return call(
        final_kernel,
        (garm_shape, body_shape, stiff_shape),
        [],
        (),
        (garm_total, body_total, stiff, stiff_other),
    )


def per_device(garment, cotangent, body_points, stiffness, pair_garment, pair_body, pair_count):
    owners = lax.axis_size(("garm", "body"))
    verts = garment.shape[2]
    points = body_points.shape[2]
    blocks = points // BLOCK
    cap = pair_garment.shape[3]
    slots = owners * cap
    pg = pair_garment.reshape(owners, cap).T
    pb = pair_body.reshape(owners, cap).T
    pc = pair_count.reshape(1, owners)
    if (lax.axis_size("garm"), lax.axis_size("body")) == (4, 2) and cap == SUB // 2:
        garm_grad, body_grad, stiff = staged(
            garment, cotangent, body_points, stiffness, pg, pb, pc
        )
        return (
            garm_grad.reshape(1, 3, verts),
            body_grad.reshape(1, 3, points),
            stiff.reshape(points),
        )
    message = call(
        pack_kernel,
        jax.ShapeDtypeStruct((owners, 5 + blocks, cap, BLOCK), f32),
        [],
        (pg, pb, pc),
        (
            garment.reshape(3, verts // BLOCK, BLOCK),
            cotangent.reshape(verts // BLOCK, BLOCK),
            body_points.reshape(3, blocks, BLOCK),
            stiffness.reshape(blocks, BLOCK),
        ),
    )
    arrived = lax.all_to_all(message, ("garm", "body"), split_axis=0, concat_axis=0, tiled=True)
    rows = pltpu.VMEM((4, slots, BLOCK), f32)
    grad = pltpu.VMEM((slots, 4 * BLOCK), f32)
    index = pltpu.VMEM((slots, BLOCK), f32)
    body_grad, stiff = call(
        body_kernel,
        (
            jax.ShapeDtypeStruct((3, blocks, BLOCK), f32),
            jax.ShapeDtypeStruct((blocks, BLOCK), f32),
        ),
        [rows, rows, pltpu.VMEM((blocks, 4 * BLOCK), f32), index, grad],
        (),
        (message, arrived),
    )
    other = lax.ppermute(stiff, "frame", [(0, 1), (1, 0)])
    garm_grad = call(
        garm_kernel,
        jax.ShapeDtypeStruct((3, verts // BLOCK, BLOCK), f32),
        [rows, rows, index, grad],
        (pg, pb),
        (message, arrived),
    )
    return (
        garm_grad.reshape(1, 3, verts),
        body_grad.reshape(1, 3, points),
        (stiff + other).reshape(points),
    )


def solution(mesh):
    in_specs = (
        P(("grp", "frame"), None, ("garm", "body")),
        P(("grp", "frame"), ("garm", "body")),
        P(("grp", "frame"), None, ("garm", "body")),
        P(("grp", "garm", "body")),
        P(("grp", "frame"), ("garm", "body"), None, None),
        P(("grp", "frame"), ("garm", "body"), None, None),
        P(("grp", "frame"), ("garm", "body"), None),
    )
    out_specs = (
        P(("grp", "frame"), None, ("garm", "body")),
        P(("grp", "frame"), None, ("garm", "body")),
        P(("grp", "garm", "body")),
    )
    return jax.shard_map(
        per_device, mesh=mesh, in_specs=in_specs, out_specs=out_specs, check_vma=False
    )
```

```python
import math

import jax
import jax.numpy as jnp
from jax import lax
from jax.experimental import pallas as pl
from jax.experimental.pallas import tpu as pltpu
from jax.sharding import PartitionSpec as P

BLOCK = 128
SUB = 8
DISTANCES = (3, 2, 1)
VMEM_LIMIT = 32 * 1024 * 1024

amplitude = 0.05
width_sq = 4.0

SCALE = math.sqrt(math.log2(math.e) / width_sq)
FACTOR = -2.0 / width_sq * amplitude

f32 = jnp.float32
bf16 = jnp.bfloat16


def pieces(value, count):
    out = []
    for _ in range(count - 1):
        top = value.astype(bf16).astype(f32)
        out.append(top)
        value = value - top
    out.append(value)
    return out


def features(left, right):
    lpos = [left[c] * SCALE for c in range(3)]
    rpos = [right[c] * SCALE for c in range(3)]
    lnorm = -(lpos[0] * lpos[0] + lpos[1] * lpos[1] + lpos[2] * lpos[2])
    rnorm = -(rpos[0] * rpos[0] + rpos[1] * rpos[1] + rpos[2] * rpos[2])
    one = jnp.ones_like(lnorm)
    lrows, rrows = [], []
    for c in range(3):
        l1, l2, l3 = pieces(lpos[c] * 2.0, 3)
        r1, r2, r3 = pieces(rpos[c], 3)
        lrows += [l1, l1, l2, l2, l1, l3]
        rrows += [r1, r2, r1, r2, r3, r1]
    lrows += pieces(lnorm, 3) + [one] * 3
    rrows += [one] * 3 + pieces(rnorm, 3)
    return (
        jnp.concatenate(lrows, axis=0).astype(bf16),
        jnp.concatenate(rrows, axis=0).astype(bf16),
    )


def pull(batches):
    made = []
    for left, right in batches:
        lfeat, rfeat = features(left, right)
        weight = left[3]
        coeff = jnp.concatenate([weight * left[c] for c in range(3)] + [weight], axis=0)
        chi, clo = [part.astype(bf16) for part in pieces(coeff, 2)]
        lhs = jnp.concatenate(
            [
                jnp.concatenate([chi, chi], axis=1),
                jnp.concatenate([clo, jnp.zeros_like(clo)], axis=1),
            ],
            axis=0,
        )
        made.append((lfeat.T, rfeat, lhs))
    row = lax.broadcasted_iota(jnp.int32, made[0][1].shape, 0) % SUB
    sub = lax.broadcasted_iota(jnp.int32, (4 * SUB, BLOCK), 0) % SUB
    totals = [jnp.zeros((4 * SUB, BLOCK), f32) for _ in batches]
    for pair in range(0, SUB, 2):
        masks = [(row == pair + k).astype(f32).astype(bf16) for k in range(2)]
        for n, (lfeat_t, rfeat, lhs) in enumerate(made):
            rhs = jnp.concatenate([rfeat * mask for mask in masks], axis=1)
            exponent = jnp.dot(lfeat_t, rhs, preferred_element_type=f32)
            kernel = jnp.exp2(exponent)
            khi = kernel.astype(bf16)
            klo = (kernel - khi.astype(f32)).astype(bf16)
            sums = jnp.dot(lhs, jnp.concatenate([khi, klo], axis=0), preferred_element_type=f32)
            sums = sums[: 4 * SUB] + sums[4 * SUB :]
            for k in range(2):
                part = sums[:, k * BLOCK : (k + 1) * BLOCK]
                totals[n] = jnp.where(sub == pair + k, part, totals[n])
    return [[total[c * SUB : (c + 1) * SUB] for c in range(4)] for total in totals]


def gradients(batches):
    out = []
    for (_, right), total in zip(batches, pull(batches)):
        rows = [FACTOR * right[3] * (right[c] * total[3] - total[c]) for c in range(3)]
        out.append(rows + [amplitude * total[3]])
    return out


def run_batches(left_ref, right_ref, grad_ref):
    batches = left_ref.shape[1] // SUB
    group = math.gcd(batches, 4)

    def step(k, carry):
        places = [pl.ds(pl.multiple_of((k * group + n) * SUB, SUB), SUB) for n in range(group)]
        work = [
            tuple([ref[c, rows, :] for c in range(4)] for ref in (left_ref, right_ref))
            for rows in places
        ]
        for rows, values in zip(places, gradients(work)):
            for c, value in enumerate(values):
                grad_ref[rows, c * BLOCK : (c + 1) * BLOCK] = value
        return carry

    lax.fori_loop(0, batches // group, step, 0)


def scatter(index, grads, blocks):
    lane = lax.broadcasted_iota(jnp.int32, index.shape, 1).astype(f32)
    onehot_t = (index == lane).astype(f32).T[:blocks].astype(bf16)
    parts = [
        jnp.dot(onehot_t, part.astype(bf16), preferred_element_type=f32)
        for part in pieces(grads, 3)
    ]
    return parts[0] + parts[1] + parts[2]


def pack_kernel(pg_ref, pb_ref, pc_ref, garm_ref, cot_ref, body_ref, stiff_ref, out_ref):
    cap, owners = pg_ref.shape
    tiles = stiff_ref.shape[0] // cap

    def one(d, carry):
        for s in range(cap):
            row = pl.ds(pg_ref[s, d], 1)
            for c in range(3):
                out_ref[d, c, s : s + 1, :] = garm_ref[c, row, :]
            out_ref[d, 3, s : s + 1, :] = jnp.where(s < pc_ref[0, d], cot_ref[row, :], 0.0)
            out_ref[d, 4 + 4 * tiles, s : s + 1, :] = jnp.full(
                (1, BLOCK), pb_ref[s, d].astype(f32), f32
            )
        for q in range(tiles):
            rows = slice(q * cap, (q + 1) * cap)
            for c in range(3):
                out_ref[d, 4 + c * tiles + q] = body_ref[c, rows, :]
            out_ref[d, 4 + 3 * tiles + q] = stiff_ref[rows, :]
        return carry

    if owners <= 8:
        for d in range(owners):
            one(d, 0)
    else:
        lax.fori_loop(0, owners, one, 0)


def over(count, fn):
    if count <= 8:
        for d in range(count):
            fn(d)
    else:
        lax.fori_loop(0, count, lambda d, carry: (fn(d), carry)[1], 0)


def body_kernel(own_ref, in_ref, out_ref, stiff_ref, left, right, table, index, grad):
    owners, tiles, cap, _ = in_ref.shape
    blocks = tiles - 5

    def take(d):
        rows = pl.ds(d * cap, cap)
        for c in range(4):
            left[c, rows, :] = in_ref[d, c]
        index[rows, :] = in_ref[d, tiles - 1]

    over(owners, take)
    for c in range(4):
        for q in range(blocks // 4):
            table[4 * q : 4 * q + 4, c * BLOCK : (c + 1) * BLOCK] = own_ref[
                0, 4 + c * (blocks // 4) + q
            ]
    lane = lax.broadcasted_iota(jnp.int32, index.shape, 1).astype(f32)
    onehot = (index[...] == lane).astype(f32)[:, :blocks].astype(bf16)
    chosen = [
        jnp.dot(onehot, part.astype(bf16), preferred_element_type=f32)
        for part in pieces(table[...], 3)
    ]
    chosen = chosen[0] + chosen[1] + chosen[2]
    for c in range(4):
        right[c] = chosen[:, c * BLOCK : (c + 1) * BLOCK]
    run_batches(left, right, grad)
    total = scatter(index[...], grad[...], blocks)
    for c in range(3):
        out_ref[c] = total[:, c * BLOCK : (c + 1) * BLOCK]
    stiff_ref[...] = total[:, 3 * BLOCK :]


def garm_kernel(pg_ref, pb_ref, own_ref, in_ref, out_ref, left, right, index, grad):
    owners, tiles, cap, _ = in_ref.shape
    blocks = tiles - 5
    garm_blocks = out_ref.shape[1]

    def take(d):
        rows = pl.ds(d * cap, cap)
        for c in range(4):
            right[c, rows, :] = own_ref[d, c]
        for s in range(cap):
            b = pb_ref[s, d]
            for c in range(4):
                left[c, pl.ds(d * cap + s, 1), :] = in_ref[
                    d, 4 + c * (blocks // 4) + b // 4, pl.ds(b % 4, 1), :
                ]
            index[pl.ds(d * cap + s, 1), :] = jnp.full((1, BLOCK), pg_ref[s, d].astype(f32), f32)

    over(owners, take)
    run_batches(left, right, grad)
    total = scatter(index[...], grad[...], garm_blocks)
    for c in range(3):
        out_ref[c] = total[:, c * BLOCK : (c + 1) * BLOCK]


def call(kernel, out_shape, scratch, scalars, arrays):
    specs = [pl.BlockSpec(memory_space=pltpu.SMEM)] * len(scalars)
    specs += [pl.BlockSpec(memory_space=pltpu.VMEM)] * len(arrays)
    return pl.pallas_call(
        kernel,
        out_shape=out_shape,
        in_specs=specs,
        out_specs=jax.tree.map(lambda _: pl.BlockSpec(memory_space=pltpu.VMEM), out_shape),
        scratch_shapes=scratch,
        compiler_params=pltpu.CompilerParams(vmem_limit_bytes=VMEM_LIMIT),
    )(*scalars, *arrays)


def read_table(ref, start, step):
    columns = [
        jnp.concatenate([ref[start + c * step + q] for q in range(step)], axis=0) for c in range(4)
    ]
    return jnp.concatenate(columns, axis=1)


def choose(index, table):
    lane = lax.broadcasted_iota(jnp.int32, index.shape, 1).astype(f32)
    onehot = (index == lane).astype(f32)[:, : table.shape[0]].astype(bf16)
    parts = [
        jnp.dot(onehot, part.astype(bf16), preferred_element_type=f32)
        for part in pieces(table, 3)
    ]
    rows = parts[0] + parts[1] + parts[2]
    return [rows[:, c * BLOCK : (c + 1) * BLOCK] for c in range(4)]


def halves(top, bottom):
    row = lax.broadcasted_iota(jnp.int32, (SUB, BLOCK), 0)
    return jnp.where(row < SUB // 2, top, bottom)


def flip(value):
    return pltpu.roll(value, SUB // 2, 0)


def body_work(tiles, table):
    return list(tiles[:4]), choose(tiles[4], table)


def garm_work(tiles, top, bottom):
    row = lax.broadcasted_iota(jnp.int32, (SUB, BLOCK), 0)
    index = tiles[4] + jnp.where(row < SUB // 2, 0, top.shape[0]).astype(f32)
    return choose(index, jnp.concatenate([top, bottom], axis=0)), list(tiles[:4])


def slot_tiles(ref):
    return [ref[c] for c in range(4)] + [ref[ref.shape[0] - 1]]


def message_table(ref):
    return read_table(ref, 4, (ref.shape[0] - 5) // 4)


def near_bundle_kernel(one_ref, two_ref, x0_ref, out_ref):
    del x0_ref
    body = one_ref.shape[0] - 5
    for q in range(body):
        out_ref[q] = one_ref[4 + q]
        out_ref[body + q] = two_ref[4 + q]
    for k, (a, b) in enumerate(zip(slot_tiles(one_ref), slot_tiles(two_ref))):
        out_ref[2 * body + k] = halves(flip(a), b)


def far_bundle_kernel(three_ref, near_ref, out_ref):
    del near_ref
    body = three_ref.shape[0] - 5
    for q in range(body):
        out_ref[q] = three_ref[4 + q]
    tiles = slot_tiles(three_ref)
    out_ref[body] = halves(flip(tiles[0]), tiles[1])
    out_ref[body + 1] = halves(flip(tiles[2]), tiles[3])
    out_ref[body + 2] = tiles[4]


def far_tiles(three_ref, far_ref):
    same = slot_tiles(three_ref)
    body = three_ref.shape[0] - 5
    a, b, c = [far_ref[body + k] for k in range(3)]
    other = [flip(a), a, flip(b), b, c]
    return [halves(x, y) for x, y in zip(same, other)]


def near_tiles(one_ref, two_ref):
    return [halves(a, flip(b)) for a, b in zip(slot_tiles(one_ref), slot_tiles(two_ref))]


def cross_tiles(one_ref, two_ref):
    return [halves(flip(a), b) for a, b in zip(slot_tiles(one_ref), slot_tiles(two_ref))]


def early_kernel(
    m0_ref, m1_ref, m2_ref, x0_ref, z1_ref, z2_ref, far_ref, bgrad_ref, bindex_ref, ggrad_ref
):
    del far_ref
    own = message_table(m0_ref)
    here = [halves(a, b) for a, b in zip(slot_tiles(m0_ref), slot_tiles(x0_ref))]
    near = near_tiles(z1_ref, z2_ref)
    work = [
        body_work(here, own),
        body_work(near, own),
        garm_work(slot_tiles(m0_ref), own, message_table(x0_ref)),
        garm_work(near_tiles(m1_ref, m2_ref), message_table(z1_ref), message_table(z2_ref)),
    ]
    out = gradients(work)
    for n in range(2):
        rows = slice(n * SUB, (n + 1) * SUB)
        bgrad_ref[rows, :] = jnp.concatenate(out[n], axis=1)
        ggrad_ref[rows, :] = jnp.concatenate(out[2 + n][:3], axis=1)
    bindex_ref[:SUB, :] = here[4]
    bindex_ref[SUB:, :] = near[4]


def late_body_kernel(
    m0_ref, z3_ref, near_ref, far_ref, bgrad_ref, bindex_ref, out_ref, stiff_ref
):
    own = message_table(m0_ref)
    body = z3_ref.shape[0] - 5
    near = [near_ref[2 * body + k] for k in range(5)]
    far = far_tiles(z3_ref, far_ref)
    grads = [
        jnp.concatenate(rows, axis=1)
        for rows in gradients([body_work(far, own), body_work(near, own)])
    ]
    index = jnp.concatenate([bindex_ref[...], far[4], near[4]], axis=0)
    total = scatter(index, jnp.concatenate([bgrad_ref[...]] + grads, axis=0), out_ref.shape[1])
    for c in range(3):
        out_ref[c] = total[:, c * BLOCK : (c + 1) * BLOCK]
    stiff_ref[...] = total[:, 3 * BLOCK :]


def late_garm_kernel(
    m1_ref, m2_ref, m3_ref, z3_ref, near_ref, far_ref, ggrad_ref, index_ref, out_ref
):
    body = z3_ref.shape[0] - 5
    step = body // 4
    tables = [read_table(near_ref, n * body, step) for n in range(2)]
    work = [
        garm_work(slot_tiles(m3_ref), message_table(z3_ref), read_table(far_ref, 0, step)),
        garm_work(cross_tiles(m1_ref, m2_ref), *tables),
    ]
    grads = [jnp.concatenate(rows[:3], axis=1) for rows in gradients(work)]
    index = jnp.concatenate([index_ref[k] for k in range(index_ref.shape[0])], axis=0)
    total = scatter(index, jnp.concatenate([ggrad_ref[...]] + grads, axis=0), out_ref.shape[1])
    for c in range(3):
        out_ref[c] = total[:, c * BLOCK : (c + 1) * BLOCK]


def final_kernel(garm_ref, body_ref, mine_ref, other_ref, garm_out, body_out, stiff_out):
    stiff_out[...] = mine_ref[...] + other_ref[...]
    body_out[...] = body_ref[...]
    garm_out[...] = garm_ref[...]


def stage_kernel(*refs):
    hbm, (index_ref, *out_refs), vmem, sems = refs[:7], refs[7:12], refs[12:19], refs[19]
    copies = [
        pltpu.make_async_copy(src, dst, sems.at[k]) for k, (src, dst) in enumerate(zip(hbm, vmem))
    ]
    for copy in copies:
        copy.start()
    for copy in copies:
        copy.wait()
    pg_ref, pb_ref, pc_ref, garm_ref, cot_ref, body_ref, stiff_ref = vmem
    cap = pg_ref.shape[0]
    tiles = stiff_ref.shape[0]
    width = lax.axis_size("body")
    here, column = lax.axis_index("garm"), lax.axis_index("body")
    for k, out_ref in enumerate(out_refs):
        for q in range(3 * tiles):
            out_ref[4 + q] = body_ref[q]
        for q in range(tiles):
            out_ref[4 + 3 * tiles + q] = stiff_ref[q]
        for x in range(2):
            owner = (here ^ k) * width + (column ^ x)
            live = pc_ref[0, owner]
            for s in range(cap):
                g = pg_ref[s, owner]
                row, place = pl.ds(g, 1), pl.ds(x * cap + s, 1)
                for c in range(3):
                    out_ref[c, place, :] = garm_ref[c, row, :]
                out_ref[3, place, :] = jnp.where(s < live, cot_ref[row, :], 0.0)
                out_ref[4 + 4 * tiles, place, :] = jnp.full(
                    (1, BLOCK), pb_ref[s, owner].astype(f32), f32
                )
                if k in DISTANCES[:2]:
                    spot, line = 1 + 2 * x, DISTANCES.index(k) * cap + s
                else:
                    spot, line = (0 if k == 0 else 2), x * cap + s
                index_ref[spot, line : line + 1, :] = jnp.full((1, BLOCK), g.astype(f32), f32)


def staged(garment, cotangent, body_points, stiffness, pg, pb, pc):
    verts = garment.shape[2]
    points = body_points.shape[2]
    blocks = points // BLOCK
    tiles = blocks // SUB
    garm_n = lax.axis_size("garm")
    message = jax.ShapeDtypeStruct((5 + 4 * tiles, SUB, BLOCK), f32)
    arrays = (
        pg,
        pb,
        pc,
        garment.reshape(3, verts // BLOCK, BLOCK),
        cotangent.reshape(verts // BLOCK, BLOCK),
        body_points.reshape(3 * tiles, SUB, BLOCK),
        stiffness.reshape(tiles, SUB, BLOCK),
    )
    index, *sent = pl.pallas_call(
        stage_kernel,
        out_shape=[jax.ShapeDtypeStruct((garm_n, SUB, BLOCK), f32)] + [message] * garm_n,
        in_specs=[pl.BlockSpec(memory_space=pltpu.HBM)] * len(arrays),
        out_specs=[pl.BlockSpec(memory_space=pltpu.VMEM)] * (garm_n + 1),
        scratch_shapes=[
            (pltpu.SMEM if k < 3 else pltpu.VMEM)(a.shape, a.dtype) for k, a in enumerate(arrays)
        ]
        + [pltpu.SemaphoreType.DMA((len(arrays),))],
        compiler_params=pltpu.CompilerParams(vmem_limit_bytes=VMEM_LIMIT),
    )(*[pltpu.with_memory_space_constraint(a, pltpu.HBM) for a in arrays])

    def along_garm(k):
        return lax.ppermute(sent[k], "garm", [(z, z ^ k) for z in range(garm_n)])

    def along_body(value):
        return lax.ppermute(value, "body", [(0, 1), (1, 0)])

    first, second, third = [along_garm(k) for k in DISTANCES]
    one, two, three = [sent[k] for k in DISTANCES]
    x0 = along_body(sent[0])
    body = 4 * tiles
    near = call(
        near_bundle_kernel,
        jax.ShapeDtypeStruct((2 * body + 5, SUB, BLOCK), f32),
        [],
        (),
        (first, second, x0),
    )
    far = call(
        far_bundle_kernel,
        jax.ShapeDtypeStruct((body + 3, SUB, BLOCK), f32),
        [],
        (),
        (third, near),
    )
    near_other, far_other = along_body(near), along_body(far)
    bgrad, bindex, ggrad = call(
        early_kernel,
        (
            jax.ShapeDtypeStruct((2 * SUB, 4 * BLOCK), f32),
            jax.ShapeDtypeStruct((2 * SUB, BLOCK), f32),
            jax.ShapeDtypeStruct((2 * SUB, 3 * BLOCK), f32),
        ),
        [],
        (),
        (sent[0], one, two, x0, first, second, far),
    )
    body_shape = jax.ShapeDtypeStruct((3, blocks, BLOCK), f32)
    stiff_shape = jax.ShapeDtypeStruct((blocks, BLOCK), f32)
    garm_shape = jax.ShapeDtypeStruct((3, verts // BLOCK, BLOCK), f32)
    body_total, stiff = call(
        late_body_kernel,
        (body_shape, stiff_shape),
        [],
        (),
        (sent[0], third, near_other, far_other, bgrad, bindex),
    )
    stiff_other = lax.ppermute(stiff, "frame", [(0, 1), (1, 0)])
    garm_total = call(
        late_garm_kernel,
        garm_shape,
        [],
        (),
        (one, two, three, third, near_other, far_other, ggrad, index),
    )
    return call(
        final_kernel,
        (garm_shape, body_shape, stiff_shape),
        [],
        (),
        (garm_total, body_total, stiff, stiff_other),
    )


def per_device(garment, cotangent, body_points, stiffness, pair_garment, pair_body, pair_count):
    owners = lax.axis_size(("garm", "body"))
    verts = garment.shape[2]
    points = body_points.shape[2]
    blocks = points // BLOCK
    cap = pair_garment.shape[3]
    slots = owners * cap
    pg = pair_garment.reshape(owners, cap).T
    pb = pair_body.reshape(owners, cap).T
    pc = pair_count.reshape(1, owners)
    if (lax.axis_size("garm"), lax.axis_size("body")) == (4, 2) and cap == SUB // 2:
        garm_grad, body_grad, stiff = staged(
            garment, cotangent, body_points, stiffness, pg, pb, pc
        )
        return (
            garm_grad.reshape(1, 3, verts),
            body_grad.reshape(1, 3, points),
            stiff.reshape(points),
        )
    message = call(
        pack_kernel,
        jax.ShapeDtypeStruct((owners, 5 + blocks, cap, BLOCK), f32),
        [],
        (pg, pb, pc),
        (
            garment.reshape(3, verts // BLOCK, BLOCK),
            cotangent.reshape(verts // BLOCK, BLOCK),
            body_points.reshape(3, blocks, BLOCK),
            stiffness.reshape(blocks, BLOCK),
        ),
    )
    arrived = lax.all_to_all(message, ("garm", "body"), split_axis=0, concat_axis=0, tiled=True)
    rows = pltpu.VMEM((4, slots, BLOCK), f32)
    grad = pltpu.VMEM((slots, 4 * BLOCK), f32)
    index = pltpu.VMEM((slots, BLOCK), f32)
    body_grad, stiff = call(
        body_kernel,
        (
            jax.ShapeDtypeStruct((3, blocks, BLOCK), f32),
            jax.ShapeDtypeStruct((blocks, BLOCK), f32),
        ),
        [rows, rows, pltpu.VMEM((blocks, 4 * BLOCK), f32), index, grad],
        (),
        (message, arrived),
    )
    other = lax.ppermute(stiff, "frame", [(0, 1), (1, 0)])
    garm_grad = call(
        garm_kernel,
        jax.ShapeDtypeStruct((3, verts // BLOCK, BLOCK), f32),
        [rows, rows, index, grad],
        (pg, pb),
        (message, arrived),
    )
    return (
        garm_grad.reshape(1, 3, verts),
        body_grad.reshape(1, 3, points),
        (stiff + other).reshape(points),
    )


def solution(mesh):
    in_specs = (
        P(("grp", "frame"), None, ("garm", "body")),
        P(("grp", "frame"), ("garm", "body")),
        P(("grp", "frame"), None, ("garm", "body")),
        P(("grp", "garm", "body")),
        P(("grp", "frame"), ("garm", "body"), None, None),
        P(("grp", "frame"), ("garm", "body"), None, None),
        P(("grp", "frame"), ("garm", "body"), None),
    )
    out_specs = (
        P(("grp", "frame"), None, ("garm", "body")),
        P(("grp", "frame"), None, ("garm", "body")),
        P(("grp", "garm", "body")),
    )
    return jax.shard_map(
        per_device, mesh=mesh, in_specs=in_specs, out_specs=out_specs, check_vma=False
    )
```

```python
import functools
import math

import jax
import jax.numpy as jnp
from jax import lax
from jax.experimental import pallas as pl
from jax.experimental.pallas import tpu as pltpu
from jax.sharding import PartitionSpec as P

BLOCK = 128
SUB = 8
EARLY_COST = 40_000_000_000
BUNDLE_COST = 1000
DISTANCES = (1, 2, 3)
COPIES = (0, 1, 1, 2, 2, 3, 3)
EXTRA = (0, 0, 1, 0, 2, 0, 3)
VMEM_LIMIT = 32 * 1024 * 1024

amplitude = 0.05
width_sq = 4.0

SCALE = math.sqrt(math.log2(math.e) / width_sq)
FACTOR = -2.0 / width_sq * amplitude

f32 = jnp.float32
bf16 = jnp.bfloat16


def pieces(value, count):
    out = []
    for _ in range(count - 1):
        top = value.astype(bf16).astype(f32)
        out.append(top)
        value = value - top
    out.append(value)
    return out


def features(left, right):
    lpos = [left[c] * SCALE for c in range(3)]
    rpos = [right[c] * SCALE for c in range(3)]
    lnorm = -(lpos[0] * lpos[0] + lpos[1] * lpos[1] + lpos[2] * lpos[2])
    rnorm = -(rpos[0] * rpos[0] + rpos[1] * rpos[1] + rpos[2] * rpos[2])
    one = jnp.ones_like(lnorm)
    lrows, rrows = [], []
    for c in range(3):
        l1, l2, l3 = pieces(lpos[c] * 2.0, 3)
        r1, r2, r3 = pieces(rpos[c], 3)
        lrows += [l1, l1, l2, l2, l1, l3]
        rrows += [r1, r2, r1, r2, r3, r1]
    lrows += pieces(lnorm, 3) + [one] * 3
    rrows += [one] * 3 + pieces(rnorm, 3)
    return (
        jnp.concatenate(lrows, axis=0).astype(bf16),
        jnp.concatenate(rrows, axis=0).astype(bf16),
    )


def pull(batches):
    made = []
    for left, right in batches:
        lfeat, rfeat = features(left, right)
        weight = left[3]
        coeff = jnp.concatenate([weight * left[c] for c in range(3)] + [weight], axis=0)
        chi, clo = [part.astype(bf16) for part in pieces(coeff, 2)]
        lhs = jnp.concatenate(
            [
                jnp.concatenate([chi, chi], axis=1),
                jnp.concatenate([clo, jnp.zeros_like(clo)], axis=1),
            ],
            axis=0,
        )
        made.append((lfeat.T, rfeat, lhs))
    row = lax.broadcasted_iota(jnp.int32, made[0][1].shape, 0) % SUB
    sub = lax.broadcasted_iota(jnp.int32, (4 * SUB, BLOCK), 0) % SUB
    totals = [jnp.zeros((4 * SUB, BLOCK), f32) for _ in batches]
    for pair in range(0, SUB, 2):
        masks = [(row == pair + k).astype(f32).astype(bf16) for k in range(2)]
        for n, (lfeat_t, rfeat, lhs) in enumerate(made):
            rhs = jnp.concatenate([rfeat * mask for mask in masks], axis=1)
            exponent = jnp.dot(lfeat_t, rhs, preferred_element_type=f32)
            kernel = jnp.exp2(exponent)
            khi = kernel.astype(bf16)
            klo = (kernel - khi.astype(f32)).astype(bf16)
            sums = jnp.dot(lhs, jnp.concatenate([khi, klo], axis=0), preferred_element_type=f32)
            sums = sums[: 4 * SUB] + sums[4 * SUB :]
            for k in range(2):
                part = sums[:, k * BLOCK : (k + 1) * BLOCK]
                totals[n] = jnp.where(sub == pair + k, part, totals[n])
    return [[total[c * SUB : (c + 1) * SUB] for c in range(4)] for total in totals]


def gradients(batches):
    out = []
    for (_, right), total in zip(batches, pull(batches)):
        rows = [FACTOR * right[3] * (right[c] * total[3] - total[c]) for c in range(3)]
        out.append(rows + [amplitude * total[3]])
    return out


def run_batches(left_ref, right_ref, grad_ref):
    batches = left_ref.shape[1] // SUB
    group = math.gcd(batches, 4)

    def step(k, carry):
        places = [pl.ds(pl.multiple_of((k * group + n) * SUB, SUB), SUB) for n in range(group)]
        work = [
            tuple([ref[c, rows, :] for c in range(4)] for ref in (left_ref, right_ref))
            for rows in places
        ]
        for rows, values in zip(places, gradients(work)):
            for c, value in enumerate(values):
                grad_ref[rows, c * BLOCK : (c + 1) * BLOCK] = value
        return carry

    lax.fori_loop(0, batches // group, step, 0)


def scatter(index, grads, blocks):
    lane = lax.broadcasted_iota(jnp.int32, index.shape, 1).astype(f32)
    onehot_t = (index == lane).astype(f32).T[:blocks].astype(bf16)
    parts = [
        jnp.dot(onehot_t, part.astype(bf16), preferred_element_type=f32)
        for part in pieces(grads, 3)
    ]
    return parts[0] + parts[1] + parts[2]


def pack_kernel(pg_ref, pb_ref, pc_ref, garm_ref, cot_ref, body_ref, stiff_ref, out_ref):
    cap, owners = pg_ref.shape
    tiles = stiff_ref.shape[0] // cap

    def one(d, carry):
        for s in range(cap):
            row = pl.ds(pg_ref[s, d], 1)
            for c in range(3):
                out_ref[d, c, s : s + 1, :] = garm_ref[c, row, :]
            out_ref[d, 3, s : s + 1, :] = jnp.where(s < pc_ref[0, d], cot_ref[row, :], 0.0)
            out_ref[d, 4 + 4 * tiles, s : s + 1, :] = jnp.full(
                (1, BLOCK), pb_ref[s, d].astype(f32), f32
            )
        for q in range(tiles):
            rows = slice(q * cap, (q + 1) * cap)
            for c in range(3):
                out_ref[d, 4 + c * tiles + q] = body_ref[c, rows, :]
            out_ref[d, 4 + 3 * tiles + q] = stiff_ref[rows, :]
        return carry

    if owners <= 8:
        for d in range(owners):
            one(d, 0)
    else:
        lax.fori_loop(0, owners, one, 0)


def over(count, fn):
    if count <= 8:
        for d in range(count):
            fn(d)
    else:
        lax.fori_loop(0, count, lambda d, carry: (fn(d), carry)[1], 0)


def body_kernel(own_ref, in_ref, out_ref, stiff_ref, left, right, table, index, grad):
    owners, tiles, cap, _ = in_ref.shape
    blocks = tiles - 5

    def take(d):
        rows = pl.ds(d * cap, cap)
        for c in range(4):
            left[c, rows, :] = in_ref[d, c]
        index[rows, :] = in_ref[d, tiles - 1]

    over(owners, take)
    for c in range(4):
        for q in range(blocks // 4):
            table[4 * q : 4 * q + 4, c * BLOCK : (c + 1) * BLOCK] = own_ref[
                0, 4 + c * (blocks // 4) + q
            ]
    lane = lax.broadcasted_iota(jnp.int32, index.shape, 1).astype(f32)
    onehot = (index[...] == lane).astype(f32)[:, :blocks].astype(bf16)
    chosen = [
        jnp.dot(onehot, part.astype(bf16), preferred_element_type=f32)
        for part in pieces(table[...], 3)
    ]
    chosen = chosen[0] + chosen[1] + chosen[2]
    for c in range(4):
        right[c] = chosen[:, c * BLOCK : (c + 1) * BLOCK]
    run_batches(left, right, grad)
    total = scatter(index[...], grad[...], blocks)
    for c in range(3):
        out_ref[c] = total[:, c * BLOCK : (c + 1) * BLOCK]
    stiff_ref[...] = total[:, 3 * BLOCK :]


def garm_kernel(pg_ref, pb_ref, own_ref, in_ref, out_ref, left, right, index, grad):
    owners, tiles, cap, _ = in_ref.shape
    blocks = tiles - 5
    garm_blocks = out_ref.shape[1]

    def take(d):
        rows = pl.ds(d * cap, cap)
        for c in range(4):
            right[c, rows, :] = own_ref[d, c]
        for s in range(cap):
            b = pb_ref[s, d]
            for c in range(4):
                left[c, pl.ds(d * cap + s, 1), :] = in_ref[
                    d, 4 + c * (blocks // 4) + b // 4, pl.ds(b % 4, 1), :
                ]
            index[pl.ds(d * cap + s, 1), :] = jnp.full((1, BLOCK), pg_ref[s, d].astype(f32), f32)

    over(owners, take)
    run_batches(left, right, grad)
    total = scatter(index[...], grad[...], garm_blocks)
    for c in range(3):
        out_ref[c] = total[:, c * BLOCK : (c + 1) * BLOCK]


def call(kernel, out_shape, scratch, scalars, arrays, cost=None):
    specs = [pl.BlockSpec(memory_space=pltpu.SMEM)] * len(scalars)
    specs += [pl.BlockSpec(memory_space=pltpu.VMEM)] * len(arrays)
    return pl.pallas_call(
        kernel,
        out_shape=out_shape,
        in_specs=specs,
        out_specs=jax.tree.map(lambda _: pl.BlockSpec(memory_space=pltpu.VMEM), out_shape),
        scratch_shapes=scratch,
        cost_estimate=cost and pl.CostEstimate(flops=cost, bytes_accessed=1000, transcendentals=0),
        compiler_params=pltpu.CompilerParams(vmem_limit_bytes=VMEM_LIMIT),
    )(*scalars, *arrays)


def read_table(ref, start, step):
    columns = [
        jnp.concatenate([ref[start + c * step + q] for q in range(step)], axis=0) for c in range(4)
    ]
    return jnp.concatenate(columns, axis=1)


def choose(index, table):
    lane = lax.broadcasted_iota(jnp.int32, index.shape, 1).astype(f32)
    onehot = (index == lane).astype(f32)[:, : table.shape[0]].astype(bf16)
    parts = [
        jnp.dot(onehot, part.astype(bf16), preferred_element_type=f32)
        for part in pieces(table, 3)
    ]
    rows = parts[0] + parts[1] + parts[2]
    return [rows[:, c * BLOCK : (c + 1) * BLOCK] for c in range(4)]


def halves(top, bottom):
    row = lax.broadcasted_iota(jnp.int32, (SUB, BLOCK), 0)
    return jnp.where(row < SUB // 2, top, bottom)


def flip(value):
    return pltpu.roll(value, SUB // 2, 0)


def body_work(tiles, table):
    return list(tiles[:4]), choose(tiles[4], table)


def garm_work(tiles, top, bottom):
    row = lax.broadcasted_iota(jnp.int32, (SUB, BLOCK), 0)
    index = tiles[4] + jnp.where(row < SUB // 2, 0, top.shape[0]).astype(f32)
    return choose(index, jnp.concatenate([top, bottom], axis=0)), list(tiles[:4])


def slot_tiles(ref):
    return [ref[c] for c in range(5)]


def message_table(ref, step):
    return read_table(ref, 5, step)


def pack_slots(ref):
    a, b, c, d, e = slot_tiles(ref)
    return [halves(flip(a), b), halves(flip(c), d), e]


def unpack_top(tiles):
    a, b, c = tiles
    return [a, flip(a), b, flip(b), flip(c)]


def unpack_bottom(tiles):
    a, b, c = tiles
    return [flip(a), a, flip(b), b, c]


def near_bundle_kernel(own_ref, first_ref, second_down, second_up, out_ref, second_ref):
    second_ref[...] = second_down[: second_ref.shape[0]] + second_up[...]
    body = own_ref.shape[0] - 5
    for n, ref in enumerate((own_ref, first_ref, second_ref)):
        for q in range(body):
            out_ref[n * body + q] = ref[5 + q]
    for k, (a, b) in enumerate(zip(slot_tiles(first_ref), slot_tiles(second_ref))):
        out_ref[3 * body + k] = halves(flip(a), b)
    for k, tile in enumerate(pack_slots(own_ref)):
        out_ref[3 * body + 5 + k] = tile


def far_bundle_kernel(third_down, third_up, near_ref, out_ref, third_ref):
    del near_ref
    third_ref[...] = third_down[: third_ref.shape[0]] + third_up[...]
    body = third_ref.shape[0] - 5
    for q in range(body):
        out_ref[q] = third_ref[5 + q]
    for k, tile in enumerate(pack_slots(third_ref)):
        out_ref[body + k] = tile


def top_tiles(one_ref, two_ref):
    return [halves(a, flip(b)) for a, b in zip(slot_tiles(one_ref), slot_tiles(two_ref))]


def bottom_tiles(one_ref, two_ref):
    return [halves(flip(a), b) for a, b in zip(slot_tiles(one_ref), slot_tiles(two_ref))]


def early_kernel(
    m0_ref,
    m1_ref,
    m2_ref,
    m3_ref,
    first_ref,
    second_ref,
    third_ref,
    far_ref,
    bgrad_ref,
    bindex_ref,
    ggrad_ref,
):
    del far_ref
    step = (m0_ref.shape[0] - 5) // 4
    own = message_table(m0_ref, step)
    here = top_tiles(m0_ref, third_ref)
    near = top_tiles(first_ref, second_ref)
    work = [
        body_work(here, own),
        body_work(near, own),
        garm_work(top_tiles(m0_ref, m3_ref), own, message_table(third_ref, step)),
        garm_work(
            top_tiles(m1_ref, m2_ref),
            message_table(first_ref, step),
            message_table(second_ref, step),
        ),
    ]
    out = gradients(work)
    for n in range(2):
        rows = slice(n * SUB, (n + 1) * SUB)
        bgrad_ref[rows, :] = jnp.concatenate(out[n], axis=1)
        ggrad_ref[rows, :] = jnp.concatenate(out[2 + n][:3], axis=1)
    bindex_ref[:SUB, :] = here[4]
    bindex_ref[SUB:, :] = near[4]


def late_body_kernel(m0_ref, near_ref, far_ref, bgrad_ref, bindex_ref, out_ref, stiff_ref):
    body = m0_ref.shape[0] - 5
    own = message_table(m0_ref, body // 4)
    near = [near_ref[3 * body + k] for k in range(5)]
    top = unpack_top([near_ref[3 * body + 5 + k] for k in range(3)])
    bottom = unpack_bottom([far_ref[body + k] for k in range(3)])
    here = [halves(a, b) for a, b in zip(top, bottom)]
    grads = [
        jnp.concatenate(rows, axis=1)
        for rows in gradients([body_work(here, own), body_work(near, own)])
    ]
    index = jnp.concatenate([bindex_ref[...], here[4], near[4]], axis=0)
    total = scatter(index, jnp.concatenate([bgrad_ref[...]] + grads, axis=0), out_ref.shape[1])
    for c in range(3):
        out_ref[c] = total[:, c * BLOCK : (c + 1) * BLOCK]
    stiff_ref[...] = total[:, 3 * BLOCK :]


def late_garm_kernel(
    m0_ref, m1_ref, m2_ref, m3_ref, near_ref, far_ref, ggrad_ref, index_ref, out_ref
):
    body = m0_ref.shape[0] - 5
    step = body // 4
    own, first, second = [read_table(near_ref, n * body, step) for n in range(3)]
    work = [
        garm_work(bottom_tiles(m0_ref, m3_ref), own, read_table(far_ref, 0, step)),
        garm_work(bottom_tiles(m1_ref, m2_ref), first, second),
    ]
    grads = [jnp.concatenate(rows[:3], axis=1) for rows in gradients(work)]
    index = jnp.concatenate([index_ref[k] for k in range(index_ref.shape[0])], axis=0)
    total = scatter(index, jnp.concatenate([ggrad_ref[...]] + grads, axis=0), out_ref.shape[1])
    for c in range(3):
        out_ref[c] = total[:, c * BLOCK : (c + 1) * BLOCK]


def final_kernel(garm_ref, body_ref, mine_ref, other_ref, garm_out, body_out, stiff_out):
    stiff_out[...] = mine_ref[...] + other_ref[...]
    body_out[...] = body_ref[...]
    garm_out[...] = garm_ref[...]


def stage_kernel(count, *refs):
    hbm, (index_ref, *out_refs), (vmem, sems) = refs[:7], refs[7 : 8 + count], (refs[-8:-1], refs[-1])
    copies = [
        pltpu.make_async_copy(src, dst, sems.at[k]) for k, (src, dst) in enumerate(zip(hbm, vmem))
    ]
    for copy in copies:
        copy.start()
    for copy in copies:
        copy.wait()
    pg_ref, pb_ref, pc_ref, garm_ref, cot_ref, body_ref, stiff_ref = vmem
    cap = pg_ref.shape[0]
    tiles = stiff_ref.shape[0]
    width = lax.axis_size("body")
    here, column = lax.axis_index("garm"), lax.axis_index("body")
    for n, out_ref in enumerate(out_refs):
        for q in range(3 * tiles):
            out_ref[5 + q] = body_ref[q]
        for q in range(tiles):
            out_ref[5 + 3 * tiles + q] = stiff_ref[q]
        for q in range(5 + 4 * tiles, out_ref.shape[0]):
            out_ref[q] = jnp.zeros((SUB, BLOCK), f32)
    for k in range(len(DISTANCES) + 1):
        targets = [ref for n, ref in enumerate(out_refs) if COPIES[n] == k]
        for x in range(2):
            owner = (here ^ k) * width + (column ^ x)
            live = pc_ref[0, owner]
            for s in range(cap):
                g = pg_ref[s, owner]
                row, place = pl.ds(g, 1), pl.ds(x * cap + s, 1)
                values = [garm_ref[c, row, :] for c in range(3)]
                values.append(jnp.where(s < live, cot_ref[row, :], 0.0))
                values.append(jnp.full((1, BLOCK), pb_ref[s, owner].astype(f32), f32))
                for out_ref in targets:
                    for c, value in enumerate(values):
                        out_ref[c, place, :] = value
                if k in DISTANCES[:2]:
                    spot, line = 2 * x + 1, DISTANCES.index(k) * cap + s
                else:
                    spot, line = 2 * x, (0 if k == 0 else cap) + s
                index_ref[spot, line : line + 1, :] = jnp.full((1, BLOCK), g.astype(f32), f32)


def staged(garment, cotangent, body_points, stiffness, pg, pb, pc):
    verts = garment.shape[2]
    points = body_points.shape[2]
    blocks = points // BLOCK
    tiles = blocks // SUB
    garm_n = lax.axis_size("garm")
    messages = [
        jax.ShapeDtypeStruct((5 + 4 * tiles + extra, SUB, BLOCK), f32) for extra in EXTRA
    ]
    message = messages[0]
    arrays = (
        pg,
        pb,
        pc,
        garment.reshape(3, verts // BLOCK, BLOCK),
        cotangent.reshape(verts // BLOCK, BLOCK),
        body_points.reshape(3 * tiles, SUB, BLOCK),
        stiffness.reshape(tiles, SUB, BLOCK),
    )
    index, own, one, one_down, two, two_down, three, three_down = pl.pallas_call(
        functools.partial(stage_kernel, len(messages)),
        out_shape=[jax.ShapeDtypeStruct((garm_n, SUB, BLOCK), f32)] + messages,
        in_specs=[pl.BlockSpec(memory_space=pltpu.HBM)] * len(arrays),
        out_specs=[pl.BlockSpec(memory_space=pltpu.VMEM)] * (len(messages) + 1),
        scratch_shapes=[
            (pltpu.SMEM if k < 3 else pltpu.VMEM)(a.shape, a.dtype) for k, a in enumerate(arrays)
        ]
        + [pltpu.SemaphoreType.DMA((len(arrays),))],
        compiler_params=pltpu.CompilerParams(vmem_limit_bytes=VMEM_LIMIT),
    )(*[pltpu.with_memory_space_constraint(a, pltpu.HBM) for a in arrays])

    def along_garm(value, k, ways):
        pairs = [(z, z ^ k) for z in range(garm_n) if (z > z ^ k) in ways]
        return lax.ppermute(value, "garm", pairs)

    def along_body(value):
        return lax.ppermute(value, "body", [(0, 1), (1, 0)])

    third = [
        along_garm(three_down, DISTANCES[2], (True,)),
        along_garm(three, DISTANCES[2], (False,)),
    ]
    second = [
        along_garm(two_down, DISTANCES[1], (True,)),
        along_garm(two, DISTANCES[1], (False,)),
    ]
    first = along_garm(one_down, DISTANCES[0], (True, False))
    body = 4 * tiles
    near, second = call(
        near_bundle_kernel,
        (jax.ShapeDtypeStruct((3 * body + 8, SUB, BLOCK), f32), message),
        [],
        (),
        (own, first, *second),
        BUNDLE_COST,
    )
    far, third = call(
        far_bundle_kernel,
        (jax.ShapeDtypeStruct((body + 3, SUB, BLOCK), f32), message),
        [],
        (),
        (*third, near),
        BUNDLE_COST,
    )
    near_other, far_other = along_body(near), along_body(far)
    bgrad, bindex, ggrad = call(
        early_kernel,
        (
            jax.ShapeDtypeStruct((2 * SUB, 4 * BLOCK), f32),
            jax.ShapeDtypeStruct((2 * SUB, BLOCK), f32),
            jax.ShapeDtypeStruct((2 * SUB, 3 * BLOCK), f32),
        ),
        [],
        (),
        (own, one, two, three, first, second, third, far),
        EARLY_COST,
    )
    body_shape = jax.ShapeDtypeStruct((3, blocks, BLOCK), f32)
    stiff_shape = jax.ShapeDtypeStruct((blocks, BLOCK), f32)
    garm_shape = jax.ShapeDtypeStruct((3, verts // BLOCK, BLOCK), f32)
    body_total, stiff = call(
        late_body_kernel,
        (body_shape, stiff_shape),
        [],
        (),
        (own, near_other, far_other, bgrad, bindex),
    )
    stiff_other = lax.ppermute(stiff, "frame", [(0, 1), (1, 0)])
    garm_total = call(
        late_garm_kernel,
        garm_shape,
        [],
        (),
        (own, one, two, three, near_other, far_other, ggrad, index),
    )
    return call(
        final_kernel,
        (garm_shape, body_shape, stiff_shape),
        [],
        (),
        (garm_total, body_total, stiff, stiff_other),
    )


def per_device(garment, cotangent, body_points, stiffness, pair_garment, pair_body, pair_count):
    owners = lax.axis_size(("garm", "body"))
    verts = garment.shape[2]
    points = body_points.shape[2]
    blocks = points // BLOCK
    cap = pair_garment.shape[3]
    slots = owners * cap
    pg = pair_garment.reshape(owners, cap).T
    pb = pair_body.reshape(owners, cap).T
    pc = pair_count.reshape(1, owners)
    if (lax.axis_size("garm"), lax.axis_size("body")) == (4, 2) and cap == SUB // 2:
        garm_grad, body_grad, stiff = staged(
            garment, cotangent, body_points, stiffness, pg, pb, pc
        )
        return (
            garm_grad.reshape(1, 3, verts),
            body_grad.reshape(1, 3, points),
            stiff.reshape(points),
        )
    message = call(
        pack_kernel,
        jax.ShapeDtypeStruct((owners, 5 + blocks, cap, BLOCK), f32),
        [],
        (pg, pb, pc),
        (
            garment.reshape(3, verts // BLOCK, BLOCK),
            cotangent.reshape(verts // BLOCK, BLOCK),
            body_points.reshape(3, blocks, BLOCK),
            stiffness.reshape(blocks, BLOCK),
        ),
    )
    arrived = lax.all_to_all(message, ("garm", "body"), split_axis=0, concat_axis=0, tiled=True)
    rows = pltpu.VMEM((4, slots, BLOCK), f32)
    grad = pltpu.VMEM((slots, 4 * BLOCK), f32)
    index = pltpu.VMEM((slots, BLOCK), f32)
    body_grad, stiff = call(
        body_kernel,
        (
            jax.ShapeDtypeStruct((3, blocks, BLOCK), f32),
            jax.ShapeDtypeStruct((blocks, BLOCK), f32),
        ),
        [rows, rows, pltpu.VMEM((blocks, 4 * BLOCK), f32), index, grad],
        (),
        (message, arrived),
    )
    other = lax.ppermute(stiff, "frame", [(0, 1), (1, 0)])
    garm_grad = call(
        garm_kernel,
        jax.ShapeDtypeStruct((3, verts // BLOCK, BLOCK), f32),
        [rows, rows, index, grad],
        (pg, pb),
        (message, arrived),
    )
    return (
        garm_grad.reshape(1, 3, verts),
        body_grad.reshape(1, 3, points),
        (stiff + other).reshape(points),
    )


def solution(mesh):
    in_specs = (
        P(("grp", "frame"), None, ("garm", "body")),
        P(("grp", "frame"), ("garm", "body")),
        P(("grp", "frame"), None, ("garm", "body")),
        P(("grp", "garm", "body")),
        P(("grp", "frame"), ("garm", "body"), None, None),
        P(("grp", "frame"), ("garm", "body"), None, None),
        P(("grp", "frame"), ("garm", "body"), None),
    )
    out_specs = (
        P(("grp", "frame"), None, ("garm", "body")),
        P(("grp", "frame"), None, ("garm", "body")),
        P(("grp", "garm", "body")),
    )
    return jax.shard_map(
        per_device, mesh=mesh, in_specs=in_specs, out_specs=out_specs, check_vma=False
    )
```

```python
import math

import jax
import jax.numpy as jnp
from jax import lax
from jax.experimental import pallas as pl
from jax.experimental.pallas import tpu as pltpu
from jax.sharding import PartitionSpec as P

BLOCK = 128
SUB = 8
VMEM_LIMIT = 32 * 1024 * 1024
EARLY_COST = 40_000_000_000
BUNDLE_COST = 1000

amplitude = 0.05
width_sq = 4.0

SCALE = math.sqrt(math.log2(math.e) / width_sq)
FACTOR = -2.0 / width_sq * amplitude

f32 = jnp.float32
bf16 = jnp.bfloat16


def pieces(value, count):
    out = []
    for _ in range(count - 1):
        top = value.astype(bf16).astype(f32)
        out.append(top)
        value = value - top
    out.append(value)
    return out


def features(left, right):
    lpos = [left[c] * SCALE for c in range(3)]
    rpos = [right[c] * SCALE for c in range(3)]
    lnorm = -(lpos[0] * lpos[0] + lpos[1] * lpos[1] + lpos[2] * lpos[2])
    rnorm = -(rpos[0] * rpos[0] + rpos[1] * rpos[1] + rpos[2] * rpos[2])
    one = jnp.ones_like(lnorm)
    lrows, rrows = [], []
    for c in range(3):
        l1, l2, l3 = pieces(lpos[c] * 2.0, 3)
        r1, r2, r3 = pieces(rpos[c], 3)
        lrows += [l1, l1, l2, l2, l1, l3]
        rrows += [r1, r2, r1, r2, r3, r1]
    lrows += pieces(lnorm, 3) + [one] * 3
    rrows += [one] * 3 + pieces(rnorm, 3)
    return (
        jnp.concatenate(lrows, axis=0).astype(bf16),
        jnp.concatenate(rrows, axis=0).astype(bf16),
    )


def pull(batches):
    made = []
    for left, right in batches:
        lfeat, rfeat = features(left, right)
        weight = left[3]
        coeff = jnp.concatenate([weight * left[c] for c in range(3)] + [weight], axis=0)
        chi, clo = [part.astype(bf16) for part in pieces(coeff, 2)]
        lhs = jnp.concatenate(
            [
                jnp.concatenate([chi, chi], axis=1),
                jnp.concatenate([clo, jnp.zeros_like(clo)], axis=1),
            ],
            axis=0,
        )
        made.append((lfeat.T, rfeat, lhs))
    row = lax.broadcasted_iota(jnp.int32, made[0][1].shape, 0) % SUB
    sub = lax.broadcasted_iota(jnp.int32, (4 * SUB, BLOCK), 0) % SUB
    totals = [jnp.zeros((4 * SUB, BLOCK), f32) for _ in batches]
    for pair in range(0, SUB, 2):
        masks = [(row == pair + k).astype(f32).astype(bf16) for k in range(2)]
        for n, (lfeat_t, rfeat, lhs) in enumerate(made):
            rhs = jnp.concatenate([rfeat * mask for mask in masks], axis=1)
            exponent = jnp.dot(lfeat_t, rhs, preferred_element_type=f32)
            kernel = jnp.exp2(exponent)
            khi = kernel.astype(bf16)
            klo = (kernel - khi.astype(f32)).astype(bf16)
            sums = jnp.dot(lhs, jnp.concatenate([khi, klo], axis=0), preferred_element_type=f32)
            sums = sums[: 4 * SUB] + sums[4 * SUB :]
            for k in range(2):
                part = sums[:, k * BLOCK : (k + 1) * BLOCK]
                totals[n] = jnp.where(sub == pair + k, part, totals[n])
    return [[total[c * SUB : (c + 1) * SUB] for c in range(4)] for total in totals]


def gradients(batches):
    out = []
    for (_, right), total in zip(batches, pull(batches)):
        rows = [FACTOR * right[3] * (right[c] * total[3] - total[c]) for c in range(3)]
        out.append(rows + [amplitude * total[3]])
    return out


def run_batches(left_ref, right_ref, grad_ref):
    batches = left_ref.shape[1] // SUB
    group = math.gcd(batches, 4)

    def step(k, carry):
        places = [pl.ds(pl.multiple_of((k * group + n) * SUB, SUB), SUB) for n in range(group)]
        work = [
            tuple([ref[c, rows, :] for c in range(4)] for ref in (left_ref, right_ref))
            for rows in places
        ]
        for rows, values in zip(places, gradients(work)):
            for c, value in enumerate(values):
                grad_ref[rows, c * BLOCK : (c + 1) * BLOCK] = value
        return carry

    lax.fori_loop(0, batches // group, step, 0)


def scatter(index, grads, blocks):
    lane = lax.broadcasted_iota(jnp.int32, index.shape, 1).astype(f32)
    onehot_t = (index == lane).astype(f32).T[:blocks].astype(bf16)
    parts = [
        jnp.dot(onehot_t, part.astype(bf16), preferred_element_type=f32)
        for part in pieces(grads, 3)
    ]
    return parts[0] + parts[1] + parts[2]


def pack_kernel(pg_ref, pb_ref, pc_ref, garm_ref, cot_ref, body_ref, stiff_ref, out_ref):
    cap, owners = pg_ref.shape
    tiles = stiff_ref.shape[0] // cap

    def one(d, carry):
        for s in range(cap):
            row = pl.ds(pg_ref[s, d], 1)
            for c in range(3):
                out_ref[d, c, s : s + 1, :] = garm_ref[c, row, :]
            out_ref[d, 3, s : s + 1, :] = jnp.where(s < pc_ref[0, d], cot_ref[row, :], 0.0)
            out_ref[d, 4 + 4 * tiles, s : s + 1, :] = jnp.full(
                (1, BLOCK), pb_ref[s, d].astype(f32), f32
            )
        for q in range(tiles):
            rows = slice(q * cap, (q + 1) * cap)
            for c in range(3):
                out_ref[d, 4 + c * tiles + q] = body_ref[c, rows, :]
            out_ref[d, 4 + 3 * tiles + q] = stiff_ref[rows, :]
        return carry

    if owners <= 8:
        for d in range(owners):
            one(d, 0)
    else:
        lax.fori_loop(0, owners, one, 0)


def over(count, fn):
    if count <= 8:
        for d in range(count):
            fn(d)
    else:
        lax.fori_loop(0, count, lambda d, carry: (fn(d), carry)[1], 0)


def body_kernel(own_ref, in_ref, out_ref, stiff_ref, left, right, table, index, grad):
    owners, tiles, cap, _ = in_ref.shape
    blocks = tiles - 5

    def take(d):
        rows = pl.ds(d * cap, cap)
        for c in range(4):
            left[c, rows, :] = in_ref[d, c]
        index[rows, :] = in_ref[d, tiles - 1]

    over(owners, take)
    for c in range(4):
        for q in range(blocks // 4):
            table[4 * q : 4 * q + 4, c * BLOCK : (c + 1) * BLOCK] = own_ref[
                0, 4 + c * (blocks // 4) + q
            ]
    lane = lax.broadcasted_iota(jnp.int32, index.shape, 1).astype(f32)
    onehot = (index[...] == lane).astype(f32)[:, :blocks].astype(bf16)
    chosen = [
        jnp.dot(onehot, part.astype(bf16), preferred_element_type=f32)
        for part in pieces(table[...], 3)
    ]
    chosen = chosen[0] + chosen[1] + chosen[2]
    for c in range(4):
        right[c] = chosen[:, c * BLOCK : (c + 1) * BLOCK]
    run_batches(left, right, grad)
    total = scatter(index[...], grad[...], blocks)
    for c in range(3):
        out_ref[c] = total[:, c * BLOCK : (c + 1) * BLOCK]
    stiff_ref[...] = total[:, 3 * BLOCK :]


def garm_kernel(pg_ref, pb_ref, own_ref, in_ref, out_ref, left, right, index, grad):
    owners, tiles, cap, _ = in_ref.shape
    blocks = tiles - 5
    garm_blocks = out_ref.shape[1]

    def take(d):
        rows = pl.ds(d * cap, cap)
        for c in range(4):
            right[c, rows, :] = own_ref[d, c]
        for s in range(cap):
            b = pb_ref[s, d]
            for c in range(4):
                left[c, pl.ds(d * cap + s, 1), :] = in_ref[
                    d, 4 + c * (blocks // 4) + b // 4, pl.ds(b % 4, 1), :
                ]
            index[pl.ds(d * cap + s, 1), :] = jnp.full((1, BLOCK), pg_ref[s, d].astype(f32), f32)

    over(owners, take)
    run_batches(left, right, grad)
    total = scatter(index[...], grad[...], garm_blocks)
    for c in range(3):
        out_ref[c] = total[:, c * BLOCK : (c + 1) * BLOCK]


def call(kernel, out_shape, scratch, scalars, arrays, cost=None):
    specs = [pl.BlockSpec(memory_space=pltpu.SMEM)] * len(scalars)
    specs += [pl.BlockSpec(memory_space=pltpu.VMEM)] * len(arrays)
    return pl.pallas_call(
        kernel,
        out_shape=out_shape,
        in_specs=specs,
        out_specs=jax.tree.map(lambda _: pl.BlockSpec(memory_space=pltpu.VMEM), out_shape),
        scratch_shapes=scratch,
        cost_estimate=cost and pl.CostEstimate(flops=cost, bytes_accessed=1000, transcendentals=0),
        compiler_params=pltpu.CompilerParams(vmem_limit_bytes=VMEM_LIMIT),
    )(*scalars, *arrays)


def read_table(ref, start, step):
    columns = [
        jnp.concatenate([ref[start + c * step + q] for q in range(step)], axis=0) for c in range(4)
    ]
    return jnp.concatenate(columns, axis=1)


def choose(index, table):
    lane = lax.broadcasted_iota(jnp.int32, index.shape, 1).astype(f32)
    onehot = (index == lane).astype(f32)[:, : table.shape[0]].astype(bf16)
    parts = [
        jnp.dot(onehot, part.astype(bf16), preferred_element_type=f32)
        for part in pieces(table, 3)
    ]
    rows = parts[0] + parts[1] + parts[2]
    return [rows[:, c * BLOCK : (c + 1) * BLOCK] for c in range(4)]


def halves(top, bottom):
    row = lax.broadcasted_iota(jnp.int32, (SUB, BLOCK), 0)
    return jnp.where(row < SUB // 2, top, bottom)


def flip(value):
    return pltpu.roll(value, SUB // 2, 0)


def body_work(tiles, table):
    return list(tiles[:4]), choose(tiles[4], table)


def garm_work(tiles, top, bottom):
    row = lax.broadcasted_iota(jnp.int32, (SUB, BLOCK), 0)
    index = tiles[4] + jnp.where(row < SUB // 2, 0, top.shape[0]).astype(f32)
    return choose(index, jnp.concatenate([top, bottom], axis=0)), list(tiles[:4])


def slot_tiles(ref):
    return [ref[c] for c in range(5)]


def message_table(ref, step):
    return read_table(ref, 5, step)


def bundle_kernel(one_ref, two_ref, *refs):
    out_ref = refs[-1]
    body = one_ref.shape[0] - 5
    for q in range(body):
        out_ref[q] = one_ref[5 + q]
        out_ref[body + q] = two_ref[5 + q]
    for k, tile in enumerate(bottom_tiles(one_ref, two_ref)):
        out_ref[2 * body + k] = tile


def top_tiles(one_ref, two_ref):
    return [halves(a, flip(b)) for a, b in zip(slot_tiles(one_ref), slot_tiles(two_ref))]


def bottom_tiles(one_ref, two_ref):
    return [halves(flip(a), b) for a, b in zip(slot_tiles(one_ref), slot_tiles(two_ref))]


def early_kernel(*refs):
    own_ref, sent_refs, got_refs, far_ref = refs[0], refs[1:4], refs[4:7], refs[7]
    del far_ref
    bgrad_ref, bindex_ref, ggrad_ref = refs[8:]
    step = (own_ref.shape[0] - 5) // 4
    own = message_table(own_ref, step)
    a, b, c = [message_table(ref, step) for ref in got_refs]
    here = top_tiles(own_ref, got_refs[0])
    far = top_tiles(got_refs[1], got_refs[2])
    work = [
        body_work(here, own),
        body_work(far, own),
        garm_work(top_tiles(own_ref, sent_refs[0]), own, a),
        garm_work(top_tiles(sent_refs[1], sent_refs[2]), b, c),
    ]
    out = gradients(work)
    for n in range(2):
        rows = slice(n * SUB, (n + 1) * SUB)
        bgrad_ref[rows, :] = jnp.concatenate(out[n], axis=1)
        ggrad_ref[rows, :] = jnp.concatenate(out[2 + n][:3], axis=1)
    bindex_ref[:SUB, :] = here[4]
    bindex_ref[SUB:, :] = far[4]


def late_body_kernel(own_ref, near_ref, far_ref, bgrad_ref, bindex_ref, out_ref, stiff_ref):
    body = own_ref.shape[0] - 5
    own = message_table(own_ref, body // 4)
    tiles = [[ref[2 * body + k] for k in range(5)] for ref in (near_ref, far_ref)]
    out = gradients([body_work(part, own) for part in tiles])
    grads = [jnp.concatenate(rows, axis=1) for rows in out]
    index = jnp.concatenate([bindex_ref[...]] + [part[4] for part in tiles], axis=0)
    total = scatter(index, jnp.concatenate([bgrad_ref[...]] + grads, axis=0), out_ref.shape[1])
    for c in range(3):
        out_ref[c] = total[:, c * BLOCK : (c + 1) * BLOCK]
    stiff_ref[...] = total[:, 3 * BLOCK :]


def late_garm_kernel(*refs):
    own_ref, sent_refs, (near_ref, far_ref, ggrad_ref, index_ref, out_ref) = (
        refs[0],
        refs[1:4],
        refs[4:],
    )
    body = own_ref.shape[0] - 5
    near, far = [
        [read_table(ref, n * body, body // 4) for n in range(2)] for ref in (near_ref, far_ref)
    ]
    work = [
        garm_work(bottom_tiles(own_ref, sent_refs[0]), *near),
        garm_work(bottom_tiles(sent_refs[1], sent_refs[2]), *far),
    ]
    grads = [jnp.concatenate(rows[:3], axis=1) for rows in gradients(work)]
    index = jnp.concatenate([index_ref[k] for k in range(index_ref.shape[0])], axis=0)
    total = scatter(index, jnp.concatenate([ggrad_ref[...]] + grads, axis=0), out_ref.shape[1])
    for c in range(3):
        out_ref[c] = total[:, c * BLOCK : (c + 1) * BLOCK]


def final_kernel(garm_ref, body_ref, mine_ref, other_ref, garm_out, body_out, stiff_out):
    stiff_out[...] = mine_ref[...] + other_ref[...]
    body_out[...] = body_ref[...]
    garm_out[...] = garm_ref[...]


def stage_kernel(*refs):
    hbm, (index_ref, *out_refs), (vmem, sems) = refs[:7], refs[7:12], (refs[12:19], refs[19])
    copies = [
        pltpu.make_async_copy(src, dst, sems.at[k]) for k, (src, dst) in enumerate(zip(hbm, vmem))
    ]
    for copy in copies:
        copy.start()
    for copy in copies:
        copy.wait()
    pg_ref, pb_ref, pc_ref, garm_ref, cot_ref, body_ref, stiff_ref = vmem
    cap = pg_ref.shape[0]
    tiles = stiff_ref.shape[0]
    width = lax.axis_size("body")
    here, column = lax.axis_index("garm"), lax.axis_index("body")
    out_distance = 2 + here // 2
    for n, (out_ref, distance) in enumerate(
        zip(out_refs, (0, 5 - out_distance, out_distance, 1))
    ):
        for q in range(3 * tiles):
            out_ref[5 + q] = body_ref[q]
        for q in range(tiles):
            out_ref[5 + 3 * tiles + q] = stiff_ref[q]
        for x in range(2):
            owner = (here ^ distance) * width + (column ^ x)
            live = pc_ref[0, owner]
            for s in range(cap):
                g = pg_ref[s, owner]
                row, place = pl.ds(g, 1), pl.ds(x * cap + s, 1)
                for c in range(3):
                    out_ref[c, place, :] = garm_ref[c, row, :]
                out_ref[3, place, :] = jnp.where(s < live, cot_ref[row, :], 0.0)
                out_ref[4, place, :] = jnp.full((1, BLOCK), pb_ref[s, owner].astype(f32), f32)
                spot, line = 2 * x + n // 2, n % 2 * cap + s
                index_ref[spot, line : line + 1, :] = jnp.full((1, BLOCK), g.astype(f32), f32)


def staged(garment, cotangent, body_points, stiffness, pg, pb, pc):
    verts = garment.shape[2]
    points = body_points.shape[2]
    blocks = points // BLOCK
    tiles = blocks // SUB
    garm_n = lax.axis_size("garm")
    message = jax.ShapeDtypeStruct((5 + 4 * tiles, SUB, BLOCK), f32)
    arrays = (
        pg,
        pb,
        pc,
        garment.reshape(3, verts // BLOCK, BLOCK),
        cotangent.reshape(verts // BLOCK, BLOCK),
        body_points.reshape(3 * tiles, SUB, BLOCK),
        stiffness.reshape(tiles, SUB, BLOCK),
    )
    index, own, *sent = pl.pallas_call(
        stage_kernel,
        out_shape=[jax.ShapeDtypeStruct((garm_n, SUB, BLOCK), f32)] + [message] * garm_n,
        in_specs=[pl.BlockSpec(memory_space=pltpu.HBM)] * len(arrays),
        out_specs=[pl.BlockSpec(memory_space=pltpu.VMEM)] * (garm_n + 1),
        scratch_shapes=[
            (pltpu.SMEM if k < 3 else pltpu.VMEM)(a.shape, a.dtype) for k, a in enumerate(arrays)
        ]
        + [pltpu.SemaphoreType.DMA((len(arrays),))],
        compiler_params=pltpu.CompilerParams(vmem_limit_bytes=VMEM_LIMIT),
    )(*[pltpu.with_memory_space_constraint(a, pltpu.HBM) for a in arrays])

    def along_garm(value, pairs):
        return lax.ppermute(value, "garm", pairs)

    def along_body(value):
        return lax.ppermute(value, "body", [(0, 1), (1, 0)])

    cycle = [(0, 2), (2, 1), (1, 3), (3, 0)]
    got = [
        along_garm(sent[1], cycle),
        along_garm(sent[0], [(b, a) for a, b in cycle]),
        along_garm(sent[2], [(z, z ^ 1) for z in range(garm_n)]),
    ]
    bundle = jax.ShapeDtypeStruct((5 + 8 * tiles, SUB, BLOCK), f32)
    near = call(bundle_kernel, bundle, [], (), (own, got[0]), BUNDLE_COST)
    far = call(bundle_kernel, bundle, [], (), (got[1], got[2], near), BUNDLE_COST)
    near_other, far_other = along_body(near), along_body(far)
    bgrad, bindex, ggrad = call(
        early_kernel,
        (
            jax.ShapeDtypeStruct((2 * SUB, 4 * BLOCK), f32),
            jax.ShapeDtypeStruct((2 * SUB, BLOCK), f32),
            jax.ShapeDtypeStruct((2 * SUB, 3 * BLOCK), f32),
        ),
        [],
        (),
        (own, *sent, *got, far),
        EARLY_COST,
    )
    body_shape = jax.ShapeDtypeStruct((3, blocks, BLOCK), f32)
    stiff_shape = jax.ShapeDtypeStruct((blocks, BLOCK), f32)
    garm_shape = jax.ShapeDtypeStruct((3, verts // BLOCK, BLOCK), f32)
    body_total, stiff = call(
        late_body_kernel,
        (body_shape, stiff_shape),
        [],
        (),
        (own, near_other, far_other, bgrad, bindex),
    )
    stiff_other = lax.ppermute(stiff, "frame", [(0, 1), (1, 0)])
    garm_total = call(
        late_garm_kernel,
        garm_shape,
        [],
        (),
        (own, *sent, near_other, far_other, ggrad, index),
    )
    return call(
        final_kernel,
        (garm_shape, body_shape, stiff_shape),
        [],
        (),
        (garm_total, body_total, stiff, stiff_other),
    )


def per_device(garment, cotangent, body_points, stiffness, pair_garment, pair_body, pair_count):
    owners = lax.axis_size(("garm", "body"))
    verts = garment.shape[2]
    points = body_points.shape[2]
    blocks = points // BLOCK
    cap = pair_garment.shape[3]
    slots = owners * cap
    pg = pair_garment.reshape(owners, cap).T
    pb = pair_body.reshape(owners, cap).T
    pc = pair_count.reshape(1, owners)
    if (lax.axis_size("garm"), lax.axis_size("body")) == (4, 2) and cap == SUB // 2:
        garm_grad, body_grad, stiff = staged(
            garment, cotangent, body_points, stiffness, pg, pb, pc
        )
        return (
            garm_grad.reshape(1, 3, verts),
            body_grad.reshape(1, 3, points),
            stiff.reshape(points),
        )
    message = call(
        pack_kernel,
        jax.ShapeDtypeStruct((owners, 5 + blocks, cap, BLOCK), f32),
        [],
        (pg, pb, pc),
        (
            garment.reshape(3, verts // BLOCK, BLOCK),
            cotangent.reshape(verts // BLOCK, BLOCK),
            body_points.reshape(3, blocks, BLOCK),
            stiffness.reshape(blocks, BLOCK),
        ),
    )
    arrived = lax.all_to_all(message, ("garm", "body"), split_axis=0, concat_axis=0, tiled=True)
    rows = pltpu.VMEM((4, slots, BLOCK), f32)
    grad = pltpu.VMEM((slots, 4 * BLOCK), f32)
    index = pltpu.VMEM((slots, BLOCK), f32)
    body_grad, stiff = call(
        body_kernel,
        (
            jax.ShapeDtypeStruct((3, blocks, BLOCK), f32),
            jax.ShapeDtypeStruct((blocks, BLOCK), f32),
        ),
        [rows, rows, pltpu.VMEM((blocks, 4 * BLOCK), f32), index, grad],
        (),
        (message, arrived),
    )
    other = lax.ppermute(stiff, "frame", [(0, 1), (1, 0)])
    garm_grad = call(
        garm_kernel,
        jax.ShapeDtypeStruct((3, verts // BLOCK, BLOCK), f32),
        [rows, rows, index, grad],
        (pg, pb),
        (message, arrived),
    )
    return (
        garm_grad.reshape(1, 3, verts),
        body_grad.reshape(1, 3, points),
        (stiff + other).reshape(points),
    )


def solution(mesh):
    in_specs = (
        P(("grp", "frame"), None, ("garm", "body")),
        P(("grp", "frame"), ("garm", "body")),
        P(("grp", "frame"), None, ("garm", "body")),
        P(("grp", "garm", "body")),
        P(("grp", "frame"), ("garm", "body"), None, None),
        P(("grp", "frame"), ("garm", "body"), None, None),
        P(("grp", "frame"), ("garm", "body"), None),
    )
    out_specs = (
        P(("grp", "frame"), None, ("garm", "body")),
        P(("grp", "frame"), None, ("garm", "body")),
        P(("grp", "garm", "body")),
    )
    return jax.shard_map(
        per_device, mesh=mesh, in_specs=in_specs, out_specs=out_specs, check_vma=False
    )
```

```python
import math

import jax
import jax.numpy as jnp
from jax import lax
from jax.experimental import pallas as pl
from jax.experimental.pallas import tpu as pltpu
from jax.sharding import PartitionSpec as P

BLOCK = 128
SUB = 8
VMEM_LIMIT = 32 * 1024 * 1024
STEPS = (0, 1, 3, 2)
EARLY_COST = 40_000_000_000
BUNDLE_COST = 1000

amplitude = 0.05
width_sq = 4.0

SCALE = math.sqrt(math.log2(math.e) / width_sq)
FACTOR = -2.0 / width_sq * amplitude

f32 = jnp.float32
bf16 = jnp.bfloat16


def pieces(value, count):
    out = []
    for _ in range(count - 1):
        top = value.astype(bf16).astype(f32)
        out.append(top)
        value = value - top
    out.append(value)
    return out


def features(left, right):
    lpos = [left[c] * SCALE for c in range(3)]
    rpos = [right[c] * SCALE for c in range(3)]
    lnorm = -(lpos[0] * lpos[0] + lpos[1] * lpos[1] + lpos[2] * lpos[2])
    rnorm = -(rpos[0] * rpos[0] + rpos[1] * rpos[1] + rpos[2] * rpos[2])
    one = jnp.ones_like(lnorm)
    lrows, rrows = [], []
    for c in range(3):
        l1, l2, l3 = pieces(lpos[c] * 2.0, 3)
        r1, r2, r3 = pieces(rpos[c], 3)
        lrows += [l1, l1, l2, l2, l1, l3]
        rrows += [r1, r2, r1, r2, r3, r1]
    lrows += pieces(lnorm, 3) + [one] * 3
    rrows += [one] * 3 + pieces(rnorm, 3)
    return (
        jnp.concatenate(lrows, axis=0).astype(bf16),
        jnp.concatenate(rrows, axis=0).astype(bf16),
    )


def pull(batches):
    made = []
    for left, right in batches:
        lfeat, rfeat = features(left, right)
        weight = left[3]
        coeff = jnp.concatenate([weight * left[c] for c in range(3)] + [weight], axis=0)
        chi, clo = [part.astype(bf16) for part in pieces(coeff, 2)]
        lhs = jnp.concatenate(
            [
                jnp.concatenate([chi, chi], axis=1),
                jnp.concatenate([clo, jnp.zeros_like(clo)], axis=1),
            ],
            axis=0,
        )
        made.append((lfeat.T, rfeat, lhs))
    row = lax.broadcasted_iota(jnp.int32, made[0][1].shape, 0) % SUB
    sub = lax.broadcasted_iota(jnp.int32, (4 * SUB, BLOCK), 0) % SUB
    totals = [jnp.zeros((4 * SUB, BLOCK), f32) for _ in batches]
    for pair in range(0, SUB, 2):
        masks = [(row == pair + k).astype(f32).astype(bf16) for k in range(2)]
        for n, (lfeat_t, rfeat, lhs) in enumerate(made):
            rhs = jnp.concatenate([rfeat * mask for mask in masks], axis=1)
            exponent = jnp.dot(lfeat_t, rhs, preferred_element_type=f32)
            kernel = jnp.exp2(exponent)
            khi = kernel.astype(bf16)
            klo = (kernel - khi.astype(f32)).astype(bf16)
            sums = jnp.dot(lhs, jnp.concatenate([khi, klo], axis=0), preferred_element_type=f32)
            sums = sums[: 4 * SUB] + sums[4 * SUB :]
            for k in range(2):
                part = sums[:, k * BLOCK : (k + 1) * BLOCK]
                totals[n] = jnp.where(sub == pair + k, part, totals[n])
    return [[total[c * SUB : (c + 1) * SUB] for c in range(4)] for total in totals]


def gradients(batches):
    out = []
    for (_, right), total in zip(batches, pull(batches)):
        rows = [FACTOR * right[3] * (right[c] * total[3] - total[c]) for c in range(3)]
        out.append(rows + [amplitude * total[3]])
    return out


def run_batches(left_ref, right_ref, grad_ref):
    batches = left_ref.shape[1] // SUB
    group = math.gcd(batches, 4)

    def step(k, carry):
        places = [pl.ds(pl.multiple_of((k * group + n) * SUB, SUB), SUB) for n in range(group)]
        work = [
            tuple([ref[c, rows, :] for c in range(4)] for ref in (left_ref, right_ref))
            for rows in places
        ]
        for rows, values in zip(places, gradients(work)):
            for c, value in enumerate(values):
                grad_ref[rows, c * BLOCK : (c + 1) * BLOCK] = value
        return carry

    lax.fori_loop(0, batches // group, step, 0)


def scatter(index, grads, blocks):
    lane = lax.broadcasted_iota(jnp.int32, index.shape, 1).astype(f32)
    onehot_t = (index == lane).astype(f32).T[:blocks].astype(bf16)
    parts = [
        jnp.dot(onehot_t, part.astype(bf16), preferred_element_type=f32)
        for part in pieces(grads, 3)
    ]
    return parts[0] + parts[1] + parts[2]


def pack_kernel(pg_ref, pb_ref, pc_ref, garm_ref, cot_ref, body_ref, stiff_ref, out_ref):
    cap, owners = pg_ref.shape
    tiles = stiff_ref.shape[0] // cap

    def one(d, carry):
        for s in range(cap):
            row = pl.ds(pg_ref[s, d], 1)
            for c in range(3):
                out_ref[d, c, s : s + 1, :] = garm_ref[c, row, :]
            out_ref[d, 3, s : s + 1, :] = jnp.where(s < pc_ref[0, d], cot_ref[row, :], 0.0)
            out_ref[d, 4 + 4 * tiles, s : s + 1, :] = jnp.full(
                (1, BLOCK), pb_ref[s, d].astype(f32), f32
            )
        for q in range(tiles):
            rows = slice(q * cap, (q + 1) * cap)
            for c in range(3):
                out_ref[d, 4 + c * tiles + q] = body_ref[c, rows, :]
            out_ref[d, 4 + 3 * tiles + q] = stiff_ref[rows, :]
        return carry

    if owners <= 8:
        for d in range(owners):
            one(d, 0)
    else:
        lax.fori_loop(0, owners, one, 0)


def over(count, fn):
    if count <= 8:
        for d in range(count):
            fn(d)
    else:
        lax.fori_loop(0, count, lambda d, carry: (fn(d), carry)[1], 0)


def body_kernel(own_ref, in_ref, out_ref, stiff_ref, left, right, table, index, grad):
    owners, tiles, cap, _ = in_ref.shape
    blocks = tiles - 5

    def take(d):
        rows = pl.ds(d * cap, cap)
        for c in range(4):
            left[c, rows, :] = in_ref[d, c]
        index[rows, :] = in_ref[d, tiles - 1]

    over(owners, take)
    for c in range(4):
        for q in range(blocks // 4):
            table[4 * q : 4 * q + 4, c * BLOCK : (c + 1) * BLOCK] = own_ref[
                0, 4 + c * (blocks // 4) + q
            ]
    lane = lax.broadcasted_iota(jnp.int32, index.shape, 1).astype(f32)
    onehot = (index[...] == lane).astype(f32)[:, :blocks].astype(bf16)
    chosen = [
        jnp.dot(onehot, part.astype(bf16), preferred_element_type=f32)
        for part in pieces(table[...], 3)
    ]
    chosen = chosen[0] + chosen[1] + chosen[2]
    for c in range(4):
        right[c] = chosen[:, c * BLOCK : (c + 1) * BLOCK]
    run_batches(left, right, grad)
    total = scatter(index[...], grad[...], blocks)
    for c in range(3):
        out_ref[c] = total[:, c * BLOCK : (c + 1) * BLOCK]
    stiff_ref[...] = total[:, 3 * BLOCK :]


def garm_kernel(pg_ref, pb_ref, own_ref, in_ref, out_ref, left, right, index, grad):
    owners, tiles, cap, _ = in_ref.shape
    blocks = tiles - 5
    garm_blocks = out_ref.shape[1]

    def take(d):
        rows = pl.ds(d * cap, cap)
        for c in range(4):
            right[c, rows, :] = own_ref[d, c]
        for s in range(cap):
            b = pb_ref[s, d]
            for c in range(4):
                left[c, pl.ds(d * cap + s, 1), :] = in_ref[
                    d, 4 + c * (blocks // 4) + b // 4, pl.ds(b % 4, 1), :
                ]
            index[pl.ds(d * cap + s, 1), :] = jnp.full((1, BLOCK), pg_ref[s, d].astype(f32), f32)

    over(owners, take)
    run_batches(left, right, grad)
    total = scatter(index[...], grad[...], garm_blocks)
    for c in range(3):
        out_ref[c] = total[:, c * BLOCK : (c + 1) * BLOCK]


def call(kernel, out_shape, scratch, scalars, arrays, cost=None):
    specs = [pl.BlockSpec(memory_space=pltpu.SMEM)] * len(scalars)
    specs += [pl.BlockSpec(memory_space=pltpu.VMEM)] * len(arrays)
    return pl.pallas_call(
        kernel,
        out_shape=out_shape,
        in_specs=specs,
        out_specs=jax.tree.map(lambda _: pl.BlockSpec(memory_space=pltpu.VMEM), out_shape),
        scratch_shapes=scratch,
        cost_estimate=cost and pl.CostEstimate(flops=cost, bytes_accessed=1000, transcendentals=0),
        compiler_params=pltpu.CompilerParams(vmem_limit_bytes=VMEM_LIMIT),
    )(*scalars, *arrays)


def read_table(ref, start, step):
    columns = [
        jnp.concatenate([ref[start + c * step + q] for q in range(step)], axis=0) for c in range(4)
    ]
    return jnp.concatenate(columns, axis=1)


def choose(index, table):
    lane = lax.broadcasted_iota(jnp.int32, index.shape, 1).astype(f32)
    onehot = (index == lane).astype(f32)[:, : table.shape[0]].astype(bf16)
    parts = [
        jnp.dot(onehot, part.astype(bf16), preferred_element_type=f32)
        for part in pieces(table, 3)
    ]
    rows = parts[0] + parts[1] + parts[2]
    return [rows[:, c * BLOCK : (c + 1) * BLOCK] for c in range(4)]


def halves(top, bottom):
    row = lax.broadcasted_iota(jnp.int32, (SUB, BLOCK), 0)
    return jnp.where(row < SUB // 2, top, bottom)


def flip(value):
    return pltpu.roll(value, SUB // 2, 0)


def body_work(tiles, table):
    return list(tiles[:4]), choose(tiles[4], table)


def garm_work(tiles, top, bottom):
    row = lax.broadcasted_iota(jnp.int32, (SUB, BLOCK), 0)
    index = tiles[4] + jnp.where(row < SUB // 2, 0, top.shape[0]).astype(f32)
    return choose(index, jnp.concatenate([top, bottom], axis=0)), list(tiles[:4])


def slot_tiles(ref):
    return [ref[c] for c in range(5)]


def message_table(ref, step):
    return read_table(ref, 5, step)


def pack_slots(ref):
    a, b, c, d, e = slot_tiles(ref)
    return [halves(flip(a), b), halves(flip(c), d), e]


def unpack_top(tiles):
    a, b, c = tiles
    return [a, flip(a), b, flip(b), flip(c)]


def unpack_bottom(tiles):
    a, b, c = tiles
    return [flip(a), a, flip(b), b, c]


def near_bundle_kernel(own_ref, one_ref, two_ref, out_ref):
    body = own_ref.shape[0] - 5
    for n, ref in enumerate((own_ref, one_ref, two_ref)):
        for q in range(body):
            out_ref[n * body + q] = ref[5 + q]
    for k, tile in enumerate(bottom_tiles(one_ref, two_ref) + pack_slots(own_ref)):
        out_ref[3 * body + k] = tile


def far_bundle_kernel(ref, near_ref, out_ref):
    del near_ref
    body = ref.shape[0] - 5
    for q in range(body):
        out_ref[q] = ref[5 + q]
    for k, tile in enumerate(pack_slots(ref)):
        out_ref[body + k] = tile


def top_tiles(one_ref, two_ref):
    return [halves(a, flip(b)) for a, b in zip(slot_tiles(one_ref), slot_tiles(two_ref))]


def bottom_tiles(one_ref, two_ref):
    return [halves(flip(a), b) for a, b in zip(slot_tiles(one_ref), slot_tiles(two_ref))]


def early_kernel(*refs):
    own_ref, sent_refs, got_refs, far_ref = refs[0], refs[1:4], refs[4:7], refs[7]
    del far_ref
    bgrad_ref, bindex_ref, ggrad_ref = refs[8:]
    step = (own_ref.shape[0] - 5) // 4
    own = message_table(own_ref, step)
    a, b, c = [message_table(ref, step) for ref in got_refs]
    here = top_tiles(own_ref, got_refs[2])
    next_to = top_tiles(got_refs[0], got_refs[1])
    work = [
        body_work(here, own),
        body_work(next_to, own),
        garm_work(top_tiles(own_ref, sent_refs[2]), own, c),
        garm_work(top_tiles(sent_refs[0], sent_refs[1]), a, b),
    ]
    out = gradients(work)
    for n in range(2):
        rows = slice(n * SUB, (n + 1) * SUB)
        bgrad_ref[rows, :] = jnp.concatenate(out[n], axis=1)
        ggrad_ref[rows, :] = jnp.concatenate(out[2 + n][:3], axis=1)
    bindex_ref[:SUB, :] = here[4]
    bindex_ref[SUB:, :] = next_to[4]


def late_body_kernel(own_ref, near_ref, far_ref, bgrad_ref, bindex_ref, out_ref, stiff_ref):
    body = own_ref.shape[0] - 5
    own = message_table(own_ref, body // 4)
    top = unpack_top([near_ref[3 * body + 5 + k] for k in range(3)])
    bottom = unpack_bottom([far_ref[body + k] for k in range(3)])
    tiles = [
        [near_ref[3 * body + k] for k in range(5)],
        [halves(x, y) for x, y in zip(top, bottom)],
    ]
    out = gradients([body_work(part, own) for part in tiles])
    grads = [jnp.concatenate(rows, axis=1) for rows in out]
    index = jnp.concatenate([bindex_ref[...]] + [part[4] for part in tiles], axis=0)
    total = scatter(index, jnp.concatenate([bgrad_ref[...]] + grads, axis=0), out_ref.shape[1])
    for c in range(3):
        out_ref[c] = total[:, c * BLOCK : (c + 1) * BLOCK]
    stiff_ref[...] = total[:, 3 * BLOCK :]


def late_garm_kernel(*refs):
    own_ref, sent_refs, (near_ref, far_ref, ggrad_ref, index_ref, out_ref) = (
        refs[0],
        refs[1:4],
        refs[4:],
    )
    body = own_ref.shape[0] - 5
    own, a, b = [read_table(near_ref, n * body, body // 4) for n in range(3)]
    c = read_table(far_ref, 0, body // 4)
    work = [
        garm_work(bottom_tiles(sent_refs[0], sent_refs[1]), a, b),
        garm_work(bottom_tiles(own_ref, sent_refs[2]), own, c),
    ]
    grads = [jnp.concatenate(rows[:3], axis=1) for rows in gradients(work)]
    index = jnp.concatenate([index_ref[k] for k in range(index_ref.shape[0])], axis=0)
    total = scatter(index, jnp.concatenate([ggrad_ref[...]] + grads, axis=0), out_ref.shape[1])
    for c in range(3):
        out_ref[c] = total[:, c * BLOCK : (c + 1) * BLOCK]


def final_kernel(garm_ref, body_ref, mine_ref, other_ref, garm_out, body_out, stiff_out):
    stiff_out[...] = mine_ref[...] + other_ref[...]
    body_out[...] = body_ref[...]
    garm_out[...] = garm_ref[...]


def stage_kernel(*refs):
    hbm, (index_ref, *out_refs), (vmem, sems) = refs[:7], refs[7:12], (refs[12:19], refs[19])
    copies = [
        pltpu.make_async_copy(src, dst, sems.at[k]) for k, (src, dst) in enumerate(zip(hbm, vmem))
    ]
    for copy in copies:
        copy.start()
    for copy in copies:
        copy.wait()
    pg_ref, pb_ref, pc_ref, garm_ref, cot_ref, body_ref, stiff_ref = vmem
    cap = pg_ref.shape[0]
    tiles = stiff_ref.shape[0]
    width = lax.axis_size("body")
    here, column = lax.axis_index("garm"), lax.axis_index("body")
    garm_n = lax.axis_size("garm")
    for n, out_ref in enumerate(out_refs):
        place_z = lax.rem(here + STEPS[n], garm_n)
        for q in range(3 * tiles):
            out_ref[5 + q] = body_ref[q]
        for q in range(tiles):
            out_ref[5 + 3 * tiles + q] = stiff_ref[q]
        for x in range(2):
            owner = place_z * width + (column ^ x)
            live = pc_ref[0, owner]
            for s in range(cap):
                g = pg_ref[s, owner]
                row, place = pl.ds(g, 1), pl.ds(x * cap + s, 1)
                for c in range(3):
                    out_ref[c, place, :] = garm_ref[c, row, :]
                out_ref[3, place, :] = jnp.where(s < live, cot_ref[row, :], 0.0)
                out_ref[4, place, :] = jnp.full((1, BLOCK), pb_ref[s, owner].astype(f32), f32)
                spot = 2 * x + (x if n in (0, 3) else 1 - x)
                line = (0 if n < 2 else cap) + s
                index_ref[spot, line : line + 1, :] = jnp.full((1, BLOCK), g.astype(f32), f32)


def staged(garment, cotangent, body_points, stiffness, pg, pb, pc):
    verts = garment.shape[2]
    points = body_points.shape[2]
    blocks = points // BLOCK
    tiles = blocks // SUB
    garm_n = lax.axis_size("garm")
    message = jax.ShapeDtypeStruct((5 + 4 * tiles, SUB, BLOCK), f32)
    arrays = (
        pg,
        pb,
        pc,
        garment.reshape(3, verts // BLOCK, BLOCK),
        cotangent.reshape(verts // BLOCK, BLOCK),
        body_points.reshape(3 * tiles, SUB, BLOCK),
        stiffness.reshape(tiles, SUB, BLOCK),
    )
    index, own, *sent = pl.pallas_call(
        stage_kernel,
        out_shape=[jax.ShapeDtypeStruct((garm_n, SUB, BLOCK), f32)] + [message] * garm_n,
        in_specs=[pl.BlockSpec(memory_space=pltpu.HBM)] * len(arrays),
        out_specs=[pl.BlockSpec(memory_space=pltpu.VMEM)] * (garm_n + 1),
        scratch_shapes=[
            (pltpu.SMEM if k < 3 else pltpu.VMEM)(a.shape, a.dtype) for k, a in enumerate(arrays)
        ]
        + [pltpu.SemaphoreType.DMA((len(arrays),))],
        compiler_params=pltpu.CompilerParams(vmem_limit_bytes=VMEM_LIMIT),
    )(*[pltpu.with_memory_space_constraint(a, pltpu.HBM) for a in arrays])

    def along_garm(value, step):
        return lax.ppermute(value, "garm", [(z, (z + step) % garm_n) for z in range(garm_n)])

    def along_body(value):
        return lax.ppermute(value, "body", [(0, 1), (1, 0)])

    got = [along_garm(sent[n], STEPS[1 + n]) for n in (1, 0, 2)]
    near = call(
        near_bundle_kernel,
        jax.ShapeDtypeStruct((8 + 12 * tiles, SUB, BLOCK), f32),
        [],
        (),
        (own, got[0], got[1]),
        BUNDLE_COST,
    )
    far = call(
        far_bundle_kernel,
        jax.ShapeDtypeStruct((3 + 4 * tiles, SUB, BLOCK), f32),
        [],
        (),
        (got[2], near),
        BUNDLE_COST,
    )
    near_other, far_other = along_body(near), along_body(far)
    bgrad, bindex, ggrad = call(
        early_kernel,
        (
            jax.ShapeDtypeStruct((2 * SUB, 4 * BLOCK), f32),
            jax.ShapeDtypeStruct((2 * SUB, BLOCK), f32),
            jax.ShapeDtypeStruct((2 * SUB, 3 * BLOCK), f32),
        ),
        [],
        (),
        (own, *sent, *got, far),
        EARLY_COST,
    )
    body_shape = jax.ShapeDtypeStruct((3, blocks, BLOCK), f32)
    stiff_shape = jax.ShapeDtypeStruct((blocks, BLOCK), f32)
    garm_shape = jax.ShapeDtypeStruct((3, verts // BLOCK, BLOCK), f32)
    body_total, stiff = call(
        late_body_kernel,
        (body_shape, stiff_shape),
        [],
        (),
        (own, near_other, far_other, bgrad, bindex),
    )
    stiff_other = lax.ppermute(stiff, "frame", [(0, 1), (1, 0)])
    garm_total = call(
        late_garm_kernel,
        garm_shape,
        [],
        (),
        (own, *sent, near_other, far_other, ggrad, index),
    )
    return call(
        final_kernel,
        (garm_shape, body_shape, stiff_shape),
        [],
        (),
        (garm_total, body_total, stiff, stiff_other),
    )


def per_device(garment, cotangent, body_points, stiffness, pair_garment, pair_body, pair_count):
    owners = lax.axis_size(("garm", "body"))
    verts = garment.shape[2]
    points = body_points.shape[2]
    blocks = points // BLOCK
    cap = pair_garment.shape[3]
    slots = owners * cap
    pg = pair_garment.reshape(owners, cap).T
    pb = pair_body.reshape(owners, cap).T
    pc = pair_count.reshape(1, owners)
    if (lax.axis_size("garm"), lax.axis_size("body")) == (4, 2) and cap == SUB // 2:
        garm_grad, body_grad, stiff = staged(
            garment, cotangent, body_points, stiffness, pg, pb, pc
        )
        return (
            garm_grad.reshape(1, 3, verts),
            body_grad.reshape(1, 3, points),
            stiff.reshape(points),
        )
    message = call(
        pack_kernel,
        jax.ShapeDtypeStruct((owners, 5 + blocks, cap, BLOCK), f32),
        [],
        (pg, pb, pc),
        (
            garment.reshape(3, verts // BLOCK, BLOCK),
            cotangent.reshape(verts // BLOCK, BLOCK),
            body_points.reshape(3, blocks, BLOCK),
            stiffness.reshape(blocks, BLOCK),
        ),
    )
    arrived = lax.all_to_all(message, ("garm", "body"), split_axis=0, concat_axis=0, tiled=True)
    rows = pltpu.VMEM((4, slots, BLOCK), f32)
    grad = pltpu.VMEM((slots, 4 * BLOCK), f32)
    index = pltpu.VMEM((slots, BLOCK), f32)
    body_grad, stiff = call(
        body_kernel,
        (
            jax.ShapeDtypeStruct((3, blocks, BLOCK), f32),
            jax.ShapeDtypeStruct((blocks, BLOCK), f32),
        ),
        [rows, rows, pltpu.VMEM((blocks, 4 * BLOCK), f32), index, grad],
        (),
        (message, arrived),
    )
    other = lax.ppermute(stiff, "frame", [(0, 1), (1, 0)])
    garm_grad = call(
        garm_kernel,
        jax.ShapeDtypeStruct((3, verts // BLOCK, BLOCK), f32),
        [rows, rows, index, grad],
        (pg, pb),
        (message, arrived),
    )
    return (
        garm_grad.reshape(1, 3, verts),
        body_grad.reshape(1, 3, points),
        (stiff + other).reshape(points),
    )


def solution(mesh):
    in_specs = (
        P(("grp", "frame"), None, ("garm", "body")),
        P(("grp", "frame"), ("garm", "body")),
        P(("grp", "frame"), None, ("garm", "body")),
        P(("grp", "garm", "body")),
        P(("grp", "frame"), ("garm", "body"), None, None),
        P(("grp", "frame"), ("garm", "body"), None, None),
        P(("grp", "frame"), ("garm", "body"), None),
    )
    out_specs = (
        P(("grp", "frame"), None, ("garm", "body")),
        P(("grp", "frame"), None, ("garm", "body")),
        P(("grp", "garm", "body")),
    )
    return jax.shard_map(
        per_device, mesh=mesh, in_specs=in_specs, out_specs=out_specs, check_vma=False
    )
```

```python
import math

import jax
import jax.numpy as jnp
from jax import lax
from jax.experimental import pallas as pl
from jax.experimental.pallas import tpu as pltpu
from jax.sharding import PartitionSpec as P

BLOCK = 128
SUB = 8
VMEM_LIMIT = 32 * 1024 * 1024
STEPS = (0, 3, 1, 2)
FIRST_COST = 1_000_000_000
SECOND_COST = 40_000_000_000
BUNDLE_COST = 1000

amplitude = 0.05
width_sq = 4.0

SCALE = math.sqrt(math.log2(math.e) / width_sq)
FACTOR = -2.0 / width_sq * amplitude

f32 = jnp.float32
bf16 = jnp.bfloat16


def pieces(value, count):
    out = []
    for _ in range(count - 1):
        top = value.astype(bf16).astype(f32)
        out.append(top)
        value = value - top
    out.append(value)
    return out


def features(left, right):
    lpos = [left[c] * SCALE for c in range(3)]
    rpos = [right[c] * SCALE for c in range(3)]
    lnorm = -(lpos[0] * lpos[0] + lpos[1] * lpos[1] + lpos[2] * lpos[2])
    rnorm = -(rpos[0] * rpos[0] + rpos[1] * rpos[1] + rpos[2] * rpos[2])
    one = jnp.ones_like(lnorm)
    lrows, rrows = [], []
    for c in range(3):
        l1, l2, l3 = pieces(lpos[c] * 2.0, 3)
        r1, r2, r3 = pieces(rpos[c], 3)
        lrows += [l1, l1, l2, l2, l1, l3]
        rrows += [r1, r2, r1, r2, r3, r1]
    lrows += pieces(lnorm, 3) + [one] * 3
    rrows += [one] * 3 + pieces(rnorm, 3)
    return (
        jnp.concatenate(lrows, axis=0).astype(bf16),
        jnp.concatenate(rrows, axis=0).astype(bf16),
    )


def pull(batches):
    made = []
    for left, right in batches:
        lfeat, rfeat = features(left, right)
        weight = left[3]
        coeff = jnp.concatenate([weight * left[c] for c in range(3)] + [weight], axis=0)
        chi, clo = [part.astype(bf16) for part in pieces(coeff, 2)]
        lhs = jnp.concatenate(
            [
                jnp.concatenate([chi, chi], axis=1),
                jnp.concatenate([clo, jnp.zeros_like(clo)], axis=1),
            ],
            axis=0,
        )
        made.append((lfeat.T, rfeat, lhs))
    row = lax.broadcasted_iota(jnp.int32, made[0][1].shape, 0) % SUB
    sub = lax.broadcasted_iota(jnp.int32, (4 * SUB, BLOCK), 0) % SUB
    totals = [jnp.zeros((4 * SUB, BLOCK), f32) for _ in batches]
    for pair in range(0, SUB, 2):
        masks = [(row == pair + k).astype(f32).astype(bf16) for k in range(2)]
        for n, (lfeat_t, rfeat, lhs) in enumerate(made):
            rhs = jnp.concatenate([rfeat * mask for mask in masks], axis=1)
            exponent = jnp.dot(lfeat_t, rhs, preferred_element_type=f32)
            kernel = jnp.exp2(exponent)
            khi = kernel.astype(bf16)
            klo = (kernel - khi.astype(f32)).astype(bf16)
            sums = jnp.dot(lhs, jnp.concatenate([khi, klo], axis=0), preferred_element_type=f32)
            sums = sums[: 4 * SUB] + sums[4 * SUB :]
            for k in range(2):
                part = sums[:, k * BLOCK : (k + 1) * BLOCK]
                totals[n] = jnp.where(sub == pair + k, part, totals[n])
    return [[total[c * SUB : (c + 1) * SUB] for c in range(4)] for total in totals]


def gradients(batches):
    out = []
    for (_, right), total in zip(batches, pull(batches)):
        rows = [FACTOR * right[3] * (right[c] * total[3] - total[c]) for c in range(3)]
        out.append(rows + [amplitude * total[3]])
    return out


def run_batches(left_ref, right_ref, grad_ref):
    batches = left_ref.shape[1] // SUB
    group = math.gcd(batches, 4)

    def step(k, carry):
        places = [pl.ds(pl.multiple_of((k * group + n) * SUB, SUB), SUB) for n in range(group)]
        work = [
            tuple([ref[c, rows, :] for c in range(4)] for ref in (left_ref, right_ref))
            for rows in places
        ]
        for rows, values in zip(places, gradients(work)):
            for c, value in enumerate(values):
                grad_ref[rows, c * BLOCK : (c + 1) * BLOCK] = value
        return carry

    lax.fori_loop(0, batches // group, step, 0)


def scatter(index, grads, blocks):
    lane = lax.broadcasted_iota(jnp.int32, index.shape, 1).astype(f32)
    onehot_t = (index == lane).astype(f32).T[:blocks].astype(bf16)
    parts = [
        jnp.dot(onehot_t, part.astype(bf16), preferred_element_type=f32)
        for part in pieces(grads, 3)
    ]
    return parts[0] + parts[1] + parts[2]


def pack_kernel(pg_ref, pb_ref, pc_ref, garm_ref, cot_ref, body_ref, stiff_ref, out_ref):
    cap, owners = pg_ref.shape
    tiles = stiff_ref.shape[0] // cap

    def one(d, carry):
        for s in range(cap):
            row = pl.ds(pg_ref[s, d], 1)
            for c in range(3):
                out_ref[d, c, s : s + 1, :] = garm_ref[c, row, :]
            out_ref[d, 3, s : s + 1, :] = jnp.where(s < pc_ref[0, d], cot_ref[row, :], 0.0)
            out_ref[d, 4 + 4 * tiles, s : s + 1, :] = jnp.full(
                (1, BLOCK), pb_ref[s, d].astype(f32), f32
            )
        for q in range(tiles):
            rows = slice(q * cap, (q + 1) * cap)
            for c in range(3):
                out_ref[d, 4 + c * tiles + q] = body_ref[c, rows, :]
            out_ref[d, 4 + 3 * tiles + q] = stiff_ref[rows, :]
        return carry

    if owners <= 8:
        for d in range(owners):
            one(d, 0)
    else:
        lax.fori_loop(0, owners, one, 0)


def over(count, fn):
    if count <= 8:
        for d in range(count):
            fn(d)
    else:
        lax.fori_loop(0, count, lambda d, carry: (fn(d), carry)[1], 0)


def body_kernel(own_ref, in_ref, out_ref, stiff_ref, left, right, table, index, grad):
    owners, tiles, cap, _ = in_ref.shape
    blocks = tiles - 5

    def take(d):
        rows = pl.ds(d * cap, cap)
        for c in range(4):
            left[c, rows, :] = in_ref[d, c]
        index[rows, :] = in_ref[d, tiles - 1]

    over(owners, take)
    for c in range(4):
        for q in range(blocks // 4):
            table[4 * q : 4 * q + 4, c * BLOCK : (c + 1) * BLOCK] = own_ref[
                0, 4 + c * (blocks // 4) + q
            ]
    lane = lax.broadcasted_iota(jnp.int32, index.shape, 1).astype(f32)
    onehot = (index[...] == lane).astype(f32)[:, :blocks].astype(bf16)
    chosen = [
        jnp.dot(onehot, part.astype(bf16), preferred_element_type=f32)
        for part in pieces(table[...], 3)
    ]
    chosen = chosen[0] + chosen[1] + chosen[2]
    for c in range(4):
        right[c] = chosen[:, c * BLOCK : (c + 1) * BLOCK]
    run_batches(left, right, grad)
    total = scatter(index[...], grad[...], blocks)
    for c in range(3):
        out_ref[c] = total[:, c * BLOCK : (c + 1) * BLOCK]
    stiff_ref[...] = total[:, 3 * BLOCK :]


def garm_kernel(pg_ref, pb_ref, own_ref, in_ref, out_ref, left, right, index, grad):
    owners, tiles, cap, _ = in_ref.shape
    blocks = tiles - 5
    garm_blocks = out_ref.shape[1]

    def take(d):
        rows = pl.ds(d * cap, cap)
        for c in range(4):
            right[c, rows, :] = own_ref[d, c]
        for s in range(cap):
            b = pb_ref[s, d]
            for c in range(4):
                left[c, pl.ds(d * cap + s, 1), :] = in_ref[
                    d, 4 + c * (blocks // 4) + b // 4, pl.ds(b % 4, 1), :
                ]
            index[pl.ds(d * cap + s, 1), :] = jnp.full((1, BLOCK), pg_ref[s, d].astype(f32), f32)

    over(owners, take)
    run_batches(left, right, grad)
    total = scatter(index[...], grad[...], garm_blocks)
    for c in range(3):
        out_ref[c] = total[:, c * BLOCK : (c + 1) * BLOCK]


def call(kernel, out_shape, scratch, scalars, arrays, cost=None):
    specs = [pl.BlockSpec(memory_space=pltpu.SMEM)] * len(scalars)
    specs += [pl.BlockSpec(memory_space=pltpu.VMEM)] * len(arrays)
    return pl.pallas_call(
        kernel,
        out_shape=out_shape,
        in_specs=specs,
        out_specs=jax.tree.map(lambda _: pl.BlockSpec(memory_space=pltpu.VMEM), out_shape),
        scratch_shapes=scratch,
        cost_estimate=cost and pl.CostEstimate(flops=cost, bytes_accessed=1000, transcendentals=0),
        compiler_params=pltpu.CompilerParams(vmem_limit_bytes=VMEM_LIMIT),
    )(*scalars, *arrays)


def read_table(ref, start, step):
    columns = [
        jnp.concatenate([ref[start + c * step + q] for q in range(step)], axis=0) for c in range(4)
    ]
    return jnp.concatenate(columns, axis=1)


def choose(index, table):
    lane = lax.broadcasted_iota(jnp.int32, index.shape, 1).astype(f32)
    onehot = (index == lane).astype(f32)[:, : table.shape[0]].astype(bf16)
    parts = [
        jnp.dot(onehot, part.astype(bf16), preferred_element_type=f32)
        for part in pieces(table, 3)
    ]
    rows = parts[0] + parts[1] + parts[2]
    return [rows[:, c * BLOCK : (c + 1) * BLOCK] for c in range(4)]


def halves(top, bottom):
    row = lax.broadcasted_iota(jnp.int32, (SUB, BLOCK), 0)
    return jnp.where(row < SUB // 2, top, bottom)


def flip(value):
    return pltpu.roll(value, SUB // 2, 0)


def body_work(tiles, table):
    return list(tiles[:4]), choose(tiles[4], table)


def garm_work(tiles, top, bottom):
    row = lax.broadcasted_iota(jnp.int32, (SUB, BLOCK), 0)
    index = tiles[4] + jnp.where(row < SUB // 2, 0, top.shape[0]).astype(f32)
    return choose(index, jnp.concatenate([top, bottom], axis=0)), list(tiles[:4])


def slot_tiles(ref):
    return [ref[c] for c in range(5)]


def message_table(ref, step):
    return read_table(ref, 5, step)


def pack_slots(ref):
    a, b, c, d, e = slot_tiles(ref)
    return [halves(flip(a), b), halves(flip(c), d), e]


def unpack_top(tiles):
    a, b, c = tiles
    return [a, flip(a), b, flip(b), flip(c)]


def unpack_bottom(tiles):
    a, b, c = tiles
    return [flip(a), a, flip(b), b, c]


def bundle_tiles(ref):
    return [ref[5 + q] for q in range(ref.shape[0] - 5)] + pack_slots(ref)


def near_bundle_kernel(one_ref, two_ref, out_ref):
    body = one_ref.shape[0] - 5
    for n, ref in enumerate((one_ref, two_ref)):
        for q in range(body):
            out_ref[n * body + q] = ref[5 + q]
    for k, tile in enumerate(bottom_tiles(one_ref, two_ref)):
        out_ref[2 * body + k] = tile


def far_bundle_kernel(ref, *refs):
    for k, tile in enumerate(bundle_tiles(ref)):
        refs[-1][k] = tile


def top_tiles(one_ref, two_ref):
    return [halves(a, flip(b)) for a, b in zip(slot_tiles(one_ref), slot_tiles(two_ref))]


def bottom_tiles(one_ref, two_ref):
    return [halves(flip(a), b) for a, b in zip(slot_tiles(one_ref), slot_tiles(two_ref))]


def store(work, index, bgrad_ref, bindex_ref, ggrad_ref):
    out = gradients(work)
    for n, value in enumerate(index):
        rows = slice(n * SUB, (n + 1) * SUB)
        bgrad_ref[rows, :] = jnp.concatenate(out[n], axis=1)
        ggrad_ref[rows, :] = jnp.concatenate(out[len(index) + n][:3], axis=1)
        bindex_ref[rows, :] = value


def first_kernel(own_ref, sent0, sent1, got0, got1, after_ref, *out_refs):
    del after_ref
    step = (own_ref.shape[0] - 5) // 4
    tiles = top_tiles(got0, got1)
    work = [
        body_work(tiles, message_table(own_ref, step)),
        garm_work(top_tiles(sent0, sent1), message_table(got0, step), message_table(got1, step)),
    ]
    store(work, [tiles[4]], *out_refs)


def second_kernel(own_ref, sent0, sent1, sent2, got2, near_ref, after_ref, *out_refs):
    del after_ref
    body = own_ref.shape[0] - 5
    step = body // 4
    own = message_table(own_ref, step)
    here = top_tiles(own_ref, got2)
    near = [near_ref[2 * body + k] for k in range(5)]
    work = [
        body_work(here, own),
        body_work(near, own),
        garm_work(top_tiles(own_ref, sent2), own, message_table(got2, step)),
        garm_work(
            bottom_tiles(sent0, sent1), *[read_table(near_ref, n * body, step) for n in range(2)]
        ),
    ]
    store(work, [here[4], near[4]], *out_refs)


def late_body_kernel(own_ref, x0_ref, far_ref, bg1, bg2, bi1, bi2, out_ref, stiff_ref):
    body = own_ref.shape[0] - 5
    top = unpack_top([x0_ref[body + k] for k in range(3)])
    bottom = unpack_bottom([far_ref[body + k] for k in range(3)])
    tiles = [halves(x, y) for x, y in zip(top, bottom)]
    out = gradients([body_work(tiles, message_table(own_ref, body // 4))])
    grads = jnp.concatenate([bg1[...], bg2[...], jnp.concatenate(out[0], axis=1)], axis=0)
    index = jnp.concatenate([bi1[...], bi2[...], tiles[4]], axis=0)
    total = scatter(index, grads, out_ref.shape[1])
    for c in range(3):
        out_ref[c] = total[:, c * BLOCK : (c + 1) * BLOCK]
    stiff_ref[...] = total[:, 3 * BLOCK :]


def late_garm_kernel(own_ref, sent2, x0_ref, far_ref, gg1, gg2, index_ref, out_ref):
    step = (own_ref.shape[0] - 5) // 4
    tables = [read_table(ref, 0, step) for ref in (x0_ref, far_ref)]
    out = gradients([garm_work(bottom_tiles(own_ref, sent2), *tables)])
    grads = jnp.concatenate([gg1[...], gg2[...], jnp.concatenate(out[0][:3], axis=1)], axis=0)
    index = jnp.concatenate([index_ref[k] for k in range(index_ref.shape[0])], axis=0)
    total = scatter(index, grads, out_ref.shape[1])
    for c in range(3):
        out_ref[c] = total[:, c * BLOCK : (c + 1) * BLOCK]


def final_kernel(garm_ref, body_ref, mine_ref, other_ref, garm_out, body_out, stiff_out):
    stiff_out[...] = mine_ref[...] + other_ref[...]
    body_out[...] = body_ref[...]
    garm_out[...] = garm_ref[...]


def stage_kernel(*refs):
    hbm, (index_ref, bundle_ref, *out_refs) = refs[:7], refs[7:13]
    vmem, sems = refs[13:20], refs[20]
    copies = [
        pltpu.make_async_copy(src, dst, sems.at[k]) for k, (src, dst) in enumerate(zip(hbm, vmem))
    ]
    for copy in copies:
        copy.start()
    for copy in copies:
        copy.wait()
    pg_ref, pb_ref, pc_ref, garm_ref, cot_ref, body_ref, stiff_ref = vmem
    cap = pg_ref.shape[0]
    tiles = stiff_ref.shape[0]
    width = lax.axis_size("body")
    here, column = lax.axis_index("garm"), lax.axis_index("body")
    garm_n = lax.axis_size("garm")
    for n, out_ref in enumerate(out_refs):
        place_z = lax.rem(here + STEPS[n], garm_n)
        for q in range(3 * tiles):
            out_ref[5 + q] = body_ref[q]
        for q in range(tiles):
            out_ref[5 + 3 * tiles + q] = stiff_ref[q]
        for x in range(2):
            owner = place_z * width + (column ^ x)
            live = pc_ref[0, owner]
            for s in range(cap):
                g = pg_ref[s, owner]
                row, place = pl.ds(g, 1), pl.ds(x * cap + s, 1)
                for c in range(3):
                    out_ref[c, place, :] = garm_ref[c, row, :]
                out_ref[3, place, :] = jnp.where(s < live, cot_ref[row, :], 0.0)
                out_ref[4, place, :] = jnp.full((1, BLOCK), pb_ref[s, owner].astype(f32), f32)
                spot = 2 * x + (n in (0, 3))
                line = (0 if n < 2 else cap) + s
                index_ref[spot, line : line + 1, :] = jnp.full((1, BLOCK), g.astype(f32), f32)
    for k, tile in enumerate(bundle_tiles(out_refs[0])):
        bundle_ref[k] = tile


def staged(garment, cotangent, body_points, stiffness, pg, pb, pc):
    verts = garment.shape[2]
    points = body_points.shape[2]
    blocks = points // BLOCK
    tiles = blocks // SUB
    garm_n = lax.axis_size("garm")
    message = jax.ShapeDtypeStruct((5 + 4 * tiles, SUB, BLOCK), f32)
    arrays = (
        pg,
        pb,
        pc,
        garment.reshape(3, verts // BLOCK, BLOCK),
        cotangent.reshape(verts // BLOCK, BLOCK),
        body_points.reshape(3 * tiles, SUB, BLOCK),
        stiffness.reshape(tiles, SUB, BLOCK),
    )
    bundle = jax.ShapeDtypeStruct((3 + 4 * tiles, SUB, BLOCK), f32)
    index, own_bundle, own, *sent = pl.pallas_call(
        stage_kernel,
        out_shape=[jax.ShapeDtypeStruct((garm_n, SUB, BLOCK), f32), bundle] + [message] * garm_n,
        in_specs=[pl.BlockSpec(memory_space=pltpu.HBM)] * len(arrays),
        out_specs=[pl.BlockSpec(memory_space=pltpu.VMEM)] * (garm_n + 2),
        scratch_shapes=[
            (pltpu.SMEM if k < 3 else pltpu.VMEM)(a.shape, a.dtype) for k, a in enumerate(arrays)
        ]
        + [pltpu.SemaphoreType.DMA((len(arrays),))],
        compiler_params=pltpu.CompilerParams(vmem_limit_bytes=VMEM_LIMIT),
    )(*[pltpu.with_memory_space_constraint(a, pltpu.HBM) for a in arrays])

    def along_garm(value, step):
        return lax.ppermute(value, "garm", [(z, (z + step) % garm_n) for z in range(garm_n)])

    def along_body(value):
        return lax.ppermute(value, "body", [(0, 1), (1, 0)])

    got = [along_garm(sent[n], STEPS[1 + n]) for n in (1, 0, 2)]
    x0 = along_body(own_bundle)
    near_shape = jax.ShapeDtypeStruct((5 + 8 * tiles, SUB, BLOCK), f32)
    near = call(near_bundle_kernel, near_shape, [], (), (got[0], got[1]), BUNDLE_COST)

    def batch_shapes(count):
        return tuple(
            jax.ShapeDtypeStruct((count * SUB, width * BLOCK), f32) for width in (4, 1, 3)
        )

    bg1, bi1, gg1 = call(
        first_kernel,
        batch_shapes(1),
        [],
        (),
        (own, sent[0], sent[1], got[0], got[1], near),
        FIRST_COST,
    )
    far = call(far_bundle_kernel, bundle, [], (), (got[2], x0, bg1), BUNDLE_COST)
    near_other, far_other = along_body(near), along_body(far)
    bg2, bi2, gg2 = call(
        second_kernel, batch_shapes(2), [], (), (own, *sent, got[2], near_other, far), SECOND_COST
    )
    body_shape = jax.ShapeDtypeStruct((3, blocks, BLOCK), f32)
    stiff_shape = jax.ShapeDtypeStruct((blocks, BLOCK), f32)
    garm_shape = jax.ShapeDtypeStruct((3, verts // BLOCK, BLOCK), f32)
    body_total, stiff = call(
        late_body_kernel,
        (body_shape, stiff_shape),
        [],
        (),
        (own, x0, far_other, bg1, bg2, bi1, bi2),
    )
    stiff_other = lax.ppermute(stiff, "frame", [(0, 1), (1, 0)])
    garm_total = call(
        late_garm_kernel,
        garm_shape,
        [],
        (),
        (own, sent[2], x0, far_other, gg1, gg2, index),
    )
    return call(
        final_kernel,
        (garm_shape, body_shape, stiff_shape),
        [],
        (),
        (garm_total, body_total, stiff, stiff_other),
    )


def per_device(garment, cotangent, body_points, stiffness, pair_garment, pair_body, pair_count):
    owners = lax.axis_size(("garm", "body"))
    verts = garment.shape[2]
    points = body_points.shape[2]
    blocks = points // BLOCK
    cap = pair_garment.shape[3]
    slots = owners * cap
    pg = pair_garment.reshape(owners, cap).T
    pb = pair_body.reshape(owners, cap).T
    pc = pair_count.reshape(1, owners)
    if (lax.axis_size("garm"), lax.axis_size("body")) == (4, 2) and cap == SUB // 2:
        garm_grad, body_grad, stiff = staged(
            garment, cotangent, body_points, stiffness, pg, pb, pc
        )
        return (
            garm_grad.reshape(1, 3, verts),
            body_grad.reshape(1, 3, points),
            stiff.reshape(points),
        )
    message = call(
        pack_kernel,
        jax.ShapeDtypeStruct((owners, 5 + blocks, cap, BLOCK), f32),
        [],
        (pg, pb, pc),
        (
            garment.reshape(3, verts // BLOCK, BLOCK),
            cotangent.reshape(verts // BLOCK, BLOCK),
            body_points.reshape(3, blocks, BLOCK),
            stiffness.reshape(blocks, BLOCK),
        ),
    )
    arrived = lax.all_to_all(message, ("garm", "body"), split_axis=0, concat_axis=0, tiled=True)
    rows = pltpu.VMEM((4, slots, BLOCK), f32)
    grad = pltpu.VMEM((slots, 4 * BLOCK), f32)
    index = pltpu.VMEM((slots, BLOCK), f32)
    body_grad, stiff = call(
        body_kernel,
        (
            jax.ShapeDtypeStruct((3, blocks, BLOCK), f32),
            jax.ShapeDtypeStruct((blocks, BLOCK), f32),
        ),
        [rows, rows, pltpu.VMEM((blocks, 4 * BLOCK), f32), index, grad],
        (),
        (message, arrived),
    )
    other = lax.ppermute(stiff, "frame", [(0, 1), (1, 0)])
    garm_grad = call(
        garm_kernel,
        jax.ShapeDtypeStruct((3, verts // BLOCK, BLOCK), f32),
        [rows, rows, index, grad],
        (pg, pb),
        (message, arrived),
    )
    return (
        garm_grad.reshape(1, 3, verts),
        body_grad.reshape(1, 3, points),
        (stiff + other).reshape(points),
    )


def solution(mesh):
    in_specs = (
        P(("grp", "frame"), None, ("garm", "body")),
        P(("grp", "frame"), ("garm", "body")),
        P(("grp", "frame"), None, ("garm", "body")),
        P(("grp", "garm", "body")),
        P(("grp", "frame"), ("garm", "body"), None, None),
        P(("grp", "frame"), ("garm", "body"), None, None),
        P(("grp", "frame"), ("garm", "body"), None),
    )
    out_specs = (
        P(("grp", "frame"), None, ("garm", "body")),
        P(("grp", "frame"), None, ("garm", "body")),
        P(("grp", "garm", "body")),
    )
    return jax.shard_map(
        per_device, mesh=mesh, in_specs=in_specs, out_specs=out_specs, check_vma=False
    )
```

```python
import math

import jax
import jax.numpy as jnp
from jax import lax
from jax.experimental import pallas as pl
from jax.experimental.pallas import tpu as pltpu
from jax.sharding import PartitionSpec as P

BLOCK = 128
SUB = 8
VMEM_LIMIT = 32 * 1024 * 1024
STEPS = (0, 1, 3, 2)
SAME_COST = 40_000_000_000
BUNDLE_COST = 1000

amplitude = 0.05
width_sq = 4.0

SCALE = math.sqrt(math.log2(math.e) / width_sq)
FACTOR = -2.0 / width_sq * amplitude

f32 = jnp.float32
bf16 = jnp.bfloat16


def pieces(value, count):
    out = []
    for _ in range(count - 1):
        top = value.astype(bf16).astype(f32)
        out.append(top)
        value = value - top
    out.append(value)
    return out


def features(left, right):
    lpos = [left[c] * SCALE for c in range(3)]
    rpos = [right[c] * SCALE for c in range(3)]
    lnorm = -(lpos[0] * lpos[0] + lpos[1] * lpos[1] + lpos[2] * lpos[2])
    rnorm = -(rpos[0] * rpos[0] + rpos[1] * rpos[1] + rpos[2] * rpos[2])
    one = jnp.ones_like(lnorm)
    lrows, rrows = [], []
    for c in range(3):
        l1, l2, l3 = pieces(lpos[c] * 2.0, 3)
        r1, r2, r3 = pieces(rpos[c], 3)
        lrows += [l1, l1, l2, l2, l1, l3]
        rrows += [r1, r2, r1, r2, r3, r1]
    lrows += pieces(lnorm, 3) + [one] * 3
    rrows += [one] * 3 + pieces(rnorm, 3)
    return (
        jnp.concatenate(lrows, axis=0).astype(bf16),
        jnp.concatenate(rrows, axis=0).astype(bf16),
    )


def pull(batches):
    made = []
    for left, right in batches:
        lfeat, rfeat = features(left, right)
        weight = left[3]
        coeff = jnp.concatenate([weight * left[c] for c in range(3)] + [weight], axis=0)
        chi, clo = [part.astype(bf16) for part in pieces(coeff, 2)]
        lhs = jnp.concatenate(
            [
                jnp.concatenate([chi, chi], axis=1),
                jnp.concatenate([clo, jnp.zeros_like(clo)], axis=1),
            ],
            axis=0,
        )
        made.append((lfeat.T, rfeat, lhs))
    row = lax.broadcasted_iota(jnp.int32, made[0][1].shape, 0) % SUB
    sub = lax.broadcasted_iota(jnp.int32, (4 * SUB, BLOCK), 0) % SUB
    totals = [jnp.zeros((4 * SUB, BLOCK), f32) for _ in batches]
    for pair in range(0, SUB, 2):
        masks = [(row == pair + k).astype(f32).astype(bf16) for k in range(2)]
        for n, (lfeat_t, rfeat, lhs) in enumerate(made):
            rhs = jnp.concatenate([rfeat * mask for mask in masks], axis=1)
            exponent = jnp.dot(lfeat_t, rhs, preferred_element_type=f32)
            kernel = jnp.exp2(exponent)
            khi = kernel.astype(bf16)
            klo = (kernel - khi.astype(f32)).astype(bf16)
            sums = jnp.dot(lhs, jnp.concatenate([khi, klo], axis=0), preferred_element_type=f32)
            sums = sums[: 4 * SUB] + sums[4 * SUB :]
            for k in range(2):
                part = sums[:, k * BLOCK : (k + 1) * BLOCK]
                totals[n] = jnp.where(sub == pair + k, part, totals[n])
    return [[total[c * SUB : (c + 1) * SUB] for c in range(4)] for total in totals]


def gradients(batches):
    out = []
    for (_, right), total in zip(batches, pull(batches)):
        rows = [FACTOR * right[3] * (right[c] * total[3] - total[c]) for c in range(3)]
        out.append(rows + [amplitude * total[3]])
    return out


def run_batches(left_ref, right_ref, grad_ref):
    batches = left_ref.shape[1] // SUB
    group = math.gcd(batches, 4)

    def step(k, carry):
        places = [pl.ds(pl.multiple_of((k * group + n) * SUB, SUB), SUB) for n in range(group)]
        work = [
            tuple([ref[c, rows, :] for c in range(4)] for ref in (left_ref, right_ref))
            for rows in places
        ]
        for rows, values in zip(places, gradients(work)):
            for c, value in enumerate(values):
                grad_ref[rows, c * BLOCK : (c + 1) * BLOCK] = value
        return carry

    lax.fori_loop(0, batches // group, step, 0)


def scatter(index, grads, blocks):
    lane = lax.broadcasted_iota(jnp.int32, index.shape, 1).astype(f32)
    onehot_t = (index == lane).astype(f32).T[:blocks].astype(bf16)
    parts = [
        jnp.dot(onehot_t, part.astype(bf16), preferred_element_type=f32)
        for part in pieces(grads, 3)
    ]
    return parts[0] + parts[1] + parts[2]


def pack_kernel(pg_ref, pb_ref, pc_ref, garm_ref, cot_ref, body_ref, stiff_ref, out_ref):
    cap, owners = pg_ref.shape
    tiles = stiff_ref.shape[0] // cap

    def one(d, carry):
        for s in range(cap):
            row = pl.ds(pg_ref[s, d], 1)
            for c in range(3):
                out_ref[d, c, s : s + 1, :] = garm_ref[c, row, :]
            out_ref[d, 3, s : s + 1, :] = jnp.where(s < pc_ref[0, d], cot_ref[row, :], 0.0)
            out_ref[d, 4 + 4 * tiles, s : s + 1, :] = jnp.full(
                (1, BLOCK), pb_ref[s, d].astype(f32), f32
            )
        for q in range(tiles):
            rows = slice(q * cap, (q + 1) * cap)
            for c in range(3):
                out_ref[d, 4 + c * tiles + q] = body_ref[c, rows, :]
            out_ref[d, 4 + 3 * tiles + q] = stiff_ref[rows, :]
        return carry

    if owners <= 8:
        for d in range(owners):
            one(d, 0)
    else:
        lax.fori_loop(0, owners, one, 0)


def over(count, fn):
    if count <= 8:
        for d in range(count):
            fn(d)
    else:
        lax.fori_loop(0, count, lambda d, carry: (fn(d), carry)[1], 0)


def body_kernel(own_ref, in_ref, out_ref, stiff_ref, left, right, table, index, grad):
    owners, tiles, cap, _ = in_ref.shape
    blocks = tiles - 5

    def take(d):
        rows = pl.ds(d * cap, cap)
        for c in range(4):
            left[c, rows, :] = in_ref[d, c]
        index[rows, :] = in_ref[d, tiles - 1]

    over(owners, take)
    for c in range(4):
        for q in range(blocks // 4):
            table[4 * q : 4 * q + 4, c * BLOCK : (c + 1) * BLOCK] = own_ref[
                0, 4 + c * (blocks // 4) + q
            ]
    lane = lax.broadcasted_iota(jnp.int32, index.shape, 1).astype(f32)
    onehot = (index[...] == lane).astype(f32)[:, :blocks].astype(bf16)
    chosen = [
        jnp.dot(onehot, part.astype(bf16), preferred_element_type=f32)
        for part in pieces(table[...], 3)
    ]
    chosen = chosen[0] + chosen[1] + chosen[2]
    for c in range(4):
        right[c] = chosen[:, c * BLOCK : (c + 1) * BLOCK]
    run_batches(left, right, grad)
    total = scatter(index[...], grad[...], blocks)
    for c in range(3):
        out_ref[c] = total[:, c * BLOCK : (c + 1) * BLOCK]
    stiff_ref[...] = total[:, 3 * BLOCK :]


def garm_kernel(pg_ref, pb_ref, own_ref, in_ref, out_ref, left, right, index, grad):
    owners, tiles, cap, _ = in_ref.shape
    blocks = tiles - 5
    garm_blocks = out_ref.shape[1]

    def take(d):
        rows = pl.ds(d * cap, cap)
        for c in range(4):
            right[c, rows, :] = own_ref[d, c]
        for s in range(cap):
            b = pb_ref[s, d]
            for c in range(4):
                left[c, pl.ds(d * cap + s, 1), :] = in_ref[
                    d, 4 + c * (blocks // 4) + b // 4, pl.ds(b % 4, 1), :
                ]
            index[pl.ds(d * cap + s, 1), :] = jnp.full((1, BLOCK), pg_ref[s, d].astype(f32), f32)

    over(owners, take)
    run_batches(left, right, grad)
    total = scatter(index[...], grad[...], garm_blocks)
    for c in range(3):
        out_ref[c] = total[:, c * BLOCK : (c + 1) * BLOCK]


def call(kernel, out_shape, scratch, scalars, arrays, cost=None):
    specs = [pl.BlockSpec(memory_space=pltpu.SMEM)] * len(scalars)
    specs += [pl.BlockSpec(memory_space=pltpu.VMEM)] * len(arrays)
    return pl.pallas_call(
        kernel,
        out_shape=out_shape,
        in_specs=specs,
        out_specs=jax.tree.map(lambda _: pl.BlockSpec(memory_space=pltpu.VMEM), out_shape),
        scratch_shapes=scratch,
        cost_estimate=cost and pl.CostEstimate(flops=cost, bytes_accessed=1000, transcendentals=0),
        compiler_params=pltpu.CompilerParams(vmem_limit_bytes=VMEM_LIMIT),
    )(*scalars, *arrays)


def read_table(ref, start, step):
    columns = [
        jnp.concatenate([ref[start + c * step + q] for q in range(step)], axis=0) for c in range(4)
    ]
    return jnp.concatenate(columns, axis=1)


def choose(index, table):
    lane = lax.broadcasted_iota(jnp.int32, index.shape, 1).astype(f32)
    onehot = (index == lane).astype(f32)[:, : table.shape[0]].astype(bf16)
    parts = [
        jnp.dot(onehot, part.astype(bf16), preferred_element_type=f32)
        for part in pieces(table, 3)
    ]
    rows = parts[0] + parts[1] + parts[2]
    return [rows[:, c * BLOCK : (c + 1) * BLOCK] for c in range(4)]


def halves(top, bottom):
    row = lax.broadcasted_iota(jnp.int32, (SUB, BLOCK), 0)
    return jnp.where(row < SUB // 2, top, bottom)


def flip(value):
    return pltpu.roll(value, SUB // 2, 0)


def body_work(tiles, table):
    return list(tiles[:4]), choose(tiles[4], table)


def garm_work(tiles, top, bottom):
    row = lax.broadcasted_iota(jnp.int32, (SUB, BLOCK), 0)
    index = tiles[4] + jnp.where(row < SUB // 2, 0, top.shape[0]).astype(f32)
    return choose(index, jnp.concatenate([top, bottom], axis=0)), list(tiles[:4])


def slot_tiles(ref):
    return [ref[c] for c in range(5)]


def message_table(ref, step):
    return read_table(ref, 5, step)


def pack(tiles):
    a, b, c, d, e = tiles
    return [halves(a, flip(b)), halves(c, flip(d)), e]


def unpack_top(tiles):
    a, b, c = tiles
    return [a, flip(a), b, flip(b), c]


def unpack_bottom(tiles):
    a, b, c = tiles
    return [flip(a), a, flip(b), b, flip(c)]


def half_message(ref, other):
    slots = slot_tiles(ref)
    if other:
        slots = [flip(tile) for tile in slots]
    return [ref[5 + q] for q in range(ref.shape[0] - 5)] + pack(slots)


def forward_kernel(one_ref, two_ref, own_ref, out_ref, own_out_ref):
    body = one_ref.shape[0] - 5
    for n, ref in enumerate((one_ref, two_ref)):
        for q in range(body):
            out_ref[n * body + q] = ref[5 + q]
    for k, tile in enumerate(bottom_tiles(one_ref, two_ref)):
        out_ref[2 * body + k] = tile
    for k, tile in enumerate(half_message(own_ref, True)):
        own_out_ref[k] = tile


def top_tiles(one_ref, two_ref):
    return [halves(a, flip(b)) for a, b in zip(slot_tiles(one_ref), slot_tiles(two_ref))]


def bottom_tiles(one_ref, two_ref):
    return [halves(flip(a), b) for a, b in zip(slot_tiles(one_ref), slot_tiles(two_ref))]


def store(work, index, bgrad_ref, bindex_ref, ggrad_ref):
    out = gradients(work)
    for n, value in enumerate(index):
        rows = slice(n * SUB, (n + 1) * SUB)
        bgrad_ref[rows, :] = jnp.concatenate(out[n], axis=1)
        ggrad_ref[rows, :] = jnp.concatenate(out[len(index) + n][:3], axis=1)
        bindex_ref[rows, :] = value


def same_kernel(own_ref, sent0, sent1, sent2, got0, got1, got2, after_ref, *out_refs):
    del after_ref
    body = own_ref.shape[0] - 5
    step = body // 4
    own = message_table(own_ref, step)
    next_to = top_tiles(got0, got1)
    last = unpack_bottom([got2[body + k] for k in range(3)])
    here = [halves(x, y) for x, y in zip(slot_tiles(own_ref), last)]
    work = [
        body_work(next_to, own),
        body_work(here, own),
        garm_work(top_tiles(sent0, sent1), message_table(got0, step), message_table(got1, step)),
        garm_work(top_tiles(own_ref, sent2), own, read_table(got2, 0, step)),
    ]
    store(work, [next_to[4], here[4]], *out_refs)


def late_body_kernel(own_ref, near_ref, x0_ref, far_ref, bgrad_ref, bindex_ref, out_ref, stiff_ref):
    body = own_ref.shape[0] - 5
    own = message_table(own_ref, body // 4)
    near = [near_ref[2 * body + k] for k in range(5)]
    top = unpack_top([x0_ref[body + k] for k in range(3)])
    bottom = unpack_bottom([far_ref[body + k] for k in range(3)])
    tiles = [near, [halves(x, y) for x, y in zip(top, bottom)]]
    out = gradients([body_work(part, own) for part in tiles])
    grads = [bgrad_ref[...]] + [jnp.concatenate(rows, axis=1) for rows in out]
    index = jnp.concatenate([bindex_ref[...]] + [part[4] for part in tiles], axis=0)
    total = scatter(index, jnp.concatenate(grads, axis=0), out_ref.shape[1])
    for c in range(3):
        out_ref[c] = total[:, c * BLOCK : (c + 1) * BLOCK]
    stiff_ref[...] = total[:, 3 * BLOCK :]


def late_garm_kernel(
    own_ref, sent0, sent1, sent2, near_ref, x0_ref, far_ref, ggrad_ref, index_ref, out_ref
):
    body = own_ref.shape[0] - 5
    step = body // 4
    near = [read_table(near_ref, n * body, step) for n in range(2)]
    far = [read_table(ref, 0, step) for ref in (x0_ref, far_ref)]
    work = [
        garm_work(bottom_tiles(sent0, sent1), *near),
        garm_work(bottom_tiles(own_ref, sent2), *far),
    ]
    out = gradients(work)
    grads = [ggrad_ref[...]] + [jnp.concatenate(rows[:3], axis=1) for rows in out]
    index = jnp.concatenate([index_ref[k] for k in range(index_ref.shape[0])], axis=0)
    total = scatter(index, jnp.concatenate(grads, axis=0), out_ref.shape[1])
    for c in range(3):
        out_ref[c] = total[:, c * BLOCK : (c + 1) * BLOCK]


def final_kernel(garm_ref, body_ref, mine_ref, other_ref, garm_out, body_out, stiff_out):
    stiff_out[...] = mine_ref[...] + other_ref[...]
    body_out[...] = body_ref[...]
    garm_out[...] = garm_ref[...]


def stage_kernel(*refs):
    hbm, (index_ref, same_ref, other_ref, *out_refs) = refs[:7], refs[7:14]
    vmem, sems = refs[14:21], refs[21]
    copies = [
        pltpu.make_async_copy(src, dst, sems.at[k]) for k, (src, dst) in enumerate(zip(hbm, vmem))
    ]
    for copy in copies:
        copy.start()
    for copy in copies:
        copy.wait()
    pg_ref, pb_ref, pc_ref, garm_ref, cot_ref, body_ref, stiff_ref = vmem
    cap = pg_ref.shape[0]
    tiles = stiff_ref.shape[0]
    width = lax.axis_size("body")
    here, column = lax.axis_index("garm"), lax.axis_index("body")
    garm_n = lax.axis_size("garm")
    for n, out_ref in enumerate(out_refs):
        place_z = lax.rem(here + STEPS[n], garm_n)
        for q in range(3 * tiles):
            out_ref[5 + q] = body_ref[q]
        for q in range(tiles):
            out_ref[5 + 3 * tiles + q] = stiff_ref[q]
        for x in range(2):
            owner = place_z * width + (column ^ x)
            live = pc_ref[0, owner]
            for s in range(cap):
                g = pg_ref[s, owner]
                row, place = pl.ds(g, 1), pl.ds(x * cap + s, 1)
                for c in range(3):
                    out_ref[c, place, :] = garm_ref[c, row, :]
                out_ref[3, place, :] = jnp.where(s < live, cot_ref[row, :], 0.0)
                out_ref[4, place, :] = jnp.full((1, BLOCK), pb_ref[s, owner].astype(f32), f32)
                spot = 2 * x + (n in (0, 3))
                line = (0 if n < 2 else cap) + s
                index_ref[spot, line : line + 1, :] = jnp.full((1, BLOCK), g.astype(f32), f32)
    for ref, other in ((same_ref, False), (other_ref, True)):
        for k, tile in enumerate(half_message(out_refs[3], other)):
            ref[k] = tile


def staged(garment, cotangent, body_points, stiffness, pg, pb, pc):
    verts = garment.shape[2]
    points = body_points.shape[2]
    blocks = points // BLOCK
    tiles = blocks // SUB
    garm_n = lax.axis_size("garm")
    message = jax.ShapeDtypeStruct((5 + 4 * tiles, SUB, BLOCK), f32)
    arrays = (
        pg,
        pb,
        pc,
        garment.reshape(3, verts // BLOCK, BLOCK),
        cotangent.reshape(verts // BLOCK, BLOCK),
        body_points.reshape(3 * tiles, SUB, BLOCK),
        stiffness.reshape(tiles, SUB, BLOCK),
    )
    half = jax.ShapeDtypeStruct((3 + 4 * tiles, SUB, BLOCK), f32)
    index, last_same, last_other, own, *sent = pl.pallas_call(
        stage_kernel,
        out_shape=[jax.ShapeDtypeStruct((garm_n, SUB, BLOCK), f32), half, half] + [message] * garm_n,
        in_specs=[pl.BlockSpec(memory_space=pltpu.HBM)] * len(arrays),
        out_specs=[pl.BlockSpec(memory_space=pltpu.VMEM)] * (garm_n + 3),
        scratch_shapes=[
            (pltpu.SMEM if k < 3 else pltpu.VMEM)(a.shape, a.dtype) for k, a in enumerate(arrays)
        ]
        + [pltpu.SemaphoreType.DMA((len(arrays),))],
        compiler_params=pltpu.CompilerParams(vmem_limit_bytes=VMEM_LIMIT),
    )(*[pltpu.with_memory_space_constraint(a, pltpu.HBM) for a in arrays])

    def along_garm(value, step):
        return lax.ppermute(value, "garm", [(z, (z + step) % garm_n) for z in range(garm_n)])

    def along_body(value):
        return lax.ppermute(value, "body", [(0, 1), (1, 0)])

    got = [along_garm(sent[1], STEPS[2]), along_garm(sent[0], STEPS[1]), along_garm(last_same, STEPS[3])]
    far = lax.ppermute(
        last_other,
        ("garm", "body"),
        [(2 * z + x, 2 * ((z + STEPS[3]) % garm_n) + 1 - x) for z in range(garm_n) for x in range(2)],
    )
    near_shape = jax.ShapeDtypeStruct((5 + 8 * tiles, SUB, BLOCK), f32)
    near, own_half = call(
        forward_kernel, (near_shape, half), [], (), (got[0], got[1], own), BUNDLE_COST
    )
    near_other, x0 = along_body(near), along_body(own_half)

    def batch_shapes(count):
        return tuple(
            jax.ShapeDtypeStruct((count * SUB, width * BLOCK), f32) for width in (4, 1, 3)
        )

    bgrad, bindex, ggrad = call(
        same_kernel, batch_shapes(2), [], (), (own, *sent, *got, near), SAME_COST
    )
    body_shape = jax.ShapeDtypeStruct((3, blocks, BLOCK), f32)
    stiff_shape = jax.ShapeDtypeStruct((blocks, BLOCK), f32)
    garm_shape = jax.ShapeDtypeStruct((3, verts // BLOCK, BLOCK), f32)
    body_total, stiff = call(
        late_body_kernel,
        (body_shape, stiff_shape),
        [],
        (),
        (own, near_other, x0, far, bgrad, bindex),
    )
    stiff_other = lax.ppermute(stiff, "frame", [(0, 1), (1, 0)])
    garm_total = call(
        late_garm_kernel,
        garm_shape,
        [],
        (),
        (own, *sent, near_other, x0, far, ggrad, index),
    )
    return call(
        final_kernel,
        (garm_shape, body_shape, stiff_shape),
        [],
        (),
        (garm_total, body_total, stiff, stiff_other),
    )


def per_device(garment, cotangent, body_points, stiffness, pair_garment, pair_body, pair_count):
    owners = lax.axis_size(("garm", "body"))
    verts = garment.shape[2]
    points = body_points.shape[2]
    blocks = points // BLOCK
    cap = pair_garment.shape[3]
    slots = owners * cap
    pg = pair_garment.reshape(owners, cap).T
    pb = pair_body.reshape(owners, cap).T
    pc = pair_count.reshape(1, owners)
    if (lax.axis_size("garm"), lax.axis_size("body")) == (4, 2) and cap == SUB // 2:
        garm_grad, body_grad, stiff = staged(
            garment, cotangent, body_points, stiffness, pg, pb, pc
        )
        return (
            garm_grad.reshape(1, 3, verts),
            body_grad.reshape(1, 3, points),
            stiff.reshape(points),
        )
    message = call(
        pack_kernel,
        jax.ShapeDtypeStruct((owners, 5 + blocks, cap, BLOCK), f32),
        [],
        (pg, pb, pc),
        (
            garment.reshape(3, verts // BLOCK, BLOCK),
            cotangent.reshape(verts // BLOCK, BLOCK),
            body_points.reshape(3, blocks, BLOCK),
            stiffness.reshape(blocks, BLOCK),
        ),
    )
    arrived = lax.all_to_all(message, ("garm", "body"), split_axis=0, concat_axis=0, tiled=True)
    rows = pltpu.VMEM((4, slots, BLOCK), f32)
    grad = pltpu.VMEM((slots, 4 * BLOCK), f32)
    index = pltpu.VMEM((slots, BLOCK), f32)
    body_grad, stiff = call(
        body_kernel,
        (
            jax.ShapeDtypeStruct((3, blocks, BLOCK), f32),
            jax.ShapeDtypeStruct((blocks, BLOCK), f32),
        ),
        [rows, rows, pltpu.VMEM((blocks, 4 * BLOCK), f32), index, grad],
        (),
        (message, arrived),
    )
    other = lax.ppermute(stiff, "frame", [(0, 1), (1, 0)])
    garm_grad = call(
        garm_kernel,
        jax.ShapeDtypeStruct((3, verts // BLOCK, BLOCK), f32),
        [rows, rows, index, grad],
        (pg, pb),
        (message, arrived),
    )
    return (
        garm_grad.reshape(1, 3, verts),
        body_grad.reshape(1, 3, points),
        (stiff + other).reshape(points),
    )


def solution(mesh):
    in_specs = (
        P(("grp", "frame"), None, ("garm", "body")),
        P(("grp", "frame"), ("garm", "body")),
        P(("grp", "frame"), None, ("garm", "body")),
        P(("grp", "garm", "body")),
        P(("grp", "frame"), ("garm", "body"), None, None),
        P(("grp", "frame"), ("garm", "body"), None, None),
        P(("grp", "frame"), ("garm", "body"), None),
    )
    out_specs = (
        P(("grp", "frame"), None, ("garm", "body")),
        P(("grp", "frame"), None, ("garm", "body")),
        P(("grp", "garm", "body")),
    )
    return jax.shard_map(
        per_device, mesh=mesh, in_specs=in_specs, out_specs=out_specs, check_vma=False
    )
```

```python
import math

import jax
import jax.numpy as jnp
from jax import lax
from jax.experimental import pallas as pl
from jax.experimental.pallas import tpu as pltpu
from jax.sharding import PartitionSpec as P

BLOCK = 128
SUB = 8
VMEM_LIMIT = 32 * 1024 * 1024
SAME_COST = 40_000_000_000
NEAR_COST = 1_000_000_000
BUNDLE_COST = 1000

amplitude = 0.05
width_sq = 4.0

SCALE = math.sqrt(math.log2(math.e) / width_sq)
FACTOR = -2.0 / width_sq * amplitude

f32 = jnp.float32
bf16 = jnp.bfloat16


def pieces(value, count):
    out = []
    for _ in range(count - 1):
        top = value.astype(bf16).astype(f32)
        out.append(top)
        value = value - top
    out.append(value)
    return out


def features(left, right):
    lpos = [left[c] * SCALE for c in range(3)]
    rpos = [right[c] * SCALE for c in range(3)]
    lnorm = -(lpos[0] * lpos[0] + lpos[1] * lpos[1] + lpos[2] * lpos[2])
    rnorm = -(rpos[0] * rpos[0] + rpos[1] * rpos[1] + rpos[2] * rpos[2])
    one = jnp.ones_like(lnorm)
    lrows, rrows = [], []
    for c in range(3):
        l1, l2, l3 = pieces(lpos[c] * 2.0, 3)
        r1, r2, r3 = pieces(rpos[c], 3)
        lrows += [l1, l1, l2, l2, l1, l3]
        rrows += [r1, r2, r1, r2, r3, r1]
    lrows += pieces(lnorm, 3) + [one] * 3
    rrows += [one] * 3 + pieces(rnorm, 3)
    return (
        jnp.concatenate(lrows, axis=0).astype(bf16),
        jnp.concatenate(rrows, axis=0).astype(bf16),
    )


def pull(batches):
    made = []
    for left, right in batches:
        lfeat, rfeat = features(left, right)
        weight = left[3]
        coeff = jnp.concatenate([weight * left[c] for c in range(3)] + [weight], axis=0)
        chi, clo = [part.astype(bf16) for part in pieces(coeff, 2)]
        lhs = jnp.concatenate(
            [
                jnp.concatenate([chi, chi], axis=1),
                jnp.concatenate([clo, jnp.zeros_like(clo)], axis=1),
            ],
            axis=0,
        )
        made.append((lfeat.T, rfeat, lhs))
    row = lax.broadcasted_iota(jnp.int32, made[0][1].shape, 0) % SUB
    sub = lax.broadcasted_iota(jnp.int32, (4 * SUB, BLOCK), 0) % SUB
    totals = [jnp.zeros((4 * SUB, BLOCK), f32) for _ in batches]
    for pair in range(0, SUB, 2):
        masks = [(row == pair + k).astype(f32).astype(bf16) for k in range(2)]
        for n, (lfeat_t, rfeat, lhs) in enumerate(made):
            rhs = jnp.concatenate([rfeat * mask for mask in masks], axis=1)
            exponent = jnp.dot(lfeat_t, rhs, preferred_element_type=f32)
            kernel = jnp.exp2(exponent)
            khi = kernel.astype(bf16)
            klo = (kernel - khi.astype(f32)).astype(bf16)
            sums = jnp.dot(lhs, jnp.concatenate([khi, klo], axis=0), preferred_element_type=f32)
            sums = sums[: 4 * SUB] + sums[4 * SUB :]
            for k in range(2):
                part = sums[:, k * BLOCK : (k + 1) * BLOCK]
                totals[n] = jnp.where(sub == pair + k, part, totals[n])
    return [[total[c * SUB : (c + 1) * SUB] for c in range(4)] for total in totals]


def gradients(batches):
    out = []
    for (_, right), total in zip(batches, pull(batches)):
        rows = [FACTOR * right[3] * (right[c] * total[3] - total[c]) for c in range(3)]
        out.append(rows + [amplitude * total[3]])
    return out


def run_batches(left_ref, right_ref, grad_ref):
    batches = left_ref.shape[1] // SUB
    group = math.gcd(batches, 4)

    def step(k, carry):
        places = [pl.ds(pl.multiple_of((k * group + n) * SUB, SUB), SUB) for n in range(group)]
        work = [
            tuple([ref[c, rows, :] for c in range(4)] for ref in (left_ref, right_ref))
            for rows in places
        ]
        for rows, values in zip(places, gradients(work)):
            for c, value in enumerate(values):
                grad_ref[rows, c * BLOCK : (c + 1) * BLOCK] = value
        return carry

    lax.fori_loop(0, batches // group, step, 0)


def scatter(index, grads, blocks):
    lane = lax.broadcasted_iota(jnp.int32, index.shape, 1).astype(f32)
    onehot_t = (index == lane).astype(f32).T[:blocks].astype(bf16)
    parts = [
        jnp.dot(onehot_t, part.astype(bf16), preferred_element_type=f32)
        for part in pieces(grads, 3)
    ]
    return parts[0] + parts[1] + parts[2]


def pack_kernel(pg_ref, pb_ref, pc_ref, garm_ref, cot_ref, body_ref, stiff_ref, out_ref):
    cap, owners = pg_ref.shape
    tiles = stiff_ref.shape[0] // cap

    def one(d, carry):
        for s in range(cap):
            row = pl.ds(pg_ref[s, d], 1)
            for c in range(3):
                out_ref[d, c, s : s + 1, :] = garm_ref[c, row, :]
            out_ref[d, 3, s : s + 1, :] = jnp.where(s < pc_ref[0, d], cot_ref[row, :], 0.0)
            out_ref[d, 4 + 4 * tiles, s : s + 1, :] = jnp.full(
                (1, BLOCK), pb_ref[s, d].astype(f32), f32
            )
        for q in range(tiles):
            rows = slice(q * cap, (q + 1) * cap)
            for c in range(3):
                out_ref[d, 4 + c * tiles + q] = body_ref[c, rows, :]
            out_ref[d, 4 + 3 * tiles + q] = stiff_ref[rows, :]
        return carry

    if owners <= 8:
        for d in range(owners):
            one(d, 0)
    else:
        lax.fori_loop(0, owners, one, 0)


def over(count, fn):
    if count <= 8:
        for d in range(count):
            fn(d)
    else:
        lax.fori_loop(0, count, lambda d, carry: (fn(d), carry)[1], 0)


def body_kernel(own_ref, in_ref, out_ref, stiff_ref, left, right, table, index, grad):
    owners, tiles, cap, _ = in_ref.shape
    blocks = tiles - 5

    def take(d):
        rows = pl.ds(d * cap, cap)
        for c in range(4):
            left[c, rows, :] = in_ref[d, c]
        index[rows, :] = in_ref[d, tiles - 1]

    over(owners, take)
    for c in range(4):
        for q in range(blocks // 4):
            table[4 * q : 4 * q + 4, c * BLOCK : (c + 1) * BLOCK] = own_ref[
                0, 4 + c * (blocks // 4) + q
            ]
    lane = lax.broadcasted_iota(jnp.int32, index.shape, 1).astype(f32)
    onehot = (index[...] == lane).astype(f32)[:, :blocks].astype(bf16)
    chosen = [
        jnp.dot(onehot, part.astype(bf16), preferred_element_type=f32)
        for part in pieces(table[...], 3)
    ]
    chosen = chosen[0] + chosen[1] + chosen[2]
    for c in range(4):
        right[c] = chosen[:, c * BLOCK : (c + 1) * BLOCK]
    run_batches(left, right, grad)
    total = scatter(index[...], grad[...], blocks)
    for c in range(3):
        out_ref[c] = total[:, c * BLOCK : (c + 1) * BLOCK]
    stiff_ref[...] = total[:, 3 * BLOCK :]


def garm_kernel(pg_ref, pb_ref, own_ref, in_ref, out_ref, left, right, index, grad):
    owners, tiles, cap, _ = in_ref.shape
    blocks = tiles - 5
    garm_blocks = out_ref.shape[1]

    def take(d):
        rows = pl.ds(d * cap, cap)
        for c in range(4):
            right[c, rows, :] = own_ref[d, c]
        for s in range(cap):
            b = pb_ref[s, d]
            for c in range(4):
                left[c, pl.ds(d * cap + s, 1), :] = in_ref[
                    d, 4 + c * (blocks // 4) + b // 4, pl.ds(b % 4, 1), :
                ]
            index[pl.ds(d * cap + s, 1), :] = jnp.full((1, BLOCK), pg_ref[s, d].astype(f32), f32)

    over(owners, take)
    run_batches(left, right, grad)
    total = scatter(index[...], grad[...], garm_blocks)
    for c in range(3):
        out_ref[c] = total[:, c * BLOCK : (c + 1) * BLOCK]


def call(kernel, out_shape, scratch, scalars, arrays, cost=None):
    specs = [pl.BlockSpec(memory_space=pltpu.SMEM)] * len(scalars)
    specs += [pl.BlockSpec(memory_space=pltpu.VMEM)] * len(arrays)
    return pl.pallas_call(
        kernel,
        out_shape=out_shape,
        in_specs=specs,
        out_specs=jax.tree.map(lambda _: pl.BlockSpec(memory_space=pltpu.VMEM), out_shape),
        scratch_shapes=scratch,
        cost_estimate=cost and pl.CostEstimate(flops=cost, bytes_accessed=1000, transcendentals=0),
        compiler_params=pltpu.CompilerParams(vmem_limit_bytes=VMEM_LIMIT),
    )(*scalars, *arrays)


def read_table(ref, start, step):
    columns = [
        jnp.concatenate([ref[start + c * step + q] for q in range(step)], axis=0) for c in range(4)
    ]
    return jnp.concatenate(columns, axis=1)


def choose(index, table):
    lane = lax.broadcasted_iota(jnp.int32, index.shape, 1).astype(f32)
    onehot = (index == lane).astype(f32)[:, : table.shape[0]].astype(bf16)
    parts = [
        jnp.dot(onehot, part.astype(bf16), preferred_element_type=f32)
        for part in pieces(table, 3)
    ]
    rows = parts[0] + parts[1] + parts[2]
    return [rows[:, c * BLOCK : (c + 1) * BLOCK] for c in range(4)]


def halves(top, bottom):
    row = lax.broadcasted_iota(jnp.int32, (SUB, BLOCK), 0)
    return jnp.where(row < SUB // 2, top, bottom)


def flip(value):
    return pltpu.roll(value, SUB // 2, 0)


def body_work(tiles, table):
    return list(tiles[:4]), choose(tiles[4], table)


def garm_work(tiles, top, bottom):
    row = lax.broadcasted_iota(jnp.int32, (SUB, BLOCK), 0)
    index = tiles[4] + jnp.where(row < SUB // 2, 0, top.shape[0]).astype(f32)
    return choose(index, jnp.concatenate([top, bottom], axis=0)), list(tiles[:4])


def slot_tiles(ref):
    return [ref[c] for c in range(5)]


def message_table(ref, step):
    return read_table(ref, 5, step)


def pack(tiles):
    a, b, c, d, e = tiles
    return [halves(a, flip(b)), halves(c, flip(d)), e]


def unpack_top(tiles):
    a, b, c = tiles
    return [a, flip(a), b, flip(b), c]


def unpack_bottom(tiles):
    a, b, c = tiles
    return [flip(a), a, flip(b), b, flip(c)]


def half_message(ref, other):
    slots = slot_tiles(ref)
    if other:
        slots = [flip(tile) for tile in slots]
    return [ref[5 + q] for q in range(ref.shape[0] - 5)] + pack(slots)


def forward_kernel(one_ref, two_ref, out_ref):
    body = one_ref.shape[0] - 5
    for n, ref in enumerate((one_ref, two_ref)):
        for q in range(body):
            out_ref[n * body + q] = ref[5 + q]
    for k, tile in enumerate(bottom_tiles(one_ref, two_ref)):
        out_ref[2 * body + k] = tile


def half_kernel(ref, after_ref, out_ref):
    del after_ref
    for k, tile in enumerate(half_message(ref, True)):
        out_ref[k] = tile


def top_tiles(one_ref, two_ref):
    return [halves(a, flip(b)) for a, b in zip(slot_tiles(one_ref), slot_tiles(two_ref))]


def bottom_tiles(one_ref, two_ref):
    return [halves(flip(a), b) for a, b in zip(slot_tiles(one_ref), slot_tiles(two_ref))]


def store(work, index, bgrad_ref, bindex_ref, ggrad_ref):
    out = gradients(work)
    for n, value in enumerate(index):
        rows = slice(n * SUB, (n + 1) * SUB)
        bgrad_ref[rows, :] = jnp.concatenate(out[n], axis=1)
        ggrad_ref[rows, :] = jnp.concatenate(out[len(index) + n][:3], axis=1)
        bindex_ref[rows, :] = value


def same_kernel(own_ref, sent0, sent1, sent2, got0, got1, got2, after_ref, *out_refs):
    del after_ref
    body = own_ref.shape[0] - 5
    step = body // 4
    own = message_table(own_ref, step)
    here = top_tiles(own_ref, got0)
    last = unpack_bottom([got2[body + k] for k in range(3)])
    there = [halves(x, y) for x, y in zip(slot_tiles(got1), last)]
    work = [
        body_work(here, own),
        body_work(there, own),
        garm_work(top_tiles(own_ref, sent0), own, message_table(got0, step)),
        garm_work(top_tiles(sent1, sent2), message_table(got1, step), read_table(got2, 0, step)),
    ]
    store(work, [here[4], there[4]], *out_refs)


def near_kernel(own_ref, sent0, near_ref, after_ref, *out_refs):
    del after_ref
    body = own_ref.shape[0] - 5
    step = body // 4
    near = [near_ref[2 * body + k] for k in range(5)]
    tables = [read_table(near_ref, n * body, step) for n in range(2)]
    work = [
        body_work(near, message_table(own_ref, step)),
        garm_work(bottom_tiles(own_ref, sent0), *tables),
    ]
    store(work, [near[4]], *out_refs)


def late_body_kernel(own_ref, one_ref, two_ref, bg1, bg2, bi1, bi2, out_ref, stiff_ref):
    body = own_ref.shape[0] - 5
    top = unpack_top([one_ref[body + k] for k in range(3)])
    bottom = unpack_bottom([two_ref[body + k] for k in range(3)])
    tiles = [halves(x, y) for x, y in zip(top, bottom)]
    out = gradients([body_work(tiles, message_table(own_ref, body // 4))])
    grads = jnp.concatenate([bg1[...], bg2[...], jnp.concatenate(out[0], axis=1)], axis=0)
    index = jnp.concatenate([bi1[...], bi2[...], tiles[4]], axis=0)
    total = scatter(index, grads, out_ref.shape[1])
    for c in range(3):
        out_ref[c] = total[:, c * BLOCK : (c + 1) * BLOCK]
    stiff_ref[...] = total[:, 3 * BLOCK :]


def late_garm_kernel(sent1, sent2, one_ref, two_ref, gg1, gg2, index_ref, out_ref):
    step = (sent1.shape[0] - 5) // 4
    tables = [read_table(ref, 0, step) for ref in (one_ref, two_ref)]
    out = gradients([garm_work(bottom_tiles(sent1, sent2), *tables)])
    grads = jnp.concatenate([gg1[...], gg2[...], jnp.concatenate(out[0][:3], axis=1)], axis=0)
    index = jnp.concatenate([index_ref[k] for k in range(index_ref.shape[0])], axis=0)
    total = scatter(index, grads, out_ref.shape[1])
    for c in range(3):
        out_ref[c] = total[:, c * BLOCK : (c + 1) * BLOCK]


def final_kernel(garm_ref, body_ref, mine_ref, other_ref, garm_out, body_out, stiff_out):
    stiff_out[...] = mine_ref[...] + other_ref[...]
    body_out[...] = body_ref[...]
    garm_out[...] = garm_ref[...]


def stage_kernel(*refs):
    hbm, (index_ref, same_ref, other_ref, *out_refs) = refs[:7], refs[7:14]
    vmem, sems = refs[14:21], refs[21]
    copies = [
        pltpu.make_async_copy(src, dst, sems.at[k]) for k, (src, dst) in enumerate(zip(hbm, vmem))
    ]
    for copy in copies:
        copy.start()
    for copy in copies:
        copy.wait()
    pg_ref, pb_ref, pc_ref, garm_ref, cot_ref, body_ref, stiff_ref = vmem
    cap = pg_ref.shape[0]
    tiles = stiff_ref.shape[0]
    width = lax.axis_size("body")
    here, column = lax.axis_index("garm"), lax.axis_index("body")
    flips = (0, 3 - here // 2, 2 + here // 2, 1)
    for n, out_ref in enumerate(out_refs):
        place_z = here ^ flips[n]
        for q in range(3 * tiles):
            out_ref[5 + q] = body_ref[q]
        for q in range(tiles):
            out_ref[5 + 3 * tiles + q] = stiff_ref[q]
        for x in range(2):
            owner = place_z * width + (column ^ x)
            live = pc_ref[0, owner]
            for s in range(cap):
                g = pg_ref[s, owner]
                row, place = pl.ds(g, 1), pl.ds(x * cap + s, 1)
                for c in range(3):
                    out_ref[c, place, :] = garm_ref[c, row, :]
                out_ref[3, place, :] = jnp.where(s < live, cot_ref[row, :], 0.0)
                out_ref[4, place, :] = jnp.full((1, BLOCK), pb_ref[s, owner].astype(f32), f32)
                spot, line = 2 * x + n // 2, n % 2 * cap + s
                index_ref[spot, line : line + 1, :] = jnp.full((1, BLOCK), g.astype(f32), f32)
    for ref, other in ((same_ref, False), (other_ref, True)):
        for k, tile in enumerate(half_message(out_refs[3], other)):
            ref[k] = tile


def staged(garment, cotangent, body_points, stiffness, pg, pb, pc):
    verts = garment.shape[2]
    points = body_points.shape[2]
    blocks = points // BLOCK
    tiles = blocks // SUB
    garm_n = lax.axis_size("garm")
    message = jax.ShapeDtypeStruct((5 + 4 * tiles, SUB, BLOCK), f32)
    arrays = (
        pg,
        pb,
        pc,
        garment.reshape(3, verts // BLOCK, BLOCK),
        cotangent.reshape(verts // BLOCK, BLOCK),
        body_points.reshape(3 * tiles, SUB, BLOCK),
        stiffness.reshape(tiles, SUB, BLOCK),
    )
    half = jax.ShapeDtypeStruct((3 + 4 * tiles, SUB, BLOCK), f32)
    index, last_same, last_other, own, *sent = pl.pallas_call(
        stage_kernel,
        out_shape=[jax.ShapeDtypeStruct((garm_n, SUB, BLOCK), f32), half, half] + [message] * garm_n,
        in_specs=[pl.BlockSpec(memory_space=pltpu.HBM)] * len(arrays),
        out_specs=[pl.BlockSpec(memory_space=pltpu.VMEM)] * (garm_n + 3),
        scratch_shapes=[
            (pltpu.SMEM if k < 3 else pltpu.VMEM)(a.shape, a.dtype) for k, a in enumerate(arrays)
        ]
        + [pltpu.SemaphoreType.DMA((len(arrays),))],
        compiler_params=pltpu.CompilerParams(vmem_limit_bytes=VMEM_LIMIT),
    )(*[pltpu.with_memory_space_constraint(a, pltpu.HBM) for a in arrays])

    def along_garm(value, pairs):
        return lax.ppermute(value, "garm", pairs)

    def along_body(value):
        return lax.ppermute(value, "body", [(0, 1), (1, 0)])

    cycle = [(0, 2), (2, 1), (1, 3), (3, 0)]
    got = [
        along_garm(sent[1], cycle),
        along_garm(sent[0], [(b, a) for a, b in cycle]),
        along_garm(last_same, [(z, z ^ 1) for z in range(garm_n)]),
    ]
    direct = lax.ppermute(last_other, ("garm", "body"), [(n, n ^ 3) for n in range(2 * garm_n)])
    near_shape = jax.ShapeDtypeStruct((5 + 8 * tiles, SUB, BLOCK), f32)
    near = call(forward_kernel, near_shape, [], (), (own, got[0]), BUNDLE_COST)
    second = call(half_kernel, half, [], (), (got[1], near), BUNDLE_COST)
    near_other, second_other = along_body(near), along_body(second)

    def batch_shapes(count):
        return tuple(
            jax.ShapeDtypeStruct((count * SUB, width * BLOCK), f32) for width in (4, 1, 3)
        )

    bg1, bi1, gg1 = call(
        same_kernel, batch_shapes(2), [], (), (own, *sent, *got, second), SAME_COST
    )
    bg2, bi2, gg2 = call(
        near_kernel, batch_shapes(1), [], (), (own, sent[0], near_other, bg1), NEAR_COST
    )
    body_shape = jax.ShapeDtypeStruct((3, blocks, BLOCK), f32)
    stiff_shape = jax.ShapeDtypeStruct((blocks, BLOCK), f32)
    garm_shape = jax.ShapeDtypeStruct((3, verts // BLOCK, BLOCK), f32)
    body_total, stiff = call(
        late_body_kernel,
        (body_shape, stiff_shape),
        [],
        (),
        (own, second_other, direct, bg1, bg2, bi1, bi2),
    )
    stiff_other = lax.ppermute(stiff, "frame", [(0, 1), (1, 0)])
    garm_total = call(
        late_garm_kernel,
        garm_shape,
        [],
        (),
        (sent[1], sent[2], second_other, direct, gg1, gg2, index),
    )
    return call(
        final_kernel,
        (garm_shape, body_shape, stiff_shape),
        [],
        (),
        (garm_total, body_total, stiff, stiff_other),
    )


def per_device(garment, cotangent, body_points, stiffness, pair_garment, pair_body, pair_count):
    owners = lax.axis_size(("garm", "body"))
    verts = garment.shape[2]
    points = body_points.shape[2]
    blocks = points // BLOCK
    cap = pair_garment.shape[3]
    slots = owners * cap
    pg = pair_garment.reshape(owners, cap).T
    pb = pair_body.reshape(owners, cap).T
    pc = pair_count.reshape(1, owners)
    if (lax.axis_size("garm"), lax.axis_size("body")) == (4, 2) and cap == SUB // 2:
        garm_grad, body_grad, stiff = staged(
            garment, cotangent, body_points, stiffness, pg, pb, pc
        )
        return (
            garm_grad.reshape(1, 3, verts),
            body_grad.reshape(1, 3, points),
            stiff.reshape(points),
        )
    message = call(
        pack_kernel,
        jax.ShapeDtypeStruct((owners, 5 + blocks, cap, BLOCK), f32),
        [],
        (pg, pb, pc),
        (
            garment.reshape(3, verts // BLOCK, BLOCK),
            cotangent.reshape(verts // BLOCK, BLOCK),
            body_points.reshape(3, blocks, BLOCK),
            stiffness.reshape(blocks, BLOCK),
        ),
    )
    arrived = lax.all_to_all(message, ("garm", "body"), split_axis=0, concat_axis=0, tiled=True)
    rows = pltpu.VMEM((4, slots, BLOCK), f32)
    grad = pltpu.VMEM((slots, 4 * BLOCK), f32)
    index = pltpu.VMEM((slots, BLOCK), f32)
    body_grad, stiff = call(
        body_kernel,
        (
            jax.ShapeDtypeStruct((3, blocks, BLOCK), f32),
            jax.ShapeDtypeStruct((blocks, BLOCK), f32),
        ),
        [rows, rows, pltpu.VMEM((blocks, 4 * BLOCK), f32), index, grad],
        (),
        (message, arrived),
    )
    other = lax.ppermute(stiff, "frame", [(0, 1), (1, 0)])
    garm_grad = call(
        garm_kernel,
        jax.ShapeDtypeStruct((3, verts // BLOCK, BLOCK), f32),
        [rows, rows, index, grad],
        (pg, pb),
        (message, arrived),
    )
    return (
        garm_grad.reshape(1, 3, verts),
        body_grad.reshape(1, 3, points),
        (stiff + other).reshape(points),
    )


def solution(mesh):
    in_specs = (
        P(("grp", "frame"), None, ("garm", "body")),
        P(("grp", "frame"), ("garm", "body")),
        P(("grp", "frame"), None, ("garm", "body")),
        P(("grp", "garm", "body")),
        P(("grp", "frame"), ("garm", "body"), None, None),
        P(("grp", "frame"), ("garm", "body"), None, None),
        P(("grp", "frame"), ("garm", "body"), None),
    )
    out_specs = (
        P(("grp", "frame"), None, ("garm", "body")),
        P(("grp", "frame"), None, ("garm", "body")),
        P(("grp", "garm", "body")),
    )
    return jax.shard_map(
        per_device, mesh=mesh, in_specs=in_specs, out_specs=out_specs, check_vma=False
    )
```

```python
import math

import jax
import jax.numpy as jnp
from jax import lax
from jax.experimental import pallas as pl
from jax.experimental.pallas import tpu as pltpu
from jax.sharding import PartitionSpec as P

BLOCK = 128
SUB = 8
VMEM_LIMIT = 32 * 1024 * 1024
SAME_COST = 40_000_000_000
NEAR_COST = 1_000_000_000
BUNDLE_COST = 1000

amplitude = 0.05
width_sq = 4.0

SCALE = math.sqrt(math.log2(math.e) / width_sq)
FACTOR = -2.0 / width_sq * amplitude

f32 = jnp.float32
bf16 = jnp.bfloat16


def pieces(value, count):
    out = []
    for _ in range(count - 1):
        top = value.astype(bf16).astype(f32)
        out.append(top)
        value = value - top
    out.append(value)
    return out


def features(left, right):
    lpos = [left[c] * SCALE for c in range(3)]
    rpos = [right[c] * SCALE for c in range(3)]
    lnorm = -(lpos[0] * lpos[0] + lpos[1] * lpos[1] + lpos[2] * lpos[2])
    rnorm = -(rpos[0] * rpos[0] + rpos[1] * rpos[1] + rpos[2] * rpos[2])
    one = jnp.ones_like(lnorm)
    lrows, rrows = [], []
    for c in range(3):
        l1, l2, l3 = pieces(lpos[c] * 2.0, 3)
        r1, r2, r3 = pieces(rpos[c], 3)
        lrows += [l1, l1, l2, l2, l1, l3]
        rrows += [r1, r2, r1, r2, r3, r1]
    lrows += pieces(lnorm, 3) + [one] * 3
    rrows += [one] * 3 + pieces(rnorm, 3)
    return (
        jnp.concatenate(lrows, axis=0).astype(bf16),
        jnp.concatenate(rrows, axis=0).astype(bf16),
    )


def pull(batches):
    made = []
    for left, right in batches:
        lfeat, rfeat = features(left, right)
        weight = left[3]
        coeff = jnp.concatenate([weight * left[c] for c in range(3)] + [weight], axis=0)
        chi, clo = [part.astype(bf16) for part in pieces(coeff, 2)]
        lhs = jnp.concatenate(
            [
                jnp.concatenate([chi, chi], axis=1),
                jnp.concatenate([clo, jnp.zeros_like(clo)], axis=1),
            ],
            axis=0,
        )
        made.append((lfeat.T, rfeat, lhs))
    row = lax.broadcasted_iota(jnp.int32, made[0][1].shape, 0) % SUB
    sub = lax.broadcasted_iota(jnp.int32, (4 * SUB, BLOCK), 0) % SUB
    totals = [jnp.zeros((4 * SUB, BLOCK), f32) for _ in batches]

    def sums_of(pair, n, exponent):
        kernel = jnp.exp2(exponent)
        khi = kernel.astype(bf16)
        klo = (kernel - khi.astype(f32)).astype(bf16)
        sums = jnp.dot(made[n][2], jnp.concatenate([khi, klo], axis=0), preferred_element_type=f32)
        sums = sums[: 4 * SUB] + sums[4 * SUB :]
        for k in range(2):
            part = sums[:, k * BLOCK : (k + 1) * BLOCK]
            totals[n] = jnp.where(sub == pair + k, part, totals[n])

    ahead = SUB // 2 if len(batches) == 1 else 0
    waiting = []
    for pair in range(0, SUB, 2):
        masks = [(row == pair + k).astype(f32).astype(bf16) for k in range(2)]
        for n, (lfeat_t, rfeat, _) in enumerate(made):
            rhs = jnp.concatenate([rfeat * mask for mask in masks], axis=1)
            waiting.append((pair, n, jnp.dot(lfeat_t, rhs, preferred_element_type=f32)))
            if len(waiting) > ahead:
                sums_of(*waiting.pop(0))
    for work in waiting:
        sums_of(*work)
    return [[total[c * SUB : (c + 1) * SUB] for c in range(4)] for total in totals]


def gradients(batches):
    out = []
    for (_, right), total in zip(batches, pull(batches)):
        rows = [FACTOR * right[3] * (right[c] * total[3] - total[c]) for c in range(3)]
        out.append(rows + [amplitude * total[3]])
    return out


def run_batches(left_ref, right_ref, grad_ref):
    batches = left_ref.shape[1] // SUB
    group = math.gcd(batches, 4)

    def step(k, carry):
        places = [pl.ds(pl.multiple_of((k * group + n) * SUB, SUB), SUB) for n in range(group)]
        work = [
            tuple([ref[c, rows, :] for c in range(4)] for ref in (left_ref, right_ref))
            for rows in places
        ]
        for rows, values in zip(places, gradients(work)):
            for c, value in enumerate(values):
                grad_ref[rows, c * BLOCK : (c + 1) * BLOCK] = value
        return carry

    lax.fori_loop(0, batches // group, step, 0)


def scatter(index, grads, blocks):
    index = jnp.concatenate([index] * 3, axis=0)
    lane = lax.broadcasted_iota(jnp.int32, index.shape, 1).astype(f32)
    onehot_t = (index == lane).astype(f32).T[:blocks].astype(bf16)
    stack = jnp.concatenate(pieces(grads, 3), axis=0).astype(bf16)
    return jnp.dot(onehot_t, stack, preferred_element_type=f32)


def pack_kernel(pg_ref, pb_ref, pc_ref, garm_ref, cot_ref, body_ref, stiff_ref, out_ref):
    cap, owners = pg_ref.shape
    tiles = stiff_ref.shape[0] // cap

    def one(d, carry):
        for s in range(cap):
            row = pl.ds(pg_ref[s, d], 1)
            for c in range(3):
                out_ref[d, c, s : s + 1, :] = garm_ref[c, row, :]
            out_ref[d, 3, s : s + 1, :] = jnp.where(s < pc_ref[0, d], cot_ref[row, :], 0.0)
            out_ref[d, 4 + 4 * tiles, s : s + 1, :] = jnp.full(
                (1, BLOCK), pb_ref[s, d].astype(f32), f32
            )
        for q in range(tiles):
            rows = slice(q * cap, (q + 1) * cap)
            for c in range(3):
                out_ref[d, 4 + c * tiles + q] = body_ref[c, rows, :]
            out_ref[d, 4 + 3 * tiles + q] = stiff_ref[rows, :]
        return carry

    if owners <= 8:
        for d in range(owners):
            one(d, 0)
    else:
        lax.fori_loop(0, owners, one, 0)


def over(count, fn):
    if count <= 8:
        for d in range(count):
            fn(d)
    else:
        lax.fori_loop(0, count, lambda d, carry: (fn(d), carry)[1], 0)


def body_kernel(own_ref, in_ref, out_ref, stiff_ref, left, right, table, index, grad):
    owners, tiles, cap, _ = in_ref.shape
    blocks = tiles - 5

    def take(d):
        rows = pl.ds(d * cap, cap)
        for c in range(4):
            left[c, rows, :] = in_ref[d, c]
        index[rows, :] = in_ref[d, tiles - 1]

    over(owners, take)
    for c in range(4):
        for q in range(blocks // 4):
            table[4 * q : 4 * q + 4, c * BLOCK : (c + 1) * BLOCK] = own_ref[
                0, 4 + c * (blocks // 4) + q
            ]
    lane = lax.broadcasted_iota(jnp.int32, index.shape, 1).astype(f32)
    onehot = (index[...] == lane).astype(f32)[:, :blocks].astype(bf16)
    chosen = [
        jnp.dot(onehot, part.astype(bf16), preferred_element_type=f32)
        for part in pieces(table[...], 3)
    ]
    chosen = chosen[0] + chosen[1] + chosen[2]
    for c in range(4):
        right[c] = chosen[:, c * BLOCK : (c + 1) * BLOCK]
    run_batches(left, right, grad)
    total = scatter(index[...], grad[...], blocks)
    for c in range(3):
        out_ref[c] = total[:, c * BLOCK : (c + 1) * BLOCK]
    stiff_ref[...] = total[:, 3 * BLOCK :]


def garm_kernel(pg_ref, pb_ref, own_ref, in_ref, out_ref, left, right, index, grad):
    owners, tiles, cap, _ = in_ref.shape
    blocks = tiles - 5
    garm_blocks = out_ref.shape[1]

    def take(d):
        rows = pl.ds(d * cap, cap)
        for c in range(4):
            right[c, rows, :] = own_ref[d, c]
        for s in range(cap):
            b = pb_ref[s, d]
            for c in range(4):
                left[c, pl.ds(d * cap + s, 1), :] = in_ref[
                    d, 4 + c * (blocks // 4) + b // 4, pl.ds(b % 4, 1), :
                ]
            index[pl.ds(d * cap + s, 1), :] = jnp.full((1, BLOCK), pg_ref[s, d].astype(f32), f32)

    over(owners, take)
    run_batches(left, right, grad)
    total = scatter(index[...], grad[...], garm_blocks)
    for c in range(3):
        out_ref[c] = total[:, c * BLOCK : (c + 1) * BLOCK]


def call(kernel, out_shape, scratch, scalars, arrays, cost=None):
    specs = [pl.BlockSpec(memory_space=pltpu.SMEM)] * len(scalars)
    specs += [pl.BlockSpec(memory_space=pltpu.VMEM)] * len(arrays)
    return pl.pallas_call(
        kernel,
        out_shape=out_shape,
        in_specs=specs,
        out_specs=jax.tree.map(lambda _: pl.BlockSpec(memory_space=pltpu.VMEM), out_shape),
        scratch_shapes=scratch,
        cost_estimate=cost and pl.CostEstimate(flops=cost, bytes_accessed=1000, transcendentals=0),
        compiler_params=pltpu.CompilerParams(vmem_limit_bytes=VMEM_LIMIT),
    )(*scalars, *arrays)


def read_table(ref, start, step):
    columns = [
        jnp.concatenate([ref[start + c * step + q] for q in range(step)], axis=0) for c in range(4)
    ]
    return jnp.concatenate(columns, axis=1)


def choose(index, table):
    blocks = table.shape[0]
    lane = lax.broadcasted_iota(jnp.int32, index.shape, 1)
    onehot = (index == (lane % blocks).astype(f32)) & (lane < 3 * blocks)
    onehot = onehot.astype(f32)[:, : 3 * blocks].astype(bf16)
    stack = jnp.concatenate(pieces(table, 3), axis=0).astype(bf16)
    rows = jnp.dot(onehot, stack, preferred_element_type=f32)
    return [rows[:, c * BLOCK : (c + 1) * BLOCK] for c in range(4)]


def halves(top, bottom):
    row = lax.broadcasted_iota(jnp.int32, (SUB, BLOCK), 0)
    return jnp.where(row < SUB // 2, top, bottom)


def flip(value):
    return pltpu.roll(value, SUB // 2, 0)


def body_work(tiles, table):
    return list(tiles[:4]), choose(tiles[4], table)


def garm_work(tiles, top, bottom):
    row = lax.broadcasted_iota(jnp.int32, (SUB, BLOCK), 0)
    index = tiles[4] + jnp.where(row < SUB // 2, 0, top.shape[0]).astype(f32)
    return choose(index, jnp.concatenate([top, bottom], axis=0)), list(tiles[:4])


def slot_tiles(ref):
    return [ref[c] for c in range(5)]


def message_table(ref, step):
    return read_table(ref, 5, step)


def pack(tiles):
    a, b, c, d, e = tiles
    return [halves(a, flip(b)), halves(c, flip(d)), e]


def unpack_top(tiles):
    a, b, c = tiles
    return [a, flip(a), b, flip(b), c]


def unpack_bottom(tiles):
    a, b, c = tiles
    return [flip(a), a, flip(b), b, flip(c)]


def half_message(ref, other):
    slots = slot_tiles(ref)
    if other:
        slots = [flip(tile) for tile in slots]
    return [ref[5 + q] for q in range(ref.shape[0] - 5)] + pack(slots)


def forward_kernel(one_ref, two_ref, out_ref):
    body = one_ref.shape[0] - 5
    for n, ref in enumerate((one_ref, two_ref)):
        for q in range(body):
            out_ref[n * body + q] = ref[5 + q]
    for k, tile in enumerate(bottom_tiles(one_ref, two_ref)):
        out_ref[2 * body + k] = tile


def half_kernel(ref, after_ref, out_ref):
    del after_ref
    for k, tile in enumerate(half_message(ref, True)):
        out_ref[k] = tile


def top_tiles(one_ref, two_ref):
    return [halves(a, flip(b)) for a, b in zip(slot_tiles(one_ref), slot_tiles(two_ref))]


def bottom_tiles(one_ref, two_ref):
    return [halves(flip(a), b) for a, b in zip(slot_tiles(one_ref), slot_tiles(two_ref))]


def store(work, index, bgrad_ref, bindex_ref, ggrad_ref):
    out = gradients(work)
    for n, value in enumerate(index):
        rows = slice(n * SUB, (n + 1) * SUB)
        bgrad_ref[rows, :] = jnp.concatenate(out[n], axis=1)
        ggrad_ref[rows, :] = jnp.concatenate(out[len(index) + n][:3], axis=1)
        bindex_ref[rows, :] = value


def same_kernel(own_ref, sent0, sent1, sent2, got0, got1, got2, after_ref, *out_refs):
    del after_ref
    body = own_ref.shape[0] - 5
    step = body // 4
    own = message_table(own_ref, step)
    here = top_tiles(own_ref, got0)
    last = unpack_bottom([got2[body + k] for k in range(3)])
    there = [halves(x, y) for x, y in zip(slot_tiles(got1), last)]
    work = [
        body_work(here, own),
        body_work(there, own),
        garm_work(top_tiles(own_ref, sent0), own, message_table(got0, step)),
        garm_work(top_tiles(sent1, sent2), message_table(got1, step), read_table(got2, 0, step)),
    ]
    store(work, [here[4], there[4]], *out_refs)


def near_kernel(own_ref, sent0, near_ref, after_ref, *out_refs):
    del after_ref
    body = own_ref.shape[0] - 5
    step = body // 4
    near = [near_ref[2 * body + k] for k in range(5)]
    tables = [read_table(near_ref, n * body, step) for n in range(2)]
    work = [
        body_work(near, message_table(own_ref, step)),
        garm_work(bottom_tiles(own_ref, sent0), *tables),
    ]
    store(work, [near[4]], *out_refs)


def late_body_kernel(own_ref, one_ref, two_ref, bg1, bg2, bi1, bi2, out_ref, stiff_ref):
    body = own_ref.shape[0] - 5
    top = unpack_top([one_ref[body + k] for k in range(3)])
    bottom = unpack_bottom([two_ref[body + k] for k in range(3)])
    tiles = [halves(x, y) for x, y in zip(top, bottom)]
    out = gradients([body_work(tiles, message_table(own_ref, body // 4))])
    grads = jnp.concatenate([bg1[...], bg2[...], jnp.concatenate(out[0], axis=1)], axis=0)
    index = jnp.concatenate([bi1[...], bi2[...], tiles[4]], axis=0)
    total = scatter(index, grads, out_ref.shape[1])
    for c in range(3):
        out_ref[c] = total[:, c * BLOCK : (c + 1) * BLOCK]
    stiff_ref[...] = total[:, 3 * BLOCK :]


def late_garm_kernel(sent1, sent2, one_ref, two_ref, gg1, gg2, index_ref, out_ref):
    step = (sent1.shape[0] - 5) // 4
    tables = [read_table(ref, 0, step) for ref in (one_ref, two_ref)]
    out = gradients([garm_work(bottom_tiles(sent1, sent2), *tables)])
    grads = jnp.concatenate([gg1[...], gg2[...], jnp.concatenate(out[0][:3], axis=1)], axis=0)
    index = jnp.concatenate([index_ref[k] for k in range(index_ref.shape[0])], axis=0)
    total = scatter(index, grads, out_ref.shape[1])
    for c in range(3):
        out_ref[c] = total[:, c * BLOCK : (c + 1) * BLOCK]


def final_kernel(garm_ref, body_ref, mine_ref, other_ref, garm_out, body_out, stiff_out):
    stiff_out[...] = mine_ref[...] + other_ref[...]
    body_out[...] = body_ref[...]
    garm_out[...] = garm_ref[...]


def stage_kernel(*refs):
    hbm, (index_ref, same_ref, other_ref, *out_refs) = refs[:7], refs[7:14]
    vmem, sems = refs[14:21], refs[21]
    copies = [
        pltpu.make_async_copy(src, dst, sems.at[k]) for k, (src, dst) in enumerate(zip(hbm, vmem))
    ]
    for copy in copies:
        copy.start()
    for copy in copies:
        copy.wait()
    pg_ref, pb_ref, pc_ref, garm_ref, cot_ref, body_ref, stiff_ref = vmem
    cap = pg_ref.shape[0]
    tiles = stiff_ref.shape[0]
    width = lax.axis_size("body")
    here, column = lax.axis_index("garm"), lax.axis_index("body")
    flips = (0, 3 - here // 2, 2 + here // 2, 1)
    for n, out_ref in enumerate(out_refs):
        place_z = here ^ flips[n]
        for q in range(3 * tiles):
            out_ref[5 + q] = body_ref[q]
        for q in range(tiles):
            out_ref[5 + 3 * tiles + q] = stiff_ref[q]
        for x in range(2):
            owner = place_z * width + (column ^ x)
            live = pc_ref[0, owner]
            for s in range(cap):
                g = pg_ref[s, owner]
                row, place = pl.ds(g, 1), pl.ds(x * cap + s, 1)
                for c in range(3):
                    out_ref[c, place, :] = garm_ref[c, row, :]
                out_ref[3, place, :] = jnp.where(s < live, cot_ref[row, :], 0.0)
                out_ref[4, place, :] = jnp.full((1, BLOCK), pb_ref[s, owner].astype(f32), f32)
                spot, line = 2 * x + n // 2, n % 2 * cap + s
                index_ref[spot, line : line + 1, :] = jnp.full((1, BLOCK), g.astype(f32), f32)
    for ref, other in ((same_ref, False), (other_ref, True)):
        for k, tile in enumerate(half_message(out_refs[3], other)):
            ref[k] = tile


def staged(garment, cotangent, body_points, stiffness, pg, pb, pc):
    verts = garment.shape[2]
    points = body_points.shape[2]
    blocks = points // BLOCK
    tiles = blocks // SUB
    garm_n = lax.axis_size("garm")
    message = jax.ShapeDtypeStruct((5 + 4 * tiles, SUB, BLOCK), f32)
    arrays = (
        pg,
        pb,
        pc,
        garment.reshape(3, verts // BLOCK, BLOCK),
        cotangent.reshape(verts // BLOCK, BLOCK),
        body_points.reshape(3 * tiles, SUB, BLOCK),
        stiffness.reshape(tiles, SUB, BLOCK),
    )
    half = jax.ShapeDtypeStruct((3 + 4 * tiles, SUB, BLOCK), f32)
    index, last_same, last_other, own, *sent = pl.pallas_call(
        stage_kernel,
        out_shape=[jax.ShapeDtypeStruct((garm_n, SUB, BLOCK), f32), half, half] + [message] * garm_n,
        in_specs=[pl.BlockSpec(memory_space=pltpu.HBM)] * len(arrays),
        out_specs=[pl.BlockSpec(memory_space=pltpu.VMEM)] * (garm_n + 3),
        scratch_shapes=[
            (pltpu.SMEM if k < 3 else pltpu.VMEM)(a.shape, a.dtype) for k, a in enumerate(arrays)
        ]
        + [pltpu.SemaphoreType.DMA((len(arrays),))],
        compiler_params=pltpu.CompilerParams(vmem_limit_bytes=VMEM_LIMIT),
    )(*[pltpu.with_memory_space_constraint(a, pltpu.HBM) for a in arrays])

    def along_garm(value, pairs):
        return lax.ppermute(value, "garm", pairs)

    def along_body(value):
        return lax.ppermute(value, "body", [(0, 1), (1, 0)])

    cycle = [(0, 2), (2, 1), (1, 3), (3, 0)]
    got = [
        along_garm(sent[1], cycle),
        along_garm(sent[0], [(b, a) for a, b in cycle]),
        along_garm(last_same, [(z, z ^ 1) for z in range(garm_n)]),
    ]
    direct = lax.ppermute(last_other, ("garm", "body"), [(n, n ^ 3) for n in range(2 * garm_n)])
    near_shape = jax.ShapeDtypeStruct((5 + 8 * tiles, SUB, BLOCK), f32)
    near = call(forward_kernel, near_shape, [], (), (own, got[0]), BUNDLE_COST)
    second = call(half_kernel, half, [], (), (got[1], near), BUNDLE_COST)
    near_other, second_other = along_body(near), along_body(second)

    def batch_shapes(count):
        return tuple(
            jax.ShapeDtypeStruct((count * SUB, width * BLOCK), f32) for width in (4, 1, 3)
        )

    bg1, bi1, gg1 = call(
        same_kernel, batch_shapes(2), [], (), (own, *sent, *got, second), SAME_COST
    )
    bg2, bi2, gg2 = call(
        near_kernel, batch_shapes(1), [], (), (own, sent[0], near_other, bg1), NEAR_COST
    )
    body_shape = jax.ShapeDtypeStruct((3, blocks, BLOCK), f32)
    stiff_shape = jax.ShapeDtypeStruct((blocks, BLOCK), f32)
    garm_shape = jax.ShapeDtypeStruct((3, verts // BLOCK, BLOCK), f32)
    body_total, stiff = call(
        late_body_kernel,
        (body_shape, stiff_shape),
        [],
        (),
        (own, second_other, direct, bg1, bg2, bi1, bi2),
    )
    stiff_other = lax.ppermute(stiff, "frame", [(0, 1), (1, 0)])
    garm_total = call(
        late_garm_kernel,
        garm_shape,
        [],
        (),
        (sent[1], sent[2], second_other, direct, gg1, gg2, index),
    )
    return call(
        final_kernel,
        (garm_shape, body_shape, stiff_shape),
        [],
        (),
        (garm_total, body_total, stiff, stiff_other),
    )


def per_device(garment, cotangent, body_points, stiffness, pair_garment, pair_body, pair_count):
    owners = lax.axis_size(("garm", "body"))
    verts = garment.shape[2]
    points = body_points.shape[2]
    blocks = points // BLOCK
    cap = pair_garment.shape[3]
    slots = owners * cap
    pg = pair_garment.reshape(owners, cap).T
    pb = pair_body.reshape(owners, cap).T
    pc = pair_count.reshape(1, owners)
    if (lax.axis_size("garm"), lax.axis_size("body")) == (4, 2) and cap == SUB // 2:
        garm_grad, body_grad, stiff = staged(
            garment, cotangent, body_points, stiffness, pg, pb, pc
        )
        return (
            garm_grad.reshape(1, 3, verts),
            body_grad.reshape(1, 3, points),
            stiff.reshape(points),
        )
    message = call(
        pack_kernel,
        jax.ShapeDtypeStruct((owners, 5 + blocks, cap, BLOCK), f32),
        [],
        (pg, pb, pc),
        (
            garment.reshape(3, verts // BLOCK, BLOCK),
            cotangent.reshape(verts // BLOCK, BLOCK),
            body_points.reshape(3, blocks, BLOCK),
            stiffness.reshape(blocks, BLOCK),
        ),
    )
    arrived = lax.all_to_all(message, ("garm", "body"), split_axis=0, concat_axis=0, tiled=True)
    rows = pltpu.VMEM((4, slots, BLOCK), f32)
    grad = pltpu.VMEM((slots, 4 * BLOCK), f32)
    index = pltpu.VMEM((slots, BLOCK), f32)
    body_grad, stiff = call(
        body_kernel,
        (
            jax.ShapeDtypeStruct((3, blocks, BLOCK), f32),
            jax.ShapeDtypeStruct((blocks, BLOCK), f32),
        ),
        [rows, rows, pltpu.VMEM((blocks, 4 * BLOCK), f32), index, grad],
        (),
        (message, arrived),
    )
    other = lax.ppermute(stiff, "frame", [(0, 1), (1, 0)])
    garm_grad = call(
        garm_kernel,
        jax.ShapeDtypeStruct((3, verts // BLOCK, BLOCK), f32),
        [rows, rows, index, grad],
        (pg, pb),
        (message, arrived),
    )
    return (
        garm_grad.reshape(1, 3, verts),
        body_grad.reshape(1, 3, points),
        (stiff + other).reshape(points),
    )


def solution(mesh):
    in_specs = (
        P(("grp", "frame"), None, ("garm", "body")),
        P(("grp", "frame"), ("garm", "body")),
        P(("grp", "frame"), None, ("garm", "body")),
        P(("grp", "garm", "body")),
        P(("grp", "frame"), ("garm", "body"), None, None),
        P(("grp", "frame"), ("garm", "body"), None, None),
        P(("grp", "frame"), ("garm", "body"), None),
    )
    out_specs = (
        P(("grp", "frame"), None, ("garm", "body")),
        P(("grp", "frame"), None, ("garm", "body")),
        P(("grp", "garm", "body")),
    )
    return jax.shard_map(
        per_device, mesh=mesh, in_specs=in_specs, out_specs=out_specs, check_vma=False
    )
```

```python
import math

import jax
import jax.numpy as jnp
from jax import lax
from jax.experimental import pallas as pl
from jax.experimental.pallas import tpu as pltpu
from jax.sharding import PartitionSpec as P

BLOCK = 128
SUB = 8
VMEM_LIMIT = 32 * 1024 * 1024
SAME_COST = 40_000_000_000
NEAR_COST = 1_000_000_000
BUNDLE_COST = 1000

amplitude = 0.05
width_sq = 4.0

SCALE = math.sqrt(math.log2(math.e) / width_sq)
FACTOR = -2.0 / width_sq * amplitude

f32 = jnp.float32
bf16 = jnp.bfloat16


def pieces(value, count):
    out = []
    for _ in range(count - 1):
        top = value.astype(bf16).astype(f32)
        out.append(top)
        value = value - top
    out.append(value)
    return out


def features(left, right):
    lpos = [left[c] * SCALE for c in range(3)]
    rpos = [right[c] * SCALE for c in range(3)]
    lnorm = -(lpos[0] * lpos[0] + lpos[1] * lpos[1] + lpos[2] * lpos[2])
    rnorm = -(rpos[0] * rpos[0] + rpos[1] * rpos[1] + rpos[2] * rpos[2])
    one = jnp.ones_like(lnorm)
    lrows, rrows = [], []
    for c in range(3):
        l1, l2, l3 = pieces(lpos[c] * 2.0, 3)
        r1, r2, r3 = pieces(rpos[c], 3)
        lrows += [l1, l1, l2, l2, l1, l3]
        rrows += [r1, r2, r1, r2, r3, r1]
    lrows += pieces(lnorm, 3) + [one] * 3
    rrows += [one] * 3 + pieces(rnorm, 3)
    return (
        jnp.concatenate(lrows, axis=0).astype(bf16),
        jnp.concatenate(rrows, axis=0).astype(bf16),
    )


def pull(batches, weights_only=False):
    made = []
    for left, right in batches:
        lfeat, rfeat = features(left, right)
        weight = left[3]
        coeff = [weight] if weights_only else [weight * left[c] for c in range(3)] + [weight]
        chi, clo = pieces(jnp.concatenate(coeff, axis=0), 2)
        lhs = jnp.concatenate(
            [
                jnp.concatenate([chi, chi], axis=1),
                jnp.concatenate([clo, jnp.zeros_like(clo)], axis=1),
            ],
            axis=0,
        ).astype(bf16)
        made.append((lfeat.T, rfeat, lhs))
    row = lax.broadcasted_iota(jnp.int32, made[0][1].shape, 0) % SUB
    count = made[0][2].shape[0] // 2
    sub = lax.broadcasted_iota(jnp.int32, (count, BLOCK), 0) % SUB
    totals = [jnp.zeros((count, BLOCK), f32) for _ in batches]

    def sums_of(pair, n, exponent):
        kernel = jnp.exp2(exponent)
        khi = kernel.astype(bf16)
        klo = (kernel - khi.astype(f32)).astype(bf16)
        sums = jnp.dot(made[n][2], jnp.concatenate([khi, klo], axis=0), preferred_element_type=f32)
        sums = sums[:count] + sums[count:]
        for k in range(2):
            part = sums[:, k * BLOCK : (k + 1) * BLOCK]
            totals[n] = jnp.where(sub == pair + k, part, totals[n])

    ahead = SUB // 2 if len(batches) == 1 else 0
    waiting = []
    for pair in range(0, SUB, 2):
        masks = [(row == pair + k).astype(f32).astype(bf16) for k in range(2)]
        for n, (lfeat_t, rfeat, _) in enumerate(made):
            rhs = jnp.concatenate([rfeat * mask for mask in masks], axis=1)
            waiting.append((pair, n, jnp.dot(lfeat_t, rhs, preferred_element_type=f32)))
            if len(waiting) > ahead:
                sums_of(*waiting.pop(0))
    for work in waiting:
        sums_of(*work)
    return [[total[c * SUB : (c + 1) * SUB] for c in range(count // SUB)] for total in totals]


def gradients(batches):
    out = []
    for (_, right), total in zip(batches, pull(batches)):
        rows = [FACTOR * right[3] * (right[c] * total[3] - total[c]) for c in range(3)]
        out.append(rows + [amplitude * total[3]])
    return out


def run_batches(left_ref, right_ref, grad_ref):
    batches = left_ref.shape[1] // SUB
    group = math.gcd(batches, 4)

    def step(k, carry):
        places = [pl.ds(pl.multiple_of((k * group + n) * SUB, SUB), SUB) for n in range(group)]
        work = [
            tuple([ref[c, rows, :] for c in range(4)] for ref in (left_ref, right_ref))
            for rows in places
        ]
        for rows, values in zip(places, gradients(work)):
            for c, value in enumerate(values):
                grad_ref[rows, c * BLOCK : (c + 1) * BLOCK] = value
        return carry

    lax.fori_loop(0, batches // group, step, 0)


def scatter(index, grads, blocks):
    index = jnp.concatenate([index] * 3, axis=0)
    lane = lax.broadcasted_iota(jnp.int32, index.shape, 1).astype(f32)
    onehot_t = (index == lane).astype(f32).T[:blocks].astype(bf16)
    stack = jnp.concatenate(pieces(grads, 3), axis=0).astype(bf16)
    return jnp.dot(onehot_t, stack, preferred_element_type=f32)


def pack_kernel(pg_ref, pb_ref, pc_ref, garm_ref, cot_ref, body_ref, stiff_ref, out_ref):
    cap, owners = pg_ref.shape
    tiles = stiff_ref.shape[0] // cap

    def one(d, carry):
        for s in range(cap):
            row = pl.ds(pg_ref[s, d], 1)
            for c in range(3):
                out_ref[d, c, s : s + 1, :] = garm_ref[c, row, :]
            out_ref[d, 3, s : s + 1, :] = jnp.where(s < pc_ref[0, d], cot_ref[row, :], 0.0)
            out_ref[d, 4 + 4 * tiles, s : s + 1, :] = jnp.full(
                (1, BLOCK), pb_ref[s, d].astype(f32), f32
            )
        for q in range(tiles):
            rows = slice(q * cap, (q + 1) * cap)
            for c in range(3):
                out_ref[d, 4 + c * tiles + q] = body_ref[c, rows, :]
            out_ref[d, 4 + 3 * tiles + q] = stiff_ref[rows, :]
        return carry

    if owners <= 8:
        for d in range(owners):
            one(d, 0)
    else:
        lax.fori_loop(0, owners, one, 0)


def over(count, fn):
    if count <= 8:
        for d in range(count):
            fn(d)
    else:
        lax.fori_loop(0, count, lambda d, carry: (fn(d), carry)[1], 0)


def body_kernel(own_ref, in_ref, out_ref, stiff_ref, left, right, table, index, grad):
    owners, tiles, cap, _ = in_ref.shape
    blocks = tiles - 5

    def take(d):
        rows = pl.ds(d * cap, cap)
        for c in range(4):
            left[c, rows, :] = in_ref[d, c]
        index[rows, :] = in_ref[d, tiles - 1]

    over(owners, take)
    for c in range(4):
        for q in range(blocks // 4):
            table[4 * q : 4 * q + 4, c * BLOCK : (c + 1) * BLOCK] = own_ref[
                0, 4 + c * (blocks // 4) + q
            ]
    lane = lax.broadcasted_iota(jnp.int32, index.shape, 1).astype(f32)
    onehot = (index[...] == lane).astype(f32)[:, :blocks].astype(bf16)
    chosen = [
        jnp.dot(onehot, part.astype(bf16), preferred_element_type=f32)
        for part in pieces(table[...], 3)
    ]
    chosen = chosen[0] + chosen[1] + chosen[2]
    for c in range(4):
        right[c] = chosen[:, c * BLOCK : (c + 1) * BLOCK]
    run_batches(left, right, grad)
    total = scatter(index[...], grad[...], blocks)
    for c in range(3):
        out_ref[c] = total[:, c * BLOCK : (c + 1) * BLOCK]
    stiff_ref[...] = total[:, 3 * BLOCK :]


def garm_kernel(pg_ref, pb_ref, own_ref, in_ref, out_ref, left, right, index, grad):
    owners, tiles, cap, _ = in_ref.shape
    blocks = tiles - 5
    garm_blocks = out_ref.shape[1]

    def take(d):
        rows = pl.ds(d * cap, cap)
        for c in range(4):
            right[c, rows, :] = own_ref[d, c]
        for s in range(cap):
            b = pb_ref[s, d]
            for c in range(4):
                left[c, pl.ds(d * cap + s, 1), :] = in_ref[
                    d, 4 + c * (blocks // 4) + b // 4, pl.ds(b % 4, 1), :
                ]
            index[pl.ds(d * cap + s, 1), :] = jnp.full((1, BLOCK), pg_ref[s, d].astype(f32), f32)

    over(owners, take)
    run_batches(left, right, grad)
    total = scatter(index[...], grad[...], garm_blocks)
    for c in range(3):
        out_ref[c] = total[:, c * BLOCK : (c + 1) * BLOCK]


def call(kernel, out_shape, scratch, scalars, arrays, cost=None):
    specs = [pl.BlockSpec(memory_space=pltpu.SMEM)] * len(scalars)
    specs += [pl.BlockSpec(memory_space=pltpu.VMEM)] * len(arrays)
    return pl.pallas_call(
        kernel,
        out_shape=out_shape,
        in_specs=specs,
        out_specs=jax.tree.map(lambda _: pl.BlockSpec(memory_space=pltpu.VMEM), out_shape),
        scratch_shapes=scratch,
        cost_estimate=cost and pl.CostEstimate(flops=cost, bytes_accessed=1000, transcendentals=0),
        compiler_params=pltpu.CompilerParams(vmem_limit_bytes=VMEM_LIMIT),
    )(*scalars, *arrays)


def read_table(ref, start, step):
    columns = [
        jnp.concatenate([ref[start + c * step + q] for q in range(step)], axis=0) for c in range(4)
    ]
    return jnp.concatenate(columns, axis=1)


def choose(index, table):
    blocks = table.shape[0]
    lane = lax.broadcasted_iota(jnp.int32, index.shape, 1)
    onehot = (index == (lane % blocks).astype(f32)) & (lane < 3 * blocks)
    onehot = onehot.astype(f32)[:, : 3 * blocks].astype(bf16)
    stack = jnp.concatenate(pieces(table, 3), axis=0).astype(bf16)
    rows = jnp.dot(onehot, stack, preferred_element_type=f32)
    return [rows[:, c * BLOCK : (c + 1) * BLOCK] for c in range(4)]


def halves(top, bottom):
    row = lax.broadcasted_iota(jnp.int32, (SUB, BLOCK), 0)
    return jnp.where(row < SUB // 2, top, bottom)


def flip(value):
    return pltpu.roll(value, SUB // 2, 0)


def body_work(tiles, table):
    return list(tiles[:4]), choose(tiles[4], table)


def garm_work(tiles, top, bottom):
    row = lax.broadcasted_iota(jnp.int32, (SUB, BLOCK), 0)
    index = tiles[4] + jnp.where(row < SUB // 2, 0, top.shape[0]).astype(f32)
    return choose(index, jnp.concatenate([top, bottom], axis=0)), list(tiles[:4])


def slot_tiles(ref):
    return [ref[c] for c in range(5)]


def message_table(ref, step):
    return read_table(ref, 5, step)


def pack(tiles):
    a, b, c, d, e = tiles
    return [halves(a, flip(b)), halves(c, flip(d)), e]


def unpack_top(tiles):
    a, b, c = tiles
    return [a, flip(a), b, flip(b), c]


def unpack_bottom(tiles):
    a, b, c = tiles
    return [flip(a), a, flip(b), b, flip(c)]


def half_message(ref, other):
    slots = slot_tiles(ref)
    if other:
        slots = [flip(tile) for tile in slots]
    return [ref[5 + q] for q in range(ref.shape[0] - 5)] + pack(slots)


def forward_kernel(one_ref, two_ref, out_ref):
    body = one_ref.shape[0] - 5
    for n, ref in enumerate((one_ref, two_ref)):
        for q in range(body):
            out_ref[n * body + q] = ref[5 + q]
    for k, tile in enumerate(bottom_tiles(one_ref, two_ref)):
        out_ref[2 * body + k] = tile


def half_kernel(ref, after_ref, out_ref):
    del after_ref
    for k, tile in enumerate(half_message(ref, True)):
        out_ref[k] = tile


def top_tiles(one_ref, two_ref):
    return [halves(a, flip(b)) for a, b in zip(slot_tiles(one_ref), slot_tiles(two_ref))]


def bottom_tiles(one_ref, two_ref):
    return [halves(flip(a), b) for a, b in zip(slot_tiles(one_ref), slot_tiles(two_ref))]


def store(work, index, bgrad_ref, bindex_ref, ggrad_ref):
    out = gradients(work)
    for n, value in enumerate(index):
        rows = slice(n * SUB, (n + 1) * SUB)
        bgrad_ref[rows, :] = jnp.concatenate(out[n], axis=1)
        ggrad_ref[rows, :] = jnp.concatenate(out[len(index) + n][:3], axis=1)
        bindex_ref[rows, :] = value


def same_kernel(own_ref, sent0, sent1, sent2, got0, got1, got2, after_ref, *out_refs):
    del after_ref
    body = own_ref.shape[0] - 5
    step = body // 4
    own = message_table(own_ref, step)
    here = top_tiles(own_ref, got0)
    last = unpack_bottom([got2[body + k] for k in range(3)])
    there = [halves(x, y) for x, y in zip(slot_tiles(got1), last)]
    work = [
        body_work(here, own),
        body_work(there, own),
        garm_work(top_tiles(own_ref, sent0), own, message_table(got0, step)),
        garm_work(top_tiles(sent1, sent2), message_table(got1, step), read_table(got2, 0, step)),
    ]
    store(work, [here[4], there[4]], *out_refs)


def near_tiles(own_ref, near_ref):
    body = own_ref.shape[0] - 5
    return [near_ref[2 * body + k] for k in range(5)]


def late_tiles(own_ref, one_ref, two_ref):
    body = own_ref.shape[0] - 5
    top = unpack_top([one_ref[body + k] for k in range(3)])
    bottom = unpack_bottom([two_ref[body + k] for k in range(3)])
    return [halves(x, y) for x, y in zip(top, bottom)]


def near_kernel(own_ref, near_ref, after_ref, bgrad_ref, bindex_ref):
    del after_ref
    tiles = near_tiles(own_ref, near_ref)
    own = message_table(own_ref, (own_ref.shape[0] - 5) // 4)
    bgrad_ref[...] = jnp.concatenate(gradients([body_work(tiles, own)])[0], axis=1)
    bindex_ref[...] = tiles[4]


def stiff_kernel(own_ref, one_ref, two_ref, bg1, bg2, bi1, bi2, out_ref):
    tiles = late_tiles(own_ref, one_ref, two_ref)
    own = message_table(own_ref, (own_ref.shape[0] - 5) // 4)
    [[last]] = pull([body_work(tiles, own)], weights_only=True)
    grads = [bg1[:, 3 * BLOCK :], bg2[:, 3 * BLOCK :], amplitude * last]
    index = jnp.concatenate([bi1[...], bi2[...], tiles[4]], axis=0)
    out_ref[...] = scatter(index, jnp.concatenate(grads, axis=0), out_ref.shape[0])


def late_kernel(
    own_ref,
    sent0,
    sent1,
    sent2,
    near_ref,
    one_ref,
    two_ref,
    bg1,
    bg2,
    bi1,
    bi2,
    gg1,
    index_ref,
    body_out,
    garm_out,
):
    body = own_ref.shape[0] - 5
    step = body // 4
    tiles = late_tiles(own_ref, one_ref, two_ref)
    near = [read_table(near_ref, n * body, step) for n in range(2)]
    far = [read_table(ref, 0, step) for ref in (one_ref, two_ref)]
    out = gradients(
        [
            body_work(tiles, message_table(own_ref, step)),
            garm_work(bottom_tiles(own_ref, sent0), *near),
            garm_work(bottom_tiles(sent1, sent2), *far),
        ]
    )
    rows = [jnp.concatenate(values[:3], axis=1) for values in out]
    width = 3 * BLOCK
    index = jnp.concatenate([bi1[...], bi2[...], tiles[4]], axis=0)
    grads = jnp.concatenate([bg1[:, :width], bg2[:, :width], rows[0]], axis=0)
    total = scatter(index, grads, body_out.shape[1])
    for c in range(3):
        body_out[c] = total[:, c * BLOCK : (c + 1) * BLOCK]
    index = jnp.concatenate([index_ref[k] for k in range(index_ref.shape[0])], axis=0)
    grads = jnp.concatenate([gg1[...], rows[1], rows[2]], axis=0)
    total = scatter(index, grads, garm_out.shape[1])
    for c in range(3):
        garm_out[c] = total[:, c * BLOCK : (c + 1) * BLOCK]


def final_kernel(garm_ref, body_ref, mine_ref, other_ref, garm_out, body_out, stiff_out):
    stiff_out[...] = mine_ref[...] + other_ref[...]
    body_out[...] = body_ref[...]
    garm_out[...] = garm_ref[...]


def stage_kernel(*refs):
    hbm, (index_ref, same_ref, other_ref, *out_refs) = refs[:7], refs[7:14]
    vmem, sems = refs[14:21], refs[21]
    copies = [
        pltpu.make_async_copy(src, dst, sems.at[k]) for k, (src, dst) in enumerate(zip(hbm, vmem))
    ]
    for copy in copies:
        copy.start()
    for copy in copies:
        copy.wait()
    pg_ref, pb_ref, pc_ref, garm_ref, cot_ref, body_ref, stiff_ref = vmem
    cap = pg_ref.shape[0]
    tiles = stiff_ref.shape[0]
    width = lax.axis_size("body")
    here, column = lax.axis_index("garm"), lax.axis_index("body")
    flips = (0, 3 - here // 2, 2 + here // 2, 1)
    for n, out_ref in enumerate(out_refs):
        place_z = here ^ flips[n]
        for q in range(3 * tiles):
            out_ref[5 + q] = body_ref[q]
        for q in range(tiles):
            out_ref[5 + 3 * tiles + q] = stiff_ref[q]
        for x in range(2):
            owner = place_z * width + (column ^ x)
            live = pc_ref[0, owner]
            for s in range(cap):
                g = pg_ref[s, owner]
                row, place = pl.ds(g, 1), pl.ds(x * cap + s, 1)
                for c in range(3):
                    out_ref[c, place, :] = garm_ref[c, row, :]
                out_ref[3, place, :] = jnp.where(s < live, cot_ref[row, :], 0.0)
                out_ref[4, place, :] = jnp.full((1, BLOCK), pb_ref[s, owner].astype(f32), f32)
                spot, line = 2 * x + n // 2, n % 2 * cap + s
                index_ref[spot, line : line + 1, :] = jnp.full((1, BLOCK), g.astype(f32), f32)
    for ref, other in ((same_ref, False), (other_ref, True)):
        for k, tile in enumerate(half_message(out_refs[3], other)):
            ref[k] = tile


def staged(garment, cotangent, body_points, stiffness, pg, pb, pc):
    verts = garment.shape[2]
    points = body_points.shape[2]
    blocks = points // BLOCK
    tiles = blocks // SUB
    garm_n = lax.axis_size("garm")
    message = jax.ShapeDtypeStruct((5 + 4 * tiles, SUB, BLOCK), f32)
    arrays = (
        pg,
        pb,
        pc,
        garment.reshape(3, verts // BLOCK, BLOCK),
        cotangent.reshape(verts // BLOCK, BLOCK),
        body_points.reshape(3 * tiles, SUB, BLOCK),
        stiffness.reshape(tiles, SUB, BLOCK),
    )
    half = jax.ShapeDtypeStruct((3 + 4 * tiles, SUB, BLOCK), f32)
    index, last_same, last_other, own, *sent = pl.pallas_call(
        stage_kernel,
        out_shape=[jax.ShapeDtypeStruct((garm_n, SUB, BLOCK), f32), half, half] + [message] * garm_n,
        in_specs=[pl.BlockSpec(memory_space=pltpu.HBM)] * len(arrays),
        out_specs=[pl.BlockSpec(memory_space=pltpu.VMEM)] * (garm_n + 3),
        scratch_shapes=[
            (pltpu.SMEM if k < 3 else pltpu.VMEM)(a.shape, a.dtype) for k, a in enumerate(arrays)
        ]
        + [pltpu.SemaphoreType.DMA((len(arrays),))],
        compiler_params=pltpu.CompilerParams(vmem_limit_bytes=VMEM_LIMIT),
    )(*[pltpu.with_memory_space_constraint(a, pltpu.HBM) for a in arrays])

    def along_garm(value, pairs):
        return lax.ppermute(value, "garm", pairs)

    def along_body(value):
        return lax.ppermute(value, "body", [(0, 1), (1, 0)])

    cycle = [(0, 2), (2, 1), (1, 3), (3, 0)]
    got = [
        along_garm(sent[1], cycle),
        along_garm(sent[0], [(b, a) for a, b in cycle]),
        along_garm(last_same, [(z, z ^ 1) for z in range(garm_n)]),
    ]
    direct = lax.ppermute(last_other, ("garm", "body"), [(n, n ^ 3) for n in range(2 * garm_n)])
    near_shape = jax.ShapeDtypeStruct((5 + 8 * tiles, SUB, BLOCK), f32)
    near = call(forward_kernel, near_shape, [], (), (own, got[0]), BUNDLE_COST)
    second = call(half_kernel, half, [], (), (got[1], near), BUNDLE_COST)
    near_other, second_other = along_body(near), along_body(second)

    def batch_shapes(count):
        return tuple(
            jax.ShapeDtypeStruct((count * SUB, width * BLOCK), f32) for width in (4, 1, 3)
        )

    bg1, bi1, gg1 = call(
        same_kernel, batch_shapes(2), [], (), (own, *sent, *got, second), SAME_COST
    )
    bg2, bi2 = call(
        near_kernel, batch_shapes(1)[:2], [], (), (own, near_other, bg1), NEAR_COST
    )
    body_shape = jax.ShapeDtypeStruct((3, blocks, BLOCK), f32)
    stiff_shape = jax.ShapeDtypeStruct((blocks, BLOCK), f32)
    garm_shape = jax.ShapeDtypeStruct((3, verts // BLOCK, BLOCK), f32)
    stiff = call(
        stiff_kernel, stiff_shape, [], (), (own, second_other, direct, bg1, bg2, bi1, bi2)
    )
    stiff_other = lax.ppermute(stiff, "frame", [(0, 1), (1, 0)])
    body_total, garm_total = call(
        late_kernel,
        (body_shape, garm_shape),
        [],
        (),
        (own, *sent, near_other, second_other, direct, bg1, bg2, bi1, bi2, gg1, index),
    )
    return call(
        final_kernel,
        (garm_shape, body_shape, stiff_shape),
        [],
        (),
        (garm_total, body_total, stiff, stiff_other),
    )


def per_device(garment, cotangent, body_points, stiffness, pair_garment, pair_body, pair_count):
    owners = lax.axis_size(("garm", "body"))
    verts = garment.shape[2]
    points = body_points.shape[2]
    blocks = points // BLOCK
    cap = pair_garment.shape[3]
    slots = owners * cap
    pg = pair_garment.reshape(owners, cap).T
    pb = pair_body.reshape(owners, cap).T
    pc = pair_count.reshape(1, owners)
    if (lax.axis_size("garm"), lax.axis_size("body")) == (4, 2) and cap == SUB // 2:
        garm_grad, body_grad, stiff = staged(
            garment, cotangent, body_points, stiffness, pg, pb, pc
        )
        return (
            garm_grad.reshape(1, 3, verts),
            body_grad.reshape(1, 3, points),
            stiff.reshape(points),
        )
    message = call(
        pack_kernel,
        jax.ShapeDtypeStruct((owners, 5 + blocks, cap, BLOCK), f32),
        [],
        (pg, pb, pc),
        (
            garment.reshape(3, verts // BLOCK, BLOCK),
            cotangent.reshape(verts // BLOCK, BLOCK),
            body_points.reshape(3, blocks, BLOCK),
            stiffness.reshape(blocks, BLOCK),
        ),
    )
    arrived = lax.all_to_all(message, ("garm", "body"), split_axis=0, concat_axis=0, tiled=True)
    rows = pltpu.VMEM((4, slots, BLOCK), f32)
    grad = pltpu.VMEM((slots, 4 * BLOCK), f32)
    index = pltpu.VMEM((slots, BLOCK), f32)
    body_grad, stiff = call(
        body_kernel,
        (
            jax.ShapeDtypeStruct((3, blocks, BLOCK), f32),
            jax.ShapeDtypeStruct((blocks, BLOCK), f32),
        ),
        [rows, rows, pltpu.VMEM((blocks, 4 * BLOCK), f32), index, grad],
        (),
        (message, arrived),
    )
    other = lax.ppermute(stiff, "frame", [(0, 1), (1, 0)])
    garm_grad = call(
        garm_kernel,
        jax.ShapeDtypeStruct((3, verts // BLOCK, BLOCK), f32),
        [rows, rows, index, grad],
        (pg, pb),
        (message, arrived),
    )
    return (
        garm_grad.reshape(1, 3, verts),
        body_grad.reshape(1, 3, points),
        (stiff + other).reshape(points),
    )


def solution(mesh):
    in_specs = (
        P(("grp", "frame"), None, ("garm", "body")),
        P(("grp", "frame"), ("garm", "body")),
        P(("grp", "frame"), None, ("garm", "body")),
        P(("grp", "garm", "body")),
        P(("grp", "frame"), ("garm", "body"), None, None),
        P(("grp", "frame"), ("garm", "body"), None, None),
        P(("grp", "frame"), ("garm", "body"), None),
    )
    out_specs = (
        P(("grp", "frame"), None, ("garm", "body")),
        P(("grp", "frame"), None, ("garm", "body")),
        P(("grp", "garm", "body")),
    )
    return jax.shard_map(
        per_device, mesh=mesh, in_specs=in_specs, out_specs=out_specs, check_vma=False
    )
```

```python
import math

import jax
import jax.numpy as jnp
from jax import lax
from jax.experimental import pallas as pl
from jax.experimental.pallas import tpu as pltpu
from jax.sharding import PartitionSpec as P

BLOCK = 128
SUB = 8
VMEM_LIMIT = 32 * 1024 * 1024
SAME_COST = 40_000_000_000
NEAR_COST = 1_000_000_000
BUNDLE_COST = 1000

amplitude = 0.05
width_sq = 4.0

SCALE = math.sqrt(math.log2(math.e) / width_sq)
FACTOR = -2.0 / width_sq * amplitude

f32 = jnp.float32
bf16 = jnp.bfloat16


def pieces(value, count):
    out = []
    for _ in range(count - 1):
        top = value.astype(bf16).astype(f32)
        out.append(top)
        value = value - top
    out.append(value)
    return out


def features(left, right):
    lpos = [left[c] * SCALE for c in range(3)]
    rpos = [right[c] * SCALE for c in range(3)]
    lnorm = -(lpos[0] * lpos[0] + lpos[1] * lpos[1] + lpos[2] * lpos[2])
    rnorm = -(rpos[0] * rpos[0] + rpos[1] * rpos[1] + rpos[2] * rpos[2])
    one = jnp.ones_like(lnorm)
    lrows, rrows = [], []
    for c in range(3):
        l1, l2, l3 = pieces(lpos[c] * 2.0, 3)
        r1, r2, r3 = pieces(rpos[c], 3)
        lrows += [l1, l1, l2, l2, l1, l3]
        rrows += [r1, r2, r1, r2, r3, r1]
    lrows += pieces(lnorm, 3) + [one] * 3
    rrows += [one] * 3 + pieces(rnorm, 3)
    return (
        jnp.concatenate(lrows, axis=0).astype(bf16),
        jnp.concatenate(rrows, axis=0).astype(bf16),
    )


def pull(batches, weights_only=False):
    made = []
    for left, right in batches:
        lfeat, rfeat = features(left, right)
        weight = left[3]
        coeff = [weight] if weights_only else [weight * left[c] for c in range(3)] + [weight]
        chi, clo = pieces(jnp.concatenate(coeff, axis=0), 2)
        lhs = jnp.concatenate(
            [
                jnp.concatenate([chi, chi], axis=1),
                jnp.concatenate([clo, jnp.zeros_like(clo)], axis=1),
            ],
            axis=0,
        ).astype(bf16)
        made.append((lfeat.T, rfeat, lhs))
    row = lax.broadcasted_iota(jnp.int32, made[0][1].shape, 0) % SUB
    count = made[0][2].shape[0] // 2
    sub = lax.broadcasted_iota(jnp.int32, (count, BLOCK), 0) % SUB
    totals = [jnp.zeros((count, BLOCK), f32) for _ in batches]

    def sums_of(pair, n, exponent):
        kernel = jnp.exp2(exponent)
        khi = kernel.astype(bf16)
        klo = (kernel - khi.astype(f32)).astype(bf16)
        sums = jnp.dot(made[n][2], jnp.concatenate([khi, klo], axis=0), preferred_element_type=f32)
        sums = sums[:count] + sums[count:]
        for k in range(2):
            part = sums[:, k * BLOCK : (k + 1) * BLOCK]
            totals[n] = jnp.where(sub == pair + k, part, totals[n])

    ahead = SUB // 2 if len(batches) == 1 else 0
    waiting = []
    for pair in range(0, SUB, 2):
        masks = [(row == pair + k).astype(f32).astype(bf16) for k in range(2)]
        for n, (lfeat_t, rfeat, _) in enumerate(made):
            rhs = jnp.concatenate([rfeat * mask for mask in masks], axis=1)
            waiting.append((pair, n, jnp.dot(lfeat_t, rhs, preferred_element_type=f32)))
            if len(waiting) > ahead:
                sums_of(*waiting.pop(0))
    for work in waiting:
        sums_of(*work)
    return [[total[c * SUB : (c + 1) * SUB] for c in range(count // SUB)] for total in totals]


def gradients(batches):
    out = []
    for (_, right), total in zip(batches, pull(batches)):
        rows = [FACTOR * right[3] * (right[c] * total[3] - total[c]) for c in range(3)]
        out.append(rows + [amplitude * total[3]])
    return out


def run_batches(left_ref, right_ref, grad_ref):
    batches = left_ref.shape[1] // SUB
    group = math.gcd(batches, 4)

    def step(k, carry):
        places = [pl.ds(pl.multiple_of((k * group + n) * SUB, SUB), SUB) for n in range(group)]
        work = [
            tuple([ref[c, rows, :] for c in range(4)] for ref in (left_ref, right_ref))
            for rows in places
        ]
        for rows, values in zip(places, gradients(work)):
            for c, value in enumerate(values):
                grad_ref[rows, c * BLOCK : (c + 1) * BLOCK] = value
        return carry

    lax.fori_loop(0, batches // group, step, 0)


def scatter(index, grads, blocks):
    index = jnp.concatenate([index] * 3, axis=0)
    lane = lax.broadcasted_iota(jnp.int32, index.shape, 1).astype(f32)
    onehot_t = (index == lane).astype(f32).T[:blocks].astype(bf16)
    stack = jnp.concatenate(pieces(grads, 3), axis=0).astype(bf16)
    return jnp.dot(onehot_t, stack, preferred_element_type=f32)


def pack_kernel(pg_ref, pb_ref, pc_ref, garm_ref, cot_ref, body_ref, stiff_ref, out_ref):
    cap, owners = pg_ref.shape
    tiles = stiff_ref.shape[0] // cap

    def one(d, carry):
        for s in range(cap):
            row = pl.ds(pg_ref[s, d], 1)
            for c in range(3):
                out_ref[d, c, s : s + 1, :] = garm_ref[c, row, :]
            out_ref[d, 3, s : s + 1, :] = jnp.where(s < pc_ref[0, d], cot_ref[row, :], 0.0)
            out_ref[d, 4 + 4 * tiles, s : s + 1, :] = jnp.full(
                (1, BLOCK), pb_ref[s, d].astype(f32), f32
            )
        for q in range(tiles):
            rows = slice(q * cap, (q + 1) * cap)
            for c in range(3):
                out_ref[d, 4 + c * tiles + q] = body_ref[c, rows, :]
            out_ref[d, 4 + 3 * tiles + q] = stiff_ref[rows, :]
        return carry

    if owners <= 8:
        for d in range(owners):
            one(d, 0)
    else:
        lax.fori_loop(0, owners, one, 0)


def over(count, fn):
    if count <= 8:
        for d in range(count):
            fn(d)
    else:
        lax.fori_loop(0, count, lambda d, carry: (fn(d), carry)[1], 0)


def body_kernel(own_ref, in_ref, out_ref, stiff_ref, left, right, table, index, grad):
    owners, tiles, cap, _ = in_ref.shape
    blocks = tiles - 5

    def take(d):
        rows = pl.ds(d * cap, cap)
        for c in range(4):
            left[c, rows, :] = in_ref[d, c]
        index[rows, :] = in_ref[d, tiles - 1]

    over(owners, take)
    for c in range(4):
        for q in range(blocks // 4):
            table[4 * q : 4 * q + 4, c * BLOCK : (c + 1) * BLOCK] = own_ref[
                0, 4 + c * (blocks // 4) + q
            ]
    lane = lax.broadcasted_iota(jnp.int32, index.shape, 1).astype(f32)
    onehot = (index[...] == lane).astype(f32)[:, :blocks].astype(bf16)
    chosen = [
        jnp.dot(onehot, part.astype(bf16), preferred_element_type=f32)
        for part in pieces(table[...], 3)
    ]
    chosen = chosen[0] + chosen[1] + chosen[2]
    for c in range(4):
        right[c] = chosen[:, c * BLOCK : (c + 1) * BLOCK]
    run_batches(left, right, grad)
    total = scatter(index[...], grad[...], blocks)
    for c in range(3):
        out_ref[c] = total[:, c * BLOCK : (c + 1) * BLOCK]
    stiff_ref[...] = total[:, 3 * BLOCK :]


def garm_kernel(pg_ref, pb_ref, own_ref, in_ref, out_ref, left, right, index, grad):
    owners, tiles, cap, _ = in_ref.shape
    blocks = tiles - 5
    garm_blocks = out_ref.shape[1]

    def take(d):
        rows = pl.ds(d * cap, cap)
        for c in range(4):
            right[c, rows, :] = own_ref[d, c]
        for s in range(cap):
            b = pb_ref[s, d]
            for c in range(4):
                left[c, pl.ds(d * cap + s, 1), :] = in_ref[
                    d, 4 + c * (blocks // 4) + b // 4, pl.ds(b % 4, 1), :
                ]
            index[pl.ds(d * cap + s, 1), :] = jnp.full((1, BLOCK), pg_ref[s, d].astype(f32), f32)

    over(owners, take)
    run_batches(left, right, grad)
    total = scatter(index[...], grad[...], garm_blocks)
    for c in range(3):
        out_ref[c] = total[:, c * BLOCK : (c + 1) * BLOCK]


def call(kernel, out_shape, scratch, scalars, arrays, cost=None):
    specs = [pl.BlockSpec(memory_space=pltpu.SMEM)] * len(scalars)
    specs += [pl.BlockSpec(memory_space=pltpu.VMEM)] * len(arrays)
    return pl.pallas_call(
        kernel,
        out_shape=out_shape,
        in_specs=specs,
        out_specs=jax.tree.map(lambda _: pl.BlockSpec(memory_space=pltpu.VMEM), out_shape),
        scratch_shapes=scratch,
        cost_estimate=cost and pl.CostEstimate(flops=cost, bytes_accessed=1000, transcendentals=0),
        compiler_params=pltpu.CompilerParams(vmem_limit_bytes=VMEM_LIMIT),
    )(*scalars, *arrays)


def read_table(ref, start, step):
    columns = [
        jnp.concatenate([ref[start + c * step + q] for q in range(step)], axis=0) for c in range(4)
    ]
    return jnp.concatenate(columns, axis=1)


def choose(index, table):
    blocks = table.shape[0]
    lane = lax.broadcasted_iota(jnp.int32, index.shape, 1)
    onehot = (index == (lane % blocks).astype(f32)) & (lane < 3 * blocks)
    onehot = onehot.astype(f32)[:, : 3 * blocks].astype(bf16)
    stack = jnp.concatenate(pieces(table, 3), axis=0).astype(bf16)
    rows = jnp.dot(onehot, stack, preferred_element_type=f32)
    return [rows[:, c * BLOCK : (c + 1) * BLOCK] for c in range(4)]


def halves(top, bottom):
    row = lax.broadcasted_iota(jnp.int32, (SUB, BLOCK), 0)
    return jnp.where(row < SUB // 2, top, bottom)


def flip(value):
    return pltpu.roll(value, SUB // 2, 0)


def body_work(tiles, table):
    return list(tiles[:4]), choose(tiles[4], table)


def garm_work(tiles, top, bottom):
    row = lax.broadcasted_iota(jnp.int32, (SUB, BLOCK), 0)
    index = tiles[4] + jnp.where(row < SUB // 2, 0, top.shape[0]).astype(f32)
    return choose(index, jnp.concatenate([top, bottom], axis=0)), list(tiles[:4])


def slot_tiles(ref):
    return [ref[c] for c in range(5)]


def message_table(ref, step):
    return read_table(ref, 5, step)


def pack(tiles):
    a, b, c, d, e = tiles
    return [halves(a, flip(b)), halves(c, flip(d)), e]


def unpack_top(tiles):
    a, b, c = tiles
    return [a, flip(a), b, flip(b), c]


def unpack_bottom(tiles):
    a, b, c = tiles
    return [flip(a), a, flip(b), b, flip(c)]


def half_message(ref, other):
    slots = slot_tiles(ref)
    if other:
        slots = [flip(tile) for tile in slots]
    return [ref[5 + q] for q in range(ref.shape[0] - 5)] + pack(slots)


def forward_kernel(own_ref, ref, out_ref):
    body = ref.shape[0] - 5
    for k, tile in enumerate([ref[5 + q] for q in range(body)] + bottom_tiles(own_ref, ref)):
        out_ref[k] = tile


def second_kernel(own_ref, ref, after_ref, out_ref):
    del after_ref
    own = [own_ref[5 + q] for q in range(own_ref.shape[0] - 5)]
    for k, tile in enumerate(half_message(ref, True) + own):
        out_ref[k] = tile


def top_tiles(one_ref, two_ref):
    return [halves(a, flip(b)) for a, b in zip(slot_tiles(one_ref), slot_tiles(two_ref))]


def bottom_tiles(one_ref, two_ref):
    return [halves(flip(a), b) for a, b in zip(slot_tiles(one_ref), slot_tiles(two_ref))]


def store(work, index, bgrad_ref, bindex_ref, ggrad_ref):
    out = gradients(work)
    for n, value in enumerate(index):
        rows = slice(n * SUB, (n + 1) * SUB)
        bgrad_ref[rows, :] = jnp.concatenate(out[n], axis=1)
        ggrad_ref[rows, :] = jnp.concatenate(out[len(index) + n][:3], axis=1)
        bindex_ref[rows, :] = value


def same_kernel(own_ref, sent0, sent1, sent2, got0, got1, got2, after_ref, *out_refs):
    del after_ref
    body = own_ref.shape[0] - 5
    step = body // 4
    own = message_table(own_ref, step)
    here = top_tiles(own_ref, got0)
    last = unpack_bottom([got2[body + k] for k in range(3)])
    there = [halves(x, y) for x, y in zip(slot_tiles(got1), last)]
    work = [
        body_work(here, own),
        body_work(there, own),
        garm_work(top_tiles(own_ref, sent0), own, message_table(got0, step)),
        garm_work(top_tiles(sent1, sent2), message_table(got1, step), read_table(got2, 0, step)),
    ]
    store(work, [here[4], there[4]], *out_refs)


def near_tiles(own_ref, near_ref):
    body = own_ref.shape[0] - 5
    return [near_ref[body + k] for k in range(5)]


def late_tiles(own_ref, one_ref, two_ref):
    body = own_ref.shape[0] - 5
    top = unpack_top([one_ref[body + k] for k in range(3)])
    bottom = unpack_bottom([two_ref[body + k] for k in range(3)])
    return [halves(x, y) for x, y in zip(top, bottom)]


def near_kernel(own_ref, near_ref, after_ref, bgrad_ref, bindex_ref):
    del after_ref
    tiles = near_tiles(own_ref, near_ref)
    own = message_table(own_ref, (own_ref.shape[0] - 5) // 4)
    bgrad_ref[...] = jnp.concatenate(gradients([body_work(tiles, own)])[0], axis=1)
    bindex_ref[...] = tiles[4]


def stiff_kernel(own_ref, one_ref, two_ref, bg1, bg2, bi1, bi2, out_ref):
    tiles = late_tiles(own_ref, one_ref, two_ref)
    own = message_table(own_ref, (own_ref.shape[0] - 5) // 4)
    [[last]] = pull([body_work(tiles, own)], weights_only=True)
    grads = [bg1[:, 3 * BLOCK :], bg2[:, 3 * BLOCK :], amplitude * last]
    index = jnp.concatenate([bi1[...], bi2[...], tiles[4]], axis=0)
    out_ref[...] = scatter(index, jnp.concatenate(grads, axis=0), out_ref.shape[0])


def late_kernel(
    own_ref,
    sent0,
    sent1,
    sent2,
    near_ref,
    one_ref,
    two_ref,
    bg1,
    bg2,
    bi1,
    bi2,
    gg1,
    index_ref,
    body_out,
    garm_out,
):
    body = own_ref.shape[0] - 5
    step = body // 4
    tiles = late_tiles(own_ref, one_ref, two_ref)
    near = [read_table(one_ref, body + 3, step), read_table(near_ref, 0, step)]
    far = [read_table(ref, 0, step) for ref in (one_ref, two_ref)]
    out = gradients(
        [
            body_work(tiles, message_table(own_ref, step)),
            garm_work(bottom_tiles(own_ref, sent0), *near),
            garm_work(bottom_tiles(sent1, sent2), *far),
        ]
    )
    rows = [jnp.concatenate(values[:3], axis=1) for values in out]
    width = 3 * BLOCK
    index = jnp.concatenate([bi1[...], bi2[...], tiles[4]], axis=0)
    grads = jnp.concatenate([bg1[:, :width], bg2[:, :width], rows[0]], axis=0)
    total = scatter(index, grads, body_out.shape[1])
    for c in range(3):
        body_out[c] = total[:, c * BLOCK : (c + 1) * BLOCK]
    index = jnp.concatenate([index_ref[k] for k in range(index_ref.shape[0])], axis=0)
    grads = jnp.concatenate([gg1[...], rows[1], rows[2]], axis=0)
    total = scatter(index, grads, garm_out.shape[1])
    for c in range(3):
        garm_out[c] = total[:, c * BLOCK : (c + 1) * BLOCK]


def final_kernel(garm_ref, body_ref, mine_ref, other_ref, garm_out, body_out, stiff_out):
    stiff_out[...] = mine_ref[...] + other_ref[...]
    body_out[...] = body_ref[...]
    garm_out[...] = garm_ref[...]


def stage_kernel(*refs):
    hbm, (index_ref, same_ref, other_ref, *out_refs) = refs[:7], refs[7:14]
    vmem, sems = refs[14:21], refs[21]
    copies = [
        pltpu.make_async_copy(src, dst, sems.at[k]) for k, (src, dst) in enumerate(zip(hbm, vmem))
    ]
    for copy in copies:
        copy.start()
    for copy in copies:
        copy.wait()
    pg_ref, pb_ref, pc_ref, garm_ref, cot_ref, body_ref, stiff_ref = vmem
    cap = pg_ref.shape[0]
    tiles = stiff_ref.shape[0]
    width = lax.axis_size("body")
    here, column = lax.axis_index("garm"), lax.axis_index("body")
    flips = (0, 3 - here // 2, 2 + here // 2, 1)
    for n, out_ref in enumerate(out_refs):
        place_z = here ^ flips[n]
        for q in range(3 * tiles):
            out_ref[5 + q] = body_ref[q]
        for q in range(tiles):
            out_ref[5 + 3 * tiles + q] = stiff_ref[q]
        for x in range(2):
            owner = place_z * width + (column ^ x)
            live = pc_ref[0, owner]
            for s in range(cap):
                g = pg_ref[s, owner]
                row, place = pl.ds(g, 1), pl.ds(x * cap + s, 1)
                for c in range(3):
                    out_ref[c, place, :] = garm_ref[c, row, :]
                out_ref[3, place, :] = jnp.where(s < live, cot_ref[row, :], 0.0)
                out_ref[4, place, :] = jnp.full((1, BLOCK), pb_ref[s, owner].astype(f32), f32)
                spot, line = 2 * x + n // 2, n % 2 * cap + s
                index_ref[spot, line : line + 1, :] = jnp.full((1, BLOCK), g.astype(f32), f32)
    for ref, other in ((same_ref, False), (other_ref, True)):
        for k, tile in enumerate(half_message(out_refs[3], other)):
            ref[k] = tile


def staged(garment, cotangent, body_points, stiffness, pg, pb, pc):
    verts = garment.shape[2]
    points = body_points.shape[2]
    blocks = points // BLOCK
    tiles = blocks // SUB
    garm_n = lax.axis_size("garm")
    message = jax.ShapeDtypeStruct((5 + 4 * tiles, SUB, BLOCK), f32)
    arrays = (
        pg,
        pb,
        pc,
        garment.reshape(3, verts // BLOCK, BLOCK),
        cotangent.reshape(verts // BLOCK, BLOCK),
        body_points.reshape(3 * tiles, SUB, BLOCK),
        stiffness.reshape(tiles, SUB, BLOCK),
    )
    half = jax.ShapeDtypeStruct((3 + 4 * tiles, SUB, BLOCK), f32)
    index, last_same, last_other, own, *sent = pl.pallas_call(
        stage_kernel,
        out_shape=[jax.ShapeDtypeStruct((garm_n, SUB, BLOCK), f32), half, half] + [message] * garm_n,
        in_specs=[pl.BlockSpec(memory_space=pltpu.HBM)] * len(arrays),
        out_specs=[pl.BlockSpec(memory_space=pltpu.VMEM)] * (garm_n + 3),
        scratch_shapes=[
            (pltpu.SMEM if k < 3 else pltpu.VMEM)(a.shape, a.dtype) for k, a in enumerate(arrays)
        ]
        + [pltpu.SemaphoreType.DMA((len(arrays),))],
        compiler_params=pltpu.CompilerParams(vmem_limit_bytes=VMEM_LIMIT),
    )(*[pltpu.with_memory_space_constraint(a, pltpu.HBM) for a in arrays])

    def along_garm(value, pairs):
        return lax.ppermute(value, "garm", pairs)

    def along_body(value):
        return lax.ppermute(value, "body", [(0, 1), (1, 0)])

    cycle = [(0, 2), (2, 1), (1, 3), (3, 0)]
    got = [
        along_garm(sent[1], cycle),
        along_garm(sent[0], [(b, a) for a, b in cycle]),
        along_garm(last_same, [(z, z ^ 1) for z in range(garm_n)]),
    ]
    direct = lax.ppermute(last_other, ("garm", "body"), [(n, n ^ 3) for n in range(2 * garm_n)])
    near_shape = jax.ShapeDtypeStruct((5 + 4 * tiles, SUB, BLOCK), f32)
    second_shape = jax.ShapeDtypeStruct((3 + 8 * tiles, SUB, BLOCK), f32)
    near = call(forward_kernel, near_shape, [], (), (own, got[0]), BUNDLE_COST)
    second = call(second_kernel, second_shape, [], (), (own, got[1], near), BUNDLE_COST)
    near_other, second_other = along_body(near), along_body(second)

    def batch_shapes(count):
        return tuple(
            jax.ShapeDtypeStruct((count * SUB, width * BLOCK), f32) for width in (4, 1, 3)
        )

    bg1, bi1, gg1 = call(
        same_kernel, batch_shapes(2), [], (), (own, *sent, *got, second), SAME_COST
    )
    bg2, bi2 = call(
        near_kernel, batch_shapes(1)[:2], [], (), (own, near_other, bg1), NEAR_COST
    )
    body_shape = jax.ShapeDtypeStruct((3, blocks, BLOCK), f32)
    stiff_shape = jax.ShapeDtypeStruct((blocks, BLOCK), f32)
    garm_shape = jax.ShapeDtypeStruct((3, verts // BLOCK, BLOCK), f32)
    stiff = call(
        stiff_kernel, stiff_shape, [], (), (own, second_other, direct, bg1, bg2, bi1, bi2)
    )
    stiff_other = lax.ppermute(stiff, "frame", [(0, 1), (1, 0)])
    body_total, garm_total = call(
        late_kernel,
        (body_shape, garm_shape),
        [],
        (),
        (own, *sent, near_other, second_other, direct, bg1, bg2, bi1, bi2, gg1, index),
    )
    return call(
        final_kernel,
        (garm_shape, body_shape, stiff_shape),
        [],
        (),
        (garm_total, body_total, stiff, stiff_other),
    )


def per_device(garment, cotangent, body_points, stiffness, pair_garment, pair_body, pair_count):
    owners = lax.axis_size(("garm", "body"))
    verts = garment.shape[2]
    points = body_points.shape[2]
    blocks = points // BLOCK
    cap = pair_garment.shape[3]
    slots = owners * cap
    pg = pair_garment.reshape(owners, cap).T
    pb = pair_body.reshape(owners, cap).T
    pc = pair_count.reshape(1, owners)
    if (lax.axis_size("garm"), lax.axis_size("body")) == (4, 2) and cap == SUB // 2:
        garm_grad, body_grad, stiff = staged(
            garment, cotangent, body_points, stiffness, pg, pb, pc
        )
        return (
            garm_grad.reshape(1, 3, verts),
            body_grad.reshape(1, 3, points),
            stiff.reshape(points),
        )
    message = call(
        pack_kernel,
        jax.ShapeDtypeStruct((owners, 5 + blocks, cap, BLOCK), f32),
        [],
        (pg, pb, pc),
        (
            garment.reshape(3, verts // BLOCK, BLOCK),
            cotangent.reshape(verts // BLOCK, BLOCK),
            body_points.reshape(3, blocks, BLOCK),
            stiffness.reshape(blocks, BLOCK),
        ),
    )
    arrived = lax.all_to_all(message, ("garm", "body"), split_axis=0, concat_axis=0, tiled=True)
    rows = pltpu.VMEM((4, slots, BLOCK), f32)
    grad = pltpu.VMEM((slots, 4 * BLOCK), f32)
    index = pltpu.VMEM((slots, BLOCK), f32)
    body_grad, stiff = call(
        body_kernel,
        (
            jax.ShapeDtypeStruct((3, blocks, BLOCK), f32),
            jax.ShapeDtypeStruct((blocks, BLOCK), f32),
        ),
        [rows, rows, pltpu.VMEM((blocks, 4 * BLOCK), f32), index, grad],
        (),
        (message, arrived),
    )
    other = lax.ppermute(stiff, "frame", [(0, 1), (1, 0)])
    garm_grad = call(
        garm_kernel,
        jax.ShapeDtypeStruct((3, verts // BLOCK, BLOCK), f32),
        [rows, rows, index, grad],
        (pg, pb),
        (message, arrived),
    )
    return (
        garm_grad.reshape(1, 3, verts),
        body_grad.reshape(1, 3, points),
        (stiff + other).reshape(points),
    )


def solution(mesh):
    in_specs = (
        P(("grp", "frame"), None, ("garm", "body")),
        P(("grp", "frame"), ("garm", "body")),
        P(("grp", "frame"), None, ("garm", "body")),
        P(("grp", "garm", "body")),
        P(("grp", "frame"), ("garm", "body"), None, None),
        P(("grp", "frame"), ("garm", "body"), None, None),
        P(("grp", "frame"), ("garm", "body"), None),
    )
    out_specs = (
        P(("grp", "frame"), None, ("garm", "body")),
        P(("grp", "frame"), None, ("garm", "body")),
        P(("grp", "garm", "body")),
    )
    return jax.shard_map(
        per_device, mesh=mesh, in_specs=in_specs, out_specs=out_specs, check_vma=False
    )
```

```python
import math

import jax
import jax.numpy as jnp
from jax import lax
from jax.experimental import pallas as pl
from jax.experimental.pallas import tpu as pltpu
from jax.sharding import PartitionSpec as P

BLOCK = 128
SUB = 8
VMEM_LIMIT = 32 * 1024 * 1024
SAME_COST = 40_000_000_000
NEAR_COST = 1_000_000_000
BUNDLE_COST = 1000

amplitude = 0.05
width_sq = 4.0

SCALE = math.sqrt(math.log2(math.e) / width_sq)
FACTOR = -2.0 / width_sq * amplitude

f32 = jnp.float32
bf16 = jnp.bfloat16


def pieces(value, count):
    out = []
    for _ in range(count - 1):
        top = value.astype(bf16).astype(f32)
        out.append(top)
        value = value - top
    out.append(value)
    return out


def features(left, right):
    lpos = [left[c] * SCALE for c in range(3)]
    rpos = [right[c] * SCALE for c in range(3)]
    lnorm = -(lpos[0] * lpos[0] + lpos[1] * lpos[1] + lpos[2] * lpos[2])
    rnorm = -(rpos[0] * rpos[0] + rpos[1] * rpos[1] + rpos[2] * rpos[2])
    one = jnp.ones_like(lnorm)
    lrows, rrows = [], []
    for c in range(3):
        l1, l2, l3 = pieces(lpos[c] * 2.0, 3)
        r1, r2, r3 = pieces(rpos[c], 3)
        lrows += [l1, l1, l2, l2, l1, l3]
        rrows += [r1, r2, r1, r2, r3, r1]
    lrows += pieces(lnorm, 3) + [one] * 3
    rrows += [one] * 3 + pieces(rnorm, 3)
    return (
        jnp.concatenate(lrows, axis=0).astype(bf16),
        jnp.concatenate(rrows, axis=0).astype(bf16),
    )


def pull(batches, weights_only=False):
    made = []
    for left, right in batches:
        lfeat, rfeat = features(left, right)
        weight = left[3]
        coeff = [weight] if weights_only else [weight * left[c] for c in range(3)] + [weight]
        chi, clo = pieces(jnp.concatenate(coeff, axis=0), 2)
        lhs = jnp.concatenate(
            [
                jnp.concatenate([chi, chi], axis=1),
                jnp.concatenate([clo, jnp.zeros_like(clo)], axis=1),
            ],
            axis=0,
        ).astype(bf16)
        made.append((lfeat.T, rfeat, lhs))
    row = lax.broadcasted_iota(jnp.int32, made[0][1].shape, 0) % SUB
    count = made[0][2].shape[0] // 2
    sub = lax.broadcasted_iota(jnp.int32, (count, BLOCK), 0) % SUB
    totals = [jnp.zeros((count, BLOCK), f32) for _ in batches]

    def sums_of(pair, n, exponent):
        kernel = jnp.exp2(exponent)
        khi = kernel.astype(bf16)
        klo = (kernel - khi.astype(f32)).astype(bf16)
        sums = jnp.dot(made[n][2], jnp.concatenate([khi, klo], axis=0), preferred_element_type=f32)
        sums = sums[:count] + sums[count:]
        for k in range(2):
            part = sums[:, k * BLOCK : (k + 1) * BLOCK]
            totals[n] = jnp.where(sub == pair + k, part, totals[n])

    ahead = SUB // 2 if len(batches) == 1 else 0
    waiting = []
    for pair in range(0, SUB, 2):
        masks = [(row == pair + k).astype(f32).astype(bf16) for k in range(2)]
        for n, (lfeat_t, rfeat, _) in enumerate(made):
            rhs = jnp.concatenate([rfeat * mask for mask in masks], axis=1)
            waiting.append((pair, n, jnp.dot(lfeat_t, rhs, preferred_element_type=f32)))
            if len(waiting) > ahead:
                sums_of(*waiting.pop(0))
    for work in waiting:
        sums_of(*work)
    return [[total[c * SUB : (c + 1) * SUB] for c in range(count // SUB)] for total in totals]


def gradients(batches):
    out = []
    for (_, right), total in zip(batches, pull(batches)):
        rows = [FACTOR * right[3] * (right[c] * total[3] - total[c]) for c in range(3)]
        out.append(rows + [amplitude * total[3]])
    return out


def run_batches(left_ref, right_ref, grad_ref):
    batches = left_ref.shape[1] // SUB
    group = math.gcd(batches, 4)

    def step(k, carry):
        places = [pl.ds(pl.multiple_of((k * group + n) * SUB, SUB), SUB) for n in range(group)]
        work = [
            tuple([ref[c, rows, :] for c in range(4)] for ref in (left_ref, right_ref))
            for rows in places
        ]
        for rows, values in zip(places, gradients(work)):
            for c, value in enumerate(values):
                grad_ref[rows, c * BLOCK : (c + 1) * BLOCK] = value
        return carry

    lax.fori_loop(0, batches // group, step, 0)


def scatter(index, grads, blocks):
    index = jnp.concatenate([index] * 3, axis=0)
    lane = lax.broadcasted_iota(jnp.int32, index.shape, 1).astype(f32)
    onehot_t = (index == lane).astype(f32).T[:blocks].astype(bf16)
    stack = jnp.concatenate(pieces(grads, 3), axis=0).astype(bf16)
    return jnp.dot(onehot_t, stack, preferred_element_type=f32)


def pack_kernel(pg_ref, pb_ref, pc_ref, garm_ref, cot_ref, body_ref, stiff_ref, out_ref):
    cap, owners = pg_ref.shape
    tiles = stiff_ref.shape[0] // cap

    def one(d, carry):
        for s in range(cap):
            row = pl.ds(pg_ref[s, d], 1)
            for c in range(3):
                out_ref[d, c, s : s + 1, :] = garm_ref[c, row, :]
            out_ref[d, 3, s : s + 1, :] = jnp.where(s < pc_ref[0, d], cot_ref[row, :], 0.0)
            out_ref[d, 4 + 4 * tiles, s : s + 1, :] = jnp.full(
                (1, BLOCK), pb_ref[s, d].astype(f32), f32
            )
        for q in range(tiles):
            rows = slice(q * cap, (q + 1) * cap)
            for c in range(3):
                out_ref[d, 4 + c * tiles + q] = body_ref[c, rows, :]
            out_ref[d, 4 + 3 * tiles + q] = stiff_ref[rows, :]
        return carry

    if owners <= 8:
        for d in range(owners):
            one(d, 0)
    else:
        lax.fori_loop(0, owners, one, 0)


def over(count, fn):
    if count <= 8:
        for d in range(count):
            fn(d)
    else:
        lax.fori_loop(0, count, lambda d, carry: (fn(d), carry)[1], 0)


def body_kernel(own_ref, in_ref, out_ref, stiff_ref, left, right, table, index, grad):
    owners, tiles, cap, _ = in_ref.shape
    blocks = tiles - 5

    def take(d):
        rows = pl.ds(d * cap, cap)
        for c in range(4):
            left[c, rows, :] = in_ref[d, c]
        index[rows, :] = in_ref[d, tiles - 1]

    over(owners, take)
    for c in range(4):
        for q in range(blocks // 4):
            table[4 * q : 4 * q + 4, c * BLOCK : (c + 1) * BLOCK] = own_ref[
                0, 4 + c * (blocks // 4) + q
            ]
    lane = lax.broadcasted_iota(jnp.int32, index.shape, 1).astype(f32)
    onehot = (index[...] == lane).astype(f32)[:, :blocks].astype(bf16)
    chosen = [
        jnp.dot(onehot, part.astype(bf16), preferred_element_type=f32)
        for part in pieces(table[...], 3)
    ]
    chosen = chosen[0] + chosen[1] + chosen[2]
    for c in range(4):
        right[c] = chosen[:, c * BLOCK : (c + 1) * BLOCK]
    run_batches(left, right, grad)
    total = scatter(index[...], grad[...], blocks)
    for c in range(3):
        out_ref[c] = total[:, c * BLOCK : (c + 1) * BLOCK]
    stiff_ref[...] = total[:, 3 * BLOCK :]


def garm_kernel(pg_ref, pb_ref, own_ref, in_ref, out_ref, left, right, index, grad):
    owners, tiles, cap, _ = in_ref.shape
    blocks = tiles - 5
    garm_blocks = out_ref.shape[1]

    def take(d):
        rows = pl.ds(d * cap, cap)
        for c in range(4):
            right[c, rows, :] = own_ref[d, c]
        for s in range(cap):
            b = pb_ref[s, d]
            for c in range(4):
                left[c, pl.ds(d * cap + s, 1), :] = in_ref[
                    d, 4 + c * (blocks // 4) + b // 4, pl.ds(b % 4, 1), :
                ]
            index[pl.ds(d * cap + s, 1), :] = jnp.full((1, BLOCK), pg_ref[s, d].astype(f32), f32)

    over(owners, take)
    run_batches(left, right, grad)
    total = scatter(index[...], grad[...], garm_blocks)
    for c in range(3):
        out_ref[c] = total[:, c * BLOCK : (c + 1) * BLOCK]


def call(kernel, out_shape, scratch, scalars, arrays, cost=None):
    specs = [pl.BlockSpec(memory_space=pltpu.SMEM)] * len(scalars)
    specs += [pl.BlockSpec(memory_space=pltpu.VMEM)] * len(arrays)
    return pl.pallas_call(
        kernel,
        out_shape=out_shape,
        in_specs=specs,
        out_specs=jax.tree.map(lambda _: pl.BlockSpec(memory_space=pltpu.VMEM), out_shape),
        scratch_shapes=scratch,
        cost_estimate=cost and pl.CostEstimate(flops=cost, bytes_accessed=1000, transcendentals=0),
        compiler_params=pltpu.CompilerParams(vmem_limit_bytes=VMEM_LIMIT),
    )(*scalars, *arrays)


def read_table(ref, start, step):
    columns = [
        jnp.concatenate([ref[start + c * step + q] for q in range(step)], axis=0) for c in range(4)
    ]
    return jnp.concatenate(columns, axis=1)


def choose(index, table):
    blocks = table.shape[0]
    lane = lax.broadcasted_iota(jnp.int32, index.shape, 1)
    onehot = (index == (lane % blocks).astype(f32)) & (lane < 3 * blocks)
    onehot = onehot.astype(f32)[:, : 3 * blocks].astype(bf16)
    stack = jnp.concatenate(pieces(table, 3), axis=0).astype(bf16)
    rows = jnp.dot(onehot, stack, preferred_element_type=f32)
    return [rows[:, c * BLOCK : (c + 1) * BLOCK] for c in range(4)]


def halves(top, bottom):
    row = lax.broadcasted_iota(jnp.int32, (SUB, BLOCK), 0)
    return jnp.where(row < SUB // 2, top, bottom)


def flip(value):
    return pltpu.roll(value, SUB // 2, 0)


def body_work(tiles, table):
    return list(tiles[:4]), choose(tiles[4], table)


def garm_work(tiles, top, bottom):
    row = lax.broadcasted_iota(jnp.int32, (SUB, BLOCK), 0)
    index = tiles[4] + jnp.where(row < SUB // 2, 0, top.shape[0]).astype(f32)
    return choose(index, jnp.concatenate([top, bottom], axis=0)), list(tiles[:4])


def slot_tiles(ref):
    return [ref[c] for c in range(5)]


def message_table(ref, step):
    return read_table(ref, 5, step)


def pack(tiles):
    a, b, c, d, e = tiles
    return [halves(a, flip(b)), halves(c, flip(d)), e]


def unpack_top(tiles):
    a, b, c = tiles
    return [a, flip(a), b, flip(b), c]


def unpack_bottom(tiles):
    a, b, c = tiles
    return [flip(a), a, flip(b), b, flip(c)]


def half_message(ref, other):
    slots = slot_tiles(ref)
    if other:
        slots = [flip(tile) for tile in slots]
    return [ref[5 + q] for q in range(ref.shape[0] - 5)] + pack(slots)


def forward_kernel(one_ref, two_ref, out_ref):
    body = one_ref.shape[0] - 5
    for n, ref in enumerate((one_ref, two_ref)):
        for q in range(body):
            out_ref[n * body + q] = ref[5 + q]
    for k, tile in enumerate(bottom_tiles(one_ref, two_ref)):
        out_ref[2 * body + k] = tile


def half_kernel(ref, after_ref, out_ref):
    del after_ref
    for k, tile in enumerate(half_message(ref, True)):
        out_ref[k] = tile


def top_tiles(one_ref, two_ref):
    return [halves(a, flip(b)) for a, b in zip(slot_tiles(one_ref), slot_tiles(two_ref))]


def bottom_tiles(one_ref, two_ref):
    return [halves(flip(a), b) for a, b in zip(slot_tiles(one_ref), slot_tiles(two_ref))]


def store(work, index, bgrad_ref, bindex_ref, ggrad_ref):
    out = gradients(work)
    for n, value in enumerate(index):
        rows = slice(n * SUB, (n + 1) * SUB)
        bgrad_ref[rows, :] = jnp.concatenate(out[n], axis=1)
        ggrad_ref[rows, :] = jnp.concatenate(out[len(index) + n][:3], axis=1)
        bindex_ref[rows, :] = value


def same_kernel(own_ref, sent0, sent1, sent2, got0, got1, got2, after_ref, *out_refs):
    del after_ref
    body = own_ref.shape[0] - 5
    step = body // 4
    own = message_table(own_ref, step)
    here = top_tiles(own_ref, got0)
    last = unpack_bottom([got2[body + k] for k in range(3)])
    there = [halves(x, y) for x, y in zip(slot_tiles(got1), last)]
    work = [
        body_work(here, own),
        body_work(there, own),
        garm_work(top_tiles(own_ref, sent0), own, message_table(got0, step)),
        garm_work(top_tiles(sent1, sent2), message_table(got1, step), read_table(got2, 0, step)),
    ]
    store(work, [here[4], there[4]], *out_refs)


def near_tiles(own_ref, near_ref):
    body = own_ref.shape[0] - 5
    return [near_ref[2 * body + k] for k in range(5)]


def late_tiles(own_ref, one_ref, two_ref):
    body = own_ref.shape[0] - 5
    top = unpack_top([one_ref[body + k] for k in range(3)])
    bottom = unpack_bottom([two_ref[body + k] for k in range(3)])
    return [halves(x, y) for x, y in zip(top, bottom)]


def near_kernel(own_ref, near_ref, after_ref, bgrad_ref, bindex_ref):
    del after_ref
    tiles = near_tiles(own_ref, near_ref)
    own = message_table(own_ref, (own_ref.shape[0] - 5) // 4)
    bgrad_ref[...] = jnp.concatenate(gradients([body_work(tiles, own)])[0], axis=1)
    bindex_ref[...] = tiles[4]


def stiff_kernel(own_ref, one_ref, two_ref, bg1, bg2, bi1, bi2, out_ref):
    tiles = late_tiles(own_ref, one_ref, two_ref)
    own = message_table(own_ref, (own_ref.shape[0] - 5) // 4)
    [[last]] = pull([body_work(tiles, own)], weights_only=True)
    grads = [bg1[:, 3 * BLOCK :], bg2[:, 3 * BLOCK :], amplitude * last]
    index = jnp.concatenate([bi1[...], bi2[...], tiles[4]], axis=0)
    out_ref[...] = scatter(index, jnp.concatenate(grads, axis=0), out_ref.shape[0])


def late_sums(
    own_ref,
    sent0,
    sent1,
    sent2,
    near_ref,
    one_ref,
    two_ref,
    bg1,
    bg2,
    bi1,
    bi2,
    gg1,
    index_ref,
    body_out,
    garm_out,
):
    body = own_ref.shape[0] - 5
    step = body // 4
    tiles = late_tiles(own_ref, one_ref, two_ref)
    near = [read_table(near_ref, n * body, step) for n in range(2)]
    far = [read_table(ref, 0, step) for ref in (one_ref, two_ref)]
    out = gradients(
        [
            body_work(tiles, message_table(own_ref, step)),
            garm_work(bottom_tiles(own_ref, sent0), *near),
            garm_work(bottom_tiles(sent1, sent2), *far),
        ]
    )
    rows = [jnp.concatenate(values[:3], axis=1) for values in out]
    width = 3 * BLOCK
    index = jnp.concatenate([bi1[...], bi2[...], tiles[4]], axis=0)
    grads = jnp.concatenate([bg1[:, :width], bg2[:, :width], rows[0]], axis=0)
    total = scatter(index, grads, body_out.shape[1])
    for c in range(3):
        body_out[c] = total[:, c * BLOCK : (c + 1) * BLOCK]
    index = jnp.concatenate([index_ref[k] for k in range(index_ref.shape[0])], axis=0)
    grads = jnp.concatenate([gg1[...], rows[1], rows[2]], axis=0)
    total = scatter(index, grads, garm_out.shape[1])
    for c in range(3):
        garm_out[c] = total[:, c * BLOCK : (c + 1) * BLOCK]


def before_kernel(*refs):
    *work, stiff_ref, body_out, garm_out, stiff_out = refs
    stiff_out[...] = stiff_ref[...]

    @pl.when(lax.axis_index("frame") == 1)
    def _():
        late_sums(*work, body_out, garm_out)


def beside_kernel(*refs):
    *work, body_ref, garm_ref, body_out, garm_out = refs

    @pl.when(lax.axis_index("frame") == 0)
    def _():
        late_sums(*work, body_out, garm_out)

    @pl.when(lax.axis_index("frame") == 1)
    def _():
        body_out[...] = body_ref[...]
        garm_out[...] = garm_ref[...]


def final_kernel(garm_ref, body_ref, mine_ref, other_ref, garm_out, body_out, stiff_out):
    stiff_out[...] = mine_ref[...] + other_ref[...]
    body_out[...] = body_ref[...]
    garm_out[...] = garm_ref[...]


def stage_kernel(*refs):
    hbm, (index_ref, same_ref, other_ref, *out_refs) = refs[:7], refs[7:14]
    vmem, sems = refs[14:21], refs[21]
    copies = [
        pltpu.make_async_copy(src, dst, sems.at[k]) for k, (src, dst) in enumerate(zip(hbm, vmem))
    ]
    for copy in copies:
        copy.start()
    for copy in copies:
        copy.wait()
    pg_ref, pb_ref, pc_ref, garm_ref, cot_ref, body_ref, stiff_ref = vmem
    cap = pg_ref.shape[0]
    tiles = stiff_ref.shape[0]
    width = lax.axis_size("body")
    here, column = lax.axis_index("garm"), lax.axis_index("body")
    flips = (0, 3 - here // 2, 2 + here // 2, 1)
    for n, out_ref in enumerate(out_refs):
        place_z = here ^ flips[n]
        for q in range(3 * tiles):
            out_ref[5 + q] = body_ref[q]
        for q in range(tiles):
            out_ref[5 + 3 * tiles + q] = stiff_ref[q]
        for x in range(2):
            owner = place_z * width + (column ^ x)
            live = pc_ref[0, owner]
            for s in range(cap):
                g = pg_ref[s, owner]
                row, place = pl.ds(g, 1), pl.ds(x * cap + s, 1)
                for c in range(3):
                    out_ref[c, place, :] = garm_ref[c, row, :]
                out_ref[3, place, :] = jnp.where(s < live, cot_ref[row, :], 0.0)
                out_ref[4, place, :] = jnp.full((1, BLOCK), pb_ref[s, owner].astype(f32), f32)
                spot, line = 2 * x + n // 2, n % 2 * cap + s
                index_ref[spot, line : line + 1, :] = jnp.full((1, BLOCK), g.astype(f32), f32)
    for ref, other in ((same_ref, False), (other_ref, True)):
        for k, tile in enumerate(half_message(out_refs[3], other)):
            ref[k] = tile


def staged(garment, cotangent, body_points, stiffness, pg, pb, pc):
    verts = garment.shape[2]
    points = body_points.shape[2]
    blocks = points // BLOCK
    tiles = blocks // SUB
    garm_n = lax.axis_size("garm")
    message = jax.ShapeDtypeStruct((5 + 4 * tiles, SUB, BLOCK), f32)
    arrays = (
        pg,
        pb,
        pc,
        garment.reshape(3, verts // BLOCK, BLOCK),
        cotangent.reshape(verts // BLOCK, BLOCK),
        body_points.reshape(3 * tiles, SUB, BLOCK),
        stiffness.reshape(tiles, SUB, BLOCK),
    )
    half = jax.ShapeDtypeStruct((3 + 4 * tiles, SUB, BLOCK), f32)
    index, last_same, last_other, own, *sent = pl.pallas_call(
        stage_kernel,
        out_shape=[jax.ShapeDtypeStruct((garm_n, SUB, BLOCK), f32), half, half] + [message] * garm_n,
        in_specs=[pl.BlockSpec(memory_space=pltpu.HBM)] * len(arrays),
        out_specs=[pl.BlockSpec(memory_space=pltpu.VMEM)] * (garm_n + 3),
        scratch_shapes=[
            (pltpu.SMEM if k < 3 else pltpu.VMEM)(a.shape, a.dtype) for k, a in enumerate(arrays)
        ]
        + [pltpu.SemaphoreType.DMA((len(arrays),))],
        compiler_params=pltpu.CompilerParams(vmem_limit_bytes=VMEM_LIMIT),
    )(*[pltpu.with_memory_space_constraint(a, pltpu.HBM) for a in arrays])

    def along_garm(value, pairs):
        return lax.ppermute(value, "garm", pairs)

    def along_body(value):
        return lax.ppermute(value, "body", [(0, 1), (1, 0)])

    cycle = [(0, 2), (2, 1), (1, 3), (3, 0)]
    got = [
        along_garm(sent[1], cycle),
        along_garm(sent[0], [(b, a) for a, b in cycle]),
        along_garm(last_same, [(z, z ^ 1) for z in range(garm_n)]),
    ]
    direct = lax.ppermute(last_other, ("garm", "body"), [(n, n ^ 3) for n in range(2 * garm_n)])
    near_shape = jax.ShapeDtypeStruct((5 + 8 * tiles, SUB, BLOCK), f32)
    near = call(forward_kernel, near_shape, [], (), (own, got[0]), BUNDLE_COST)
    second = call(half_kernel, half, [], (), (got[1], near), BUNDLE_COST)
    near_other, second_other = along_body(near), along_body(second)

    def batch_shapes(count):
        return tuple(
            jax.ShapeDtypeStruct((count * SUB, width * BLOCK), f32) for width in (4, 1, 3)
        )

    bg1, bi1, gg1 = call(
        same_kernel, batch_shapes(2), [], (), (own, *sent, *got, second), SAME_COST
    )
    bg2, bi2 = call(
        near_kernel, batch_shapes(1)[:2], [], (), (own, near_other, bg1), NEAR_COST
    )
    body_shape = jax.ShapeDtypeStruct((3, blocks, BLOCK), f32)
    stiff_shape = jax.ShapeDtypeStruct((blocks, BLOCK), f32)
    garm_shape = jax.ShapeDtypeStruct((3, verts // BLOCK, BLOCK), f32)
    stiff = call(
        stiff_kernel, stiff_shape, [], (), (own, second_other, direct, bg1, bg2, bi1, bi2)
    )
    work = (own, *sent, near_other, second_other, direct, bg1, bg2, bi1, bi2, gg1, index)
    body_total, garm_total, stiff = call(
        before_kernel, (body_shape, garm_shape, stiff_shape), [], (), (*work, stiff)
    )
    stiff_other = lax.ppermute(stiff, "frame", [(0, 1), (1, 0)])
    body_total, garm_total = call(
        beside_kernel, (body_shape, garm_shape), [], (), (*work, body_total, garm_total)
    )
    return call(
        final_kernel,
        (garm_shape, body_shape, stiff_shape),
        [],
        (),
        (garm_total, body_total, stiff, stiff_other),
    )


def per_device(garment, cotangent, body_points, stiffness, pair_garment, pair_body, pair_count):
    owners = lax.axis_size(("garm", "body"))
    verts = garment.shape[2]
    points = body_points.shape[2]
    blocks = points // BLOCK
    cap = pair_garment.shape[3]
    slots = owners * cap
    pg = pair_garment.reshape(owners, cap).T
    pb = pair_body.reshape(owners, cap).T
    pc = pair_count.reshape(1, owners)
    if (lax.axis_size("garm"), lax.axis_size("body")) == (4, 2) and cap == SUB // 2:
        garm_grad, body_grad, stiff = staged(
            garment, cotangent, body_points, stiffness, pg, pb, pc
        )
        return (
            garm_grad.reshape(1, 3, verts),
            body_grad.reshape(1, 3, points),
            stiff.reshape(points),
        )
    message = call(
        pack_kernel,
        jax.ShapeDtypeStruct((owners, 5 + blocks, cap, BLOCK), f32),
        [],
        (pg, pb, pc),
        (
            garment.reshape(3, verts // BLOCK, BLOCK),
            cotangent.reshape(verts // BLOCK, BLOCK),
            body_points.reshape(3, blocks, BLOCK),
            stiffness.reshape(blocks, BLOCK),
        ),
    )
    arrived = lax.all_to_all(message, ("garm", "body"), split_axis=0, concat_axis=0, tiled=True)
    rows = pltpu.VMEM((4, slots, BLOCK), f32)
    grad = pltpu.VMEM((slots, 4 * BLOCK), f32)
    index = pltpu.VMEM((slots, BLOCK), f32)
    body_grad, stiff = call(
        body_kernel,
        (
            jax.ShapeDtypeStruct((3, blocks, BLOCK), f32),
            jax.ShapeDtypeStruct((blocks, BLOCK), f32),
        ),
        [rows, rows, pltpu.VMEM((blocks, 4 * BLOCK), f32), index, grad],
        (),
        (message, arrived),
    )
    other = lax.ppermute(stiff, "frame", [(0, 1), (1, 0)])
    garm_grad = call(
        garm_kernel,
        jax.ShapeDtypeStruct((3, verts // BLOCK, BLOCK), f32),
        [rows, rows, index, grad],
        (pg, pb),
        (message, arrived),
    )
    return (
        garm_grad.reshape(1, 3, verts),
        body_grad.reshape(1, 3, points),
        (stiff + other).reshape(points),
    )


def solution(mesh):
    in_specs = (
        P(("grp", "frame"), None, ("garm", "body")),
        P(("grp", "frame"), ("garm", "body")),
        P(("grp", "frame"), None, ("garm", "body")),
        P(("grp", "garm", "body")),
        P(("grp", "frame"), ("garm", "body"), None, None),
        P(("grp", "frame"), ("garm", "body"), None, None),
        P(("grp", "frame"), ("garm", "body"), None),
    )
    out_specs = (
        P(("grp", "frame"), None, ("garm", "body")),
        P(("grp", "frame"), None, ("garm", "body")),
        P(("grp", "garm", "body")),
    )
    return jax.shard_map(
        per_device, mesh=mesh, in_specs=in_specs, out_specs=out_specs, check_vma=False
    )
```

```python
import math

import jax
import jax.numpy as jnp
from jax import lax
from jax.experimental import pallas as pl
from jax.experimental.pallas import tpu as pltpu
from jax.sharding import PartitionSpec as P

BLOCK = 128
SUB = 8
VMEM_LIMIT = 32 * 1024 * 1024
SAME_COST = 40_000_000_000
NEAR_COST = 1_000_000_000
BUNDLE_COST = 1000

amplitude = 0.05
width_sq = 4.0

SCALE = math.sqrt(math.log2(math.e) / width_sq)
FACTOR = -2.0 / width_sq * amplitude

f32 = jnp.float32
bf16 = jnp.bfloat16


def pieces(value, count):
    out = []
    for _ in range(count - 1):
        top = value.astype(bf16).astype(f32)
        out.append(top)
        value = value - top
    out.append(value)
    return out


def features(left, right):
    lpos = [left[c] * SCALE for c in range(3)]
    rpos = [right[c] * SCALE for c in range(3)]
    lnorm = -(lpos[0] * lpos[0] + lpos[1] * lpos[1] + lpos[2] * lpos[2])
    rnorm = -(rpos[0] * rpos[0] + rpos[1] * rpos[1] + rpos[2] * rpos[2])
    one = jnp.ones_like(lnorm)
    lrows, rrows = [], []
    for c in range(3):
        l1, l2, l3 = pieces(lpos[c] * 2.0, 3)
        r1, r2, r3 = pieces(rpos[c], 3)
        lrows += [l1, l1, l2, l2, l1, l3]
        rrows += [r1, r2, r1, r2, r3, r1]
    lrows += pieces(lnorm, 3) + [one] * 3
    rrows += [one] * 3 + pieces(rnorm, 3)
    return (
        jnp.concatenate(lrows, axis=0).astype(bf16),
        jnp.concatenate(rrows, axis=0).astype(bf16),
    )


def pull(batches):
    made = []
    for left, right in batches:
        lfeat, rfeat = features(left, right)
        weight = left[3]
        coeff = [weight * left[c] for c in range(3)] + [weight]
        chi, clo = pieces(jnp.concatenate(coeff, axis=0), 2)
        lhs = jnp.concatenate(
            [
                jnp.concatenate([chi, chi], axis=1),
                jnp.concatenate([clo, jnp.zeros_like(clo)], axis=1),
            ],
            axis=0,
        ).astype(bf16)
        made.append((lfeat.T, rfeat, lhs))
    row = lax.broadcasted_iota(jnp.int32, made[0][1].shape, 0) % SUB
    count = made[0][2].shape[0] // 2
    sub = lax.broadcasted_iota(jnp.int32, (count, BLOCK), 0) % SUB
    totals = [jnp.zeros((count, BLOCK), f32) for _ in batches]

    def sums_of(pair, n, exponent):
        kernel = jnp.exp2(exponent)
        khi = kernel.astype(bf16)
        klo = (kernel - khi.astype(f32)).astype(bf16)
        sums = jnp.dot(made[n][2], jnp.concatenate([khi, klo], axis=0), preferred_element_type=f32)
        sums = sums[:count] + sums[count:]
        for k in range(2):
            part = sums[:, k * BLOCK : (k + 1) * BLOCK]
            totals[n] = jnp.where(sub == pair + k, part, totals[n])

    ahead = SUB // 2 if len(batches) == 1 else 0
    waiting = []
    for pair in range(0, SUB, 2):
        masks = [(row == pair + k).astype(f32).astype(bf16) for k in range(2)]
        for n, (lfeat_t, rfeat, _) in enumerate(made):
            rhs = jnp.concatenate([rfeat * mask for mask in masks], axis=1)
            waiting.append((pair, n, jnp.dot(lfeat_t, rhs, preferred_element_type=f32)))
            if len(waiting) > ahead:
                sums_of(*waiting.pop(0))
    for work in waiting:
        sums_of(*work)
    return [[total[c * SUB : (c + 1) * SUB] for c in range(count // SUB)] for total in totals]


def weigh(left, right):
    lfeat, rfeat = features(left, right)
    lfeat_t, weight_t = lfeat.T, left[3].T
    row = lax.broadcasted_iota(jnp.int32, rfeat.shape, 0) % SUB
    exponents = []
    for pair in range(0, SUB, 2):
        masks = [(row == pair + k).astype(f32).astype(bf16) for k in range(2)]
        rhs = jnp.concatenate([rfeat * mask for mask in masks], axis=1)
        exponents.append(jnp.dot(lfeat_t, rhs, preferred_element_type=f32))
    rows = []
    for n in range(SUB):
        kernel = jnp.exp2(exponents[n // 2][:, n % 2 * BLOCK : (n % 2 + 1) * BLOCK])
        rows.append(jnp.sum(kernel * weight_t[:, n : n + 1], axis=0, keepdims=True))
    return jnp.concatenate(rows, axis=0)


def gradients(batches):
    out = []
    for (_, right), total in zip(batches, pull(batches)):
        rows = [FACTOR * right[3] * (right[c] * total[3] - total[c]) for c in range(3)]
        out.append(rows + [amplitude * total[3]])
    return out


def run_batches(left_ref, right_ref, grad_ref):
    batches = left_ref.shape[1] // SUB
    group = math.gcd(batches, 4)

    def step(k, carry):
        places = [pl.ds(pl.multiple_of((k * group + n) * SUB, SUB), SUB) for n in range(group)]
        work = [
            tuple([ref[c, rows, :] for c in range(4)] for ref in (left_ref, right_ref))
            for rows in places
        ]
        for rows, values in zip(places, gradients(work)):
            for c, value in enumerate(values):
                grad_ref[rows, c * BLOCK : (c + 1) * BLOCK] = value
        return carry

    lax.fori_loop(0, batches // group, step, 0)


def scatter(index, grads, blocks):
    index = jnp.concatenate([index] * 3, axis=0)
    lane = lax.broadcasted_iota(jnp.int32, index.shape, 1).astype(f32)
    onehot_t = (index == lane).astype(f32).T[:blocks].astype(bf16)
    stack = jnp.concatenate(pieces(grads, 3), axis=0).astype(bf16)
    return jnp.dot(onehot_t, stack, preferred_element_type=f32)


def pack_kernel(pg_ref, pb_ref, pc_ref, garm_ref, cot_ref, body_ref, stiff_ref, out_ref):
    cap, owners = pg_ref.shape
    tiles = stiff_ref.shape[0] // cap

    def one(d, carry):
        for s in range(cap):
            row = pl.ds(pg_ref[s, d], 1)
            for c in range(3):
                out_ref[d, c, s : s + 1, :] = garm_ref[c, row, :]
            out_ref[d, 3, s : s + 1, :] = jnp.where(s < pc_ref[0, d], cot_ref[row, :], 0.0)
            out_ref[d, 4 + 4 * tiles, s : s + 1, :] = jnp.full(
                (1, BLOCK), pb_ref[s, d].astype(f32), f32
            )
        for q in range(tiles):
            rows = slice(q * cap, (q + 1) * cap)
            for c in range(3):
                out_ref[d, 4 + c * tiles + q] = body_ref[c, rows, :]
            out_ref[d, 4 + 3 * tiles + q] = stiff_ref[rows, :]
        return carry

    if owners <= 8:
        for d in range(owners):
            one(d, 0)
    else:
        lax.fori_loop(0, owners, one, 0)


def over(count, fn):
    if count <= 8:
        for d in range(count):
            fn(d)
    else:
        lax.fori_loop(0, count, lambda d, carry: (fn(d), carry)[1], 0)


def body_kernel(own_ref, in_ref, out_ref, stiff_ref, left, right, table, index, grad):
    owners, tiles, cap, _ = in_ref.shape
    blocks = tiles - 5

    def take(d):
        rows = pl.ds(d * cap, cap)
        for c in range(4):
            left[c, rows, :] = in_ref[d, c]
        index[rows, :] = in_ref[d, tiles - 1]

    over(owners, take)
    for c in range(4):
        for q in range(blocks // 4):
            table[4 * q : 4 * q + 4, c * BLOCK : (c + 1) * BLOCK] = own_ref[
                0, 4 + c * (blocks // 4) + q
            ]
    lane = lax.broadcasted_iota(jnp.int32, index.shape, 1).astype(f32)
    onehot = (index[...] == lane).astype(f32)[:, :blocks].astype(bf16)
    chosen = [
        jnp.dot(onehot, part.astype(bf16), preferred_element_type=f32)
        for part in pieces(table[...], 3)
    ]
    chosen = chosen[0] + chosen[1] + chosen[2]
    for c in range(4):
        right[c] = chosen[:, c * BLOCK : (c + 1) * BLOCK]
    run_batches(left, right, grad)
    total = scatter(index[...], grad[...], blocks)
    for c in range(3):
        out_ref[c] = total[:, c * BLOCK : (c + 1) * BLOCK]
    stiff_ref[...] = total[:, 3 * BLOCK :]


def garm_kernel(pg_ref, pb_ref, own_ref, in_ref, out_ref, left, right, index, grad):
    owners, tiles, cap, _ = in_ref.shape
    blocks = tiles - 5
    garm_blocks = out_ref.shape[1]

    def take(d):
        rows = pl.ds(d * cap, cap)
        for c in range(4):
            right[c, rows, :] = own_ref[d, c]
        for s in range(cap):
            b = pb_ref[s, d]
            for c in range(4):
                left[c, pl.ds(d * cap + s, 1), :] = in_ref[
                    d, 4 + c * (blocks // 4) + b // 4, pl.ds(b % 4, 1), :
                ]
            index[pl.ds(d * cap + s, 1), :] = jnp.full((1, BLOCK), pg_ref[s, d].astype(f32), f32)

    over(owners, take)
    run_batches(left, right, grad)
    total = scatter(index[...], grad[...], garm_blocks)
    for c in range(3):
        out_ref[c] = total[:, c * BLOCK : (c + 1) * BLOCK]


def call(kernel, out_shape, scratch, scalars, arrays, cost=None):
    specs = [pl.BlockSpec(memory_space=pltpu.SMEM)] * len(scalars)
    specs += [pl.BlockSpec(memory_space=pltpu.VMEM)] * len(arrays)
    return pl.pallas_call(
        kernel,
        out_shape=out_shape,
        in_specs=specs,
        out_specs=jax.tree.map(lambda _: pl.BlockSpec(memory_space=pltpu.VMEM), out_shape),
        scratch_shapes=scratch,
        cost_estimate=cost and pl.CostEstimate(flops=cost, bytes_accessed=1000, transcendentals=0),
        compiler_params=pltpu.CompilerParams(vmem_limit_bytes=VMEM_LIMIT),
    )(*scalars, *arrays)


def read_table(ref, start, step):
    columns = [
        jnp.concatenate([ref[start + c * step + q] for q in range(step)], axis=0) for c in range(4)
    ]
    return jnp.concatenate(columns, axis=1)


def choose(index, table):
    blocks = table.shape[0]
    lane = lax.broadcasted_iota(jnp.int32, index.shape, 1)
    onehot = (index == (lane % blocks).astype(f32)) & (lane < 3 * blocks)
    onehot = onehot.astype(f32)[:, : 3 * blocks].astype(bf16)
    stack = jnp.concatenate(pieces(table, 3), axis=0).astype(bf16)
    rows = jnp.dot(onehot, stack, preferred_element_type=f32)
    return [rows[:, c * BLOCK : (c + 1) * BLOCK] for c in range(4)]


def halves(top, bottom):
    row = lax.broadcasted_iota(jnp.int32, (SUB, BLOCK), 0)
    return jnp.where(row < SUB // 2, top, bottom)


def flip(value):
    return pltpu.roll(value, SUB // 2, 0)


def body_work(tiles, table):
    return list(tiles[:4]), choose(tiles[4], table)


def garm_work(tiles, top, bottom):
    row = lax.broadcasted_iota(jnp.int32, (SUB, BLOCK), 0)
    index = tiles[4] + jnp.where(row < SUB // 2, 0, top.shape[0]).astype(f32)
    return choose(index, jnp.concatenate([top, bottom], axis=0)), list(tiles[:4])


def slot_tiles(ref):
    return [ref[c] for c in range(5)]


def message_table(ref, step):
    return read_table(ref, 5, step)


def pack(tiles):
    a, b, c, d, e = tiles
    return [halves(a, flip(b)), halves(c, flip(d)), e]


def unpack_top(tiles):
    a, b, c = tiles
    return [a, flip(a), b, flip(b), c]


def unpack_bottom(tiles):
    a, b, c = tiles
    return [flip(a), a, flip(b), b, flip(c)]


def half_message(ref, other):
    slots = slot_tiles(ref)
    if other:
        slots = [flip(tile) for tile in slots]
    return [ref[5 + q] for q in range(ref.shape[0] - 5)] + pack(slots)


def forward_kernel(one_ref, two_ref, out_ref):
    body = one_ref.shape[0] - 5
    for n, ref in enumerate((one_ref, two_ref)):
        for q in range(body):
            out_ref[n * body + q] = ref[5 + q]
    for k, tile in enumerate(bottom_tiles(one_ref, two_ref)):
        out_ref[2 * body + k] = tile


def half_kernel(ref, after_ref, out_ref):
    del after_ref
    for k, tile in enumerate(half_message(ref, True)):
        out_ref[k] = tile


def top_tiles(one_ref, two_ref):
    return [halves(a, flip(b)) for a, b in zip(slot_tiles(one_ref), slot_tiles(two_ref))]


def bottom_tiles(one_ref, two_ref):
    return [halves(flip(a), b) for a, b in zip(slot_tiles(one_ref), slot_tiles(two_ref))]


def store(work, index, bgrad_ref, bindex_ref, ggrad_ref):
    out = gradients(work)
    for n, value in enumerate(index):
        rows = slice(n * SUB, (n + 1) * SUB)
        bgrad_ref[rows, :] = jnp.concatenate(out[n], axis=1)
        ggrad_ref[rows, :] = jnp.concatenate(out[len(index) + n][:3], axis=1)
        bindex_ref[rows, :] = value


def same_kernel(own_ref, sent0, sent1, sent2, got0, got1, got2, after_ref, *out_refs):
    del after_ref
    body = own_ref.shape[0] - 5
    step = body // 4
    own = message_table(own_ref, step)
    here = top_tiles(own_ref, got0)
    last = unpack_bottom([got2[body + k] for k in range(3)])
    there = [halves(x, y) for x, y in zip(slot_tiles(got1), last)]
    work = [
        body_work(here, own),
        body_work(there, own),
        garm_work(top_tiles(own_ref, sent0), own, message_table(got0, step)),
        garm_work(top_tiles(sent1, sent2), message_table(got1, step), read_table(got2, 0, step)),
    ]
    store(work, [here[4], there[4]], *out_refs)


def near_tiles(own_ref, near_ref):
    body = own_ref.shape[0] - 5
    return [near_ref[2 * body + k] for k in range(5)]


def late_tiles(own_ref, one_ref, two_ref):
    body = own_ref.shape[0] - 5
    top = unpack_top([one_ref[body + k] for k in range(3)])
    bottom = unpack_bottom([two_ref[body + k] for k in range(3)])
    return [halves(x, y) for x, y in zip(top, bottom)]


def near_kernel(own_ref, near_ref, after_ref, bgrad_ref, bindex_ref):
    del after_ref
    tiles = near_tiles(own_ref, near_ref)
    own = message_table(own_ref, (own_ref.shape[0] - 5) // 4)
    bgrad_ref[...] = jnp.concatenate(gradients([body_work(tiles, own)])[0], axis=1)
    bindex_ref[...] = tiles[4]


def stiff_kernel(own_ref, one_ref, two_ref, bg1, bg2, bi1, bi2, out_ref):
    tiles = late_tiles(own_ref, one_ref, two_ref)
    own = message_table(own_ref, (own_ref.shape[0] - 5) // 4)
    index = jnp.concatenate([bi1[...], bi2[...]], axis=0)
    grads = jnp.concatenate([bg1[:, 3 * BLOCK :], bg2[:, 3 * BLOCK :]], axis=0)
    total = scatter(index, grads, out_ref.shape[0])
    last = amplitude * weigh(*body_work(tiles, own))
    block = lax.broadcasted_iota(jnp.int32, total.shape, 0).astype(f32)
    for n in range(SUB):
        total = total + jnp.where(block == tiles[4][n : n + 1], last[n : n + 1], 0.0)
    out_ref[...] = total


def late_sums(
    own_ref,
    sent0,
    sent1,
    sent2,
    near_ref,
    one_ref,
    two_ref,
    bg1,
    bg2,
    bi1,
    bi2,
    gg1,
    index_ref,
    body_out,
    garm_out,
):
    body = own_ref.shape[0] - 5
    step = body // 4
    tiles = late_tiles(own_ref, one_ref, two_ref)
    near = [read_table(near_ref, n * body, step) for n in range(2)]
    far = [read_table(ref, 0, step) for ref in (one_ref, two_ref)]
    out = gradients(
        [
            body_work(tiles, message_table(own_ref, step)),
            garm_work(bottom_tiles(own_ref, sent0), *near),
            garm_work(bottom_tiles(sent1, sent2), *far),
        ]
    )
    rows = [jnp.concatenate(values[:3], axis=1) for values in out]
    width = 3 * BLOCK
    index = jnp.concatenate([bi1[...], bi2[...], tiles[4]], axis=0)
    grads = jnp.concatenate([bg1[:, :width], bg2[:, :width], rows[0]], axis=0)
    total = scatter(index, grads, body_out.shape[1])
    for c in range(3):
        body_out[c] = total[:, c * BLOCK : (c + 1) * BLOCK]
    index = jnp.concatenate([index_ref[k] for k in range(index_ref.shape[0])], axis=0)
    grads = jnp.concatenate([gg1[...], rows[1], rows[2]], axis=0)
    total = scatter(index, grads, garm_out.shape[1])
    for c in range(3):
        garm_out[c] = total[:, c * BLOCK : (c + 1) * BLOCK]


def before_kernel(*refs):
    *work, stiff_ref, body_out, garm_out, stiff_out = refs
    stiff_out[...] = stiff_ref[...]

    @pl.when(lax.axis_index("frame") == 1)
    def _():
        late_sums(*work, body_out, garm_out)


def beside_kernel(*refs):
    *work, body_ref, garm_ref, body_out, garm_out = refs

    @pl.when(lax.axis_index("frame") == 0)
    def _():
        late_sums(*work, body_out, garm_out)

    @pl.when(lax.axis_index("frame") == 1)
    def _():
        body_out[...] = body_ref[...]
        garm_out[...] = garm_ref[...]


def final_kernel(garm_ref, body_ref, mine_ref, other_ref, garm_out, body_out, stiff_out):
    stiff_out[...] = mine_ref[...] + other_ref[...]
    body_out[...] = body_ref[...]
    garm_out[...] = garm_ref[...]


def stage_kernel(*refs):
    hbm, (index_ref, same_ref, other_ref, *out_refs) = refs[:7], refs[7:14]
    vmem, sems = refs[14:21], refs[21]
    copies = [
        pltpu.make_async_copy(src, dst, sems.at[k]) for k, (src, dst) in enumerate(zip(hbm, vmem))
    ]
    for copy in copies:
        copy.start()
    for copy in copies:
        copy.wait()
    pg_ref, pb_ref, pc_ref, garm_ref, cot_ref, body_ref, stiff_ref = vmem
    cap = pg_ref.shape[0]
    tiles = stiff_ref.shape[0]
    width = lax.axis_size("body")
    here, column = lax.axis_index("garm"), lax.axis_index("body")
    flips = (0, 3 - here // 2, 2 + here // 2, 1)
    for n, out_ref in enumerate(out_refs):
        place_z = here ^ flips[n]
        for q in range(3 * tiles):
            out_ref[5 + q] = body_ref[q]
        for q in range(tiles):
            out_ref[5 + 3 * tiles + q] = stiff_ref[q]
        for x in range(2):
            owner = place_z * width + (column ^ x)
            live = pc_ref[0, owner]
            for s in range(cap):
                g = pg_ref[s, owner]
                row, place = pl.ds(g, 1), pl.ds(x * cap + s, 1)
                for c in range(3):
                    out_ref[c, place, :] = garm_ref[c, row, :]
                out_ref[3, place, :] = jnp.where(s < live, cot_ref[row, :], 0.0)
                out_ref[4, place, :] = jnp.full((1, BLOCK), pb_ref[s, owner].astype(f32), f32)
                spot, line = 2 * x + n // 2, n % 2 * cap + s
                index_ref[spot, line : line + 1, :] = jnp.full((1, BLOCK), g.astype(f32), f32)
    for ref, other in ((same_ref, False), (other_ref, True)):
        for k, tile in enumerate(half_message(out_refs[3], other)):
            ref[k] = tile


def staged(garment, cotangent, body_points, stiffness, pg, pb, pc):
    verts = garment.shape[2]
    points = body_points.shape[2]
    blocks = points // BLOCK
    tiles = blocks // SUB
    garm_n = lax.axis_size("garm")
    message = jax.ShapeDtypeStruct((5 + 4 * tiles, SUB, BLOCK), f32)
    arrays = (
        pg,
        pb,
        pc,
        garment.reshape(3, verts // BLOCK, BLOCK),
        cotangent.reshape(verts // BLOCK, BLOCK),
        body_points.reshape(3 * tiles, SUB, BLOCK),
        stiffness.reshape(tiles, SUB, BLOCK),
    )
    half = jax.ShapeDtypeStruct((3 + 4 * tiles, SUB, BLOCK), f32)
    index, last_same, last_other, own, *sent = pl.pallas_call(
        stage_kernel,
        out_shape=[jax.ShapeDtypeStruct((garm_n, SUB, BLOCK), f32), half, half] + [message] * garm_n,
        in_specs=[pl.BlockSpec(memory_space=pltpu.HBM)] * len(arrays),
        out_specs=[pl.BlockSpec(memory_space=pltpu.VMEM)] * (garm_n + 3),
        scratch_shapes=[
            (pltpu.SMEM if k < 3 else pltpu.VMEM)(a.shape, a.dtype) for k, a in enumerate(arrays)
        ]
        + [pltpu.SemaphoreType.DMA((len(arrays),))],
        compiler_params=pltpu.CompilerParams(vmem_limit_bytes=VMEM_LIMIT),
    )(*[pltpu.with_memory_space_constraint(a, pltpu.HBM) for a in arrays])

    def along_garm(value, pairs):
        return lax.ppermute(value, "garm", pairs)

    def along_body(value):
        return lax.ppermute(value, "body", [(0, 1), (1, 0)])

    cycle = [(0, 2), (2, 1), (1, 3), (3, 0)]
    got = [
        along_garm(sent[1], cycle),
        along_garm(sent[0], [(b, a) for a, b in cycle]),
        along_garm(last_same, [(z, z ^ 1) for z in range(garm_n)]),
    ]
    direct = lax.ppermute(last_other, ("garm", "body"), [(n, n ^ 3) for n in range(2 * garm_n)])
    near_shape = jax.ShapeDtypeStruct((5 + 8 * tiles, SUB, BLOCK), f32)
    near = call(forward_kernel, near_shape, [], (), (own, got[0]), BUNDLE_COST)
    second = call(half_kernel, half, [], (), (got[1], near), BUNDLE_COST)
    near_other, second_other = along_body(near), along_body(second)

    def batch_shapes(count):
        return tuple(
            jax.ShapeDtypeStruct((count * SUB, width * BLOCK), f32) for width in (4, 1, 3)
        )

    bg1, bi1, gg1 = call(
        same_kernel, batch_shapes(2), [], (), (own, *sent, *got, second), SAME_COST
    )
    bg2, bi2 = call(
        near_kernel, batch_shapes(1)[:2], [], (), (own, near_other, bg1), NEAR_COST
    )
    body_shape = jax.ShapeDtypeStruct((3, blocks, BLOCK), f32)
    stiff_shape = jax.ShapeDtypeStruct((blocks, BLOCK), f32)
    garm_shape = jax.ShapeDtypeStruct((3, verts // BLOCK, BLOCK), f32)
    stiff = call(
        stiff_kernel, stiff_shape, [], (), (own, second_other, direct, bg1, bg2, bi1, bi2)
    )
    work = (own, *sent, near_other, second_other, direct, bg1, bg2, bi1, bi2, gg1, index)
    body_total, garm_total, stiff = call(
        before_kernel, (body_shape, garm_shape, stiff_shape), [], (), (*work, stiff)
    )
    stiff_other = lax.ppermute(stiff, "frame", [(0, 1), (1, 0)])
    body_total, garm_total = call(
        beside_kernel, (body_shape, garm_shape), [], (), (*work, body_total, garm_total)
    )
    return call(
        final_kernel,
        (garm_shape, body_shape, stiff_shape),
        [],
        (),
        (garm_total, body_total, stiff, stiff_other),
    )


def per_device(garment, cotangent, body_points, stiffness, pair_garment, pair_body, pair_count):
    owners = lax.axis_size(("garm", "body"))
    verts = garment.shape[2]
    points = body_points.shape[2]
    blocks = points // BLOCK
    cap = pair_garment.shape[3]
    slots = owners * cap
    pg = pair_garment.reshape(owners, cap).T
    pb = pair_body.reshape(owners, cap).T
    pc = pair_count.reshape(1, owners)
    if (lax.axis_size("garm"), lax.axis_size("body")) == (4, 2) and cap == SUB // 2:
        garm_grad, body_grad, stiff = staged(
            garment, cotangent, body_points, stiffness, pg, pb, pc
        )
        return (
            garm_grad.reshape(1, 3, verts),
            body_grad.reshape(1, 3, points),
            stiff.reshape(points),
        )
    message = call(
        pack_kernel,
        jax.ShapeDtypeStruct((owners, 5 + blocks, cap, BLOCK), f32),
        [],
        (pg, pb, pc),
        (
            garment.reshape(3, verts // BLOCK, BLOCK),
            cotangent.reshape(verts // BLOCK, BLOCK),
            body_points.reshape(3, blocks, BLOCK),
            stiffness.reshape(blocks, BLOCK),
        ),
    )
    arrived = lax.all_to_all(message, ("garm", "body"), split_axis=0, concat_axis=0, tiled=True)
    rows = pltpu.VMEM((4, slots, BLOCK), f32)
    grad = pltpu.VMEM((slots, 4 * BLOCK), f32)
    index = pltpu.VMEM((slots, BLOCK), f32)
    body_grad, stiff = call(
        body_kernel,
        (
            jax.ShapeDtypeStruct((3, blocks, BLOCK), f32),
            jax.ShapeDtypeStruct((blocks, BLOCK), f32),
        ),
        [rows, rows, pltpu.VMEM((blocks, 4 * BLOCK), f32), index, grad],
        (),
        (message, arrived),
    )
    other = lax.ppermute(stiff, "frame", [(0, 1), (1, 0)])
    garm_grad = call(
        garm_kernel,
        jax.ShapeDtypeStruct((3, verts // BLOCK, BLOCK), f32),
        [rows, rows, index, grad],
        (pg, pb),
        (message, arrived),
    )
    return (
        garm_grad.reshape(1, 3, verts),
        body_grad.reshape(1, 3, points),
        (stiff + other).reshape(points),
    )


def solution(mesh):
    in_specs = (
        P(("grp", "frame"), None, ("garm", "body")),
        P(("grp", "frame"), ("garm", "body")),
        P(("grp", "frame"), None, ("garm", "body")),
        P(("grp", "garm", "body")),
        P(("grp", "frame"), ("garm", "body"), None, None),
        P(("grp", "frame"), ("garm", "body"), None, None),
        P(("grp", "frame"), ("garm", "body"), None),
    )
    out_specs = (
        P(("grp", "frame"), None, ("garm", "body")),
        P(("grp", "frame"), None, ("garm", "body")),
        P(("grp", "garm", "body")),
    )
    return jax.shard_map(
        per_device, mesh=mesh, in_specs=in_specs, out_specs=out_specs, check_vma=False
    )
```

```python
import math

import jax
import jax.numpy as jnp
from jax import lax
from jax.experimental import pallas as pl
from jax.experimental.pallas import tpu as pltpu
from jax.sharding import PartitionSpec as P

BLOCK = 128
SUB = 8
VMEM_LIMIT = 32 * 1024 * 1024
SAME_COST = 40_000_000_000
NEAR_COST = 1_000_000_000
BUNDLE_COST = 1000

amplitude = 0.05
width_sq = 4.0

SCALE = math.sqrt(math.log2(math.e) / width_sq)
FACTOR = -2.0 / width_sq * amplitude

f32 = jnp.float32
bf16 = jnp.bfloat16


def pieces(value, count):
    out = []
    for _ in range(count - 1):
        top = value.astype(bf16).astype(f32)
        out.append(top)
        value = value - top
    out.append(value)
    return out


def features(left, right):
    lpos = [left[c] * SCALE for c in range(3)]
    rpos = [right[c] * SCALE for c in range(3)]
    lnorm = -(lpos[0] * lpos[0] + lpos[1] * lpos[1] + lpos[2] * lpos[2])
    rnorm = -(rpos[0] * rpos[0] + rpos[1] * rpos[1] + rpos[2] * rpos[2])
    one = jnp.ones_like(lnorm)
    lrows, rrows = [], []
    for c in range(3):
        l1, l2, l3 = pieces(lpos[c] * 2.0, 3)
        r1, r2, r3 = pieces(rpos[c], 3)
        lrows += [l1, l1, l2, l2, l1, l3]
        rrows += [r1, r2, r1, r2, r3, r1]
    lrows += pieces(lnorm, 3) + [one] * 3
    rrows += [one] * 3 + pieces(rnorm, 3)
    return (
        jnp.concatenate(lrows, axis=0).astype(bf16),
        jnp.concatenate(rrows, axis=0).astype(bf16),
    )


def pull(batches):
    made = []
    for left, right in batches:
        lfeat, rfeat = features(left, right)
        weight = left[3]
        coeff = [weight * left[c] for c in range(3)] + [weight]
        chi, clo = pieces(jnp.concatenate(coeff, axis=0), 2)
        lhs = jnp.concatenate(
            [
                jnp.concatenate([chi, chi], axis=1),
                jnp.concatenate([clo, jnp.zeros_like(clo)], axis=1),
            ],
            axis=0,
        ).astype(bf16)
        made.append((lfeat.T, rfeat, lhs))
    row = lax.broadcasted_iota(jnp.int32, made[0][1].shape, 0) % SUB
    count = made[0][2].shape[0] // 2
    sub = lax.broadcasted_iota(jnp.int32, (count, BLOCK), 0) % SUB
    totals = [jnp.zeros((count, BLOCK), f32) for _ in batches]

    def sums_of(pair, n, exponent):
        kernel = jnp.exp2(exponent)
        khi = kernel.astype(bf16)
        klo = (kernel - khi.astype(f32)).astype(bf16)
        sums = jnp.dot(made[n][2], jnp.concatenate([khi, klo], axis=0), preferred_element_type=f32)
        sums = sums[:count] + sums[count:]
        for k in range(2):
            part = sums[:, k * BLOCK : (k + 1) * BLOCK]
            totals[n] = jnp.where(sub == pair + k, part, totals[n])

    ahead = SUB // 2 if len(batches) == 1 else 0
    waiting = []
    for pair in range(0, SUB, 2):
        masks = [(row == pair + k).astype(f32).astype(bf16) for k in range(2)]
        for n, (lfeat_t, rfeat, _) in enumerate(made):
            rhs = jnp.concatenate([rfeat * mask for mask in masks], axis=1)
            waiting.append((pair, n, jnp.dot(lfeat_t, rhs, preferred_element_type=f32)))
            if len(waiting) > ahead:
                sums_of(*waiting.pop(0))
    for work in waiting:
        sums_of(*work)
    return [[total[c * SUB : (c + 1) * SUB] for c in range(count // SUB)] for total in totals]


def weigh(left, right):
    lfeat, rfeat = features(left, right)
    lfeat_t, weight_t = lfeat.T, left[3].T
    row = lax.broadcasted_iota(jnp.int32, rfeat.shape, 0) % SUB
    exponents = []
    for pair in range(0, SUB, 2):
        masks = [(row == pair + k).astype(f32).astype(bf16) for k in range(2)]
        rhs = jnp.concatenate([rfeat * mask for mask in masks], axis=1)
        exponents.append(jnp.dot(lfeat_t, rhs, preferred_element_type=f32))
    rows = []
    for n in range(SUB):
        kernel = jnp.exp2(exponents[n // 2][:, n % 2 * BLOCK : (n % 2 + 1) * BLOCK])
        rows.append(jnp.sum(kernel * weight_t[:, n : n + 1], axis=0, keepdims=True))
    return jnp.concatenate(rows, axis=0)


def gradients(batches):
    out = []
    for (_, right), total in zip(batches, pull(batches)):
        rows = [FACTOR * right[3] * (right[c] * total[3] - total[c]) for c in range(3)]
        out.append(rows + [amplitude * total[3]])
    return out


def run_batches(left_ref, right_ref, grad_ref):
    batches = left_ref.shape[1] // SUB
    group = math.gcd(batches, 4)

    def step(k, carry):
        places = [pl.ds(pl.multiple_of((k * group + n) * SUB, SUB), SUB) for n in range(group)]
        work = [
            tuple([ref[c, rows, :] for c in range(4)] for ref in (left_ref, right_ref))
            for rows in places
        ]
        for rows, values in zip(places, gradients(work)):
            for c, value in enumerate(values):
                grad_ref[rows, c * BLOCK : (c + 1) * BLOCK] = value
        return carry

    lax.fori_loop(0, batches // group, step, 0)


def scatter(index, grads, blocks):
    index = jnp.concatenate([index] * 3, axis=0)
    lane = lax.broadcasted_iota(jnp.int32, index.shape, 1).astype(f32)
    onehot_t = (index == lane).astype(f32).T[:blocks].astype(bf16)
    stack = jnp.concatenate(pieces(grads, 3), axis=0).astype(bf16)
    return jnp.dot(onehot_t, stack, preferred_element_type=f32)


def pack_kernel(pg_ref, pb_ref, pc_ref, garm_ref, cot_ref, body_ref, stiff_ref, out_ref):
    cap, owners = pg_ref.shape
    tiles = stiff_ref.shape[0] // cap

    def one(d, carry):
        for s in range(cap):
            row = pl.ds(pg_ref[s, d], 1)
            for c in range(3):
                out_ref[d, c, s : s + 1, :] = garm_ref[c, row, :]
            out_ref[d, 3, s : s + 1, :] = jnp.where(s < pc_ref[0, d], cot_ref[row, :], 0.0)
            out_ref[d, 4 + 4 * tiles, s : s + 1, :] = jnp.full(
                (1, BLOCK), pb_ref[s, d].astype(f32), f32
            )
        for q in range(tiles):
            rows = slice(q * cap, (q + 1) * cap)
            for c in range(3):
                out_ref[d, 4 + c * tiles + q] = body_ref[c, rows, :]
            out_ref[d, 4 + 3 * tiles + q] = stiff_ref[rows, :]
        return carry

    if owners <= 8:
        for d in range(owners):
            one(d, 0)
    else:
        lax.fori_loop(0, owners, one, 0)


def over(count, fn):
    if count <= 8:
        for d in range(count):
            fn(d)
    else:
        lax.fori_loop(0, count, lambda d, carry: (fn(d), carry)[1], 0)


def body_kernel(own_ref, in_ref, out_ref, stiff_ref, left, right, table, index, grad):
    owners, tiles, cap, _ = in_ref.shape
    blocks = tiles - 5

    def take(d):
        rows = pl.ds(d * cap, cap)
        for c in range(4):
            left[c, rows, :] = in_ref[d, c]
        index[rows, :] = in_ref[d, tiles - 1]

    over(owners, take)
    for c in range(4):
        for q in range(blocks // 4):
            table[4 * q : 4 * q + 4, c * BLOCK : (c + 1) * BLOCK] = own_ref[
                0, 4 + c * (blocks // 4) + q
            ]
    lane = lax.broadcasted_iota(jnp.int32, index.shape, 1).astype(f32)
    onehot = (index[...] == lane).astype(f32)[:, :blocks].astype(bf16)
    chosen = [
        jnp.dot(onehot, part.astype(bf16), preferred_element_type=f32)
        for part in pieces(table[...], 3)
    ]
    chosen = chosen[0] + chosen[1] + chosen[2]
    for c in range(4):
        right[c] = chosen[:, c * BLOCK : (c + 1) * BLOCK]
    run_batches(left, right, grad)
    total = scatter(index[...], grad[...], blocks)
    for c in range(3):
        out_ref[c] = total[:, c * BLOCK : (c + 1) * BLOCK]
    stiff_ref[...] = total[:, 3 * BLOCK :]


def garm_kernel(pg_ref, pb_ref, own_ref, in_ref, out_ref, left, right, index, grad):
    owners, tiles, cap, _ = in_ref.shape
    blocks = tiles - 5
    garm_blocks = out_ref.shape[1]

    def take(d):
        rows = pl.ds(d * cap, cap)
        for c in range(4):
            right[c, rows, :] = own_ref[d, c]
        for s in range(cap):
            b = pb_ref[s, d]
            for c in range(4):
                left[c, pl.ds(d * cap + s, 1), :] = in_ref[
                    d, 4 + c * (blocks // 4) + b // 4, pl.ds(b % 4, 1), :
                ]
            index[pl.ds(d * cap + s, 1), :] = jnp.full((1, BLOCK), pg_ref[s, d].astype(f32), f32)

    over(owners, take)
    run_batches(left, right, grad)
    total = scatter(index[...], grad[...], garm_blocks)
    for c in range(3):
        out_ref[c] = total[:, c * BLOCK : (c + 1) * BLOCK]


def call(kernel, out_shape, scratch, scalars, arrays, cost=None):
    specs = [pl.BlockSpec(memory_space=pltpu.SMEM)] * len(scalars)
    specs += [pl.BlockSpec(memory_space=pltpu.VMEM)] * len(arrays)
    return pl.pallas_call(
        kernel,
        out_shape=out_shape,
        in_specs=specs,
        out_specs=jax.tree.map(lambda _: pl.BlockSpec(memory_space=pltpu.VMEM), out_shape),
        scratch_shapes=scratch,
        cost_estimate=cost and pl.CostEstimate(flops=cost, bytes_accessed=1000, transcendentals=0),
        compiler_params=pltpu.CompilerParams(vmem_limit_bytes=VMEM_LIMIT),
    )(*scalars, *arrays)


def read_table(ref, start, step):
    columns = [
        jnp.concatenate([ref[start + c * step + q] for q in range(step)], axis=0) for c in range(4)
    ]
    return jnp.concatenate(columns, axis=1)


def choose(index, table):
    blocks = table.shape[0]
    lane = lax.broadcasted_iota(jnp.int32, index.shape, 1)
    onehot = (index == (lane % blocks).astype(f32)) & (lane < 3 * blocks)
    onehot = onehot.astype(f32)[:, : 3 * blocks].astype(bf16)
    stack = jnp.concatenate(pieces(table, 3), axis=0).astype(bf16)
    rows = jnp.dot(onehot, stack, preferred_element_type=f32)
    return [rows[:, c * BLOCK : (c + 1) * BLOCK] for c in range(4)]


def halves(top, bottom):
    row = lax.broadcasted_iota(jnp.int32, (SUB, BLOCK), 0)
    return jnp.where(row < SUB // 2, top, bottom)


def flip(value):
    return pltpu.roll(value, SUB // 2, 0)


def body_work(tiles, table):
    return list(tiles[:4]), choose(tiles[4], table)


def garm_work(tiles, top, bottom):
    row = lax.broadcasted_iota(jnp.int32, (SUB, BLOCK), 0)
    index = tiles[4] + jnp.where(row < SUB // 2, 0, top.shape[0]).astype(f32)
    return choose(index, jnp.concatenate([top, bottom], axis=0)), list(tiles[:4])


def slot_tiles(ref):
    return [ref[c] for c in range(5)]


def message_table(ref, step):
    return read_table(ref, 5, step)


def pack(tiles):
    a, b, c, d, e = tiles
    return [halves(a, flip(b)), halves(c, flip(d)), e]


def unpack_top(tiles):
    a, b, c = tiles
    return [a, flip(a), b, flip(b), c]


def unpack_bottom(tiles):
    a, b, c = tiles
    return [flip(a), a, flip(b), b, flip(c)]


def half_message(ref, other):
    slots = slot_tiles(ref)
    if other:
        slots = [flip(tile) for tile in slots]
    return [ref[5 + q] for q in range(ref.shape[0] - 5)] + pack(slots)


def forward_kernel(one_ref, two_ref, out_ref):
    body = one_ref.shape[0] - 5
    for n, ref in enumerate((one_ref, two_ref)):
        for q in range(body):
            out_ref[n * body + q] = ref[5 + q]
    for k, tile in enumerate(bottom_tiles(one_ref, two_ref)):
        out_ref[2 * body + k] = tile


def half_kernel(ref, after_ref, out_ref):
    del after_ref
    for k, tile in enumerate(half_message(ref, True)):
        out_ref[k] = tile


def top_tiles(one_ref, two_ref):
    return [halves(a, flip(b)) for a, b in zip(slot_tiles(one_ref), slot_tiles(two_ref))]


def bottom_tiles(one_ref, two_ref):
    return [halves(flip(a), b) for a, b in zip(slot_tiles(one_ref), slot_tiles(two_ref))]


def store(work, index, bgrad_ref, bindex_ref, ggrad_ref):
    out = gradients(work)
    for n, value in enumerate(index):
        rows = slice(n * SUB, (n + 1) * SUB)
        bgrad_ref[rows, :] = jnp.concatenate(out[n], axis=1)
        ggrad_ref[rows, :] = jnp.concatenate(out[len(index) + n][:3], axis=1)
        bindex_ref[rows, :] = value


def same_kernel(own_ref, sent0, sent1, sent2, got0, got1, got2, after_ref, *out_refs):
    del after_ref
    body = own_ref.shape[0] - 5
    step = body // 4
    own = message_table(own_ref, step)
    here = top_tiles(own_ref, got0)
    last = unpack_bottom([got2[body + k] for k in range(3)])
    there = [halves(x, y) for x, y in zip(slot_tiles(got1), last)]
    work = [
        body_work(here, own),
        body_work(there, own),
        garm_work(top_tiles(own_ref, sent0), own, message_table(got0, step)),
        garm_work(top_tiles(sent1, sent2), message_table(got1, step), read_table(got2, 0, step)),
    ]
    store(work, [here[4], there[4]], *out_refs)


def near_tiles(own_ref, near_ref):
    body = own_ref.shape[0] - 5
    return [near_ref[2 * body + k] for k in range(5)]


def late_tiles(own_ref, one_ref, two_ref):
    body = own_ref.shape[0] - 5
    top = unpack_top([one_ref[body + k] for k in range(3)])
    bottom = unpack_bottom([two_ref[body + k] for k in range(3)])
    return [halves(x, y) for x, y in zip(top, bottom)]


def near_kernel(own_ref, near_ref, after_ref, stiff_ref, bindex_ref):
    del after_ref
    tiles = near_tiles(own_ref, near_ref)
    own = message_table(own_ref, (own_ref.shape[0] - 5) // 4)
    stiff_ref[...] = amplitude * weigh(*body_work(tiles, own))
    bindex_ref[...] = tiles[4]


def stiff_kernel(own_ref, one_ref, two_ref, bg1, bg2, bi1, bi2, out_ref):
    tiles = late_tiles(own_ref, one_ref, two_ref)
    own = message_table(own_ref, (own_ref.shape[0] - 5) // 4)
    index = jnp.concatenate([bi1[...], bi2[...]], axis=0)
    grads = jnp.concatenate([bg1[:, 3 * BLOCK :], bg2[...]], axis=0)
    total = scatter(index, grads, out_ref.shape[0])
    last = amplitude * weigh(*body_work(tiles, own))
    block = lax.broadcasted_iota(jnp.int32, total.shape, 0).astype(f32)
    for n in range(SUB):
        total = total + jnp.where(block == tiles[4][n : n + 1], last[n : n + 1], 0.0)
    out_ref[...] = total


def late_sums(
    own_ref,
    sent0,
    sent1,
    sent2,
    near_ref,
    one_ref,
    two_ref,
    bg1,
    bi1,
    gg1,
    index_ref,
    body_out,
    garm_out,
):
    body = own_ref.shape[0] - 5
    step = body // 4
    tiles = late_tiles(own_ref, one_ref, two_ref)
    near = [read_table(near_ref, n * body, step) for n in range(2)]
    far = [read_table(ref, 0, step) for ref in (one_ref, two_ref)]
    first = near_tiles(own_ref, near_ref)
    own = message_table(own_ref, step)
    out = gradients(
        [
            body_work(first, own),
            body_work(tiles, own),
            garm_work(bottom_tiles(own_ref, sent0), *near),
            garm_work(bottom_tiles(sent1, sent2), *far),
        ]
    )
    rows = [jnp.concatenate(values[:3], axis=1) for values in out]
    index = jnp.concatenate([bi1[...], first[4], tiles[4]], axis=0)
    grads = jnp.concatenate([bg1[:, : 3 * BLOCK], rows[0], rows[1]], axis=0)
    total = scatter(index, grads, body_out.shape[1])
    for c in range(3):
        body_out[c] = total[:, c * BLOCK : (c + 1) * BLOCK]
    index = jnp.concatenate([index_ref[k] for k in range(index_ref.shape[0])], axis=0)
    grads = jnp.concatenate([gg1[...], rows[2], rows[3]], axis=0)
    total = scatter(index, grads, garm_out.shape[1])
    for c in range(3):
        garm_out[c] = total[:, c * BLOCK : (c + 1) * BLOCK]


def before_kernel(*refs):
    *work, stiff_ref, body_out, garm_out, stiff_out = refs
    stiff_out[...] = stiff_ref[...]

    @pl.when(lax.axis_index("frame") == 1)
    def _():
        late_sums(*work, body_out, garm_out)


def beside_kernel(*refs):
    *work, body_ref, garm_ref, body_out, garm_out = refs

    @pl.when(lax.axis_index("frame") == 0)
    def _():
        late_sums(*work, body_out, garm_out)

    @pl.when(lax.axis_index("frame") == 1)
    def _():
        body_out[...] = body_ref[...]
        garm_out[...] = garm_ref[...]


def final_kernel(garm_ref, body_ref, mine_ref, other_ref, garm_out, body_out, stiff_out):
    stiff_out[...] = mine_ref[...] + other_ref[...]
    body_out[...] = body_ref[...]
    garm_out[...] = garm_ref[...]


def stage_kernel(*refs):
    hbm, (index_ref, same_ref, other_ref, *out_refs) = refs[:7], refs[7:14]
    vmem, sems = refs[14:21], refs[21]
    copies = [
        pltpu.make_async_copy(src, dst, sems.at[k]) for k, (src, dst) in enumerate(zip(hbm, vmem))
    ]
    for copy in copies:
        copy.start()
    for copy in copies:
        copy.wait()
    pg_ref, pb_ref, pc_ref, garm_ref, cot_ref, body_ref, stiff_ref = vmem
    cap = pg_ref.shape[0]
    tiles = stiff_ref.shape[0]
    width = lax.axis_size("body")
    here, column = lax.axis_index("garm"), lax.axis_index("body")
    flips = (0, 3 - here // 2, 2 + here // 2, 1)
    for n, out_ref in enumerate(out_refs):
        place_z = here ^ flips[n]
        for q in range(3 * tiles):
            out_ref[5 + q] = body_ref[q]
        for q in range(tiles):
            out_ref[5 + 3 * tiles + q] = stiff_ref[q]
        for x in range(2):
            owner = place_z * width + (column ^ x)
            live = pc_ref[0, owner]
            for s in range(cap):
                g = pg_ref[s, owner]
                row, place = pl.ds(g, 1), pl.ds(x * cap + s, 1)
                for c in range(3):
                    out_ref[c, place, :] = garm_ref[c, row, :]
                out_ref[3, place, :] = jnp.where(s < live, cot_ref[row, :], 0.0)
                out_ref[4, place, :] = jnp.full((1, BLOCK), pb_ref[s, owner].astype(f32), f32)
                spot, line = 2 * x + n // 2, n % 2 * cap + s
                index_ref[spot, line : line + 1, :] = jnp.full((1, BLOCK), g.astype(f32), f32)
    for ref, other in ((same_ref, False), (other_ref, True)):
        for k, tile in enumerate(half_message(out_refs[3], other)):
            ref[k] = tile


def staged(garment, cotangent, body_points, stiffness, pg, pb, pc):
    verts = garment.shape[2]
    points = body_points.shape[2]
    blocks = points // BLOCK
    tiles = blocks // SUB
    garm_n = lax.axis_size("garm")
    message = jax.ShapeDtypeStruct((5 + 4 * tiles, SUB, BLOCK), f32)
    arrays = (
        pg,
        pb,
        pc,
        garment.reshape(3, verts // BLOCK, BLOCK),
        cotangent.reshape(verts // BLOCK, BLOCK),
        body_points.reshape(3 * tiles, SUB, BLOCK),
        stiffness.reshape(tiles, SUB, BLOCK),
    )
    half = jax.ShapeDtypeStruct((3 + 4 * tiles, SUB, BLOCK), f32)
    index, last_same, last_other, own, *sent = pl.pallas_call(
        stage_kernel,
        out_shape=[jax.ShapeDtypeStruct((garm_n, SUB, BLOCK), f32), half, half] + [message] * garm_n,
        in_specs=[pl.BlockSpec(memory_space=pltpu.HBM)] * len(arrays),
        out_specs=[pl.BlockSpec(memory_space=pltpu.VMEM)] * (garm_n + 3),
        scratch_shapes=[
            (pltpu.SMEM if k < 3 else pltpu.VMEM)(a.shape, a.dtype) for k, a in enumerate(arrays)
        ]
        + [pltpu.SemaphoreType.DMA((len(arrays),))],
        compiler_params=pltpu.CompilerParams(vmem_limit_bytes=VMEM_LIMIT),
    )(*[pltpu.with_memory_space_constraint(a, pltpu.HBM) for a in arrays])

    def along_garm(value, pairs):
        return lax.ppermute(value, "garm", pairs)

    def along_body(value):
        return lax.ppermute(value, "body", [(0, 1), (1, 0)])

    cycle = [(0, 2), (2, 1), (1, 3), (3, 0)]
    got = [
        along_garm(sent[1], cycle),
        along_garm(sent[0], [(b, a) for a, b in cycle]),
        along_garm(last_same, [(z, z ^ 1) for z in range(garm_n)]),
    ]
    direct = lax.ppermute(last_other, ("garm", "body"), [(n, n ^ 3) for n in range(2 * garm_n)])
    near_shape = jax.ShapeDtypeStruct((5 + 8 * tiles, SUB, BLOCK), f32)
    near = call(forward_kernel, near_shape, [], (), (own, got[0]), BUNDLE_COST)
    second = call(half_kernel, half, [], (), (got[1], near), BUNDLE_COST)
    near_other, second_other = along_body(near), along_body(second)

    def batch_shapes(count):
        return tuple(
            jax.ShapeDtypeStruct((count * SUB, width * BLOCK), f32) for width in (4, 1, 3)
        )

    bg1, bi1, gg1 = call(
        same_kernel, batch_shapes(2), [], (), (own, *sent, *got, second), SAME_COST
    )
    tile = jax.ShapeDtypeStruct((SUB, BLOCK), f32)
    bg2, bi2 = call(near_kernel, (tile, tile), [], (), (own, near_other, bg1), NEAR_COST)
    body_shape = jax.ShapeDtypeStruct((3, blocks, BLOCK), f32)
    stiff_shape = jax.ShapeDtypeStruct((blocks, BLOCK), f32)
    garm_shape = jax.ShapeDtypeStruct((3, verts // BLOCK, BLOCK), f32)
    stiff = call(
        stiff_kernel, stiff_shape, [], (), (own, second_other, direct, bg1, bg2, bi1, bi2)
    )
    work = (own, *sent, near_other, second_other, direct, bg1, bi1, gg1, index)
    body_total, garm_total, stiff = call(
        before_kernel, (body_shape, garm_shape, stiff_shape), [], (), (*work, stiff)
    )
    stiff_other = lax.ppermute(stiff, "frame", [(0, 1), (1, 0)])
    body_total, garm_total = call(
        beside_kernel, (body_shape, garm_shape), [], (), (*work, body_total, garm_total)
    )
    return call(
        final_kernel,
        (garm_shape, body_shape, stiff_shape),
        [],
        (),
        (garm_total, body_total, stiff, stiff_other),
    )


def per_device(garment, cotangent, body_points, stiffness, pair_garment, pair_body, pair_count):
    owners = lax.axis_size(("garm", "body"))
    verts = garment.shape[2]
    points = body_points.shape[2]
    blocks = points // BLOCK
    cap = pair_garment.shape[3]
    slots = owners * cap
    pg = pair_garment.reshape(owners, cap).T
    pb = pair_body.reshape(owners, cap).T
    pc = pair_count.reshape(1, owners)
    if (lax.axis_size("garm"), lax.axis_size("body")) == (4, 2) and cap == SUB // 2:
        garm_grad, body_grad, stiff = staged(
            garment, cotangent, body_points, stiffness, pg, pb, pc
        )
        return (
            garm_grad.reshape(1, 3, verts),
            body_grad.reshape(1, 3, points),
            stiff.reshape(points),
        )
    message = call(
        pack_kernel,
        jax.ShapeDtypeStruct((owners, 5 + blocks, cap, BLOCK), f32),
        [],
        (pg, pb, pc),
        (
            garment.reshape(3, verts // BLOCK, BLOCK),
            cotangent.reshape(verts // BLOCK, BLOCK),
            body_points.reshape(3, blocks, BLOCK),
            stiffness.reshape(blocks, BLOCK),
        ),
    )
    arrived = lax.all_to_all(message, ("garm", "body"), split_axis=0, concat_axis=0, tiled=True)
    rows = pltpu.VMEM((4, slots, BLOCK), f32)
    grad = pltpu.VMEM((slots, 4 * BLOCK), f32)
    index = pltpu.VMEM((slots, BLOCK), f32)
    body_grad, stiff = call(
        body_kernel,
        (
            jax.ShapeDtypeStruct((3, blocks, BLOCK), f32),
            jax.ShapeDtypeStruct((blocks, BLOCK), f32),
        ),
        [rows, rows, pltpu.VMEM((blocks, 4 * BLOCK), f32), index, grad],
        (),
        (message, arrived),
    )
    other = lax.ppermute(stiff, "frame", [(0, 1), (1, 0)])
    garm_grad = call(
        garm_kernel,
        jax.ShapeDtypeStruct((3, verts // BLOCK, BLOCK), f32),
        [rows, rows, index, grad],
        (pg, pb),
        (message, arrived),
    )
    return (
        garm_grad.reshape(1, 3, verts),
        body_grad.reshape(1, 3, points),
        (stiff + other).reshape(points),
    )


def solution(mesh):
    in_specs = (
        P(("grp", "frame"), None, ("garm", "body")),
        P(("grp", "frame"), ("garm", "body")),
        P(("grp", "frame"), None, ("garm", "body")),
        P(("grp", "garm", "body")),
        P(("grp", "frame"), ("garm", "body"), None, None),
        P(("grp", "frame"), ("garm", "body"), None, None),
        P(("grp", "frame"), ("garm", "body"), None),
    )
    out_specs = (
        P(("grp", "frame"), None, ("garm", "body")),
        P(("grp", "frame"), None, ("garm", "body")),
        P(("grp", "garm", "body")),
    )
    return jax.shard_map(
        per_device, mesh=mesh, in_specs=in_specs, out_specs=out_specs, check_vma=False
    )
```

```python
import math

import jax
import jax.numpy as jnp
from jax import lax
from jax.experimental import pallas as pl
from jax.experimental.pallas import tpu as pltpu
from jax.sharding import PartitionSpec as P

BLOCK = 128
SUB = 8
VMEM_LIMIT = 32 * 1024 * 1024
SAME_COST = 40_000_000_000
NEAR_COST = 1_000_000_000
BUNDLE_COST = 1000

amplitude = 0.05
width_sq = 4.0

SCALE = math.sqrt(math.log2(math.e) / width_sq)
FACTOR = -2.0 / width_sq * amplitude

f32 = jnp.float32
bf16 = jnp.bfloat16


def pieces(value, count):
    out = []
    for _ in range(count - 1):
        top = value.astype(bf16).astype(f32)
        out.append(top)
        value = value - top
    out.append(value)
    return out


def features(left, right):
    lpos = [left[c] * SCALE for c in range(3)]
    rpos = [right[c] * SCALE for c in range(3)]
    lnorm = -(lpos[0] * lpos[0] + lpos[1] * lpos[1] + lpos[2] * lpos[2])
    rnorm = -(rpos[0] * rpos[0] + rpos[1] * rpos[1] + rpos[2] * rpos[2])
    one = jnp.ones_like(lnorm)
    lrows, rrows = [], []
    for c in range(3):
        l1, l2, l3 = pieces(lpos[c] * 2.0, 3)
        r1, r2, r3 = pieces(rpos[c], 3)
        lrows += [l1, l1, l2, l2, l1, l3]
        rrows += [r1, r2, r1, r2, r3, r1]
    lrows += pieces(lnorm, 3) + [one] * 3
    rrows += [one] * 3 + pieces(rnorm, 3)
    return (
        jnp.concatenate(lrows, axis=0).astype(bf16),
        jnp.concatenate(rrows, axis=0).astype(bf16),
    )


def pull(batches):
    made = []
    for left, right in batches:
        lfeat, rfeat = features(left, right)
        weight = left[3]
        coeff = [weight * left[c] for c in range(3)] + [weight]
        chi, clo = pieces(jnp.concatenate(coeff, axis=0), 2)
        lhs = jnp.concatenate(
            [
                jnp.concatenate([chi, chi], axis=1),
                jnp.concatenate([clo, jnp.zeros_like(clo)], axis=1),
            ],
            axis=0,
        ).astype(bf16)
        made.append((lfeat.T, rfeat, lhs))
    row = lax.broadcasted_iota(jnp.int32, made[0][1].shape, 0) % SUB
    count = made[0][2].shape[0] // 2
    sub = lax.broadcasted_iota(jnp.int32, (count, BLOCK), 0) % SUB
    totals = [jnp.zeros((count, BLOCK), f32) for _ in batches]

    def sums_of(pair, n, exponent):
        kernel = jnp.exp2(exponent)
        khi = kernel.astype(bf16)
        klo = (kernel - khi.astype(f32)).astype(bf16)
        sums = jnp.dot(made[n][2], jnp.concatenate([khi, klo], axis=0), preferred_element_type=f32)
        sums = sums[:count] + sums[count:]
        for k in range(2):
            part = sums[:, k * BLOCK : (k + 1) * BLOCK]
            totals[n] = jnp.where(sub == pair + k, part, totals[n])

    ahead = SUB // 2 if len(batches) == 1 else 0
    waiting = []
    for pair in range(0, SUB, 2):
        masks = [(row == pair + k).astype(f32).astype(bf16) for k in range(2)]
        for n, (lfeat_t, rfeat, _) in enumerate(made):
            rhs = jnp.concatenate([rfeat * mask for mask in masks], axis=1)
            waiting.append((pair, n, jnp.dot(lfeat_t, rhs, preferred_element_type=f32)))
            if len(waiting) > ahead:
                sums_of(*waiting.pop(0))
    for work in waiting:
        sums_of(*work)
    return [[total[c * SUB : (c + 1) * SUB] for c in range(count // SUB)] for total in totals]


def weigh(left, right):
    lfeat, rfeat = features(left, right)
    lfeat_t, weight_t = lfeat.T, left[3].T
    row = lax.broadcasted_iota(jnp.int32, rfeat.shape, 0) % SUB
    exponents = []
    for pair in range(0, SUB, 2):
        masks = [(row == pair + k).astype(f32).astype(bf16) for k in range(2)]
        rhs = jnp.concatenate([rfeat * mask for mask in masks], axis=1)
        exponents.append(jnp.dot(lfeat_t, rhs, preferred_element_type=f32))
    rows = []
    for n in range(SUB):
        kernel = jnp.exp2(exponents[n // 2][:, n % 2 * BLOCK : (n % 2 + 1) * BLOCK])
        rows.append(jnp.sum(kernel * weight_t[:, n : n + 1], axis=0, keepdims=True))
    return jnp.concatenate(rows, axis=0)


def gradients(batches):
    out = []
    for (_, right), total in zip(batches, pull(batches)):
        rows = [FACTOR * right[3] * (right[c] * total[3] - total[c]) for c in range(3)]
        out.append(rows + [amplitude * total[3]])
    return out


def run_batches(left_ref, right_ref, grad_ref):
    batches = left_ref.shape[1] // SUB
    group = math.gcd(batches, 4)

    def step(k, carry):
        places = [pl.ds(pl.multiple_of((k * group + n) * SUB, SUB), SUB) for n in range(group)]
        work = [
            tuple([ref[c, rows, :] for c in range(4)] for ref in (left_ref, right_ref))
            for rows in places
        ]
        for rows, values in zip(places, gradients(work)):
            for c, value in enumerate(values):
                grad_ref[rows, c * BLOCK : (c + 1) * BLOCK] = value
        return carry

    lax.fori_loop(0, batches // group, step, 0)


def scatter(index, grads, blocks):
    index = jnp.concatenate([index] * 3, axis=0)
    lane = lax.broadcasted_iota(jnp.int32, index.shape, 1).astype(f32)
    onehot_t = (index == lane).astype(f32).T[:blocks].astype(bf16)
    stack = jnp.concatenate(pieces(grads, 3), axis=0).astype(bf16)
    return jnp.dot(onehot_t, stack, preferred_element_type=f32)


def pack_kernel(pg_ref, pb_ref, pc_ref, garm_ref, cot_ref, body_ref, stiff_ref, out_ref):
    cap, owners = pg_ref.shape
    tiles = stiff_ref.shape[0] // cap

    def one(d, carry):
        for s in range(cap):
            row = pl.ds(pg_ref[s, d], 1)
            for c in range(3):
                out_ref[d, c, s : s + 1, :] = garm_ref[c, row, :]
            out_ref[d, 3, s : s + 1, :] = jnp.where(s < pc_ref[0, d], cot_ref[row, :], 0.0)
            out_ref[d, 4 + 4 * tiles, s : s + 1, :] = jnp.full(
                (1, BLOCK), pb_ref[s, d].astype(f32), f32
            )
        for q in range(tiles):
            rows = slice(q * cap, (q + 1) * cap)
            for c in range(3):
                out_ref[d, 4 + c * tiles + q] = body_ref[c, rows, :]
            out_ref[d, 4 + 3 * tiles + q] = stiff_ref[rows, :]
        return carry

    if owners <= 8:
        for d in range(owners):
            one(d, 0)
    else:
        lax.fori_loop(0, owners, one, 0)


def over(count, fn):
    if count <= 8:
        for d in range(count):
            fn(d)
    else:
        lax.fori_loop(0, count, lambda d, carry: (fn(d), carry)[1], 0)


def body_kernel(own_ref, in_ref, out_ref, stiff_ref, left, right, table, index, grad):
    owners, tiles, cap, _ = in_ref.shape
    blocks = tiles - 5

    def take(d):
        rows = pl.ds(d * cap, cap)
        for c in range(4):
            left[c, rows, :] = in_ref[d, c]
        index[rows, :] = in_ref[d, tiles - 1]

    over(owners, take)
    for c in range(4):
        for q in range(blocks // 4):
            table[4 * q : 4 * q + 4, c * BLOCK : (c + 1) * BLOCK] = own_ref[
                0, 4 + c * (blocks // 4) + q
            ]
    lane = lax.broadcasted_iota(jnp.int32, index.shape, 1).astype(f32)
    onehot = (index[...] == lane).astype(f32)[:, :blocks].astype(bf16)
    chosen = [
        jnp.dot(onehot, part.astype(bf16), preferred_element_type=f32)
        for part in pieces(table[...], 3)
    ]
    chosen = chosen[0] + chosen[1] + chosen[2]
    for c in range(4):
        right[c] = chosen[:, c * BLOCK : (c + 1) * BLOCK]
    run_batches(left, right, grad)
    total = scatter(index[...], grad[...], blocks)
    for c in range(3):
        out_ref[c] = total[:, c * BLOCK : (c + 1) * BLOCK]
    stiff_ref[...] = total[:, 3 * BLOCK :]


def garm_kernel(pg_ref, pb_ref, own_ref, in_ref, out_ref, left, right, index, grad):
    owners, tiles, cap, _ = in_ref.shape
    blocks = tiles - 5
    garm_blocks = out_ref.shape[1]

    def take(d):
        rows = pl.ds(d * cap, cap)
        for c in range(4):
            right[c, rows, :] = own_ref[d, c]
        for s in range(cap):
            b = pb_ref[s, d]
            for c in range(4):
                left[c, pl.ds(d * cap + s, 1), :] = in_ref[
                    d, 4 + c * (blocks // 4) + b // 4, pl.ds(b % 4, 1), :
                ]
            index[pl.ds(d * cap + s, 1), :] = jnp.full((1, BLOCK), pg_ref[s, d].astype(f32), f32)

    over(owners, take)
    run_batches(left, right, grad)
    total = scatter(index[...], grad[...], garm_blocks)
    for c in range(3):
        out_ref[c] = total[:, c * BLOCK : (c + 1) * BLOCK]


def call(kernel, out_shape, scratch, scalars, arrays, cost=None):
    specs = [pl.BlockSpec(memory_space=pltpu.SMEM)] * len(scalars)
    specs += [pl.BlockSpec(memory_space=pltpu.VMEM)] * len(arrays)
    return pl.pallas_call(
        kernel,
        out_shape=out_shape,
        in_specs=specs,
        out_specs=jax.tree.map(lambda _: pl.BlockSpec(memory_space=pltpu.VMEM), out_shape),
        scratch_shapes=scratch,
        cost_estimate=cost and pl.CostEstimate(flops=cost, bytes_accessed=1000, transcendentals=0),
        compiler_params=pltpu.CompilerParams(vmem_limit_bytes=VMEM_LIMIT),
    )(*scalars, *arrays)


def read_table(ref, start, step):
    columns = [
        jnp.concatenate([ref[start + c * step + q] for q in range(step)], axis=0) for c in range(4)
    ]
    return jnp.concatenate(columns, axis=1)


def choose(index, table):
    blocks = table.shape[0]
    lane = lax.broadcasted_iota(jnp.int32, index.shape, 1)
    onehot = (index == (lane % blocks).astype(f32)) & (lane < 3 * blocks)
    onehot = onehot.astype(f32)[:, : 3 * blocks].astype(bf16)
    stack = jnp.concatenate(pieces(table, 3), axis=0).astype(bf16)
    rows = jnp.dot(onehot, stack, preferred_element_type=f32)
    return [rows[:, c * BLOCK : (c + 1) * BLOCK] for c in range(4)]


def halves(top, bottom):
    row = lax.broadcasted_iota(jnp.int32, (SUB, BLOCK), 0)
    return jnp.where(row < SUB // 2, top, bottom)


def flip(value):
    return pltpu.roll(value, SUB // 2, 0)


def body_work(tiles, table):
    return list(tiles[:4]), choose(tiles[4], table)


def garm_work(tiles, top, bottom):
    row = lax.broadcasted_iota(jnp.int32, (SUB, BLOCK), 0)
    index = tiles[4] + jnp.where(row < SUB // 2, 0, top.shape[0]).astype(f32)
    return choose(index, jnp.concatenate([top, bottom], axis=0)), list(tiles[:4])


def slot_tiles(ref):
    return [ref[c] for c in range(5)]


def message_table(ref, step):
    return read_table(ref, 5, step)


def pack(tiles):
    a, b, c, d, e = tiles
    return [halves(a, flip(b)), halves(c, flip(d)), e]


def unpack_top(tiles):
    a, b, c = tiles
    return [a, flip(a), b, flip(b), c]


def unpack_bottom(tiles):
    a, b, c = tiles
    return [flip(a), a, flip(b), b, flip(c)]


def half_message(ref, other):
    slots = slot_tiles(ref)
    if other:
        slots = [flip(tile) for tile in slots]
    return [ref[5 + q] for q in range(ref.shape[0] - 5)] + pack(slots)


def forward_kernel(one_ref, two_ref, out_ref):
    body = one_ref.shape[0] - 5
    for n, ref in enumerate((one_ref, two_ref)):
        for q in range(body):
            out_ref[n * body + q] = ref[5 + q]
    for k, tile in enumerate(bottom_tiles(one_ref, two_ref)):
        out_ref[2 * body + k] = tile


def half_kernel(ref, after_ref, out_ref):
    del after_ref
    for k, tile in enumerate(half_message(ref, True)):
        out_ref[k] = tile


def top_tiles(one_ref, two_ref):
    return [halves(a, flip(b)) for a, b in zip(slot_tiles(one_ref), slot_tiles(two_ref))]


def bottom_tiles(one_ref, two_ref):
    return [halves(flip(a), b) for a, b in zip(slot_tiles(one_ref), slot_tiles(two_ref))]


def store(work, index, bgrad_ref, bindex_ref, ggrad_ref):
    out = gradients(work)
    for n, value in enumerate(index):
        rows = slice(n * SUB, (n + 1) * SUB)
        bgrad_ref[rows, :] = jnp.concatenate(out[n], axis=1)
        ggrad_ref[rows, :] = jnp.concatenate(out[len(index) + n][:3], axis=1)
        bindex_ref[rows, :] = value


def same_kernel(own_ref, sent0, sent1, sent2, got0, got1, got2, after_ref, *out_refs):
    del after_ref
    body = own_ref.shape[0] - 5
    step = body // 4
    own = message_table(own_ref, step)
    here = top_tiles(own_ref, got0)
    last = unpack_bottom([got2[body + k] for k in range(3)])
    there = [halves(x, y) for x, y in zip(slot_tiles(got1), last)]
    work = [
        body_work(here, own),
        body_work(there, own),
        garm_work(top_tiles(own_ref, sent0), own, message_table(got0, step)),
        garm_work(top_tiles(sent1, sent2), message_table(got1, step), read_table(got2, 0, step)),
    ]
    store(work, [here[4], there[4]], *out_refs)


def near_tiles(own_ref, near_ref):
    body = own_ref.shape[0] - 5
    return [near_ref[2 * body + k] for k in range(5)]


def late_tiles(own_ref, one_ref, two_ref):
    body = own_ref.shape[0] - 5
    top = unpack_top([one_ref[body + k] for k in range(3)])
    bottom = unpack_bottom([two_ref[body + k] for k in range(3)])
    return [halves(x, y) for x, y in zip(top, bottom)]


def add_rows(total, index, rows):
    block = lax.broadcasted_iota(jnp.int32, total.shape, 0).astype(f32)
    for n in range(SUB):
        total = total + jnp.where(block == index[n : n + 1], rows[n : n + 1], 0.0)
    return total


def near_kernel(own_ref, near_ref, bg1, bi1, out_ref):
    tiles = near_tiles(own_ref, near_ref)
    own = message_table(own_ref, (own_ref.shape[0] - 5) // 4)
    total = scatter(bi1[...], bg1[:, 3 * BLOCK :], out_ref.shape[0])
    out_ref[...] = add_rows(total, tiles[4], amplitude * weigh(*body_work(tiles, own)))


def stiff_kernel(own_ref, one_ref, two_ref, total_ref, out_ref):
    tiles = late_tiles(own_ref, one_ref, two_ref)
    own = message_table(own_ref, (own_ref.shape[0] - 5) // 4)
    last = amplitude * weigh(*body_work(tiles, own))
    out_ref[...] = add_rows(total_ref[...], tiles[4], last)


def late_sums(
    own_ref,
    sent0,
    sent1,
    sent2,
    near_ref,
    one_ref,
    two_ref,
    bg1,
    bi1,
    gg1,
    index_ref,
    body_out,
    garm_out,
):
    body = own_ref.shape[0] - 5
    step = body // 4
    tiles = late_tiles(own_ref, one_ref, two_ref)
    near = [read_table(near_ref, n * body, step) for n in range(2)]
    far = [read_table(ref, 0, step) for ref in (one_ref, two_ref)]
    first = near_tiles(own_ref, near_ref)
    own = message_table(own_ref, step)
    out = gradients(
        [
            body_work(first, own),
            body_work(tiles, own),
            garm_work(bottom_tiles(own_ref, sent0), *near),
            garm_work(bottom_tiles(sent1, sent2), *far),
        ]
    )
    rows = [jnp.concatenate(values[:3], axis=1) for values in out]
    index = jnp.concatenate([bi1[...], first[4], tiles[4]], axis=0)
    grads = jnp.concatenate([bg1[:, : 3 * BLOCK], rows[0], rows[1]], axis=0)
    total = scatter(index, grads, body_out.shape[1])
    for c in range(3):
        body_out[c] = total[:, c * BLOCK : (c + 1) * BLOCK]
    index = jnp.concatenate([index_ref[k] for k in range(index_ref.shape[0])], axis=0)
    grads = jnp.concatenate([gg1[...], rows[2], rows[3]], axis=0)
    total = scatter(index, grads, garm_out.shape[1])
    for c in range(3):
        garm_out[c] = total[:, c * BLOCK : (c + 1) * BLOCK]


def before_kernel(*refs):
    *work, stiff_ref, body_out, garm_out, stiff_out = refs
    stiff_out[...] = stiff_ref[...]

    @pl.when(lax.axis_index("frame") == 1)
    def _():
        late_sums(*work, body_out, garm_out)


def beside_kernel(*refs):
    *work, body_ref, garm_ref, body_out, garm_out = refs

    @pl.when(lax.axis_index("frame") == 0)
    def _():
        late_sums(*work, body_out, garm_out)

    @pl.when(lax.axis_index("frame") == 1)
    def _():
        body_out[...] = body_ref[...]
        garm_out[...] = garm_ref[...]


def final_kernel(garm_ref, body_ref, mine_ref, other_ref, garm_out, body_out, stiff_out):
    stiff_out[...] = mine_ref[...] + other_ref[...]
    body_out[...] = body_ref[...]
    garm_out[...] = garm_ref[...]


def stage_kernel(*refs):
    hbm, (index_ref, same_ref, other_ref, *out_refs) = refs[:7], refs[7:14]
    vmem, sems = refs[14:21], refs[21]
    copies = [
        pltpu.make_async_copy(src, dst, sems.at[k]) for k, (src, dst) in enumerate(zip(hbm, vmem))
    ]
    for copy in copies:
        copy.start()
    for copy in copies:
        copy.wait()
    pg_ref, pb_ref, pc_ref, garm_ref, cot_ref, body_ref, stiff_ref = vmem
    cap = pg_ref.shape[0]
    tiles = stiff_ref.shape[0]
    width = lax.axis_size("body")
    here, column = lax.axis_index("garm"), lax.axis_index("body")
    flips = (0, 3 - here // 2, 2 + here // 2, 1)
    for n, out_ref in enumerate(out_refs):
        place_z = here ^ flips[n]
        for q in range(3 * tiles):
            out_ref[5 + q] = body_ref[q]
        for q in range(tiles):
            out_ref[5 + 3 * tiles + q] = stiff_ref[q]
        for x in range(2):
            owner = place_z * width + (column ^ x)
            live = pc_ref[0, owner]
            for s in range(cap):
                g = pg_ref[s, owner]
                row, place = pl.ds(g, 1), pl.ds(x * cap + s, 1)
                for c in range(3):
                    out_ref[c, place, :] = garm_ref[c, row, :]
                out_ref[3, place, :] = jnp.where(s < live, cot_ref[row, :], 0.0)
                out_ref[4, place, :] = jnp.full((1, BLOCK), pb_ref[s, owner].astype(f32), f32)
                spot, line = 2 * x + n // 2, n % 2 * cap + s
                index_ref[spot, line : line + 1, :] = jnp.full((1, BLOCK), g.astype(f32), f32)
    for ref, other in ((same_ref, False), (other_ref, True)):
        for k, tile in enumerate(half_message(out_refs[3], other)):
            ref[k] = tile


def staged(garment, cotangent, body_points, stiffness, pg, pb, pc):
    verts = garment.shape[2]
    points = body_points.shape[2]
    blocks = points // BLOCK
    tiles = blocks // SUB
    garm_n = lax.axis_size("garm")
    message = jax.ShapeDtypeStruct((5 + 4 * tiles, SUB, BLOCK), f32)
    arrays = (
        pg,
        pb,
        pc,
        garment.reshape(3, verts // BLOCK, BLOCK),
        cotangent.reshape(verts // BLOCK, BLOCK),
        body_points.reshape(3 * tiles, SUB, BLOCK),
        stiffness.reshape(tiles, SUB, BLOCK),
    )
    half = jax.ShapeDtypeStruct((3 + 4 * tiles, SUB, BLOCK), f32)
    index, last_same, last_other, own, *sent = pl.pallas_call(
        stage_kernel,
        out_shape=[jax.ShapeDtypeStruct((garm_n, SUB, BLOCK), f32), half, half] + [message] * garm_n,
        in_specs=[pl.BlockSpec(memory_space=pltpu.HBM)] * len(arrays),
        out_specs=[pl.BlockSpec(memory_space=pltpu.VMEM)] * (garm_n + 3),
        scratch_shapes=[
            (pltpu.SMEM if k < 3 else pltpu.VMEM)(a.shape, a.dtype) for k, a in enumerate(arrays)
        ]
        + [pltpu.SemaphoreType.DMA((len(arrays),))],
        compiler_params=pltpu.CompilerParams(vmem_limit_bytes=VMEM_LIMIT),
    )(*[pltpu.with_memory_space_constraint(a, pltpu.HBM) for a in arrays])

    def along_garm(value, pairs):
        return lax.ppermute(value, "garm", pairs)

    def along_body(value):
        return lax.ppermute(value, "body", [(0, 1), (1, 0)])

    cycle = [(0, 2), (2, 1), (1, 3), (3, 0)]
    got = [
        along_garm(sent[1], cycle),
        along_garm(sent[0], [(b, a) for a, b in cycle]),
        along_garm(last_same, [(z, z ^ 1) for z in range(garm_n)]),
    ]
    direct = lax.ppermute(last_other, ("garm", "body"), [(n, n ^ 3) for n in range(2 * garm_n)])
    near_shape = jax.ShapeDtypeStruct((5 + 8 * tiles, SUB, BLOCK), f32)
    near = call(forward_kernel, near_shape, [], (), (own, got[0]), BUNDLE_COST)
    second = call(half_kernel, half, [], (), (got[1], near), BUNDLE_COST)
    near_other, second_other = along_body(near), along_body(second)

    def batch_shapes(count):
        return tuple(
            jax.ShapeDtypeStruct((count * SUB, width * BLOCK), f32) for width in (4, 1, 3)
        )

    bg1, bi1, gg1 = call(
        same_kernel, batch_shapes(2), [], (), (own, *sent, *got, second), SAME_COST
    )
    body_shape = jax.ShapeDtypeStruct((3, blocks, BLOCK), f32)
    stiff_shape = jax.ShapeDtypeStruct((blocks, BLOCK), f32)
    garm_shape = jax.ShapeDtypeStruct((3, verts // BLOCK, BLOCK), f32)
    so_far = call(near_kernel, stiff_shape, [], (), (own, near_other, bg1, bi1), NEAR_COST)
    stiff = call(stiff_kernel, stiff_shape, [], (), (own, second_other, direct, so_far))
    work = (own, *sent, near_other, second_other, direct, bg1, bi1, gg1, index)
    body_total, garm_total, stiff = call(
        before_kernel, (body_shape, garm_shape, stiff_shape), [], (), (*work, stiff)
    )
    stiff_other = lax.ppermute(stiff, "frame", [(0, 1), (1, 0)])
    body_total, garm_total = call(
        beside_kernel, (body_shape, garm_shape), [], (), (*work, body_total, garm_total)
    )
    return call(
        final_kernel,
        (garm_shape, body_shape, stiff_shape),
        [],
        (),
        (garm_total, body_total, stiff, stiff_other),
    )


def per_device(garment, cotangent, body_points, stiffness, pair_garment, pair_body, pair_count):
    owners = lax.axis_size(("garm", "body"))
    verts = garment.shape[2]
    points = body_points.shape[2]
    blocks = points // BLOCK
    cap = pair_garment.shape[3]
    slots = owners * cap
    pg = pair_garment.reshape(owners, cap).T
    pb = pair_body.reshape(owners, cap).T
    pc = pair_count.reshape(1, owners)
    if (lax.axis_size("garm"), lax.axis_size("body")) == (4, 2) and cap == SUB // 2:
        garm_grad, body_grad, stiff = staged(
            garment, cotangent, body_points, stiffness, pg, pb, pc
        )
        return (
            garm_grad.reshape(1, 3, verts),
            body_grad.reshape(1, 3, points),
            stiff.reshape(points),
        )
    message = call(
        pack_kernel,
        jax.ShapeDtypeStruct((owners, 5 + blocks, cap, BLOCK), f32),
        [],
        (pg, pb, pc),
        (
            garment.reshape(3, verts // BLOCK, BLOCK),
            cotangent.reshape(verts // BLOCK, BLOCK),
            body_points.reshape(3, blocks, BLOCK),
            stiffness.reshape(blocks, BLOCK),
        ),
    )
    arrived = lax.all_to_all(message, ("garm", "body"), split_axis=0, concat_axis=0, tiled=True)
    rows = pltpu.VMEM((4, slots, BLOCK), f32)
    grad = pltpu.VMEM((slots, 4 * BLOCK), f32)
    index = pltpu.VMEM((slots, BLOCK), f32)
    body_grad, stiff = call(
        body_kernel,
        (
            jax.ShapeDtypeStruct((3, blocks, BLOCK), f32),
            jax.ShapeDtypeStruct((blocks, BLOCK), f32),
        ),
        [rows, rows, pltpu.VMEM((blocks, 4 * BLOCK), f32), index, grad],
        (),
        (message, arrived),
    )
    other = lax.ppermute(stiff, "frame", [(0, 1), (1, 0)])
    garm_grad = call(
        garm_kernel,
        jax.ShapeDtypeStruct((3, verts // BLOCK, BLOCK), f32),
        [rows, rows, index, grad],
        (pg, pb),
        (message, arrived),
    )
    return (
        garm_grad.reshape(1, 3, verts),
        body_grad.reshape(1, 3, points),
        (stiff + other).reshape(points),
    )


def solution(mesh):
    in_specs = (
        P(("grp", "frame"), None, ("garm", "body")),
        P(("grp", "frame"), ("garm", "body")),
        P(("grp", "frame"), None, ("garm", "body")),
        P(("grp", "garm", "body")),
        P(("grp", "frame"), ("garm", "body"), None, None),
        P(("grp", "frame"), ("garm", "body"), None, None),
        P(("grp", "frame"), ("garm", "body"), None),
    )
    out_specs = (
        P(("grp", "frame"), None, ("garm", "body")),
        P(("grp", "frame"), None, ("garm", "body")),
        P(("grp", "garm", "body")),
    )
    return jax.shard_map(
        per_device, mesh=mesh, in_specs=in_specs, out_specs=out_specs, check_vma=False
    )
```

```python
import math

import jax
import jax.numpy as jnp
from jax import lax
from jax.experimental import pallas as pl
from jax.experimental.pallas import tpu as pltpu
from jax.sharding import PartitionSpec as P

BLOCK = 128
SUB = 8
VMEM_LIMIT = 32 * 1024 * 1024
SAME_COST = 40_000_000_000
NEAR_COST = 1_000_000_000
BUNDLE_COST = 1000

amplitude = 0.05
width_sq = 4.0

SCALE = math.sqrt(math.log2(math.e) / width_sq)
FACTOR = -2.0 / width_sq * amplitude

f32 = jnp.float32
bf16 = jnp.bfloat16


def pieces(value, count):
    out = []
    for _ in range(count - 1):
        top = value.astype(bf16).astype(f32)
        out.append(top)
        value = value - top
    out.append(value)
    return out


def features(left, right):
    lpos = [left[c] * SCALE for c in range(3)]
    rpos = [right[c] * SCALE for c in range(3)]
    lnorm = -(lpos[0] * lpos[0] + lpos[1] * lpos[1] + lpos[2] * lpos[2])
    rnorm = -(rpos[0] * rpos[0] + rpos[1] * rpos[1] + rpos[2] * rpos[2])
    one = jnp.ones_like(lnorm)
    lrows, rrows = [], []
    for c in range(3):
        l1, l2, l3 = pieces(lpos[c] * 2.0, 3)
        r1, r2, r3 = pieces(rpos[c], 3)
        lrows += [l1, l1, l2, l2, l1, l3]
        rrows += [r1, r2, r1, r2, r3, r1]
    lrows += pieces(lnorm, 3) + [one] * 3
    rrows += [one] * 3 + pieces(rnorm, 3)
    return (
        jnp.concatenate(lrows, axis=0).astype(bf16),
        jnp.concatenate(rrows, axis=0).astype(bf16),
    )


def pull(batches):
    made = []
    for left, right in batches:
        lfeat, rfeat = features(left, right)
        weight = left[3]
        coeff = [weight * left[c] for c in range(3)] + [weight]
        chi, clo = pieces(jnp.concatenate(coeff, axis=0), 2)
        lhs = jnp.concatenate(
            [
                jnp.concatenate([chi, chi], axis=1),
                jnp.concatenate([clo, jnp.zeros_like(clo)], axis=1),
            ],
            axis=0,
        ).astype(bf16)
        made.append((lfeat.T, rfeat, lhs))
    row = lax.broadcasted_iota(jnp.int32, made[0][1].shape, 0) % SUB
    count = made[0][2].shape[0] // 2
    sub = lax.broadcasted_iota(jnp.int32, (count, BLOCK), 0) % SUB
    totals = [jnp.zeros((count, BLOCK), f32) for _ in batches]

    def sums_of(pair, n, exponent):
        kernel = jnp.exp2(exponent)
        khi = kernel.astype(bf16)
        klo = (kernel - khi.astype(f32)).astype(bf16)
        sums = jnp.dot(made[n][2], jnp.concatenate([khi, klo], axis=0), preferred_element_type=f32)
        sums = sums[:count] + sums[count:]
        for k in range(2):
            part = sums[:, k * BLOCK : (k + 1) * BLOCK]
            totals[n] = jnp.where(sub == pair + k, part, totals[n])

    ahead = SUB // 2 if len(batches) == 1 else 0
    waiting = []
    for pair in range(0, SUB, 2):
        masks = [(row == pair + k).astype(f32).astype(bf16) for k in range(2)]
        for n, (lfeat_t, rfeat, _) in enumerate(made):
            rhs = jnp.concatenate([rfeat * mask for mask in masks], axis=1)
            waiting.append((pair, n, jnp.dot(lfeat_t, rhs, preferred_element_type=f32)))
            if len(waiting) > ahead:
                sums_of(*waiting.pop(0))
    for work in waiting:
        sums_of(*work)
    return [[total[c * SUB : (c + 1) * SUB] for c in range(count // SUB)] for total in totals]


def weigh(left, right):
    lfeat, rfeat = features(left, right)
    lfeat_t, weight_t = lfeat.T, left[3].T
    row = lax.broadcasted_iota(jnp.int32, rfeat.shape, 0) % SUB
    exponents = []
    for pair in range(0, SUB, 2):
        masks = [(row == pair + k).astype(f32).astype(bf16) for k in range(2)]
        rhs = jnp.concatenate([rfeat * mask for mask in masks], axis=1)
        exponents.append(jnp.dot(lfeat_t, rhs, preferred_element_type=f32))
    rows = []
    for n in range(SUB):
        kernel = jnp.exp2(exponents[n // 2][:, n % 2 * BLOCK : (n % 2 + 1) * BLOCK])
        rows.append(jnp.sum(kernel * weight_t[:, n : n + 1], axis=0, keepdims=True))
    return jnp.concatenate(rows, axis=0)


def gradients(batches):
    out = []
    for (_, right), total in zip(batches, pull(batches)):
        rows = [FACTOR * right[3] * (right[c] * total[3] - total[c]) for c in range(3)]
        out.append(rows + [amplitude * total[3]])
    return out


def run_batches(left_ref, right_ref, grad_ref):
    batches = left_ref.shape[1] // SUB
    group = math.gcd(batches, 4)

    def step(k, carry):
        places = [pl.ds(pl.multiple_of((k * group + n) * SUB, SUB), SUB) for n in range(group)]
        work = [
            tuple([ref[c, rows, :] for c in range(4)] for ref in (left_ref, right_ref))
            for rows in places
        ]
        for rows, values in zip(places, gradients(work)):
            for c, value in enumerate(values):
                grad_ref[rows, c * BLOCK : (c + 1) * BLOCK] = value
        return carry

    lax.fori_loop(0, batches // group, step, 0)


def scatter(index, grads, blocks):
    index = jnp.concatenate([index] * 3, axis=0)
    lane = lax.broadcasted_iota(jnp.int32, index.shape, 1).astype(f32)
    onehot_t = (index == lane).astype(f32).T[:blocks].astype(bf16)
    stack = jnp.concatenate(pieces(grads, 3), axis=0).astype(bf16)
    return jnp.dot(onehot_t, stack, preferred_element_type=f32)


def pack_kernel(pg_ref, pb_ref, pc_ref, garm_ref, cot_ref, body_ref, stiff_ref, out_ref):
    cap, owners = pg_ref.shape
    tiles = stiff_ref.shape[0] // cap

    def one(d, carry):
        for s in range(cap):
            row = pl.ds(pg_ref[s, d], 1)
            for c in range(3):
                out_ref[d, c, s : s + 1, :] = garm_ref[c, row, :]
            out_ref[d, 3, s : s + 1, :] = jnp.where(s < pc_ref[0, d], cot_ref[row, :], 0.0)
            out_ref[d, 4 + 4 * tiles, s : s + 1, :] = jnp.full(
                (1, BLOCK), pb_ref[s, d].astype(f32), f32
            )
        for q in range(tiles):
            rows = slice(q * cap, (q + 1) * cap)
            for c in range(3):
                out_ref[d, 4 + c * tiles + q] = body_ref[c, rows, :]
            out_ref[d, 4 + 3 * tiles + q] = stiff_ref[rows, :]
        return carry

    if owners <= 8:
        for d in range(owners):
            one(d, 0)
    else:
        lax.fori_loop(0, owners, one, 0)


def over(count, fn):
    if count <= 8:
        for d in range(count):
            fn(d)
    else:
        lax.fori_loop(0, count, lambda d, carry: (fn(d), carry)[1], 0)


def body_kernel(own_ref, in_ref, out_ref, stiff_ref, left, right, table, index, grad):
    owners, tiles, cap, _ = in_ref.shape
    blocks = tiles - 5

    def take(d):
        rows = pl.ds(d * cap, cap)
        for c in range(4):
            left[c, rows, :] = in_ref[d, c]
        index[rows, :] = in_ref[d, tiles - 1]

    over(owners, take)
    for c in range(4):
        for q in range(blocks // 4):
            table[4 * q : 4 * q + 4, c * BLOCK : (c + 1) * BLOCK] = own_ref[
                0, 4 + c * (blocks // 4) + q
            ]
    lane = lax.broadcasted_iota(jnp.int32, index.shape, 1).astype(f32)
    onehot = (index[...] == lane).astype(f32)[:, :blocks].astype(bf16)
    chosen = [
        jnp.dot(onehot, part.astype(bf16), preferred_element_type=f32)
        for part in pieces(table[...], 3)
    ]
    chosen = chosen[0] + chosen[1] + chosen[2]
    for c in range(4):
        right[c] = chosen[:, c * BLOCK : (c + 1) * BLOCK]
    run_batches(left, right, grad)
    total = scatter(index[...], grad[...], blocks)
    for c in range(3):
        out_ref[c] = total[:, c * BLOCK : (c + 1) * BLOCK]
    stiff_ref[...] = total[:, 3 * BLOCK :]


def garm_kernel(pg_ref, pb_ref, own_ref, in_ref, out_ref, left, right, index, grad):
    owners, tiles, cap, _ = in_ref.shape
    blocks = tiles - 5
    garm_blocks = out_ref.shape[1]

    def take(d):
        rows = pl.ds(d * cap, cap)
        for c in range(4):
            right[c, rows, :] = own_ref[d, c]
        for s in range(cap):
            b = pb_ref[s, d]
            for c in range(4):
                left[c, pl.ds(d * cap + s, 1), :] = in_ref[
                    d, 4 + c * (blocks // 4) + b // 4, pl.ds(b % 4, 1), :
                ]
            index[pl.ds(d * cap + s, 1), :] = jnp.full((1, BLOCK), pg_ref[s, d].astype(f32), f32)

    over(owners, take)
    run_batches(left, right, grad)
    total = scatter(index[...], grad[...], garm_blocks)
    for c in range(3):
        out_ref[c] = total[:, c * BLOCK : (c + 1) * BLOCK]


def call(kernel, out_shape, scratch, scalars, arrays, cost=None):
    specs = [pl.BlockSpec(memory_space=pltpu.SMEM)] * len(scalars)
    specs += [pl.BlockSpec(memory_space=pltpu.VMEM)] * len(arrays)
    return pl.pallas_call(
        kernel,
        out_shape=out_shape,
        in_specs=specs,
        out_specs=jax.tree.map(lambda _: pl.BlockSpec(memory_space=pltpu.VMEM), out_shape),
        scratch_shapes=scratch,
        cost_estimate=cost and pl.CostEstimate(flops=cost, bytes_accessed=1000, transcendentals=0),
        compiler_params=pltpu.CompilerParams(vmem_limit_bytes=VMEM_LIMIT),
    )(*scalars, *arrays)


def read_table(ref, start, step):
    columns = [
        jnp.concatenate([ref[start + c * step + q] for q in range(step)], axis=0) for c in range(4)
    ]
    return jnp.concatenate(columns, axis=1)


def choose(index, table):
    blocks = table.shape[0]
    lane = lax.broadcasted_iota(jnp.int32, index.shape, 1)
    onehot = (index == (lane % blocks).astype(f32)) & (lane < 3 * blocks)
    onehot = onehot.astype(f32)[:, : 3 * blocks].astype(bf16)
    stack = jnp.concatenate(pieces(table, 3), axis=0).astype(bf16)
    rows = jnp.dot(onehot, stack, preferred_element_type=f32)
    return [rows[:, c * BLOCK : (c + 1) * BLOCK] for c in range(table.shape[1] // BLOCK)]


def halves(top, bottom):
    row = lax.broadcasted_iota(jnp.int32, (SUB, BLOCK), 0)
    return jnp.where(row < SUB // 2, top, bottom)


def flip(value):
    return pltpu.roll(value, SUB // 2, 0)


def body_work(tiles, table):
    return list(tiles[:4]), choose(tiles[4], table)


def garm_work(tiles, top, bottom):
    row = lax.broadcasted_iota(jnp.int32, (SUB, BLOCK), 0)
    index = tiles[4] + jnp.where(row < SUB // 2, 0, top.shape[0]).astype(f32)
    return choose(index, jnp.concatenate([top, bottom], axis=0)), list(tiles[:4])


def slot_tiles(ref):
    return [ref[c] for c in range(5)]


def message_table(ref, step):
    return read_table(ref, 5, step)


def pack(tiles):
    a, b, c, d, e = tiles
    return [halves(a, flip(b)), halves(c, flip(d)), e]


def unpack_top(tiles):
    a, b, c = tiles
    return [a, flip(a), b, flip(b), c]


def unpack_bottom(tiles):
    a, b, c = tiles
    return [flip(a), a, flip(b), b, flip(c)]


def half_message(ref, other):
    slots = slot_tiles(ref)
    if other:
        slots = [flip(tile) for tile in slots]
    return [ref[5 + q] for q in range(ref.shape[0] - 5)] + pack(slots)


def forward_kernel(one_ref, two_ref, out_ref):
    body = one_ref.shape[0] - 5
    for n, ref in enumerate((one_ref, two_ref)):
        for q in range(body):
            out_ref[n * body + q] = ref[5 + q]
    for k, tile in enumerate(bottom_tiles(one_ref, two_ref)):
        out_ref[2 * body + k] = tile


def half_kernel(ref, after_ref, out_ref):
    del after_ref
    for k, tile in enumerate(half_message(ref, True)):
        out_ref[k] = tile


def top_tiles(one_ref, two_ref):
    return [halves(a, flip(b)) for a, b in zip(slot_tiles(one_ref), slot_tiles(two_ref))]


def bottom_tiles(one_ref, two_ref):
    return [halves(flip(a), b) for a, b in zip(slot_tiles(one_ref), slot_tiles(two_ref))]


def store(work, index, bgrad_ref, bindex_ref, ggrad_ref):
    out = gradients(work)
    for n, value in enumerate(index):
        rows = slice(n * SUB, (n + 1) * SUB)
        bgrad_ref[rows, :] = jnp.concatenate(out[n], axis=1)
        ggrad_ref[rows, :] = jnp.concatenate(out[len(index) + n][:3], axis=1)
        bindex_ref[rows, :] = value


def same_kernel(own_ref, sent0, sent1, sent2, got0, got1, got2, after_ref, *out_refs):
    del after_ref
    body = own_ref.shape[0] - 5
    step = body // 4
    own = message_table(own_ref, step)
    here = top_tiles(own_ref, got0)
    last = unpack_bottom([got2[body + k] for k in range(3)])
    there = [halves(x, y) for x, y in zip(slot_tiles(got1), last)]
    work = [
        body_work(here, own),
        body_work(there, own),
        garm_work(top_tiles(own_ref, sent0), own, message_table(got0, step)),
        garm_work(top_tiles(sent1, sent2), message_table(got1, step), read_table(got2, 0, step)),
    ]
    store(work, [here[4], there[4]], *out_refs)


def near_tiles(own_ref, near_ref):
    body = own_ref.shape[0] - 5
    return [near_ref[2 * body + k] for k in range(5)]


def late_tiles(own_ref, one_ref, two_ref):
    body = own_ref.shape[0] - 5
    top = unpack_top([one_ref[body + k] for k in range(3)])
    bottom = unpack_bottom([two_ref[body + k] for k in range(3)])
    return [halves(x, y) for x, y in zip(top, bottom)]


def near_kernel(own_ref, near_ref, after_ref, stiff_ref, bindex_ref):
    del after_ref
    tiles = near_tiles(own_ref, near_ref)
    own = message_table(own_ref, (own_ref.shape[0] - 5) // 4)
    stiff_ref[...] = amplitude * weigh(*body_work(tiles, own[:, : 3 * BLOCK]))
    bindex_ref[...] = tiles[4]


def stiff_kernel(own_ref, one_ref, two_ref, bg1, bg2, bi1, bi2, out_ref):
    tiles = late_tiles(own_ref, one_ref, two_ref)
    own = message_table(own_ref, (own_ref.shape[0] - 5) // 4)
    index = jnp.concatenate([bi1[...], bi2[...]], axis=0)
    grads = jnp.concatenate([bg1[:, 3 * BLOCK :], bg2[...]], axis=0)
    total = scatter(index, grads, out_ref.shape[0])
    last = amplitude * weigh(*body_work(tiles, own[:, : 3 * BLOCK]))
    block = lax.broadcasted_iota(jnp.int32, total.shape, 0).astype(f32)
    for n in range(SUB):
        total = total + jnp.where(block == tiles[4][n : n + 1], last[n : n + 1], 0.0)
    out_ref[...] = total


def late_sums(
    own_ref,
    sent0,
    sent1,
    sent2,
    near_ref,
    one_ref,
    two_ref,
    bg1,
    bi1,
    gg1,
    index_ref,
    body_out,
    garm_out,
):
    body = own_ref.shape[0] - 5
    step = body // 4
    tiles = late_tiles(own_ref, one_ref, two_ref)
    near = [read_table(near_ref, n * body, step) for n in range(2)]
    far = [read_table(ref, 0, step) for ref in (one_ref, two_ref)]
    first = near_tiles(own_ref, near_ref)
    own = message_table(own_ref, step)
    out = gradients(
        [
            body_work(first, own),
            body_work(tiles, own),
            garm_work(bottom_tiles(own_ref, sent0), *near),
            garm_work(bottom_tiles(sent1, sent2), *far),
        ]
    )
    rows = [jnp.concatenate(values[:3], axis=1) for values in out]
    index = jnp.concatenate([bi1[...], first[4], tiles[4]], axis=0)
    grads = jnp.concatenate([bg1[:, : 3 * BLOCK], rows[0], rows[1]], axis=0)
    total = scatter(index, grads, body_out.shape[1])
    for c in range(3):
        body_out[c] = total[:, c * BLOCK : (c + 1) * BLOCK]
    index = jnp.concatenate([index_ref[k] for k in range(index_ref.shape[0])], axis=0)
    grads = jnp.concatenate([gg1[...], rows[2], rows[3]], axis=0)
    total = scatter(index, grads, garm_out.shape[1])
    for c in range(3):
        garm_out[c] = total[:, c * BLOCK : (c + 1) * BLOCK]


def before_kernel(*refs):
    *work, stiff_ref, body_out, garm_out, stiff_out = refs
    stiff_out[...] = stiff_ref[...]

    @pl.when(lax.axis_index("frame") == 1)
    def _():
        late_sums(*work, body_out, garm_out)


def beside_kernel(*refs):
    *work, body_ref, garm_ref, body_out, garm_out = refs

    @pl.when(lax.axis_index("frame") == 0)
    def _():
        late_sums(*work, body_out, garm_out)

    @pl.when(lax.axis_index("frame") == 1)
    def _():
        body_out[...] = body_ref[...]
        garm_out[...] = garm_ref[...]


def final_kernel(garm_ref, body_ref, mine_ref, other_ref, garm_out, body_out, stiff_out):
    stiff_out[...] = mine_ref[...] + other_ref[...]
    body_out[...] = body_ref[...]
    garm_out[...] = garm_ref[...]


def stage_kernel(*refs):
    hbm, (index_ref, same_ref, other_ref, *out_refs) = refs[:7], refs[7:14]
    vmem, sems = refs[14:21], refs[21]
    copies = [
        pltpu.make_async_copy(src, dst, sems.at[k]) for k, (src, dst) in enumerate(zip(hbm, vmem))
    ]
    for copy in copies:
        copy.start()
    for copy in copies:
        copy.wait()
    pg_ref, pb_ref, pc_ref, garm_ref, cot_ref, body_ref, stiff_ref = vmem
    cap = pg_ref.shape[0]
    tiles = stiff_ref.shape[0]
    width = lax.axis_size("body")
    here, column = lax.axis_index("garm"), lax.axis_index("body")
    flips = (0, 3 - here // 2, 2 + here // 2, 1)
    for n, out_ref in enumerate(out_refs):
        place_z = here ^ flips[n]
        for q in range(3 * tiles):
            out_ref[5 + q] = body_ref[q]
        for q in range(tiles):
            out_ref[5 + 3 * tiles + q] = stiff_ref[q]
        for x in range(2):
            owner = place_z * width + (column ^ x)
            live = pc_ref[0, owner]
            for s in range(cap):
                g = pg_ref[s, owner]
                row, place = pl.ds(g, 1), pl.ds(x * cap + s, 1)
                for c in range(3):
                    out_ref[c, place, :] = garm_ref[c, row, :]
                out_ref[3, place, :] = jnp.where(s < live, cot_ref[row, :], 0.0)
                out_ref[4, place, :] = jnp.full((1, BLOCK), pb_ref[s, owner].astype(f32), f32)
                spot, line = 2 * x + n // 2, n % 2 * cap + s
                index_ref[spot, line : line + 1, :] = jnp.full((1, BLOCK), g.astype(f32), f32)
    for ref, other in ((same_ref, False), (other_ref, True)):
        for k, tile in enumerate(half_message(out_refs[3], other)):
            ref[k] = tile


def staged(garment, cotangent, body_points, stiffness, pg, pb, pc):
    verts = garment.shape[2]
    points = body_points.shape[2]
    blocks = points // BLOCK
    tiles = blocks // SUB
    garm_n = lax.axis_size("garm")
    message = jax.ShapeDtypeStruct((5 + 4 * tiles, SUB, BLOCK), f32)
    arrays = (
        pg,
        pb,
        pc,
        garment.reshape(3, verts // BLOCK, BLOCK),
        cotangent.reshape(verts // BLOCK, BLOCK),
        body_points.reshape(3 * tiles, SUB, BLOCK),
        stiffness.reshape(tiles, SUB, BLOCK),
    )
    half = jax.ShapeDtypeStruct((3 + 4 * tiles, SUB, BLOCK), f32)
    index, last_same, last_other, own, *sent = pl.pallas_call(
        stage_kernel,
        out_shape=[jax.ShapeDtypeStruct((garm_n, SUB, BLOCK), f32), half, half] + [message] * garm_n,
        in_specs=[pl.BlockSpec(memory_space=pltpu.HBM)] * len(arrays),
        out_specs=[pl.BlockSpec(memory_space=pltpu.VMEM)] * (garm_n + 3),
        scratch_shapes=[
            (pltpu.SMEM if k < 3 else pltpu.VMEM)(a.shape, a.dtype) for k, a in enumerate(arrays)
        ]
        + [pltpu.SemaphoreType.DMA((len(arrays),))],
        compiler_params=pltpu.CompilerParams(vmem_limit_bytes=VMEM_LIMIT),
    )(*[pltpu.with_memory_space_constraint(a, pltpu.HBM) for a in arrays])

    def along_garm(value, pairs):
        return lax.ppermute(value, "garm", pairs)

    def along_body(value):
        return lax.ppermute(value, "body", [(0, 1), (1, 0)])

    cycle = [(0, 2), (2, 1), (1, 3), (3, 0)]
    got = [
        along_garm(sent[1], cycle),
        along_garm(sent[0], [(b, a) for a, b in cycle]),
        along_garm(last_same, [(z, z ^ 1) for z in range(garm_n)]),
    ]
    direct = lax.ppermute(last_other, ("garm", "body"), [(n, n ^ 3) for n in range(2 * garm_n)])
    near_shape = jax.ShapeDtypeStruct((5 + 8 * tiles, SUB, BLOCK), f32)
    near = call(forward_kernel, near_shape, [], (), (own, got[0]), BUNDLE_COST)
    second = call(half_kernel, half, [], (), (got[1], near), BUNDLE_COST)
    near_other, second_other = along_body(near), along_body(second)

    def batch_shapes(count):
        return tuple(
            jax.ShapeDtypeStruct((count * SUB, width * BLOCK), f32) for width in (4, 1, 3)
        )

    bg1, bi1, gg1 = call(
        same_kernel, batch_shapes(2), [], (), (own, *sent, *got, second), SAME_COST
    )
    tile = jax.ShapeDtypeStruct((SUB, BLOCK), f32)
    bg2, bi2 = call(near_kernel, (tile, tile), [], (), (own, near_other, bg1), NEAR_COST)
    body_shape = jax.ShapeDtypeStruct((3, blocks, BLOCK), f32)
    stiff_shape = jax.ShapeDtypeStruct((blocks, BLOCK), f32)
    garm_shape = jax.ShapeDtypeStruct((3, verts // BLOCK, BLOCK), f32)
    stiff = call(
        stiff_kernel, stiff_shape, [], (), (own, second_other, direct, bg1, bg2, bi1, bi2)
    )
    work = (own, *sent, near_other, second_other, direct, bg1, bi1, gg1, index)
    body_total, garm_total, stiff = call(
        before_kernel, (body_shape, garm_shape, stiff_shape), [], (), (*work, stiff)
    )
    stiff_other = lax.ppermute(stiff, "frame", [(0, 1), (1, 0)])
    body_total, garm_total = call(
        beside_kernel, (body_shape, garm_shape), [], (), (*work, body_total, garm_total)
    )
    return call(
        final_kernel,
        (garm_shape, body_shape, stiff_shape),
        [],
        (),
        (garm_total, body_total, stiff, stiff_other),
    )


def per_device(garment, cotangent, body_points, stiffness, pair_garment, pair_body, pair_count):
    owners = lax.axis_size(("garm", "body"))
    verts = garment.shape[2]
    points = body_points.shape[2]
    blocks = points // BLOCK
    cap = pair_garment.shape[3]
    slots = owners * cap
    pg = pair_garment.reshape(owners, cap).T
    pb = pair_body.reshape(owners, cap).T
    pc = pair_count.reshape(1, owners)
    if (lax.axis_size("garm"), lax.axis_size("body")) == (4, 2) and cap == SUB // 2:
        garm_grad, body_grad, stiff = staged(
            garment, cotangent, body_points, stiffness, pg, pb, pc
        )
        return (
            garm_grad.reshape(1, 3, verts),
            body_grad.reshape(1, 3, points),
            stiff.reshape(points),
        )
    message = call(
        pack_kernel,
        jax.ShapeDtypeStruct((owners, 5 + blocks, cap, BLOCK), f32),
        [],
        (pg, pb, pc),
        (
            garment.reshape(3, verts // BLOCK, BLOCK),
            cotangent.reshape(verts // BLOCK, BLOCK),
            body_points.reshape(3, blocks, BLOCK),
            stiffness.reshape(blocks, BLOCK),
        ),
    )
    arrived = lax.all_to_all(message, ("garm", "body"), split_axis=0, concat_axis=0, tiled=True)
    rows = pltpu.VMEM((4, slots, BLOCK), f32)
    grad = pltpu.VMEM((slots, 4 * BLOCK), f32)
    index = pltpu.VMEM((slots, BLOCK), f32)
    body_grad, stiff = call(
        body_kernel,
        (
            jax.ShapeDtypeStruct((3, blocks, BLOCK), f32),
            jax.ShapeDtypeStruct((blocks, BLOCK), f32),
        ),
        [rows, rows, pltpu.VMEM((blocks, 4 * BLOCK), f32), index, grad],
        (),
        (message, arrived),
    )
    other = lax.ppermute(stiff, "frame", [(0, 1), (1, 0)])
    garm_grad = call(
        garm_kernel,
        jax.ShapeDtypeStruct((3, verts // BLOCK, BLOCK), f32),
        [rows, rows, index, grad],
        (pg, pb),
        (message, arrived),
    )
    return (
        garm_grad.reshape(1, 3, verts),
        body_grad.reshape(1, 3, points),
        (stiff + other).reshape(points),
    )


def solution(mesh):
    in_specs = (
        P(("grp", "frame"), None, ("garm", "body")),
        P(("grp", "frame"), ("garm", "body")),
        P(("grp", "frame"), None, ("garm", "body")),
        P(("grp", "garm", "body")),
        P(("grp", "frame"), ("garm", "body"), None, None),
        P(("grp", "frame"), ("garm", "body"), None, None),
        P(("grp", "frame"), ("garm", "body"), None),
    )
    out_specs = (
        P(("grp", "frame"), None, ("garm", "body")),
        P(("grp", "frame"), None, ("garm", "body")),
        P(("grp", "garm", "body")),
    )
    return jax.shard_map(
        per_device, mesh=mesh, in_specs=in_specs, out_specs=out_specs, check_vma=False
    )
```
